32 devices in a mesh: group: 4 (over x, core), seq: 8 (over z, y).
Axes of the slice: x: 2, y: 2, z: 4, core: 2. Of those that a mesh axis runs over, the one named last changes fastest.
Arguments:
- source_short: bfloat16 [128, 128, 512], P(('group', 'seq')), may hold values from -6 to 6
- target_short: bfloat16 [128, 128, 512], P(('group', 'seq')), may hold values from -6 to 6
- source_segment: int32 [128, 128], P(('group', 'seq')), may hold values from 0 to 7, never falling along the last dimension, each value on 1 to 32 neighbouring positions
- target_segment: int32 [128, 128], P(('group', 'seq')), may hold values from 0 to 7, never falling along the last dimension, each value on 1 to 32 neighbouring positions
- source_long: bfloat16 [8, 1024, 512], P('group', 'seq'), may hold values from -6 to 6
- target_long: bfloat16 [8, 1024, 512], P('group', 'seq'), may hold values from -6 to 6
- source_length: int32 [8], P('group'), may hold values from 1 to 1024, as said below
- target_length: int32 [8], P('group'), may hold values from 1 to 1024, as said below
- cotangent_short: bfloat16 [128, 128, 512], P(('group', 'seq')), may hold values from -6 to 6
- cotangent_long: bfloat16 [8, 1024, 512], P('group', 'seq'), may hold values from -6 to 6
- encoder_project: bfloat16 [3, 512, 512], replicated, may hold values from -0.25 to 0.25
- encoder_output: bfloat16 [512, 512], replicated, may hold values from -1 to 1
- encoder_up: bfloat16 [512, 2048], replicated, may hold values from -0.25 to 0.25
- encoder_down: bfloat16 [2048, 512], replicated, may hold values from -0.125 to 0.125
- encoder_gain: float32 [2, 512], replicated, may hold values from 0.1 to 1.9
- encoder_bias: float32 [2, 512], replicated, may hold values from -3 to 3
- decoder_project: bfloat16 [3, 512, 512], replicated, may hold values from -0.25 to 0.25
- decoder_output: bfloat16 [512, 512], replicated, may hold values from -1 to 1
- cross_project: bfloat16 [3, 512, 512], replicated, may hold values from -0.25 to 0.25
- cross_output: bfloat16 [512, 512], replicated, may hold values from -1 to 1
- decoder_up: bfloat16 [512, 2048], replicated, may hold values from -0.25 to 0.25
- decoder_down: bfloat16 [2048, 512], replicated, may hold values from -0.125 to 0.125
- decoder_gain: float32 [3, 512], replicated, may hold values from 0.1 to 1.9
- decoder_bias: float32 [3, 512], replicated, may hold values from -3 to 3
Outputs:
- output_short: float32 [128, 128, 512], P(('group', 'seq'))
- output_long: float32 [8, 1024, 512], P('group', 'seq')
- grad_source_short: float32 [128, 128, 512], P(('group', 'seq'))
- grad_target_short: float32 [128, 128, 512], P(('group', 'seq'))
- grad_source_long: float32 [8, 1024, 512], P('group', 'seq')
- grad_target_long: float32 [8, 1024, 512], P('group', 'seq')
- grad_encoder_project: float32 [3, 512, 512], replicated
- grad_encoder_output: float32 [512, 512], replicated
- grad_encoder_up: float32 [512, 2048], replicated
- grad_encoder_down: float32 [2048, 512], replicated
- grad_encoder_gain: float32 [2, 512], replicated
- grad_encoder_bias: float32 [2, 512], replicated
- grad_decoder_project: float32 [3, 512, 512], replicated
- grad_decoder_output: float32 [512, 512], replicated
- grad_cross_project: float32 [3, 512, 512], replicated
- grad_cross_output: float32 [512, 512], replicated
- grad_decoder_up: float32 [512, 2048], replicated
- grad_decoder_down: float32 [2048, 512], replicated
- grad_decoder_gain: float32 [3, 512], replicated
- grad_decoder_bias: float32 [3, 512], replicated
The draws below stay inside these ranges and needn't reach their ends.
Inputs may be any that keep to these rules, and one draw needn't show every extreme that they name: `source_length`: each group's 2 source sequences (and likewise its target sequences) include one of exactly 1024 tokens; the others are shorter, most much shorter. `target_length`: each group's 2 target sequences include one of exactly 1024 tokens; the others are shorter, most much shorter. `source_segment`: every block holds each of the 8 sentence numbers, in rising runs of at most 32 positions. `target_segment`: as for source_segment.
All inputs are finite; a program needn't handle non-finite values.
Results may differ from the reference program's by a relative error of at most 0.04.
Values may be sent and summed in bfloat16 or wider, within the bound.
No kernel may reach another device: no remote copies, remote signals or barrier semaphores. Data moves between devices by JAX's collectives and lax.ppermute only.
A program may use at most 448 MiB of HBM per device.

```python
import math
import jax
import jax.numpy as jnp
import numpy as np
from jax import lax

D = 512
HEADS = 8
HEAD_DIM = 64
FF = 2048
LONG_PAIRS = 2
BLK = 128
SENTS = 8
SMAX = 32
LONG = 1024
LONG_SEQS = 8
SHORT_BLOCKS = 128


def long_lengths(key):
    key_one, key_two, key_three = jax.random.split(key, 3)
    loose_len = jnp.minimum(jax.random.randint(key_one, (LONG_SEQS,), 1, LONG + 1), jax.random.randint(key_two, (LONG_SEQS,), 1, LONG + 1))
    chosen = jax.random.randint(key_three, (LONG_SEQS // LONG_PAIRS,), 0, LONG_PAIRS)
    slot_index = jnp.arange(LONG_SEQS) % LONG_PAIRS
    group_of = jnp.arange(LONG_SEQS) // LONG_PAIRS
    return jnp.where(slot_index == chosen[group_of], LONG, loose_len).astype(jnp.int32)


def draw_source_length(key, part):
    key = jax.random.fold_in(key, 11)
    return long_lengths(key)


def draw_target_length(key, part):
    key = jax.random.fold_in(key, 12)
    return long_lengths(key)


def steps_of(rng, dims, pieces, low, high):
    loudness = 1.0
    for dim, blocks in pieces:
        draws = jax.random.uniform(jax.random.fold_in(jax.random.fold_in(rng, 6), dim), (blocks,), jnp.float32, low / len(pieces), high / len(pieces))
        loudness = loudness * jnp.repeat(jnp.exp(draws), dims[dim] // blocks).reshape((-1,) + (1,) * (len(dims) - 1 - dim))
    return loudness


def profile(number_of, total, bound, slope):
    weights = [(1 << 20) // math.isqrt(grade ** slope) + 1 for grade in range(2, number_of + 1)]
    surplus, holding = total - bound - (number_of - 1), [1] * (number_of - 1)
    while surplus > 0:
        movable = [i for i in range(number_of - 1) if holding[i] < bound]
        pool, budget = sum([weights[i] for i in movable]), surplus
        for i in movable:
            more = min(bound - holding[i], max(1, budget * weights[i] // pool), surplus)
            holding[i] = holding[i] + more
            surplus = surplus - more
    return np.array([bound] + holding)


def uneven(rng, count, total, most, slope):
    if count == 2:
        one = jax.random.randint(rng, (), max(1, total - most), min(most, total - 1) + 1)
        return jnp.stack([one, total - one])
    lengths = jnp.asarray(profile(count, total, most, slope), jnp.int32)
    couples = (count - 1) // 2
    source_of, sink = lengths[1:1 + 2 * couples:2], lengths[2:2 + 2 * couples:2]
    room = jnp.minimum(source_of - 1, most - sink)
    shifted = jax.random.randint(jax.random.fold_in(rng, 1), (couples,), 0, 1 << 20) % (room + 1)
    lengths = lengths.at[1:1 + 2 * couples:2].set(source_of - shifted).at[2:2 + 2 * couples:2].set(sink + shifted)
    return lengths[jax.random.permutation(jax.random.fold_in(rng, 2), count)]


def noise(rng, shape, scale, limit, cuts=(), kind=jnp.bfloat16):
    values = jax.random.normal(rng, shape, jnp.float32) * scale
    if len(cuts) > 0:
        values = steps_of(rng, shape, cuts, -0.22, 0.18) * values
    return jnp.clip(values, min=-limit, max=limit).astype(kind)


def setup_inputs(seed: int = 0) -> dict:
    seeds = jax.random.split(jax.random.key(seed), 25)
    return {
        "source_short": noise(seeds[0], (SHORT_BLOCKS, BLK, D), 1.0, 6.0, ((0, 32),)),
        "target_short": noise(seeds[1], (SHORT_BLOCKS, BLK, D), 1.0, 6.0, ((0, 32),)),
        "source_segment": jax.vmap(lambda own: jnp.searchsorted(jnp.cumsum(uneven(own, SENTS, BLK, SMAX, 2)), jnp.arange(BLK), side="right"))(jax.random.split(seeds[2], SHORT_BLOCKS)).reshape((SHORT_BLOCKS, BLK)).astype(jnp.int32),
        "target_segment": jax.vmap(lambda own: jnp.searchsorted(jnp.cumsum(uneven(own, SENTS, BLK, SMAX, 2)), jnp.arange(BLK), side="right"))(jax.random.split(seeds[3], SHORT_BLOCKS)).reshape((SHORT_BLOCKS, BLK)).astype(jnp.int32),
        "source_long": noise(seeds[4], (LONG_SEQS, LONG, D), 1.0, 6.0, ((0, 4), (1, 8))),
        "target_long": noise(seeds[5], (LONG_SEQS, LONG, D), 1.0, 6.0, ((0, 4), (1, 8))),
        "source_length": draw_source_length(jax.random.fold_in(seeds[24], 71), 0),
        "target_length": draw_target_length(jax.random.fold_in(seeds[24], 71), 0),
        "cotangent_short": noise(seeds[8], (SHORT_BLOCKS, BLK, D), 1.0, 6.0, ((0, 32),)),
        "cotangent_long": noise(seeds[9], (LONG_SEQS, LONG, D), 1.0, 6.0, ((0, 4), (1, 8))),
        "encoder_project": noise(seeds[10], (3, D, D), D ** -0.5, 0.25),
        "encoder_output": noise(seeds[11], (D, D), (D // 16) ** -0.5, 1.0),
        "encoder_up": noise(seeds[12], (D, FF), D ** -0.5, 0.25),
        "encoder_down": noise(seeds[13], (FF, D), FF ** -0.5, 0.125),
        "encoder_gain": jnp.clip(1.0 + 0.18 * jax.random.normal(seeds[14], (2, D), jnp.float32), 0.1, 1.9),
        "encoder_bias": noise(seeds[15], (2, D), 0.5, 3.0, (), jnp.float32),
        "decoder_project": noise(seeds[16], (3, D, D), D ** -0.5, 0.25),
        "decoder_output": noise(seeds[17], (D, D), (D // 16) ** -0.5, 1.0),
        "cross_project": noise(seeds[18], (3, D, D), D ** -0.5, 0.25),
        "cross_output": noise(seeds[19], (D, D), (D // 16) ** -0.5, 1.0),
        "decoder_up": noise(seeds[20], (D, FF), D ** -0.5, 0.25),
        "decoder_down": noise(seeds[21], (FF, D), FF ** -0.5, 0.125),
        "decoder_gain": jnp.clip(1.0 + 0.18 * jax.random.normal(seeds[22], (3, D), jnp.float32), 0.1, 1.9),
        "decoder_bias": noise(seeds[23], (3, D), 0.5, 3.0, (), jnp.float32),
    }


@jax.custom_vjp
def low(v):
    return lax.optimization_barrier(v.astype(jnp.bfloat16)).astype(jnp.float32)

@jax.custom_vjp
def low_back(v):
    return v

def low_keep(v):
    return (low(v), None)

def low_pass(kept, grad):
    return (grad,)

def back_keep(v):
    return (v, None)

def back_low(kept, grad):
    return (low(grad),)
low.defvjp(low_keep, low_pass)
low_back.defvjp(back_keep, back_low)
PRECISE = lax.Precision.HIGHEST
FLOOR_SCORE = -1e+30

def project_rows(rows, matrix):
    return jnp.einsum('bsd,de->bse', rows, matrix, precision=PRECISE)

def layer_norm(residual, gain_row, bias_row):
    centred = residual - lax.optimization_barrier(jnp.mean(residual, axis=-1, keepdims=True))
    variance = lax.optimization_barrier(jnp.mean(centred * centred, axis=-1, keepdims=True))
    return centred * lax.rsqrt(variance + 1e-05) * gain_row + bias_row

def attention(query_in, context_in, project, output_weight, allowed):
    batch_size, row_count, feature_count = query_in.shape
    key_count = context_in.shape[1]
    queries = low(low_back(project_rows(query_in, project[0]) * HEAD_DIM ** (-0.5))).reshape(batch_size, row_count, HEADS, HEAD_DIM)
    key_rows = low(low_back(project_rows(context_in, project[1]))).reshape(batch_size, key_count, HEADS, HEAD_DIM)
    value_rows = low(low_back(project_rows(context_in, project[2]))).reshape(batch_size, key_count, HEADS, HEAD_DIM)
    scores = low_back(jnp.einsum('bqhd,bkhd->bhqk', queries, key_rows, precision=PRECISE))
    scores = jnp.where(allowed[:, None], scores, FLOOR_SCORE)
    log_total = jax.nn.logsumexp(scores, axis=-1, keepdims=True)
    weights = low(jnp.exp(scores - log_total))
    mixed = jnp.einsum('bhqk,bkhd->bqhd', weights, value_rows, precision=PRECISE).reshape(batch_size, row_count, feature_count)
    return low_back(project_rows(low(low_back(mixed)), output_weight))

def feed_forward(normed, up_weight, down_weight):
    hidden = low_back(project_rows(low(normed), up_weight))
    return low_back(project_rows(low(jax.nn.silu(hidden)), down_weight))

def layer(source, target, encoder_mask, self_mask, cross_mask, params):
    encoder_project, encoder_output, encoder_up, encoder_down, encoder_gain, encoder_bias, decoder_project, decoder_output, cross_project, cross_output, decoder_up, decoder_down, decoder_gain, decoder_bias = params
    source_low = low(source)
    first = layer_norm(source + attention(source_low, source_low, encoder_project, encoder_output, encoder_mask), encoder_gain[0], encoder_bias[0])
    encoded = layer_norm(first + feed_forward(first, encoder_up, encoder_down), encoder_gain[1], encoder_bias[1])
    target_low = low(target)
    upper = layer_norm(target + attention(target_low, target_low, decoder_project, decoder_output, self_mask), decoder_gain[0], decoder_bias[0])
    middle = layer_norm(upper + attention(low(upper), low(encoded), cross_project, cross_output, cross_mask), decoder_gain[1], decoder_bias[1])
    return layer_norm(middle + feed_forward(middle, decoder_up, decoder_down), decoder_gain[2], decoder_bias[2])

def short_masks(source_seg, target_seg):
    causal = jnp.arange(BLK)[:, None] >= jnp.arange(BLK)[None, :]
    encoder_mask = source_seg[:, :, None] == source_seg[:, None, :]
    self_mask = (target_seg[:, :, None] == target_seg[:, None, :]) & causal[None]
    cross_mask = target_seg[:, :, None] == source_seg[:, None, :]
    return (encoder_mask, self_mask, cross_mask)

def long_masks(source_len, target_len):
    places = jnp.arange(LONG, dtype=jnp.int32)
    encoder_mask = jnp.broadcast_to((places[None, :] < source_len)[None], (1, LONG, LONG))
    self_mask = ((places[None, :] < target_len) & (places[None, :] <= places[:, None]))[None]
    return (encoder_mask, self_mask, encoder_mask)

def short_part(items, params):
    source, target, source_seg, target_seg = items
    encoder_mask, self_mask, cross_mask = short_masks(source_seg, target_seg)
    return layer(source, target, encoder_mask, self_mask, cross_mask, params)

def long_part(items, params):
    source, target, source_len, target_len = items
    encoder_mask, self_mask, cross_mask = long_masks(source_len, target_len)
    return layer(source[None], target[None], encoder_mask, self_mask, cross_mask, params)[0]

def reference(source_short, target_short, source_segment, target_segment, source_long, target_long, source_length, target_length, cotangent_short, cotangent_long, encoder_project, encoder_output, encoder_up, encoder_down, encoder_gain, encoder_bias, decoder_project, decoder_output, cross_project, cross_output, decoder_up, decoder_down, decoder_gain, decoder_bias):
    blocks = source_short.shape[0]
    per_step = math.gcd(blocks, 32)
    steps = blocks // per_step
    short_checked = jax.checkpoint(short_part)
    long_checked = jax.checkpoint(long_part)

    def forward(src_rows, tgt_rows, src_seq, tgt_seq, *params):

        def run_short(items):
            return short_checked(items, params)

        def run_long(items):
            return long_checked(items, params)
        out_short = lax.map(run_short, (src_rows.reshape(steps, per_step, BLK, D), tgt_rows.reshape(steps, per_step, BLK, D), source_segment.reshape(steps, per_step, BLK), target_segment.reshape(steps, per_step, BLK)))
        out_long = lax.map(run_long, (src_seq, tgt_seq, source_length, target_length))
        return (out_short.reshape(blocks, BLK, D), out_long)
    weights_in = (encoder_project, encoder_output, encoder_up, encoder_down, encoder_gain, encoder_bias, decoder_project, decoder_output, cross_project, cross_output, decoder_up, decoder_down, decoder_gain, decoder_bias)
    primals = (source_short.astype(jnp.float32), target_short.astype(jnp.float32), source_long.astype(jnp.float32), target_long.astype(jnp.float32)) + tuple((weight.astype(jnp.float32) for weight in weights_in))
    outputs, pull = jax.vjp(forward, *primals)
    grads = pull((cotangent_short.astype(jnp.float32), cotangent_long.astype(jnp.float32)))
    return (outputs[0], outputs[1], grads[0], grads[1], grads[2], grads[3], grads[4], grads[5], grads[6], grads[7], grads[8], grads[9], grads[10], grads[11], grads[12], grads[13], grads[14], grads[15], grads[16], grads[17])
```

```python
import functools
import random
import jax
import jax.numpy as jnp
from jax import lax
from jax.experimental import pallas as pl
from jax.experimental.pallas import tpu as pltpu
from jax.sharding import Mesh, PartitionSpec as P

HEADS = 8
HEAD_DIM = 64
PAIR = 2 * HEAD_DIM
PAIRS = HEADS // 2
SCALE = HEAD_DIM**-0.5
FLOOR_SCORE = -1e30
EPSILON = 1e-05
KEY_BLOCK = 256
CHUNK = 512
F32 = jnp.float32
BF16 = jnp.bfloat16
CORE, X, INNER, OUTER = "core", "x", "inner", "outer"


def nn(left, right):
    return lax.dot_general(left, right, (((1,), (0,)), ((), ())), preferred_element_type=F32)


def nt(left, right):
    return lax.dot_general(left, right, (((1,), (1,)), ((), ())), preferred_element_type=F32)


def tn(left, right):
    return lax.dot_general(left, right, (((0,), (0,)), ((), ())), preferred_element_type=F32)


def two_heads(rows):
    lane = lax.broadcasted_iota(jnp.int32, rows.shape, 1)
    zero = jnp.zeros_like(rows)
    first = jnp.where(lane < HEAD_DIM, rows, zero)
    second = jnp.where(lane < HEAD_DIM, zero, rows)
    return jnp.concatenate([first, second], axis=0)


def diagonal(product):
    half = product.shape[1] // 2
    return jnp.concatenate([product[:HEAD_DIM, :half], product[HEAD_DIM:, half:]], axis=0)


def delta_rows(grad_out, outputs):
    product = grad_out.astype(F32) * outputs.astype(F32)
    high = product.astype(BF16)
    low = (product - high.astype(F32)).astype(BF16)
    width = product.shape[1]
    head = lax.broadcasted_iota(jnp.int32, (HEADS, width), 0)
    lane = lax.broadcasted_iota(jnp.int32, (HEADS, width), 1)
    pick = jnp.where(lax.div(lane, HEAD_DIM) == head, 1.0, 0.0).astype(BF16)
    return nt(pick, high) + nt(pick, low)


def pair_row(rows, pair):
    return jnp.concatenate([rows[2 * pair : 2 * pair + 1], rows[2 * pair + 1 : 2 * pair + 2]], axis=1)


def pair_lanes(pair):
    return slice(pair * PAIR, (pair + 1) * PAIR)


def norm(residual, gain, bias):
    centred = residual - jnp.mean(residual, axis=1, keepdims=True)
    inverse = lax.rsqrt(jnp.mean(centred * centred, axis=1, keepdims=True) + EPSILON)
    normed = centred * inverse
    return normed * gain + bias, normed, inverse


def norm_back(upstream, normed, inverse, gain):
    normed = normed.astype(F32)
    scaled = upstream * gain
    grad = inverse * (
        scaled
        - jnp.mean(scaled, axis=1, keepdims=True)
        - normed * jnp.mean(scaled * normed, axis=1, keepdims=True)
    )
    return (
        grad,
        jnp.sum(upstream * normed, axis=0, keepdims=True),
        jnp.sum(upstream, axis=0, keepdims=True),
    )


def feed_forward(rows, up_ref, down_ref, act_ref, gate_ref):
    low = rows.astype(BF16)
    total = rows
    for start in range(0, up_ref.shape[1], CHUNK):
        part = slice(start, start + CHUNK)
        hidden = nn(low, up_ref[:, part])
        sigmoid = 0.5 * jnp.tanh(0.5 * hidden) + 0.5
        active = hidden * sigmoid
        gate_ref[:, part] = (sigmoid + active * (1.0 - sigmoid)).astype(BF16)
        active = active.astype(BF16)
        act_ref[:, part] = active
        total = total + nn(active, down_ref[part, :])
    return low, total


def feed_back(grad, gate_ref, up_ref, down_ref, hidden_grad_ref):
    low = grad.astype(BF16)
    total = grad
    for start in range(0, up_ref.shape[1], CHUNK):
        part = slice(start, start + CHUNK)
        hidden = nt(low, down_ref[part, :]) * gate_ref[:, part].astype(F32)
        hidden = hidden.astype(BF16)
        hidden_grad_ref[:, part] = hidden
        total = total + nt(hidden, up_ref[:, part])
    return low, total


def short_allowed(key_segment, query_segment, causal):
    allowed = key_segment == query_segment
    if causal:
        key = lax.broadcasted_iota(jnp.int32, key_segment.shape, 0)
        query = lax.broadcasted_iota(jnp.int32, key_segment.shape, 1)
        allowed = allowed & (key <= query)
    return jnp.concatenate([allowed, allowed], axis=1)


def short_attend(causal, q_ref, k_ref, v_ref, kseg_ref, qseg_ref, o_ref, lse_ref):
    size = kseg_ref.shape[1]
    for block in range(kseg_ref.shape[0]):
        rows = slice(block * size, (block + 1) * size)
        allowed = short_allowed(kseg_ref[block], qseg_ref[block], causal)
        logs = []
        for pair in range(PAIRS):
            lanes = pair_lanes(pair)
            scores = nt(k_ref[rows, lanes], two_heads(q_ref[rows, lanes]))
            scores = jnp.where(allowed, scores, FLOOR_SCORE)
            top = jnp.max(scores, axis=0, keepdims=True)
            weights = jnp.exp(scores - top)
            total = jnp.sum(weights, axis=0, keepdims=True)
            mixed = nn(v_ref[rows, lanes].T, weights.astype(BF16)) / total
            o_ref[rows, lanes] = diagonal(mixed).T.astype(BF16)
            log_total = top + jnp.log(total)
            logs += [log_total[:, :size], log_total[:, size:]]
        lse_ref[block] = jnp.concatenate(logs, axis=0)


def short_attend_back(
    causal, q_ref, k_ref, v_ref, kseg_ref, qseg_ref, o_ref, lse_ref, go_ref, dq_ref, dk_ref, dv_ref
):
    size = kseg_ref.shape[1]
    for block in range(kseg_ref.shape[0]):
        rows = slice(block * size, (block + 1) * size)
        allowed = short_allowed(kseg_ref[block], qseg_ref[block], causal)
        delta = delta_rows(go_ref[rows, :], o_ref[rows, :])
        lse = lse_ref[block]
        for pair in range(PAIRS):
            lanes = pair_lanes(pair)
            queries, grads = two_heads(q_ref[rows, lanes]), two_heads(go_ref[rows, lanes])
            scores = nt(k_ref[rows, lanes], queries)
            weights = jnp.where(allowed, jnp.exp(scores - pair_row(lse, pair)), 0.0)
            grad_weights = nt(v_ref[rows, lanes], grads)
            grad_scores = (weights * (grad_weights - pair_row(delta, pair))).astype(BF16)
            dv_ref[rows, lanes] = nn(weights.astype(BF16), grads).astype(BF16)
            dk_ref[rows, lanes] = nn(grad_scores, queries).astype(BF16)
            turned = diagonal(nn(k_ref[rows, lanes].T, grad_scores)).T
            dq_ref[rows, lanes] = (turned.astype(BF16).astype(F32) * SCALE).astype(BF16)


def load_keys(ref, pair_index, block, lanes):
    pieces = KEY_BLOCK // ref.shape[2]
    rows = ref[pl.ds(block * pieces, pieces), pair_index, :, lanes]
    return rows.reshape(KEY_BLOCK, rows.shape[2])


def store_keys(ref, pair_index, block, lanes, rows):
    pieces = KEY_BLOCK // ref.shape[2]
    ref[pl.ds(block * pieces, pieces), pair_index, :, lanes] = rows.astype(BF16).reshape(
        pieces, ref.shape[2], rows.shape[1]
    )


def store_part(ref, info_ref, pair_index, block, rows):
    partners, _, pairs, size, _ = ref.shape
    for piece in range(KEY_BLOCK // size):
        place = block * (KEY_BLOCK // size) + piece
        inner = lax.rem(place, partners) ^ info_ref[pairs + 1]
        outer = lax.div(place, partners) ^ info_ref[pairs + 3]
        ref[inner, outer, pair_index] = rows[piece * size : (piece + 1) * size]


def long_limit(info_ref, causal, pair_index, size, pairs):
    length = info_ref[pair_index]
    limit = length
    if causal:
        limit = jnp.minimum(length, info_ref[pairs] + size)
    return length, lax.div(limit + KEY_BLOCK - 1, KEY_BLOCK)


def long_allowed(start, causal, length, block, shape):
    key = lax.broadcasted_iota(jnp.int32, shape, 0) + block * KEY_BLOCK
    allowed = key < length
    if causal:
        half = shape[1] // 2
        lane = lax.broadcasted_iota(jnp.int32, shape, 1)
        query = jnp.where(lane < half, lane, lane - half) + start
        allowed = allowed & (key <= query)
    return allowed


def long_attend(
    causal, info_ref, q_ref, x_ref, k_w, v_w, k_ref, v_ref, o_ref, lse_ref, score_ref, sum_ref, mix_ref
):
    places, pairs, size, width = x_ref.shape
    shape = (KEY_BLOCK, 2 * size)
    everything = slice(None)

    def one(pair_index, carry):
        length, count = long_limit(info_ref, causal, pair_index, size, pairs)
        own = pl.ds(pl.multiple_of(pair_index * size, size), size)

        def first(block, tops):
            rows = pl.ds(pl.multiple_of(block * KEY_BLOCK, KEY_BLOCK), KEY_BLOCK)
            allowed = long_allowed(info_ref[pairs], causal, length, block, shape)
            context = load_keys(x_ref, pair_index, block, everything)
            store_keys(k_ref, pair_index, block, everything, nn(context, k_w[...]))
            store_keys(v_ref, pair_index, block, everything, nn(context, v_w[...]))
            after = []
            for pair in range(PAIRS):
                lanes = pair_lanes(pair)
                keys = load_keys(k_ref, pair_index, block, lanes)
                scores = nt(keys, two_heads(q_ref[own, lanes]))
                scores = jnp.where(allowed, scores, FLOOR_SCORE)
                score_ref[pair, rows] = scores
                folded = jnp.max(scores.reshape(KEY_BLOCK // 8, 8, 2 * size), axis=0)
                after.append(jnp.maximum(tops[pair], folded))
            return tuple(after)

        start = tuple(jnp.full((8, 2 * size), FLOOR_SCORE, F32) for _ in range(PAIRS))
        tops = lax.fori_loop(0, count, first, start)
        tops = [jnp.max(top, axis=0, keepdims=True) for top in tops]
        sum_ref[...] = jnp.zeros_like(sum_ref)
        mix_ref[...] = jnp.zeros_like(mix_ref)

        def second(block, carry):
            rows = pl.ds(pl.multiple_of(block * KEY_BLOCK, KEY_BLOCK), KEY_BLOCK)
            for pair in range(PAIRS):
                weights = jnp.exp(score_ref[pair, rows] - tops[pair])
                sum_ref[pair] += jnp.sum(weights.reshape(KEY_BLOCK // 8, 8, 2 * size), axis=0)
                values = load_keys(v_ref, pair_index, block, pair_lanes(pair))
                mix_ref[pair] += nn(values.T, weights.astype(BF16))
            return carry

        lax.fori_loop(0, count, second, 0)
        logs = []
        for pair in range(PAIRS):
            total = jnp.sum(sum_ref[pair], axis=0, keepdims=True)
            mixed = mix_ref[pair] / total
            o_ref[own, pair_lanes(pair)] = diagonal(mixed).T.astype(BF16)
            log_total = tops[pair] + jnp.log(total)
            logs += [log_total[:, :size], log_total[:, size:]]
        lse_ref[pair_index] = jnp.concatenate(logs, axis=0)
        return carry

    lax.fori_loop(0, pairs, one, 0)


def long_attend_back(
    causal,
    info_ref,
    q_ref,
    k_ref,
    v_ref,
    o_ref,
    lse_ref,
    go_ref,
    k_w,
    v_w,
    dq_ref,
    dk_ref,
    dv_ref,
    part_ref,
    mix_ref,
):
    places, pairs, size, width = k_ref.shape
    shape = (KEY_BLOCK, 2 * size)
    everything = slice(None)

    def one(pair_index, carry):
        length, count = long_limit(info_ref, causal, pair_index, size, pairs)
        own = pl.ds(pl.multiple_of(pair_index * size, size), size)
        delta = delta_rows(go_ref[own, :], o_ref[own, :])
        lse = lse_ref[pair_index]
        mix_ref[...] = jnp.zeros_like(mix_ref)

        def step(block, carry):
            allowed = long_allowed(info_ref[pairs], causal, length, block, shape)
            for pair in range(PAIRS):
                lanes = pair_lanes(pair)
                queries, grads = two_heads(q_ref[own, lanes]), two_heads(go_ref[own, lanes])
                keys = load_keys(k_ref, pair_index, block, lanes)
                scores = nt(keys, queries)
                weights = jnp.where(allowed, jnp.exp(scores - pair_row(lse, pair)), 0.0)
                grad_weights = nt(load_keys(v_ref, pair_index, block, lanes), grads)
                grad_scores = (weights * (grad_weights - pair_row(delta, pair))).astype(BF16)
                store_keys(dv_ref, pair_index, block, lanes, nn(weights.astype(BF16), grads))
                store_keys(dk_ref, pair_index, block, lanes, nn(grad_scores, queries))
                mix_ref[pair] += nn(keys.T, grad_scores)
            part = nt(load_keys(dk_ref, pair_index, block, everything), k_w[...])
            part = part + nt(load_keys(dv_ref, pair_index, block, everything), v_w[...])
            store_part(part_ref, info_ref, pair_index, block, part.astype(BF16))
            return carry

        lax.fori_loop(0, count, step, 0)

        def clear(block, carry):
            nothing = jnp.zeros((KEY_BLOCK, width), BF16)
            store_keys(dk_ref, pair_index, block, everything, nothing)
            store_keys(dv_ref, pair_index, block, everything, nothing)
            store_part(part_ref, info_ref, pair_index, block, nothing)
            return carry

        lax.fori_loop(count, places * size // KEY_BLOCK, clear, 0)
        for pair in range(PAIRS):
            turned = diagonal(mix_ref[pair]).T
            dq_ref[own, pair_lanes(pair)] = (turned.astype(BF16).astype(F32) * SCALE).astype(BF16)
        return carry

    lax.fori_loop(0, pairs, one, 0)


class Refs(dict):
    def __init__(self, *args):
        super().__init__(*args)
        self.coming, self.leaving = {}, {}

    def __getattr__(self, name):
        if name in self.coming:
            self.coming.pop(name).wait()
        return self[name]

    def leave(self, *names):
        for name in names:
            self["left"].add(name)
            for copy in self.leaving.get(name, ()):
                copy.start()


def copied(shape, dtype):
    size = dtype.itemsize
    for length in shape:
        size *= length
    return shape[-1] % 128 == 0 and size >= 2**16


def launch(body, arrays, gives, scratch=(), info=None, after=(), pieces=(), plain=False, cost=10):
    memory = pl.BlockSpec(memory_space=pltpu.VMEM)
    far = pl.BlockSpec(memory_space=pl.ANY)
    ins, specs = [], []
    if info is not None:
        ins.append(info)
        specs.append(pl.BlockSpec(memory_space=pltpu.SMEM))
    moved_in = [
        name for name, array in arrays.items() if not plain and copied(array.shape, array.dtype)
    ]
    moved_out = [
        name
        for name, (shape, dtype) in gives.items()
        if name in pieces or not plain and copied(shape, jnp.dtype(dtype))
    ]
    for name, array in arrays.items():
        ins.append(array)
        specs.append(far if name in moved_in else memory)
    for array in after:
        ins.append(array)
        specs.append(far)
    count_out = sum(gives[name][0][0] if name in pieces else 1 for name in moved_out)
    rooms = [pltpu.VMEM(arrays[name].shape, arrays[name].dtype) for name in moved_in]
    rooms += [pltpu.VMEM(*gives[name]) for name in moved_out]
    rooms += [pltpu.SemaphoreType.DMA((max(len(moved_in), 1),))]
    rooms += [pltpu.SemaphoreType.DMA((max(count_out, 1),))]
    names = [name for name, _ in scratch]

    def run(*refs):
        refs = list(refs)
        r = Refs()
        if info is not None:
            r["info"] = refs.pop(0)
        outer = {name: refs.pop(0) for name in arrays}
        del refs[: len(after)]
        outer.update((name, refs.pop(0)) for name in gives)
        room = {name: refs.pop(0) for name in moved_in + moved_out}
        come, go = refs.pop(0), refs.pop(0)
        r.update(outer)
        r.update(room)
        r.update(zip(names, refs))
        for place, name in enumerate(moved_in):
            copy = pltpu.make_async_copy(outer[name], room[name], come.at[place])
            copy.start()
            r.coming[name] = copy
        place = 0
        for name in moved_out:
            copies = []
            if name in pieces:
                for piece in range(gives[name][0][0]):
                    source, target = room[name].at[piece], outer[name].at[piece]
                    copies.append(pltpu.make_async_copy(source, target, go.at[place]))
                    place += 1
            else:
                copies.append(pltpu.make_async_copy(room[name], outer[name], go.at[place]))
                place += 1
            r.leaving[name] = copies
        left = set()
        r["left"] = left
        body(r)
        for name in list(r.coming):
            r.coming.pop(name).wait()
        for name in moved_out:
            if name not in left and name not in pieces:
                r.leave(name)
        for name in moved_out:
            for copy in r.leaving[name]:
                copy.wait()

    out = pl.pallas_call(
        run,
        in_specs=specs,
        out_specs=[far if name in moved_out else memory for name in gives],
        out_shape=[jax.ShapeDtypeStruct(shape, dtype) for shape, dtype in gives.values()],
        scratch_shapes=rooms + [shape for _, shape in scratch],
        compiler_params=pltpu.CompilerParams(vmem_limit_bytes=VMEM_LIMIT),
        cost_estimate=pl.CostEstimate(
            flops=int(cost * 1.1e9), bytes_accessed=int(cost * 3.5e6), transcendentals=0
        ),
    )(*ins)
    return Refs(zip(gives, out))


VMEM_LIMIT = 56 * 2**20


def add_sums(ref, rows):
    ref[...] = jnp.concatenate(rows, axis=0)


def encoder_tail(r, o_ref):
    residual = r.x[...].astype(F32) + nn(o_ref[...], r.w_o[...])
    first, normed, inverse = norm(residual, r.gain[0:1], r.bias[0:1])
    r.n1[...] = normed.astype(BF16)
    r.i1[...] = inverse
    low, total = feed_forward(first, r.up, r.down, r.act, r.gate)
    r.y[...] = low
    r.leave("n1", "act", "gate", "y")
    encoded, normed, inverse = norm(total, r.gain[1:2], r.bias[1:2])
    r.n2[...] = normed.astype(BF16)
    r.i2[...] = inverse
    r.enc[...] = encoded.astype(BF16)


def project_short(r, name, rows, w_q, w_k, w_v, context=None):
    context = rows if context is None else context
    r["q" + name][...] = (nn(rows, w_q) * SCALE).astype(BF16)
    r["k" + name][...] = nn(context, w_k).astype(BF16)
    r["v" + name][...] = nn(context, w_v).astype(BF16)


def short_encoder_forward(r):
    project_short(r, "", r.x[...], r.w_in[0], r.w_in[1], r.w_in[2])
    r.leave("q", "k", "v")
    short_attend(False, r.q, r.k, r.v, r.kseg, r.qseg, r.o, r.lse)
    r.leave("o")
    encoder_tail(r, r.o)


def decoder_middle(r, o_ref):
    residual = r.t[...].astype(F32) + nn(o_ref[...], r.w_o[...])
    upper, normed, inverse = norm(residual, r.gain[0:1], r.bias[0:1])
    r.n3[...] = normed.astype(BF16)
    r.i3[...] = inverse
    r.u[...] = upper.astype(BF16)
    return upper


def decoder_tail(r, upper, o_ref):
    gain, bias = r.gain, r.bias
    residual = upper + nn(o_ref[...], r.w_co[...])
    middle, normed4, inverse4 = norm(residual, gain[1:2], bias[1:2])
    low, total = feed_forward(middle, r.up, r.down, r.act, r.gate)
    r.m[...] = low
    r.leave("m", "act", "gate")
    final, normed5, inverse5 = norm(total, gain[2:3], bias[2:3])
    r.final[...] = final
    r.leave("final")
    grad, gain5, bias5 = norm_back(r.cot[...].astype(F32), normed5, inverse5, gain[2:3])
    low, grad = feed_back(grad, r.gate, r.up, r.down, r.dh)
    r.b5[...] = low
    r.leave("b5", "dh")
    grad, gain4, bias4 = norm_back(grad, normed4, inverse4, gain[1:2])
    low = grad.astype(BF16)
    r.b4[...] = low
    r.d4[...] = grad
    r.go_c[...] = nt(low, r.w_co[...]).astype(BF16)
    add_sums(r.small, [gain4, gain5, bias4, bias5])


def short_decoder_forward(r):
    project_short(r, "", r.t[...], r.w_in[0], r.w_in[1], r.w_in[2])
    r.leave("q", "k", "v")
    short_attend(True, r.q, r.k, r.v, r.tkseg, r.tqseg, r.o, r.lse)
    r.leave("o")
    r.upper[...] = decoder_middle(r, r.o)


def short_cross_forward(r):
    project_short(r, "_c", r.u[...], r.w_cin[0], r.w_cin[1], r.w_cin[2], r.enc[...])
    r.leave("q_c", "k_c", "v_c")
    short_attend(False, r.q_c, r.k_c, r.v_c, r.kseg, r.tqseg, r.o_c, r.lse_c)
    r.leave("o_c")
    decoder_tail(r, r.upper[...], r.o_c)


def decoder_middle_back(r):
    grad = r.d4[...] + nt(r.dq_c[...], r.w_cin[0])
    grad, gain3, bias3 = norm_back(grad, r.n3[...], r.i3[...], r.gain[0:1])
    low = grad.astype(BF16)
    r.b3[...] = low
    r.go[...] = nt(low, r.w_o[...]).astype(BF16)
    add_sums(r.small, [gain3, bias3])
    return grad


def short_decoder_back(r):
    short_attend_back(
        False, r.q_c, r.k_c, r.v_c, r.kseg, r.tqseg, r.o_c, r.lse_c, r.go_c, r.dq_c, r.dk_c, r.dv_c
    )
    r.denc[...] = nt(r.dk_c[...], r.w_cin[1]) + nt(r.dv_c[...], r.w_cin[2])
    r.leave("dq_c", "dk_c", "dv_c", "denc")
    r.d3[...] = decoder_middle_back(r)
    short_attend_back(
        True, r.q, r.k, r.v, r.tkseg, r.tqseg, r.o, r.lse, r.go, r.dq, r.dk, r.dv
    )
    r.leave("dq", "dk", "dv")
    grad = r.d3[...] + nt(r.dq[...], r.w_in[0])
    r.dt[...] = grad + nt(r.dk[...], r.w_in[1]) + nt(r.dv[...], r.w_in[2])


def encoder_tail_back(r, grad):
    grad, gain2, bias2 = norm_back(grad, r.n2[...], r.i2[...], r.gain[1:2])
    low, grad = feed_back(grad, r.gate, r.up, r.down, r.dh)
    r.b2[...] = low
    r.leave("b2", "dh")
    grad, gain1, bias1 = norm_back(grad, r.n1[...], r.i1[...], r.gain[0:1])
    low = grad.astype(BF16)
    r.b1[...] = low
    r.go[...] = nt(low, r.w_o[...]).astype(BF16)
    r.d1[...] = grad
    add_sums(r.small, [gain1, gain2, bias1, bias2])


def short_encoder_back(r):
    encoder_tail_back(r, r.denc[...])
    short_attend_back(
        False, r.q, r.k, r.v, r.kseg, r.qseg, r.o, r.lse, r.go, r.dq, r.dk, r.dv
    )
    r.leave("dq", "dk", "dv")
    grad = r.d1[...] + nt(r.dq[...], r.w_in[0])
    r.dx[...] = grad + nt(r.dk[...], r.w_in[1]) + nt(r.dv[...], r.w_in[2])


def long_encoder_forward(r):
    r.q[...] = (nn(r.x[...], r.w_in[0]) * SCALE).astype(BF16)
    long_attend(
        False, r.info, r.q, r.xg, r.w_in.at[1], r.w_in.at[2], r.k, r.v, r.o, r.lse, r.s, r.a, r.mix
    )
    r.leave("q", "k", "v", "o")
    encoder_tail(r, r.o)


def long_self_forward(r):
    r.q[...] = (nn(r.t[...], r.w_in[0]) * SCALE).astype(BF16)
    long_attend(
        True, r.info, r.q, r.tg, r.w_in.at[1], r.w_in.at[2], r.k, r.v, r.o, r.lse, r.s, r.a, r.mix
    )
    r.leave("q", "k", "v", "o")
    upper = decoder_middle(r, r.o)
    r.upper[...] = upper
    r.q_c[...] = (nn(upper.astype(BF16), r.w_cin[0]) * SCALE).astype(BF16)


def long_cross(r):
    k_w, v_w = r.w_cin.at[1], r.w_cin.at[2]
    long_attend(
        False, r.info, r.q_c, r.eg, k_w, v_w, r.k_c, r.v_c, r.o_c, r.lse_c, r.s, r.a, r.mix
    )
    r.leave("k_c", "v_c", "o_c")
    decoder_tail(r, r.upper[...], r.o_c)


def long_cross_back(r):
    long_attend_back(
        False,
        r.info,
        r.q_c,
        r.k_c,
        r.v_c,
        r.o_c,
        r.lse_c,
        r.go_c,
        r.w_cin.at[1],
        r.w_cin.at[2],
        r.dq_c,
        r.dk_c,
        r.dv_c,
        r.part,
        r.mix,
    )


def long_self_back(r):
    grad = decoder_middle_back(r)
    long_attend_back(
        True,
        r.info,
        r.q,
        r.k,
        r.v,
        r.o,
        r.lse,
        r.go,
        r.w_in.at[1],
        r.w_in.at[2],
        r.dq,
        r.dk,
        r.dv,
        r.part,
        r.mix,
    )
    r.dt[...] = grad + nt(r.dq[...], r.w_in[0])


def long_encoder_tail_back(r):
    grad = r.part0[...].astype(F32) + r.part1[...].astype(F32)
    grad = grad + r.part2[...].astype(F32) + r.part3[...].astype(F32)
    encoder_tail_back(r, grad)


def long_encoder_back(r):
    long_attend_back(
        False,
        r.info,
        r.q,
        r.k,
        r.v,
        r.o,
        r.lse,
        r.go,
        r.w_in.at[1],
        r.w_in.at[2],
        r.dq,
        r.dk,
        r.dv,
        r.part,
        r.mix,
    )
    r.dx[...] = r.d1[...] + nt(r.dq[...], r.w_in[0])


SIDE = 512


class Weights:
    def __init__(self, pairs):
        self.arrays, self.plan, known = {}, [], {}

        def place(rows):
            if isinstance(rows, tuple):
                return rows
            if id(rows) not in known:
                known[id(rows)] = "w%d" % len(known)
                self.arrays[known[id(rows)]] = rows
            return known[id(rows)], rows.shape[1]

        for terms in pairs:
            terms = [(place(a), place(b)) for a, b in terms]
            (_, height), (_, width) = terms[0]
            for row in range(0, height, SIDE):
                for column in range(0, width, SIDE):
                    self.plan.append([(a[0], row, b[0], column) for a, b in terms])
        count = len(self.plan)
        self.gives = {name: ((count, SIDE // 2, SIDE), BF16) for name in ("kept", "sent")}

    def body(self, r, core):
        half = SIDE // 2
        for index, terms in enumerate(self.plan):
            for flip, name in enumerate(("kept", "sent")):
                total = None
                for a, row, b, column in terms:
                    left, right = getattr(r, a), getattr(r, b)
                    begin = pl.multiple_of(row + (core ^ flip) * half, half)
                    across = slice(column, column + SIDE)
                    if len(left.shape) == 4:
                        tall = left.shape[0] * left.shape[1] * left.shape[2]
                        rows = left[:, :, :, pl.ds(begin, half)].reshape(tall, half)
                    else:
                        rows = left[:, pl.ds(begin, half)]
                    if len(right.shape) == 4:
                        tall = right.shape[0] * right.shape[1] * right.shape[2]
                        product = tn(rows, right[:, :, :, across].reshape(tall, SIDE))
                    else:
                        product = tn(rows, right[:, across])
                    total = product if total is None else total + product
                r[name][index] = total.astype(BF16)
                r.leaving[name][index].start()


def weight_tiles(pairs, core_info, after=(), cost=10):
    weights = Weights(pairs)
    out = launch(
        lambda r: weights.body(r, r.info[0]),
        weights.arrays,
        weights.gives,
        info=core_info,
        after=after,
        pieces=("kept", "sent"),
        cost=cost,
    )
    return [out.kept, out.sent]


def send(piece, axis, offset):
    count = lax.axis_size(axis)
    return lax.ppermute(piece, axis, [(i, i ^ offset) for i in range(count)])


def ordered(pieces, place, dim):
    if len(pieces) == 1:
        return pieces[0]
    level = len(pieces) // 2
    inside = lax.rem(place, level)
    low = ordered(pieces[:level], inside, dim)
    high = ordered(pieces[level:], inside, dim)
    return jnp.where(
        place >= level, jnp.concatenate([high, low], dim), jnp.concatenate([low, high], dim)
    )


def hold(value, token):
    return lax.optimization_barrier((value, token))[0]


def gather_first(piece, axis):
    return [piece] + [send(piece, axis, k) for k in range(1, lax.axis_size(axis))]


def gather_last(pieces, axis, dim, token=None):
    if token is not None:
        pieces = hold(pieces, token)
    return ordered(pieces, lax.axis_index(axis), dim)


def added(pieces):
    total = pieces[0].astype(F32)
    for piece in pieces[1:]:
        total = total + piece.astype(F32)
    return total.astype(BF16)


def scatter_step(pending, axis, dim, token=None):
    if token is not None:
        pending = hold(pending, token)
    place, count = lax.axis_index(axis), lax.axis_size(axis)
    size = pending[0].shape[dim] // count
    after = []
    for k in range(count):
        parts = [
            lax.dynamic_slice_in_dim(piece, (place ^ k) * size, size, dim) for piece in pending
        ]
        block = added(parts)
        after.append(send(block, axis, k) if k else block)
    return after


def gather_step(piece, axis, dim):
    return gather_last(gather_first(piece, axis), axis, dim)


def gather_early(rows):
    return lax.all_gather(rows, (OUTER, INNER), axis=0, tiled=False)


SEQ = (OUTER, INNER)


class Chain:
    def __init__(self, halves, order, small=None, doubled=False):
        self.order = (CORE,) + order
        self.doubled = doubled
        self.stage = 0
        self.tiles = halves[0].shape[0]
        self.small, self.carried = None, 0
        if small is not None:
            self.carried = small.shape[0]
            halves = [jnp.concatenate([self.flat(half), small]) for half in halves]
        self.held = [halves[0], send(halves[1], CORE, 1)]

    def flat(self, block):
        return block.reshape(-1, block.shape[-1])

    def parts(self):
        if not self.carried:
            return self.held, None
        body = [piece[: -self.carried] for piece in self.held]
        body = [piece.reshape(self.tiles, -1, piece.shape[-1]) for piece in body]
        return body, added([piece[-self.carried :] for piece in self.held])

    def next_axis(self):
        stage, count = self.stage + 1, len(self.order)
        return self.order[stage] if stage < count else self.order[2 * count - 1 - stage]

    def over(self):
        return self.stage == 2 * len(self.order) - 1

    def go(self):
        axis = self.next_axis()
        self.stage += 1
        count = len(self.order)
        if self.doubled and self.stage in (count - 1, count):
            total = added(self.held)
            self.held = [total, send(total, OUTER, self.stage - count + 2)]
            return
        if self.doubled and self.stage == count + 1:
            pending, self.small = self.parts()
            self.held = gather_first(added(pending), axis)
            return
        if self.stage < count:
            pending, small = self.parts()
            place, members = lax.axis_index(axis), lax.axis_size(axis)
            size = pending[0].shape[1] // members
            self.held = []
            for k in range(members):
                begin = (place ^ k) * size
                block = added([lax.dynamic_slice_in_dim(p, begin, size, 1) for p in pending])
                if small is not None:
                    block = jnp.concatenate([self.flat(block), small])
                self.held.append(send(block, axis, k) if k else block)
            return
        if self.stage == count:
            pending, self.small = self.parts()
            piece = added(pending)
        else:
            piece = gather_last(self.held, self.order[2 * count - self.stage], 1)
        self.held = gather_first(piece, axis)

    def volume(self):
        return self.held[0].size * 2 / 2**20


class Spread:
    def __init__(self, part, straight):
        self.straight, self.stage = straight, 0
        self.held = [send(part[k], INNER, k) if k else part[k] for k in range(part.shape[0])]

    def next_axis(self):
        return OUTER

    def over(self):
        return self.stage == (1 if self.straight else 2)

    def go(self):
        self.stage += 1
        if self.straight:
            blocks = [added([piece[k] for piece in self.held]) for k in range(4)]
            self.held = [send(block, OUTER, k) if k else block for k, block in enumerate(blocks)]
            return
        if self.stage == 1:
            pick, offset = (lambda piece, odd: jnp.stack([piece[odd], piece[2 + odd]])), 1
        else:
            pick, offset = (lambda piece, odd: piece[odd]), 2
        mine, theirs = [added([pick(piece, odd) for piece in self.held]) for odd in (0, 1)]
        self.held = [mine, send(theirs, OUTER, offset)]

    def volume(self):
        return self.held[0].size * 2 / 2**20

    def result(self):
        return added(self.held)


def finish(chains, *tokens):
    held, _ = lax.optimization_barrier(([chain.held for chain in chains], tokens))
    for chain, pieces in zip(chains, held):
        chain.held = pieces


def go(*chains):
    for chain in chains:
        chain.go()


FLOW = {CORE: 3.5, X: 21.0, INNER: 21.0, OUTER: 84.0}


def plan_of(chain):
    if isinstance(chain, Spread):
        return [(INNER, 21.0, 1), (OUTER, 10.5, 1), (OUTER, 10.5, 1)][chain.stage :]
    size, out = chain.tiles * 0.5, []
    for axis in chain.order:
        count = lax.axis_size(axis)
        if axis == OUTER and chain.doubled:
            out += [(OUTER, 21.0 * size, 1), (OUTER, 42.0 * size, 1)]
            continue
        size = size / count
        out.append((axis, FLOW[axis] * size, count - 1))
    back = [entry for entry in reversed(out)]
    if chain.doubled:
        back = [entry for entry in back if entry[0] != OUTER]
    return (out + back)[chain.stage :]


def rehearse(plans, first, gate, weights, slack):
    free = dict.fromkeys(FLOW, 0.0)
    position, queue, order, clock, waiting = [0] * len(plans), [], [], 0.0, []

    def depart(index, when):
        axis, long, _ = plans[index][position[index]]
        begin = max(when, free[axis])
        free[axis] = begin + long
        queue.append((free[axis] + 6.0, index))

    def left(index):
        rest = plans[index][position[index] :]
        return weights[index] * sum(long + 10.0 for _, long, _ in rest)

    for index, since in first:
        depart(index, -since)
    while queue or waiting:
        soon = min(queue)[0] if queue else clock + 99.0
        if waiting and soon > clock + 4.0:
            clock += 6.5
            order.append((waiting.pop(0), True))
            continue
        near = [entry for entry in queue if entry[0] <= max(clock, soon) + slack]
        entry = max(near, key=lambda entry: left(entry[1]))
        queue.remove(entry)
        arrival, index = entry
        clock = max(clock, arrival)
        position[index] += 1
        order.append((index, False))
        if position[index] == len(plans[index]):
            clock += 1.0
            waiting.append(index)
            continue
        axis, long, sends = plans[index][position[index]]
        clock += 2.0 + 1.5 * sends + 0.03 * long
        depart(index, clock)
        if gate[1] == index and position[index] == 1:
            clock += 2.0
            depart(gate[0], clock)
    return clock, order


def run_out(flights, later):
    chains, ends = [chain for chain, _, _ in flights], [end for _, _, end in flights]
    plans = [plan_of(chain) for chain in chains]
    plans.append([(INNER, 21.0, 1), (OUTER, 10.5, 1), (OUTER, 10.5, 1)])
    first = [(index, since) for index, (_, since, _) in enumerate(flights)]
    rng, best = random.Random(7), None
    for trial in range(1500):
        weights = [1.0 if trial < 4 else rng.uniform(0.3, 2.0) for _ in plans]
        slack = (0.0, 2.0, 4.0, 8.0)[trial % 4]
        found = rehearse(plans, first, (len(chains), 0), weights, slack)
        if best is None or found[0] < best[0]:
            best = found
    token, results = (), {}
    for index, is_end in best[1]:
        chain = chains[index]
        if is_end:
            results[index] = ends[index](chain, token)
            token = (results[index][0],)
            continue
        finish([chain], *token)
        if chain.over():
            token = tuple(chain.held)
            continue
        chain.go()
        token = (chain.held[0],)
        if index == 0 and chain.stage == 1:
            chain, _, end = later(token)
            chains.append(chain)
            ends.append(end)
    return [results[index] for index in range(len(chains))]


def assemble(chain, core_info, shapes, after=()):
    tiles, half, side = chain.held[0].shape

    def body(r):
        low = pl.multiple_of(r.info[0] * half, half)
        high = pl.multiple_of((1 - r.info[0]) * half, half)
        tile = 0
        for name, shape in shapes.items():
            out = r[name]
            for start in range(0, shape[-2] * shape[-1] * (shape[0] if len(shape) > 2 else 1), side * side):
                place = start // (side * side)
                for begin, source in ((low, r.mine), (high, r.other)):
                    rows = source[tile].astype(F32)
                    if len(shape) > 2:
                        out[place, pl.ds(begin, half), :] = rows
                    elif shape[1] > shape[0]:
                        out[pl.ds(begin, half), place * side : (place + 1) * side] = rows
                    else:
                        out[pl.ds(begin + place * side, half), :] = rows
                tile += 1
            r.leave(name)

    gives = {name: (shape, F32) for name, shape in shapes.items()}
    arrays = {"mine": chain.held[0], "other": chain.held[1]}
    return list(launch(body, arrays, gives, info=core_info, after=after, cost=5).values())


def shards(
    source_short,
    target_short,
    source_segment,
    target_segment,
    source_long,
    target_long,
    source_length,
    target_length,
    cotangent_short,
    cotangent_long,
    encoder_project,
    encoder_output,
    encoder_up,
    encoder_down,
    encoder_gain,
    encoder_bias,
    decoder_project,
    decoder_output,
    cross_project,
    cross_output,
    decoder_up,
    decoder_down,
    decoder_gain,
    decoder_bias,
):
    blocks, size, width = source_short.shape
    hidden = encoder_up.shape[1]
    rows = blocks * size
    pairs, own, _ = source_long.shape
    rows_long = pairs * own
    flat = lambda a: a.reshape(-1, width)
    start = lax.axis_index((OUTER, INNER)) * own
    core = lax.axis_index(CORE)
    here = [start, lax.axis_index(INNER), core, lax.axis_index(OUTER)]
    here = jnp.stack(here).astype(jnp.int32)
    info_of = lambda lengths: jnp.concatenate([lengths, here])
    core_info = core.astype(jnp.int32)[None]
    source_info, target_info = info_of(source_length), info_of(target_length)

    spread = lambda s: jnp.broadcast_to(s[:, :, None], (blocks, size, size))
    line = lambda s: s[:, None, :]
    encoder_in = {
        "w_in": encoder_project,
        "w_o": encoder_output,
        "up": encoder_up,
        "down": encoder_down,
        "gain": encoder_gain,
        "bias": encoder_bias,
    }
    decoder_in = {
        "w_in": decoder_project,
        "w_o": decoder_output,
        "w_cin": cross_project,
        "w_co": cross_output,
        "up": decoder_up,
        "down": decoder_down,
        "gain": decoder_gain,
        "bias": decoder_bias,
    }

    def pick(table, names):
        return {name: table[name] for name in names}

    def rows_of(n, names):
        return {name: ((n, width), BF16) for name in names}

    def wide_of(n, names):
        return {name: ((n, hidden), BF16) for name in names}

    def floats(n, names):
        return {name: ((n, width), F32) for name in names}

    def column(n, names):
        return {name: ((n, 1), F32) for name in names}

    def logs(n, names):
        return {name: ((n, HEADS, size), F32) for name in names}

    def sums(n):
        return {"small": ((n, width), F32)}

    def keys_of(names):
        shape = (places, pairs, own, width)
        return {name: (shape, BF16) for name in names}

    def parts():
        inner = lax.axis_size(INNER)
        return {"part": ((inner, places // inner, pairs, own, width), BF16)}

    def saved(kernel, names):
        return {name: kernel[name] for name in names}

    whole_source = gather_early(source_long)
    places = lax.axis_size(OUTER) * lax.axis_size(INNER)
    keys = places * own
    work = [
        ("s", pltpu.VMEM((PAIRS, keys, 2 * own), F32)),
        ("a", pltpu.VMEM((PAIRS, 8, 2 * own), F32)),
        ("mix", pltpu.VMEM((PAIRS, PAIR, 2 * own), F32)),
    ]
    mix = work[2:]

    segments = {"kseg": spread(source_segment), "qseg": line(source_segment)}
    turned = {"tkseg": spread(target_segment), "tqseg": line(target_segment)}
    encoder_keeps = lambda n: {
        **rows_of(n, ("n1", "y", "n2", "enc")),
        **wide_of(n, ("act", "gate")),
        **column(n, ("i1", "i2")),
    }
    se = launch(
        short_encoder_forward,
        {"x": flat(source_short), **segments, **encoder_in},
        {**rows_of(rows, ("q", "k", "v", "o")), **logs(blocks, ("lse",)), **encoder_keeps(rows)},
        cost=0.01,
    )
    decoder_keeps = lambda n: {
        **rows_of(n, ("m", "b5", "b4", "go_c")),
        **wide_of(n, ("act", "gate", "dh")),
        **floats(n, ("final", "d4")),
        **sums(4),
    }
    sd = launch(
        short_decoder_forward,
        {
            "t": flat(target_short),
            **turned,
            **pick(decoder_in, ("w_in", "w_o", "gain", "bias")),
        },
        {
            **rows_of(rows, ("q", "k", "v", "o", "n3", "u")),
            **logs(blocks, ("lse",)),
            **column(rows, ("i3",)),
            **floats(rows, ("upper",)),
        },
        after=(se.lse,),
        cost=0.01,
    )
    early_target = gather_first(hold(target_long, sd.lse)[None, None], OUTER)
    sc = launch(
        short_cross_forward,
        {
            "u": sd.u,
            "upper": sd.upper,
            "enc": se.enc,
            "cot": flat(cotangent_short),
            "kseg": segments["kseg"],
            "tqseg": turned["tqseg"],
            **pick(decoder_in, ("w_cin", "w_co", "up", "down", "gain", "bias")),
        },
        {
            **rows_of(rows, ("q_c", "k_c", "v_c", "o_c")),
            **logs(blocks, ("lse_c",)),
            **decoder_keeps(rows),
        },
        after=(sd.lse,),
        cost=0.01,
    )

    sb = launch(
        short_decoder_back,
        {
            **saved(sd, ("q", "k", "v", "o", "lse", "n3", "i3")),
            **saved(sc, ("q_c", "k_c", "v_c", "o_c", "lse_c", "go_c", "d4")),
            "kseg": segments["kseg"],
            **turned,
            **pick(decoder_in, ("w_in", "w_o", "w_cin", "gain")),
        },
        {
            **rows_of(rows, ("dq_c", "dk_c", "dv_c", "dq", "dk", "dv", "b3", "go")),
            **floats(rows, ("denc", "dt")),
            **sums(2),
        },
        scratch=[("d3", pltpu.VMEM((rows, width), F32))],
        after=(sc.small,),
        cost=0.01,
    )

    early_target = gather_last(early_target, OUTER, 0, sb.small)
    late_target = gather_first(early_target, INNER)

    whole_source = hold(whole_source, sb.small)
    x_long, t_long = flat(source_long), flat(target_long)
    le = launch(
        long_encoder_forward,
        {"x": x_long, "xg": whole_source, **encoder_in},
        {
            **rows_of(rows_long, ("q", "o")),
            **keys_of(("k", "v")),
            **logs(pairs, ("lse",)),
            **encoder_keeps(rows_long),
        },
        scratch=work,
        info=source_info,
        after=(sb.small, early_target),
        cost=13,
        plain=True,
    )
    whole_encoded = gather_early(le.enc.reshape(pairs, own, width))

    seb = launch(
        short_encoder_back,
        {
            "denc": sb.denc,
            **saved(se, ("q", "k", "v", "o", "lse", "n1", "i1", "n2", "i2", "gate")),
            **segments,
            **pick(encoder_in, ("w_in", "w_o", "up", "down", "gain")),
        },
        {
            **rows_of(rows, ("dq", "dk", "dv", "b1", "b2", "go")),
            **wide_of(rows, ("dh",)),
            **floats(rows, ("dx",)),
            **sums(4),
        },
        scratch=[("d1", pltpu.VMEM((rows, width), F32))],
        after=(le.lse,),
        cost=16,
    )

    whole_target = gather_last(late_target, INNER, 1, seb.small)
    whole_target = whole_target.reshape(places, pairs, own, width)
    ls = launch(
        long_self_forward,
        {
            "t": t_long,
            "tg": whole_target,
            **pick(decoder_in, ("w_in", "w_o", "w_cin", "gain", "bias")),
        },
        {
            **rows_of(rows_long, ("q", "o", "n3", "u", "q_c")),
            **keys_of(("k", "v")),
            **logs(pairs, ("lse",)),
            **column(rows_long, ("i3",)),
            **floats(rows_long, ("upper",)),
        },
        scratch=work,
        info=target_info,
        after=(seb.small,),
        cost=10,
        plain=True,
    )

    whole_encoded = hold(whole_encoded, ls.lse)
    lc = launch(
        long_cross,
        {
            "eg": whole_encoded,
            "upper": ls.upper,
            "q_c": ls.q_c,
            "cot": flat(cotangent_long),
            **pick(decoder_in, ("w_cin", "w_co", "up", "down", "gain", "bias")),
        },
        {
            **rows_of(rows_long, ("o_c",)),
            **keys_of(("k_c", "v_c")),
            **logs(pairs, ("lse_c",)),
            **decoder_keeps(rows_long),
        },
        scratch=work,
        info=source_info,
        after=(ls.lse,),
        cost=14,
        plain=True,
    )
    lcb = launch(
        long_cross_back,
        {
            "q_c": ls.q_c,
            **saved(lc, ("k_c", "v_c", "o_c", "lse_c", "go_c")),
            **pick(decoder_in, ("w_cin",)),
        },
        {**rows_of(rows_long, ("dq_c",)), **keys_of(("dk_c", "dv_c")), **parts()},
        scratch=mix,
        info=source_info,
        after=(lc.small,),
        cost=14,
        plain=True,
    )
    encoded_back = Spread(lcb.part, True)
    first_weights = Weights(
        [[(sc.m, sc.dh), (lc.m, lc.dh)], [(sc.act, sc.b5), (lc.act, lc.b5)]]
    )

    def self_back_and_weights(r):
        first_weights.body(r, r.info[pairs + 2])
        long_self_back(r)

    lsb = launch(
        self_back_and_weights,
        {
            **first_weights.arrays,
            "d4": lc.d4,
            "dq_c": lcb.dq_c,
            **saved(ls, ("q", "k", "v", "o", "lse", "n3", "i3")),
            **pick(decoder_in, ("w_in", "w_o", "w_cin", "gain")),
        },
        {
            **first_weights.gives,
            **rows_of(rows_long, ("dq", "b3")),
            **keys_of(("dk", "dv")),
            **parts(),
            **floats(rows_long, ("dt",)),
            **sums(2),
        },
        scratch=mix + [("go", pltpu.VMEM((rows_long, width), BF16))],
        info=target_info,
        after=(lcb.dq_c,),
        pieces=("kept", "sent"),
        cost=22,
    )
    decoder_ffn = Chain([lsb.kept, lsb.sent], (X, INNER, OUTER))
    finish([encoded_back], lsb.small)
    go(encoded_back)
    target_back = Spread(lsb.part, False)
    grad_attention = weight_tiles(
        [
            [(sd.u, sb.dq_c), (ls.u, lcb.dq_c)],
            [(se.enc, sb.dk_c), (flat(whole_encoded), flat(lcb.dk_c))],
            [(se.enc, sb.dv_c), (flat(whole_encoded), flat(lcb.dv_c))],
            [(sc.o_c, sc.b4), (lc.o_c, lc.b4)],
            [(flat(target_short), sb.dq), (t_long, lsb.dq)],
            [(flat(target_short), sb.dk), (flat(whole_target), flat(lsb.dk))],
            [(flat(target_short), sb.dv), (flat(whole_target), flat(lsb.dv))],
            [(sd.o, sb.b3), (ls.o, lsb.b3)],
        ],
        core_info,
        after=(lsb.small, encoded_back.held[0]),
        cost=15,
    )
    finish([encoded_back, decoder_ffn], grad_attention[0])
    go(decoder_ffn)
    attention = Chain(grad_attention, (INNER, X, OUTER))
    ffn_weights = Weights(
        [
            [(se.y, seb.dh), (le.y, ("dh", hidden))],
            [(se.act, seb.b2), (le.act, ("b2", width))],
        ]
    )

    def encoder_back_and_weights(r):
        long_encoder_tail_back(r)
        ffn_weights.body(r, r.info[0])

    leb = launch(
        encoder_back_and_weights,
        {
            **{"part%d" % k: flat(piece) for k, piece in enumerate(encoded_back.held)},
            **saved(le, ("n1", "i1", "n2", "i2", "gate")),
            **pick(encoder_in, ("down", "up", "w_o", "gain")),
            **ffn_weights.arrays,
        },
        {
            **ffn_weights.gives,
            **rows_of(rows_long, ("b1", "b2", "go")),
            **wide_of(rows_long, ("dh",)),
            **floats(rows_long, ("d1",)),
            **sums(4),
        },
        info=core_info,
        after=(grad_attention[0], decoder_ffn.held[0]),
        pieces=("kept", "sent"),
        cost=12,
    )
    small = jnp.concatenate([seb.small + leb.small, sb.small + lsb.small, sc.small + lc.small])
    small = jnp.pad(small, ((0, 16 - small.shape[0]), (0, 0))).astype(BF16)
    finish([attention], leb.small)
    go(attention)
    encoder_ffn = Chain([leb.kept, leb.sent], (X, INNER, OUTER))
    attention_weights = Weights(
        [
            [(flat(source_short), seb.dq), (x_long, ("dq", width))],
            [(flat(source_short), seb.dk), (whole_source, ("dk", width))],
            [(flat(source_short), seb.dv), (whole_source, ("dv", width))],
            [(se.o, seb.b1), (le.o, leb.b1)],
        ]
    )

    def attention_back_and_weights(r):
        long_encoder_back(r)
        r.leave("part", "dx")
        attention_weights.body(r, r.info[pairs + 2])

    lea = launch(
        attention_back_and_weights,
        {
            **saved(le, ("q", "k", "v")),
            "o": le.o,
            "lse": le.lse,
            **saved(leb, ("go", "d1")),
            **pick(encoder_in, ("w_in",)),
            **attention_weights.arrays,
        },
        {
            **attention_weights.gives,
            **parts(),
            **floats(rows_long, ("dx",)),
        },
        scratch=mix
        + [
            ("dq", pltpu.VMEM((rows_long, width), BF16)),
            ("dk", pltpu.VMEM((places, pairs, own, width), BF16)),
            ("dv", pltpu.VMEM((places, pairs, own, width), BF16)),
        ],
        info=source_info,
        after=(leb.small, attention.held[0]),
        pieces=("kept", "sent"),
        cost=19,
    )
    done = lea.dx
    finish([decoder_ffn, encoder_ffn, target_back], done)
    encoder = Chain([lea.kept, lea.sent], (INNER, X, OUTER), small, True)
    go(decoder_ffn, encoder_ffn, target_back)
    square = (3, width, width)
    feed = {"up": encoder_up.shape, "down": encoder_down.shape}
    one = {"project": square, "output": square[1:]}
    two = {"cross_in": square, "cross_out": square[1:], "self_in": square, "self_out": square[1:]}

    def out(shapes):
        return lambda chain, token: assemble(chain, core_info, shapes, token)

    rows_out = lambda rows: lambda chain, token: [chain.result().astype(F32) + rows]
    flights = [
        (encoder, 0.0, out(one)),
        (decoder_ffn, 0.0, out(feed)),
        (attention, 20.0, out(two)),
        (encoder_ffn, 0.0, out(feed)),
        (target_back, 0.0, rows_out(lsb.dt.reshape(source_long.shape))),
    ]

    def source_back(token):
        chain = Spread(hold(lea.part, token), False)
        return chain, 0.0, rows_out(lea.dx.reshape(source_long.shape))

    results = run_out(flights, source_back)
    (encoder_in_out, encoder_out_out), (decoder_up_out, decoder_down_out) = results[:2]
    (cross_in, cross_out, self_in, self_out), (encoder_up_out, encoder_down_out) = results[2:4]
    (grad_target,), (grad_source,) = results[4:]
    small = encoder.small.astype(F32)
    return (
        sc.final.reshape(source_short.shape),
        lc.final.reshape(source_long.shape),
        seb.dx.reshape(source_short.shape),
        sb.dt.reshape(source_short.shape),
        grad_source,
        grad_target,
        encoder_in_out,
        encoder_out_out,
        encoder_up_out,
        encoder_down_out,
        small[0:2],
        small[2:4],
        self_in,
        self_out,
        cross_in,
        cross_out,
        decoder_up_out,
        decoder_down_out,
        jnp.stack([small[4], small[6], small[7]]),
        jnp.stack([small[5], small[8], small[9]]),
    )


def solution(mesh):
    group, seq = mesh.devices.shape
    fine = Mesh(
        mesh.devices.reshape(group // 2, 2, 4, seq // 4), (X, CORE, OUTER, INNER)
    )
    groups, positions = (X, CORE), (OUTER, INNER)
    blocks = P(groups + positions, None, None)
    long_rows = P(groups, positions, None)
    in_specs = (
        (blocks, blocks, P(groups + positions, None), P(groups + positions, None))
        + (long_rows, long_rows, P(groups), P(groups), blocks, long_rows)
        + (P(),) * 14
    )
    out_specs = (blocks, long_rows, blocks, blocks, long_rows, long_rows) + (P(),) * 14
    return jax.shard_map(
        shards, mesh=fine, in_specs=in_specs, out_specs=out_specs, check_vma=False
    )
```

```python
import functools
import random
import jax
import jax.numpy as jnp
from jax import lax
from jax.experimental import pallas as pl
from jax.experimental.pallas import tpu as pltpu
from jax.sharding import Mesh, PartitionSpec as P

HEADS = 8
HEAD_DIM = 64
PAIR = 2 * HEAD_DIM
PAIRS = HEADS // 2
SCALE = HEAD_DIM**-0.5
FLOOR_SCORE = -1e30
EPSILON = 1e-05
KEY_BLOCK = 256
CHUNK = 512
F32 = jnp.float32
BF16 = jnp.bfloat16
CORE, X, INNER, OUTER = "core", "x", "inner", "outer"


def nn(left, right):
    return lax.dot_general(left, right, (((1,), (0,)), ((), ())), preferred_element_type=F32)


def nt(left, right):
    return lax.dot_general(left, right, (((1,), (1,)), ((), ())), preferred_element_type=F32)


def tn(left, right):
    return lax.dot_general(left, right, (((0,), (0,)), ((), ())), preferred_element_type=F32)


def two_heads(rows):
    lane = lax.broadcasted_iota(jnp.int32, rows.shape, 1)
    zero = jnp.zeros_like(rows)
    first = jnp.where(lane < HEAD_DIM, rows, zero)
    second = jnp.where(lane < HEAD_DIM, zero, rows)
    return jnp.concatenate([first, second], axis=0)


def diagonal(product):
    half = product.shape[1] // 2
    return jnp.concatenate([product[:HEAD_DIM, :half], product[HEAD_DIM:, half:]], axis=0)


def delta_rows(grad_out, outputs):
    product = grad_out.astype(F32) * outputs.astype(F32)
    high = product.astype(BF16)
    low = (product - high.astype(F32)).astype(BF16)
    width = product.shape[1]
    head = lax.broadcasted_iota(jnp.int32, (HEADS, width), 0)
    lane = lax.broadcasted_iota(jnp.int32, (HEADS, width), 1)
    pick = jnp.where(lax.div(lane, HEAD_DIM) == head, 1.0, 0.0).astype(BF16)
    return nt(pick, high) + nt(pick, low)


def pair_row(rows, pair):
    return jnp.concatenate([rows[2 * pair : 2 * pair + 1], rows[2 * pair + 1 : 2 * pair + 2]], axis=1)


def pair_lanes(pair):
    return slice(pair * PAIR, (pair + 1) * PAIR)


def norm(residual, gain, bias):
    centred = residual - jnp.mean(residual, axis=1, keepdims=True)
    inverse = lax.rsqrt(jnp.mean(centred * centred, axis=1, keepdims=True) + EPSILON)
    normed = centred * inverse
    return normed * gain + bias, normed, inverse


def norm_back(upstream, normed, inverse, gain):
    normed = normed.astype(F32)
    scaled = upstream * gain
    grad = inverse * (
        scaled
        - jnp.mean(scaled, axis=1, keepdims=True)
        - normed * jnp.mean(scaled * normed, axis=1, keepdims=True)
    )
    return (
        grad,
        jnp.sum(upstream * normed, axis=0, keepdims=True),
        jnp.sum(upstream, axis=0, keepdims=True),
    )


def feed_forward(rows, up_ref, down_ref, act_ref, gate_ref):
    low = rows.astype(BF16)
    total = rows
    for start in range(0, up_ref.shape[1], CHUNK):
        part = slice(start, start + CHUNK)
        hidden = nn(low, up_ref[:, part])
        sigmoid = 0.5 * jnp.tanh(0.5 * hidden) + 0.5
        active = hidden * sigmoid
        gate_ref[:, part] = (sigmoid + active * (1.0 - sigmoid)).astype(BF16)
        active = active.astype(BF16)
        act_ref[:, part] = active
        total = total + nn(active, down_ref[part, :])
    return low, total


def feed_back(grad, gate_ref, up_ref, down_ref, hidden_grad_ref):
    low = grad.astype(BF16)
    total = grad
    for start in range(0, up_ref.shape[1], CHUNK):
        part = slice(start, start + CHUNK)
        hidden = nt(low, down_ref[part, :]) * gate_ref[:, part].astype(F32)
        hidden = hidden.astype(BF16)
        hidden_grad_ref[:, part] = hidden
        total = total + nt(hidden, up_ref[:, part])
    return low, total


def short_allowed(key_segment, query_segment, causal):
    allowed = key_segment == query_segment
    if causal:
        key = lax.broadcasted_iota(jnp.int32, key_segment.shape, 0)
        query = lax.broadcasted_iota(jnp.int32, key_segment.shape, 1)
        allowed = allowed & (key <= query)
    return jnp.concatenate([allowed, allowed], axis=1)


def short_attend(causal, q_ref, k_ref, v_ref, kseg_ref, qseg_ref, o_ref, lse_ref):
    size = kseg_ref.shape[1]
    for block in range(kseg_ref.shape[0]):
        rows = slice(block * size, (block + 1) * size)
        allowed = short_allowed(kseg_ref[block], qseg_ref[block], causal)
        logs = []
        for pair in range(PAIRS):
            lanes = pair_lanes(pair)
            scores = nt(k_ref[rows, lanes], two_heads(q_ref[rows, lanes]))
            scores = jnp.where(allowed, scores, FLOOR_SCORE)
            top = jnp.max(scores, axis=0, keepdims=True)
            weights = jnp.exp(scores - top)
            total = jnp.sum(weights, axis=0, keepdims=True)
            mixed = nn(v_ref[rows, lanes].T, weights.astype(BF16)) / total
            o_ref[rows, lanes] = diagonal(mixed).T.astype(BF16)
            log_total = top + jnp.log(total)
            logs += [log_total[:, :size], log_total[:, size:]]
        lse_ref[block] = jnp.concatenate(logs, axis=0)


def short_attend_back(
    causal, q_ref, k_ref, v_ref, kseg_ref, qseg_ref, o_ref, lse_ref, go_ref, dq_ref, dk_ref, dv_ref
):
    size = kseg_ref.shape[1]
    for block in range(kseg_ref.shape[0]):
        rows = slice(block * size, (block + 1) * size)
        allowed = short_allowed(kseg_ref[block], qseg_ref[block], causal)
        delta = delta_rows(go_ref[rows, :], o_ref[rows, :])
        lse = lse_ref[block]
        for pair in range(PAIRS):
            lanes = pair_lanes(pair)
            queries, grads = two_heads(q_ref[rows, lanes]), two_heads(go_ref[rows, lanes])
            scores = nt(k_ref[rows, lanes], queries)
            weights = jnp.where(allowed, jnp.exp(scores - pair_row(lse, pair)), 0.0)
            grad_weights = nt(v_ref[rows, lanes], grads)
            grad_scores = (weights * (grad_weights - pair_row(delta, pair))).astype(BF16)
            dv_ref[rows, lanes] = nn(weights.astype(BF16), grads).astype(BF16)
            dk_ref[rows, lanes] = nn(grad_scores, queries).astype(BF16)
            turned = diagonal(nn(k_ref[rows, lanes].T, grad_scores)).T
            dq_ref[rows, lanes] = (turned.astype(BF16).astype(F32) * SCALE).astype(BF16)


def load_keys(ref, pair_index, block, lanes):
    pieces = KEY_BLOCK // ref.shape[2]
    rows = ref[pl.ds(block * pieces, pieces), pair_index, :, lanes]
    return rows.reshape(KEY_BLOCK, rows.shape[2])


def store_keys(ref, pair_index, block, lanes, rows):
    pieces = KEY_BLOCK // ref.shape[2]
    ref[pl.ds(block * pieces, pieces), pair_index, :, lanes] = rows.astype(BF16).reshape(
        pieces, ref.shape[2], rows.shape[1]
    )


def store_part(ref, info_ref, pair_index, block, rows):
    partners, _, pairs, size, _ = ref.shape
    for piece in range(KEY_BLOCK // size):
        place = block * (KEY_BLOCK // size) + piece
        inner = lax.rem(place, partners) ^ info_ref[pairs + 1]
        outer = lax.div(place, partners) ^ info_ref[pairs + 3]
        ref[inner, outer, pair_index] = rows[piece * size : (piece + 1) * size]


def long_limit(info_ref, causal, pair_index, size, pairs):
    length = info_ref[pair_index]
    limit = length
    if causal:
        limit = jnp.minimum(length, info_ref[pairs] + size)
    return length, lax.div(limit + KEY_BLOCK - 1, KEY_BLOCK)


def long_allowed(start, causal, length, block, shape):
    key = lax.broadcasted_iota(jnp.int32, shape, 0) + block * KEY_BLOCK
    allowed = key < length
    if causal:
        half = shape[1] // 2
        lane = lax.broadcasted_iota(jnp.int32, shape, 1)
        query = jnp.where(lane < half, lane, lane - half) + start
        allowed = allowed & (key <= query)
    return allowed


def long_attend(
    causal, info_ref, q_ref, x_ref, k_w, v_w, k_ref, v_ref, o_ref, lse_ref, score_ref, sum_ref, mix_ref
):
    places, pairs, size, width = x_ref.shape
    shape = (KEY_BLOCK, 2 * size)
    everything = slice(None)

    def one(pair_index, carry):
        length, count = long_limit(info_ref, causal, pair_index, size, pairs)
        own = pl.ds(pl.multiple_of(pair_index * size, size), size)

        def first(block, tops):
            rows = pl.ds(pl.multiple_of(block * KEY_BLOCK, KEY_BLOCK), KEY_BLOCK)
            allowed = long_allowed(info_ref[pairs], causal, length, block, shape)
            context = load_keys(x_ref, pair_index, block, everything)
            store_keys(k_ref, pair_index, block, everything, nn(context, k_w[...]))
            store_keys(v_ref, pair_index, block, everything, nn(context, v_w[...]))
            after = []
            for pair in range(PAIRS):
                lanes = pair_lanes(pair)
                keys = load_keys(k_ref, pair_index, block, lanes)
                scores = nt(keys, two_heads(q_ref[own, lanes]))
                scores = jnp.where(allowed, scores, FLOOR_SCORE)
                score_ref[pair, rows] = scores
                folded = jnp.max(scores.reshape(KEY_BLOCK // 8, 8, 2 * size), axis=0)
                after.append(jnp.maximum(tops[pair], folded))
            return tuple(after)

        start = tuple(jnp.full((8, 2 * size), FLOOR_SCORE, F32) for _ in range(PAIRS))
        tops = lax.fori_loop(0, count, first, start)
        tops = [jnp.max(top, axis=0, keepdims=True) for top in tops]
        sum_ref[...] = jnp.zeros_like(sum_ref)
        mix_ref[...] = jnp.zeros_like(mix_ref)

        def second(block, carry):
            rows = pl.ds(pl.multiple_of(block * KEY_BLOCK, KEY_BLOCK), KEY_BLOCK)
            for pair in range(PAIRS):
                weights = jnp.exp(score_ref[pair, rows] - tops[pair])
                sum_ref[pair] += jnp.sum(weights.reshape(KEY_BLOCK // 8, 8, 2 * size), axis=0)
                values = load_keys(v_ref, pair_index, block, pair_lanes(pair))
                mix_ref[pair] += nn(values.T, weights.astype(BF16))
            return carry

        lax.fori_loop(0, count, second, 0)
        logs = []
        for pair in range(PAIRS):
            total = jnp.sum(sum_ref[pair], axis=0, keepdims=True)
            mixed = mix_ref[pair] / total
            o_ref[own, pair_lanes(pair)] = diagonal(mixed).T.astype(BF16)
            log_total = tops[pair] + jnp.log(total)
            logs += [log_total[:, :size], log_total[:, size:]]
        lse_ref[pair_index] = jnp.concatenate(logs, axis=0)
        return carry

    lax.fori_loop(0, pairs, one, 0)


def long_attend_back(
    causal,
    info_ref,
    q_ref,
    k_ref,
    v_ref,
    o_ref,
    lse_ref,
    go_ref,
    k_w,
    v_w,
    dq_ref,
    dk_ref,
    dv_ref,
    part_ref,
    mix_ref,
):
    places, pairs, size, width = k_ref.shape
    shape = (KEY_BLOCK, 2 * size)
    everything = slice(None)

    def one(pair_index, carry):
        length, count = long_limit(info_ref, causal, pair_index, size, pairs)
        own = pl.ds(pl.multiple_of(pair_index * size, size), size)
        delta = delta_rows(go_ref[own, :], o_ref[own, :])
        lse = lse_ref[pair_index]
        mix_ref[...] = jnp.zeros_like(mix_ref)

        def step(block, carry):
            allowed = long_allowed(info_ref[pairs], causal, length, block, shape)
            for pair in range(PAIRS):
                lanes = pair_lanes(pair)
                queries, grads = two_heads(q_ref[own, lanes]), two_heads(go_ref[own, lanes])
                keys = load_keys(k_ref, pair_index, block, lanes)
                scores = nt(keys, queries)
                weights = jnp.where(allowed, jnp.exp(scores - pair_row(lse, pair)), 0.0)
                grad_weights = nt(load_keys(v_ref, pair_index, block, lanes), grads)
                grad_scores = (weights * (grad_weights - pair_row(delta, pair))).astype(BF16)
                store_keys(dv_ref, pair_index, block, lanes, nn(weights.astype(BF16), grads))
                store_keys(dk_ref, pair_index, block, lanes, nn(grad_scores, queries))
                mix_ref[pair] += nn(keys.T, grad_scores)
            part = nt(load_keys(dk_ref, pair_index, block, everything), k_w[...])
            part = part + nt(load_keys(dv_ref, pair_index, block, everything), v_w[...])
            store_part(part_ref, info_ref, pair_index, block, part.astype(BF16))
            return carry

        lax.fori_loop(0, count, step, 0)

        def clear(block, carry):
            nothing = jnp.zeros((KEY_BLOCK, width), BF16)
            store_keys(dk_ref, pair_index, block, everything, nothing)
            store_keys(dv_ref, pair_index, block, everything, nothing)
            store_part(part_ref, info_ref, pair_index, block, nothing)
            return carry

        lax.fori_loop(count, places * size // KEY_BLOCK, clear, 0)
        for pair in range(PAIRS):
            turned = diagonal(mix_ref[pair]).T
            dq_ref[own, pair_lanes(pair)] = (turned.astype(BF16).astype(F32) * SCALE).astype(BF16)
        return carry

    lax.fori_loop(0, pairs, one, 0)


class Refs(dict):
    def __init__(self, *args):
        super().__init__(*args)
        self.coming, self.leaving = {}, {}

    def __getattr__(self, name):
        if name in self.coming:
            self.coming.pop(name).wait()
        return self[name]

    def leave(self, *names):
        for name in names:
            self["left"].add(name)
            for copy in self.leaving.get(name, ()):
                copy.start()


def copied(shape, dtype):
    size = dtype.itemsize
    for length in shape:
        size *= length
    return shape[-1] % 128 == 0 and size >= 2**16


def launch(body, arrays, gives, scratch=(), info=None, after=(), pieces=(), plain=False, cost=10):
    memory = pl.BlockSpec(memory_space=pltpu.VMEM)
    far = pl.BlockSpec(memory_space=pl.ANY)
    ins, specs = [], []
    if info is not None:
        ins.append(info)
        specs.append(pl.BlockSpec(memory_space=pltpu.SMEM))
    moved_in = [
        name for name, array in arrays.items() if not plain and copied(array.shape, array.dtype)
    ]
    moved_out = [
        name
        for name, (shape, dtype) in gives.items()
        if name in pieces or not plain and copied(shape, jnp.dtype(dtype))
    ]
    for name, array in arrays.items():
        ins.append(array)
        specs.append(far if name in moved_in else memory)
    for array in after:
        ins.append(array)
        specs.append(far)
    count_out = sum(gives[name][0][0] if name in pieces else 1 for name in moved_out)
    rooms = [pltpu.VMEM(arrays[name].shape, arrays[name].dtype) for name in moved_in]
    rooms += [pltpu.VMEM(*gives[name]) for name in moved_out]
    rooms += [pltpu.SemaphoreType.DMA((max(len(moved_in), 1),))]
    rooms += [pltpu.SemaphoreType.DMA((max(count_out, 1),))]
    names = [name for name, _ in scratch]

    def run(*refs):
        refs = list(refs)
        r = Refs()
        if info is not None:
            r["info"] = refs.pop(0)
        outer = {name: refs.pop(0) for name in arrays}
        del refs[: len(after)]
        outer.update((name, refs.pop(0)) for name in gives)
        room = {name: refs.pop(0) for name in moved_in + moved_out}
        come, go = refs.pop(0), refs.pop(0)
        r.update(outer)
        r.update(room)
        r.update(zip(names, refs))
        for place, name in enumerate(moved_in):
            copy = pltpu.make_async_copy(outer[name], room[name], come.at[place])
            copy.start()
            r.coming[name] = copy
        place = 0
        for name in moved_out:
            copies = []
            if name in pieces:
                for piece in range(gives[name][0][0]):
                    source, target = room[name].at[piece], outer[name].at[piece]
                    copies.append(pltpu.make_async_copy(source, target, go.at[place]))
                    place += 1
            else:
                copies.append(pltpu.make_async_copy(room[name], outer[name], go.at[place]))
                place += 1
            r.leaving[name] = copies
        left = set()
        r["left"] = left
        body(r)
        for name in list(r.coming):
            r.coming.pop(name).wait()
        for name in moved_out:
            if name not in left and name not in pieces:
                r.leave(name)
        for name in moved_out:
            for copy in r.leaving[name]:
                copy.wait()

    out = pl.pallas_call(
        run,
        in_specs=specs,
        out_specs=[far if name in moved_out else memory for name in gives],
        out_shape=[jax.ShapeDtypeStruct(shape, dtype) for shape, dtype in gives.values()],
        scratch_shapes=rooms + [shape for _, shape in scratch],
        compiler_params=pltpu.CompilerParams(vmem_limit_bytes=VMEM_LIMIT),
        cost_estimate=pl.CostEstimate(
            flops=int(cost * 1.1e9), bytes_accessed=int(cost * 3.5e6), transcendentals=0
        ),
    )(*ins)
    return Refs(zip(gives, out))


VMEM_LIMIT = 56 * 2**20


def add_sums(ref, rows):
    ref[...] = jnp.concatenate(rows, axis=0)


def encoder_tail(r, o_ref):
    residual = r.x[...].astype(F32) + nn(o_ref[...], r.w_o[...])
    first, normed, inverse = norm(residual, r.gain[0:1], r.bias[0:1])
    r.n1[...] = normed.astype(BF16)
    r.i1[...] = inverse
    low, total = feed_forward(first, r.up, r.down, r.act, r.gate)
    r.y[...] = low
    r.leave("n1", "act", "gate", "y")
    encoded, normed, inverse = norm(total, r.gain[1:2], r.bias[1:2])
    r.n2[...] = normed.astype(BF16)
    r.i2[...] = inverse
    r.enc[...] = encoded.astype(BF16)


def project_short(r, name, rows, w_q, w_k, w_v, context=None):
    context = rows if context is None else context
    r["q" + name][...] = (nn(rows, w_q) * SCALE).astype(BF16)
    r["k" + name][...] = nn(context, w_k).astype(BF16)
    r["v" + name][...] = nn(context, w_v).astype(BF16)


def short_encoder_forward(r):
    project_short(r, "", r.x[...], r.w_in[0], r.w_in[1], r.w_in[2])
    r.leave("q", "k", "v")
    short_attend(False, r.q, r.k, r.v, r.kseg, r.qseg, r.o, r.lse)
    r.leave("o")
    encoder_tail(r, r.o)


def decoder_middle(r, o_ref):
    residual = r.t[...].astype(F32) + nn(o_ref[...], r.w_o[...])
    upper, normed, inverse = norm(residual, r.gain[0:1], r.bias[0:1])
    r.n3[...] = normed.astype(BF16)
    r.i3[...] = inverse
    r.u[...] = upper.astype(BF16)
    return upper


def decoder_tail(r, upper, o_ref):
    gain, bias = r.gain, r.bias
    residual = upper + nn(o_ref[...], r.w_co[...])
    middle, normed4, inverse4 = norm(residual, gain[1:2], bias[1:2])
    low, total = feed_forward(middle, r.up, r.down, r.act, r.gate)
    r.m[...] = low
    r.leave("m", "act", "gate")
    final, normed5, inverse5 = norm(total, gain[2:3], bias[2:3])
    r.final[...] = final
    r.leave("final")
    grad, gain5, bias5 = norm_back(r.cot[...].astype(F32), normed5, inverse5, gain[2:3])
    low, grad = feed_back(grad, r.gate, r.up, r.down, r.dh)
    r.b5[...] = low
    r.leave("b5", "dh")
    grad, gain4, bias4 = norm_back(grad, normed4, inverse4, gain[1:2])
    low = grad.astype(BF16)
    r.b4[...] = low
    r.d4[...] = grad
    r.go_c[...] = nt(low, r.w_co[...]).astype(BF16)
    add_sums(r.small, [gain4, gain5, bias4, bias5])


def short_decoder_forward(r):
    project_short(r, "", r.t[...], r.w_in[0], r.w_in[1], r.w_in[2])
    r.leave("q", "k", "v")
    short_attend(True, r.q, r.k, r.v, r.tkseg, r.tqseg, r.o, r.lse)
    r.leave("o")
    r.upper[...] = decoder_middle(r, r.o)


def short_cross_forward(r):
    project_short(r, "_c", r.u[...], r.w_cin[0], r.w_cin[1], r.w_cin[2], r.enc[...])
    r.leave("q_c", "k_c", "v_c")
    short_attend(False, r.q_c, r.k_c, r.v_c, r.kseg, r.tqseg, r.o_c, r.lse_c)
    r.leave("o_c")
    decoder_tail(r, r.upper[...], r.o_c)


def decoder_middle_back(r):
    grad = r.d4[...] + nt(r.dq_c[...], r.w_cin[0])
    grad, gain3, bias3 = norm_back(grad, r.n3[...], r.i3[...], r.gain[0:1])
    low = grad.astype(BF16)
    r.b3[...] = low
    r.go[...] = nt(low, r.w_o[...]).astype(BF16)
    add_sums(r.small, [gain3, bias3])
    return grad


def short_decoder_back(r):
    short_attend_back(
        False, r.q_c, r.k_c, r.v_c, r.kseg, r.tqseg, r.o_c, r.lse_c, r.go_c, r.dq_c, r.dk_c, r.dv_c
    )
    r.denc[...] = nt(r.dk_c[...], r.w_cin[1]) + nt(r.dv_c[...], r.w_cin[2])
    r.leave("dq_c", "dk_c", "dv_c", "denc")
    r.d3[...] = decoder_middle_back(r)
    short_attend_back(
        True, r.q, r.k, r.v, r.tkseg, r.tqseg, r.o, r.lse, r.go, r.dq, r.dk, r.dv
    )
    r.leave("dq", "dk", "dv")
    grad = r.d3[...] + nt(r.dq[...], r.w_in[0])
    r.dt[...] = grad + nt(r.dk[...], r.w_in[1]) + nt(r.dv[...], r.w_in[2])


def encoder_tail_back(r, grad):
    grad, gain2, bias2 = norm_back(grad, r.n2[...], r.i2[...], r.gain[1:2])
    low, grad = feed_back(grad, r.gate, r.up, r.down, r.dh)
    r.b2[...] = low
    r.leave("b2", "dh")
    grad, gain1, bias1 = norm_back(grad, r.n1[...], r.i1[...], r.gain[0:1])
    low = grad.astype(BF16)
    r.b1[...] = low
    r.go[...] = nt(low, r.w_o[...]).astype(BF16)
    r.d1[...] = grad
    add_sums(r.small, [gain1, gain2, bias1, bias2])


def short_encoder_back(r):
    encoder_tail_back(r, r.denc[...])
    short_attend_back(
        False, r.q, r.k, r.v, r.kseg, r.qseg, r.o, r.lse, r.go, r.dq, r.dk, r.dv
    )
    r.leave("dq", "dk", "dv")
    grad = r.d1[...] + nt(r.dq[...], r.w_in[0])
    r.dx[...] = grad + nt(r.dk[...], r.w_in[1]) + nt(r.dv[...], r.w_in[2])


def long_encoder_forward(r):
    r.q[...] = (nn(r.x[...], r.w_in[0]) * SCALE).astype(BF16)
    long_attend(
        False, r.info, r.q, r.xg, r.w_in.at[1], r.w_in.at[2], r.k, r.v, r.o, r.lse, r.s, r.a, r.mix
    )
    r.leave("q", "k", "v", "o")
    encoder_tail(r, r.o)


def long_self_forward(r):
    r.q[...] = (nn(r.t[...], r.w_in[0]) * SCALE).astype(BF16)
    long_attend(
        True, r.info, r.q, r.tg, r.w_in.at[1], r.w_in.at[2], r.k, r.v, r.o, r.lse, r.s, r.a, r.mix
    )
    r.leave("q", "k", "v", "o")
    upper = decoder_middle(r, r.o)
    r.upper[...] = upper
    r.q_c[...] = (nn(upper.astype(BF16), r.w_cin[0]) * SCALE).astype(BF16)


def long_cross(r):
    k_w, v_w = r.w_cin.at[1], r.w_cin.at[2]
    long_attend(
        False, r.info, r.q_c, r.eg, k_w, v_w, r.k_c, r.v_c, r.o_c, r.lse_c, r.s, r.a, r.mix
    )
    r.leave("k_c", "v_c", "o_c")
    decoder_tail(r, r.upper[...], r.o_c)


def long_cross_back(r):
    long_attend_back(
        False,
        r.info,
        r.q_c,
        r.k_c,
        r.v_c,
        r.o_c,
        r.lse_c,
        r.go_c,
        r.w_cin.at[1],
        r.w_cin.at[2],
        r.dq_c,
        r.dk_c,
        r.dv_c,
        r.part,
        r.mix,
    )


def long_self_back(r):
    grad = decoder_middle_back(r)
    long_attend_back(
        True,
        r.info,
        r.q,
        r.k,
        r.v,
        r.o,
        r.lse,
        r.go,
        r.w_in.at[1],
        r.w_in.at[2],
        r.dq,
        r.dk,
        r.dv,
        r.part,
        r.mix,
    )
    r.dt[...] = grad + nt(r.dq[...], r.w_in[0])


def long_encoder_tail_back(r):
    grad = r.part0[...].astype(F32) + r.part1[...].astype(F32)
    grad = grad + r.part2[...].astype(F32) + r.part3[...].astype(F32)
    encoder_tail_back(r, grad)


def long_encoder_back(r):
    long_attend_back(
        False,
        r.info,
        r.q,
        r.k,
        r.v,
        r.o,
        r.lse,
        r.go,
        r.w_in.at[1],
        r.w_in.at[2],
        r.dq,
        r.dk,
        r.dv,
        r.part,
        r.mix,
    )
    r.dx[...] = r.d1[...] + nt(r.dq[...], r.w_in[0])


SIDE = 512


class Weights:
    def __init__(self, pairs, base=None):
        self.arrays, self.plan, known = {}, [], {}

        def place(rows):
            if isinstance(rows, tuple):
                return rows
            if id(rows) not in known:
                known[id(rows)] = "w%d" % len(known)
                self.arrays[known[id(rows)]] = rows
            return known[id(rows)], rows.shape[1]

        for terms in pairs:
            terms = [(place(a), place(b)) for a, b in terms]
            (_, height), (_, width) = terms[0]
            for row in range(0, height, SIDE):
                for column in range(0, width, SIDE):
                    self.plan.append([(a[0], row, b[0], column) for a, b in terms])
        count = len(self.plan)
        self.gives = {name: ((count, SIDE // 2, SIDE), BF16) for name in ("kept", "sent")}
        if base is not None:
            self.arrays["base"] = base

    def body(self, r, core):
        half = SIDE // 2
        for index, terms in enumerate(self.plan):
            for flip, name in enumerate(("kept", "sent")):
                total = None
                if "base" in self.arrays:
                    begin = pl.multiple_of((core ^ flip) * half, half)
                    total = r.base[index, pl.ds(begin, half), :].astype(F32)
                for a, row, b, column in terms:
                    left, right = getattr(r, a), getattr(r, b)
                    begin = pl.multiple_of(row + (core ^ flip) * half, half)
                    across = slice(column, column + SIDE)
                    if len(left.shape) == 4:
                        tall = left.shape[0] * left.shape[1] * left.shape[2]
                        rows = left[:, :, :, pl.ds(begin, half)].reshape(tall, half)
                    else:
                        rows = left[:, pl.ds(begin, half)]
                    if len(right.shape) == 4:
                        tall = right.shape[0] * right.shape[1] * right.shape[2]
                        product = tn(rows, right[:, :, :, across].reshape(tall, SIDE))
                    else:
                        product = tn(rows, right[:, across])
                    total = product if total is None else total + product
                r[name][index] = total.astype(BF16)
                r.leaving[name][index].start()


def whole_tiles(chunks, after=(), cost=10):
    weights = [Weights([[pair] for pair in chunk]) for chunk in chunks]
    arrays, gives = {}, {}
    for number, part in enumerate(weights):
        gives["c%d" % number] = ((len(part.plan), SIDE, SIDE), BF16)
        arrays.update((name + "c%d" % number, array) for name, array in part.arrays.items())

    def body(r):
        for number, part in enumerate(weights):
            tag = "c%d" % number
            for index, ((a, row, b, column),) in enumerate(part.plan):
                left, right = getattr(r, a + tag), getattr(r, b + tag)
                product = tn(left[:, row : row + SIDE], right[:, column : column + SIDE])
                r[tag][index] = product.astype(BF16)
                r.leaving[tag][index].start()

    out = launch(body, arrays, gives, after=after, pieces=tuple(gives), cost=cost)
    return list(out.values())


def weight_tiles(pairs, core_info, after=(), cost=10, base=None):
    weights = Weights(pairs, base)
    out = launch(
        lambda r: weights.body(r, r.info[0]),
        weights.arrays,
        weights.gives,
        info=core_info,
        after=after,
        pieces=("kept", "sent"),
        cost=cost,
    )
    return [out.kept, out.sent]


def send(piece, axis, offset):
    count = lax.axis_size(axis)
    return lax.ppermute(piece, axis, [(i, i ^ offset) for i in range(count)])


def ordered(pieces, place, dim):
    if len(pieces) == 1:
        return pieces[0]
    level = len(pieces) // 2
    inside = lax.rem(place, level)
    low = ordered(pieces[:level], inside, dim)
    high = ordered(pieces[level:], inside, dim)
    return jnp.where(
        place >= level, jnp.concatenate([high, low], dim), jnp.concatenate([low, high], dim)
    )


def hold(value, token):
    return lax.optimization_barrier((value, token))[0]


def gather_first(piece, axis):
    return [piece] + [send(piece, axis, k) for k in range(1, lax.axis_size(axis))]


def gather_last(pieces, axis, dim, token=None):
    if token is not None:
        pieces = hold(pieces, token)
    return ordered(pieces, lax.axis_index(axis), dim)


def added(pieces):
    total = pieces[0].astype(F32)
    for piece in pieces[1:]:
        total = total + piece.astype(F32)
    return total.astype(BF16)


def scatter_step(pending, axis, dim, token=None):
    if token is not None:
        pending = hold(pending, token)
    place, count = lax.axis_index(axis), lax.axis_size(axis)
    size = pending[0].shape[dim] // count
    after = []
    for k in range(count):
        parts = [
            lax.dynamic_slice_in_dim(piece, (place ^ k) * size, size, dim) for piece in pending
        ]
        block = added(parts)
        after.append(send(block, axis, k) if k else block)
    return after


def gather_step(piece, axis, dim):
    return gather_last(gather_first(piece, axis), axis, dim)


def gather_early(rows):
    return lax.all_gather(rows, (OUTER, INNER), axis=0, tiled=False)


SEQ = (OUTER, INNER)


class Chain:
    def __init__(self, halves, order, small=None, doubled=False):
        self.order = (CORE,) + order
        self.doubled = doubled
        self.stage = 0
        self.tiles = halves[0].shape[0]
        self.small, self.carried = None, 0
        if small is not None:
            self.carried = small.shape[0]
            halves = [jnp.concatenate([self.flat(half), small]) for half in halves]
        self.held = [halves[0], send(halves[1], CORE, 1)]

    def flat(self, block):
        return block.reshape(-1, block.shape[-1])

    def parts(self):
        if not self.carried:
            return self.held, None
        body = [piece[: -self.carried] for piece in self.held]
        body = [piece.reshape(self.tiles, -1, piece.shape[-1]) for piece in body]
        return body, added([piece[-self.carried :] for piece in self.held])

    def next_axis(self):
        stage, count = self.stage + 1, len(self.order)
        return self.order[stage] if stage < count else self.order[2 * count - 1 - stage]

    def over(self):
        return self.stage == 2 * len(self.order) - 1

    def go(self):
        axis = self.next_axis()
        self.stage += 1
        count = len(self.order)
        if self.doubled and self.stage in (count - 1, count):
            total = added(self.held)
            self.held = [total, send(total, OUTER, self.stage - count + 2)]
            return
        if self.doubled and self.stage == count + 1:
            pending, self.small = self.parts()
            self.held = gather_first(added(pending), axis)
            return
        if self.stage < count:
            pending, small = self.parts()
            place, members = lax.axis_index(axis), lax.axis_size(axis)
            size = pending[0].shape[1] // members
            self.held = []
            for k in range(members):
                begin = (place ^ k) * size
                block = added([lax.dynamic_slice_in_dim(p, begin, size, 1) for p in pending])
                if small is not None:
                    block = jnp.concatenate([self.flat(block), small])
                self.held.append(send(block, axis, k) if k else block)
            return
        if self.stage == count:
            pending, self.small = self.parts()
            piece = added(pending)
        else:
            piece = gather_last(self.held, self.order[2 * count - self.stage], 1)
        self.held = gather_first(piece, axis)

    def volume(self):
        return self.held[0].size * 2 / 2**20


class Spread:
    def __init__(self, part, straight):
        self.straight, self.stage = straight, 0
        self.held = [send(part[k], INNER, k) if k else part[k] for k in range(part.shape[0])]

    def next_axis(self):
        return OUTER

    def over(self):
        return self.stage == (1 if self.straight else 2)

    def go(self):
        self.stage += 1
        if self.straight:
            blocks = [added([piece[k] for piece in self.held]) for k in range(4)]
            self.held = [send(block, OUTER, k) if k else block for k, block in enumerate(blocks)]
            return
        if self.stage == 1:
            pick, offset = (lambda piece, odd: jnp.stack([piece[odd], piece[2 + odd]])), 1
        else:
            pick, offset = (lambda piece, odd: piece[odd]), 2
        mine, theirs = [added([pick(piece, odd) for piece in self.held]) for odd in (0, 1)]
        self.held = [mine, send(theirs, OUTER, offset)]

    def volume(self):
        return self.held[0].size * 2 / 2**20

    def result(self):
        return added(self.held)


def finish(chains, *tokens):
    held, _ = lax.optimization_barrier(([chain.held for chain in chains], tokens))
    for chain, pieces in zip(chains, held):
        chain.held = pieces


def go(*chains):
    for chain in chains:
        chain.go()


FLOW = {CORE: 3.5, X: 21.0, INNER: 21.0, OUTER: 84.0}


def plan_of(chain):
    if isinstance(chain, Spread):
        return [(INNER, 21.0, 1), (OUTER, 10.5, 1), (OUTER, 10.5, 1)][chain.stage :]
    size, out = chain.tiles * 0.5, []
    for axis in chain.order:
        count = lax.axis_size(axis)
        if axis == OUTER and chain.doubled:
            out += [(OUTER, 21.0 * size, 1), (OUTER, 42.0 * size, 1)]
            continue
        size = size / count
        out.append((axis, FLOW[axis] * size, count - 1))
    back = [entry for entry in reversed(out)]
    if chain.doubled:
        back = [entry for entry in back if entry[0] != OUTER]
    return (out + back)[chain.stage :]


def rehearse(plans, first, gate, weights, slack):
    free = dict.fromkeys(FLOW, 0.0)
    position, queue, order, clock, waiting = [0] * len(plans), [], [], 0.0, []

    def depart(index, when):
        axis, long, _ = plans[index][position[index]]
        begin = max(when, free[axis])
        free[axis] = begin + long
        queue.append((free[axis] + 6.0, index))

    def left(index):
        rest = plans[index][position[index] :]
        return weights[index] * sum(long + 10.0 for _, long, _ in rest)

    for index, since in first:
        depart(index, -since)
    while queue or waiting:
        soon = min(queue)[0] if queue else clock + 99.0
        if waiting and soon > clock + 4.0:
            clock += 6.5
            order.append((waiting.pop(0), True))
            continue
        near = [entry for entry in queue if entry[0] <= max(clock, soon) + slack]
        entry = max(near, key=lambda entry: left(entry[1]))
        queue.remove(entry)
        arrival, index = entry
        clock = max(clock, arrival)
        position[index] += 1
        order.append((index, False))
        if position[index] == len(plans[index]):
            clock += 1.0
            waiting.append(index)
            continue
        axis, long, sends = plans[index][position[index]]
        clock += 2.0 + 1.5 * sends + 0.03 * long
        depart(index, clock)
        if gate[1] == index and position[index] == 1:
            clock += 2.0
            depart(gate[0], clock)
    return clock, order


def run_out(flights, later):
    chains, ends = [chain for chain, _, _ in flights], [end for _, _, end in flights]
    plans = [plan_of(chain) for chain in chains]
    plans.append([(INNER, 21.0, 1), (OUTER, 10.5, 1), (OUTER, 10.5, 1)])
    first = [(index, since) for index, (_, since, _) in enumerate(flights)]
    rng, best = random.Random(7), None
    for trial in range(1500):
        weights = [1.0 if trial < 4 else rng.uniform(0.3, 2.0) for _ in plans]
        slack = (0.0, 2.0, 4.0, 8.0)[trial % 4]
        found = rehearse(plans, first, (len(chains), 0), weights, slack)
        if best is None or found[0] < best[0]:
            best = found
    token, results = (), {}
    for index, is_end in best[1]:
        chain = chains[index]
        if is_end:
            results[index] = ends[index](chain, token)
            token = (results[index][0],)
            continue
        finish([chain], *token)
        if chain.over():
            token = tuple(chain.held)
            continue
        chain.go()
        token = (chain.held[0],)
        if index == 0 and chain.stage == 1:
            chain, _, end = later(token)
            chains.append(chain)
            ends.append(end)
    return [results[index] for index in range(len(chains))]


def assemble(chain, core_info, shapes, after=()):
    tiles, half, side = chain.held[0].shape

    places = []
    for name, shape in shapes.items():
        blocks = shape[0] if len(shape) > 2 else shape[0] * shape[1] // (side * side)
        for block in range(blocks):
            if len(shape) > 2:
                places.append((name, lambda rows, b=block: (b, rows, slice(None))))
            elif shape[1] > shape[0]:
                lanes = slice(block * side, (block + 1) * side)
                places.append((name, lambda rows, l=lanes: (rows, l)))
            else:
                places.append((name, lambda rows, b=block: (pl.ds(rows.start + b * side, half), slice(None))))

    def body(info, mine, other, *refs):
        outs = dict(zip(shapes, refs))
        room, full, come, go = refs[len(shapes) :]
        starts = [pl.multiple_of((info[0] ^ flip) * half, half) for flip in (0, 1)]
        arrive, leave = [], []
        for tile in range(tiles):
            for flip, source in enumerate((mine, other)):
                index = 2 * tile + flip
                arrive.append(pltpu.make_async_copy(source.at[tile], room.at[index], come.at[index]))
                arrive[-1].start()
        for tile, (name, where) in enumerate(places):
            for flip in (0, 1):
                index = 2 * tile + flip
                arrive[index].wait()
                full[index] = room[index].astype(F32)
                target = outs[name].at[where(pl.ds(starts[flip], half))]
                leave.append(pltpu.make_async_copy(full.at[index], target, go.at[index]))
                leave[-1].start()
        for copy in leave:
            copy.wait()

    far = pl.BlockSpec(memory_space=pl.ANY)
    return pl.pallas_call(
        lambda info, mine, other, *refs: body(info, mine, other, *refs[len(after) :]),
        in_specs=[pl.BlockSpec(memory_space=pltpu.SMEM)] + [far] * (2 + len(after)),
        out_specs=[far] * len(shapes),
        out_shape=[jax.ShapeDtypeStruct(shape, F32) for shape in shapes.values()],
        scratch_shapes=[
            pltpu.VMEM((2 * tiles, half, side), BF16),
            pltpu.VMEM((2 * tiles, half, side), F32),
            pltpu.SemaphoreType.DMA((2 * tiles,)),
            pltpu.SemaphoreType.DMA((2 * tiles,)),
        ],
        compiler_params=pltpu.CompilerParams(vmem_limit_bytes=VMEM_LIMIT),
        cost_estimate=pl.CostEstimate(flops=5 * 10**9, bytes_accessed=2 * 10**7, transcendentals=0),
    )(core_info, chain.held[0], chain.held[1], *after)


def shards(
    source_short,
    target_short,
    source_segment,
    target_segment,
    source_long,
    target_long,
    source_length,
    target_length,
    cotangent_short,
    cotangent_long,
    encoder_project,
    encoder_output,
    encoder_up,
    encoder_down,
    encoder_gain,
    encoder_bias,
    decoder_project,
    decoder_output,
    cross_project,
    cross_output,
    decoder_up,
    decoder_down,
    decoder_gain,
    decoder_bias,
):
    blocks, size, width = source_short.shape
    hidden = encoder_up.shape[1]
    rows = blocks * size
    pairs, own, _ = source_long.shape
    rows_long = pairs * own
    flat = lambda a: a.reshape(-1, width)
    start = lax.axis_index((OUTER, INNER)) * own
    core = lax.axis_index(CORE)
    here = [start, lax.axis_index(INNER), core, lax.axis_index(OUTER)]
    here = jnp.stack(here).astype(jnp.int32)
    info_of = lambda lengths: jnp.concatenate([lengths, here])
    core_info = core.astype(jnp.int32)[None]
    source_info, target_info = info_of(source_length), info_of(target_length)

    spread = lambda s: jnp.broadcast_to(s[:, :, None], (blocks, size, size))
    line = lambda s: s[:, None, :]
    encoder_in = {
        "w_in": encoder_project,
        "w_o": encoder_output,
        "up": encoder_up,
        "down": encoder_down,
        "gain": encoder_gain,
        "bias": encoder_bias,
    }
    decoder_in = {
        "w_in": decoder_project,
        "w_o": decoder_output,
        "w_cin": cross_project,
        "w_co": cross_output,
        "up": decoder_up,
        "down": decoder_down,
        "gain": decoder_gain,
        "bias": decoder_bias,
    }

    def pick(table, names):
        return {name: table[name] for name in names}

    def rows_of(n, names):
        return {name: ((n, width), BF16) for name in names}

    def wide_of(n, names):
        return {name: ((n, hidden), BF16) for name in names}

    def floats(n, names):
        return {name: ((n, width), F32) for name in names}

    def column(n, names):
        return {name: ((n, 1), F32) for name in names}

    def logs(n, names):
        return {name: ((n, HEADS, size), F32) for name in names}

    def sums(n):
        return {"small": ((n, width), F32)}

    def keys_of(names):
        shape = (places, pairs, own, width)
        return {name: (shape, BF16) for name in names}

    def parts():
        inner = lax.axis_size(INNER)
        return {"part": ((inner, places // inner, pairs, own, width), BF16)}

    def saved(kernel, names):
        return {name: kernel[name] for name in names}

    whole_source = gather_early(source_long)
    places = lax.axis_size(OUTER) * lax.axis_size(INNER)
    keys = places * own
    work = [
        ("s", pltpu.VMEM((PAIRS, keys, 2 * own), F32)),
        ("a", pltpu.VMEM((PAIRS, 8, 2 * own), F32)),
        ("mix", pltpu.VMEM((PAIRS, PAIR, 2 * own), F32)),
    ]
    mix = work[2:]

    segments = {"kseg": spread(source_segment), "qseg": line(source_segment)}
    turned = {"tkseg": spread(target_segment), "tqseg": line(target_segment)}
    encoder_keeps = lambda n: {
        **rows_of(n, ("n1", "y", "n2", "enc")),
        **wide_of(n, ("act", "gate")),
        **column(n, ("i1", "i2")),
    }
    se = launch(
        short_encoder_forward,
        {"x": flat(source_short), **segments, **encoder_in},
        {**rows_of(rows, ("q", "k", "v", "o")), **logs(blocks, ("lse",)), **encoder_keeps(rows)},
        cost=0.01,
    )
    decoder_keeps = lambda n: {
        **rows_of(n, ("m", "b5", "b4", "go_c")),
        **wide_of(n, ("act", "gate", "dh")),
        **floats(n, ("final", "d4")),
        **sums(4),
    }
    sd = launch(
        short_decoder_forward,
        {
            "t": flat(target_short),
            **turned,
            **pick(decoder_in, ("w_in", "w_o", "gain", "bias")),
        },
        {
            **rows_of(rows, ("q", "k", "v", "o", "n3", "u")),
            **logs(blocks, ("lse",)),
            **column(rows, ("i3",)),
            **floats(rows, ("upper",)),
        },
        after=(se.lse,),
        cost=0.01,
    )
    early_target = gather_first(hold(target_long, sd.lse)[None, None], OUTER)
    sc = launch(
        short_cross_forward,
        {
            "u": sd.u,
            "upper": sd.upper,
            "enc": se.enc,
            "cot": flat(cotangent_short),
            "kseg": segments["kseg"],
            "tqseg": turned["tqseg"],
            **pick(decoder_in, ("w_cin", "w_co", "up", "down", "gain", "bias")),
        },
        {
            **rows_of(rows, ("q_c", "k_c", "v_c", "o_c")),
            **logs(blocks, ("lse_c",)),
            **decoder_keeps(rows),
        },
        after=(sd.lse,),
        cost=0.01,
    )

    sb = launch(
        short_decoder_back,
        {
            **saved(sd, ("q", "k", "v", "o", "lse", "n3", "i3")),
            **saved(sc, ("q_c", "k_c", "v_c", "o_c", "lse_c", "go_c", "d4")),
            "kseg": segments["kseg"],
            **turned,
            **pick(decoder_in, ("w_in", "w_o", "w_cin", "gain")),
        },
        {
            **rows_of(rows, ("dq_c", "dk_c", "dv_c", "dq", "dk", "dv", "b3", "go")),
            **floats(rows, ("denc", "dt")),
            **sums(2),
        },
        scratch=[("d3", pltpu.VMEM((rows, width), F32))],
        after=(sc.small,),
        cost=0.01,
    )

    early_target = gather_last(early_target, OUTER, 0, sb.small)
    late_target = gather_first(early_target, INNER)

    whole_source = hold(whole_source, sb.small)
    x_long, t_long = flat(source_long), flat(target_long)
    le = launch(
        long_encoder_forward,
        {"x": x_long, "xg": whole_source, **encoder_in},
        {
            **rows_of(rows_long, ("q", "o")),
            **keys_of(("k", "v")),
            **logs(pairs, ("lse",)),
            **encoder_keeps(rows_long),
        },
        scratch=work,
        info=source_info,
        after=(sb.small, early_target),
        cost=13,
        plain=True,
    )
    whole_encoded = gather_early(le.enc.reshape(pairs, own, width))

    seb = launch(
        short_encoder_back,
        {
            "denc": sb.denc,
            **saved(se, ("q", "k", "v", "o", "lse", "n1", "i1", "n2", "i2", "gate")),
            **segments,
            **pick(encoder_in, ("w_in", "w_o", "up", "down", "gain")),
        },
        {
            **rows_of(rows, ("dq", "dk", "dv", "b1", "b2", "go")),
            **wide_of(rows, ("dh",)),
            **floats(rows, ("dx",)),
            **sums(4),
        },
        scratch=[("d1", pltpu.VMEM((rows, width), F32))],
        after=(le.lse,),
        cost=16,
    )

    t_short, x_short = flat(target_short), flat(source_short)
    short_weights = whole_tiles(
        [
            [(sc.m, sc.dh), (sc.act, sc.b5)],
            [
                (sd.u, sb.dq_c),
                (se.enc, sb.dk_c),
                (se.enc, sb.dv_c),
                (sc.o_c, sc.b4),
                (t_short, sb.dq),
                (t_short, sb.dk),
                (t_short, sb.dv),
                (sd.o, sb.b3),
            ],
            [(se.y, seb.dh), (se.act, seb.b2)],
            [(x_short, seb.dq), (x_short, seb.dk), (x_short, seb.dv), (se.o, seb.b1)],
        ],
        after=(seb.small,),
        cost=15,
    )
    whole_target = gather_last(late_target, INNER, 1, short_weights[0])
    whole_target = whole_target.reshape(places, pairs, own, width)
    ls = launch(
        long_self_forward,
        {
            "t": t_long,
            "tg": whole_target,
            **pick(decoder_in, ("w_in", "w_o", "w_cin", "gain", "bias")),
        },
        {
            **rows_of(rows_long, ("q", "o", "n3", "u", "q_c")),
            **keys_of(("k", "v")),
            **logs(pairs, ("lse",)),
            **column(rows_long, ("i3",)),
            **floats(rows_long, ("upper",)),
        },
        scratch=work,
        info=target_info,
        after=(short_weights[0],),
        cost=10,
        plain=True,
    )

    whole_encoded = hold(whole_encoded, ls.lse)
    lc = launch(
        long_cross,
        {
            "eg": whole_encoded,
            "upper": ls.upper,
            "q_c": ls.q_c,
            "cot": flat(cotangent_long),
            **pick(decoder_in, ("w_cin", "w_co", "up", "down", "gain", "bias")),
        },
        {
            **rows_of(rows_long, ("o_c",)),
            **keys_of(("k_c", "v_c")),
            **logs(pairs, ("lse_c",)),
            **decoder_keeps(rows_long),
        },
        scratch=work,
        info=source_info,
        after=(ls.lse,),
        cost=14,
        plain=True,
    )
    lcb = launch(
        long_cross_back,
        {
            "q_c": ls.q_c,
            **saved(lc, ("k_c", "v_c", "o_c", "lse_c", "go_c")),
            **pick(decoder_in, ("w_cin",)),
        },
        {**rows_of(rows_long, ("dq_c",)), **keys_of(("dk_c", "dv_c")), **parts()},
        scratch=mix,
        info=source_info,
        after=(lc.small,),
        cost=14,
        plain=True,
    )
    encoded_back = Spread(lcb.part, True)
    first_weights = Weights(
        [[(lc.m, lc.dh)], [(lc.act, lc.b5)]], short_weights[0]
    )

    def self_back_and_weights(r):
        first_weights.body(r, r.info[pairs + 2])
        long_self_back(r)

    lsb = launch(
        self_back_and_weights,
        {
            **first_weights.arrays,
            "d4": lc.d4,
            "dq_c": lcb.dq_c,
            **saved(ls, ("q", "k", "v", "o", "lse", "n3", "i3")),
            **pick(decoder_in, ("w_in", "w_o", "w_cin", "gain")),
        },
        {
            **first_weights.gives,
            **rows_of(rows_long, ("dq", "b3")),
            **keys_of(("dk", "dv")),
            **parts(),
            **floats(rows_long, ("dt",)),
            **sums(2),
        },
        scratch=mix + [("go", pltpu.VMEM((rows_long, width), BF16))],
        info=target_info,
        after=(lcb.dq_c,),
        pieces=("kept", "sent"),
        cost=22,
    )
    decoder_ffn = Chain([lsb.kept, lsb.sent], (X, INNER, OUTER))
    finish([encoded_back], lsb.small)
    go(encoded_back)
    target_back = Spread(lsb.part, False)
    grad_attention = weight_tiles(
        [
            [(ls.u, lcb.dq_c)],
            [(flat(whole_encoded), flat(lcb.dk_c))],
            [(flat(whole_encoded), flat(lcb.dv_c))],
            [(lc.o_c, lc.b4)],
            [(t_long, lsb.dq)],
            [(flat(whole_target), flat(lsb.dk))],
            [(flat(whole_target), flat(lsb.dv))],
            [(ls.o, lsb.b3)],
        ],
        core_info,
        after=(lsb.small, encoded_back.held[0]),
        base=short_weights[1],
        cost=15,
    )
    finish([encoded_back, decoder_ffn], grad_attention[0])
    go(decoder_ffn)
    attention = Chain(grad_attention, (INNER, X, OUTER))
    ffn_weights = Weights(
        [
            [(le.y, ("dh", hidden))],
            [(le.act, ("b2", width))],
        ],
        short_weights[2],
    )

    def encoder_back_and_weights(r):
        long_encoder_tail_back(r)
        ffn_weights.body(r, r.info[0])

    leb = launch(
        encoder_back_and_weights,
        {
            **{"part%d" % k: flat(piece) for k, piece in enumerate(encoded_back.held)},
            **saved(le, ("n1", "i1", "n2", "i2", "gate")),
            **pick(encoder_in, ("down", "up", "w_o", "gain")),
            **ffn_weights.arrays,
        },
        {
            **ffn_weights.gives,
            **rows_of(rows_long, ("b1", "b2", "go")),
            **wide_of(rows_long, ("dh",)),
            **floats(rows_long, ("d1",)),
            **sums(4),
        },
        info=core_info,
        after=(grad_attention[0], decoder_ffn.held[0]),
        pieces=("kept", "sent"),
        cost=12,
    )
    small = jnp.concatenate([seb.small + leb.small, sb.small + lsb.small, sc.small + lc.small])
    small = jnp.pad(small, ((0, 16 - small.shape[0]), (0, 0))).astype(BF16)
    finish([attention], leb.small)
    go(attention)
    encoder_ffn = Chain([leb.kept, leb.sent], (X, INNER, OUTER))
    attention_weights = Weights(
        [
            [(x_long, ("dq", width))],
            [(whole_source, ("dk", width))],
            [(whole_source, ("dv", width))],
            [(le.o, leb.b1)],
        ],
        short_weights[3],
    )

    def attention_back_and_weights(r):
        long_encoder_back(r)
        r.leave("part", "dx")
        attention_weights.body(r, r.info[pairs + 2])

    lea = launch(
        attention_back_and_weights,
        {
            **saved(le, ("q", "k", "v")),
            "o": le.o,
            "lse": le.lse,
            **saved(leb, ("go", "d1")),
            **pick(encoder_in, ("w_in",)),
            **attention_weights.arrays,
        },
        {
            **attention_weights.gives,
            **parts(),
            **floats(rows_long, ("dx",)),
        },
        scratch=mix
        + [
            ("dq", pltpu.VMEM((rows_long, width), BF16)),
            ("dk", pltpu.VMEM((places, pairs, own, width), BF16)),
            ("dv", pltpu.VMEM((places, pairs, own, width), BF16)),
        ],
        info=source_info,
        after=(leb.small, attention.held[0]),
        pieces=("kept", "sent"),
        cost=19,
    )
    done = lea.dx
    finish([decoder_ffn, encoder_ffn, target_back], done)
    encoder = Chain([lea.kept, lea.sent], (INNER, X, OUTER), small, True)
    go(decoder_ffn, encoder_ffn, target_back)
    square = (3, width, width)
    feed = {"up": encoder_up.shape, "down": encoder_down.shape}
    one = {"project": square, "output": square[1:]}
    two = {"cross_in": square, "cross_out": square[1:], "self_in": square, "self_out": square[1:]}

    def out(shapes):
        return lambda chain, token: assemble(chain, core_info, shapes, token)

    rows_out = lambda rows: lambda chain, token: [chain.result().astype(F32) + rows]
    flights = [
        (encoder, 0.0, out(one)),
        (decoder_ffn, 0.0, out(feed)),
        (attention, 20.0, out(two)),
        (encoder_ffn, 0.0, out(feed)),
        (target_back, 0.0, rows_out(lsb.dt.reshape(source_long.shape))),
    ]

    def source_back(token):
        chain = Spread(hold(lea.part, token), False)
        return chain, 0.0, rows_out(lea.dx.reshape(source_long.shape))

    results = run_out(flights, source_back)
    (encoder_in_out, encoder_out_out), (decoder_up_out, decoder_down_out) = results[:2]
    (cross_in, cross_out, self_in, self_out), (encoder_up_out, encoder_down_out) = results[2:4]
    (grad_target,), (grad_source,) = results[4:]
    small = encoder.small.astype(F32)
    return (
        sc.final.reshape(source_short.shape),
        lc.final.reshape(source_long.shape),
        seb.dx.reshape(source_short.shape),
        sb.dt.reshape(source_short.shape),
        grad_source,
        grad_target,
        encoder_in_out,
        encoder_out_out,
        encoder_up_out,
        encoder_down_out,
        small[0:2],
        small[2:4],
        self_in,
        self_out,
        cross_in,
        cross_out,
        decoder_up_out,
        decoder_down_out,
        jnp.stack([small[4], small[6], small[7]]),
        jnp.stack([small[5], small[8], small[9]]),
    )


def solution(mesh):
    group, seq = mesh.devices.shape
    fine = Mesh(
        mesh.devices.reshape(group // 2, 2, 4, seq // 4), (X, CORE, OUTER, INNER)
    )
    groups, positions = (X, CORE), (OUTER, INNER)
    blocks = P(groups + positions, None, None)
    long_rows = P(groups, positions, None)
    in_specs = (
        (blocks, blocks, P(groups + positions, None), P(groups + positions, None))
        + (long_rows, long_rows, P(groups), P(groups), blocks, long_rows)
        + (P(),) * 14
    )
    out_specs = (blocks, long_rows, blocks, blocks, long_rows, long_rows) + (P(),) * 14
    return jax.shard_map(
        shards, mesh=fine, in_specs=in_specs, out_specs=out_specs, check_vma=False
    )
```

```python
import functools
import random
import jax
import jax.numpy as jnp
from jax import lax
from jax.experimental import pallas as pl
from jax.experimental.pallas import tpu as pltpu
from jax.sharding import Mesh, PartitionSpec as P

HEADS = 8
HEAD_DIM = 64
PAIR = 2 * HEAD_DIM
PAIRS = HEADS // 2
SCALE = HEAD_DIM**-0.5
FLOOR_SCORE = -1e30
EPSILON = 1e-05
KEY_BLOCK = 256
CHUNK = 512
F32 = jnp.float32
BF16 = jnp.bfloat16
CORE, X, INNER, OUTER = "core", "x", "inner", "outer"


def nn(left, right):
    return lax.dot_general(left, right, (((1,), (0,)), ((), ())), preferred_element_type=F32)


def nt(left, right):
    return lax.dot_general(left, right, (((1,), (1,)), ((), ())), preferred_element_type=F32)


def tn(left, right):
    return lax.dot_general(left, right, (((0,), (0,)), ((), ())), preferred_element_type=F32)


def two_heads(rows):
    lane = lax.broadcasted_iota(jnp.int32, rows.shape, 1)
    zero = jnp.zeros_like(rows)
    first = jnp.where(lane < HEAD_DIM, rows, zero)
    second = jnp.where(lane < HEAD_DIM, zero, rows)
    return jnp.concatenate([first, second], axis=0)


def diagonal(product):
    half = product.shape[1] // 2
    return jnp.concatenate([product[:HEAD_DIM, :half], product[HEAD_DIM:, half:]], axis=0)


def delta_rows(grad_out, outputs):
    product = grad_out.astype(F32) * outputs.astype(F32)
    high = product.astype(BF16)
    low = (product - high.astype(F32)).astype(BF16)
    width = product.shape[1]
    head = lax.broadcasted_iota(jnp.int32, (HEADS, width), 0)
    lane = lax.broadcasted_iota(jnp.int32, (HEADS, width), 1)
    pick = jnp.where(lax.div(lane, HEAD_DIM) == head, 1.0, 0.0).astype(BF16)
    return nt(pick, high) + nt(pick, low)


def pair_row(rows, pair):
    return jnp.concatenate([rows[2 * pair : 2 * pair + 1], rows[2 * pair + 1 : 2 * pair + 2]], axis=1)


def pair_lanes(pair):
    return slice(pair * PAIR, (pair + 1) * PAIR)


def norm(residual, gain, bias):
    centred = residual - jnp.mean(residual, axis=1, keepdims=True)
    inverse = lax.rsqrt(jnp.mean(centred * centred, axis=1, keepdims=True) + EPSILON)
    normed = centred * inverse
    return normed * gain + bias, normed, inverse


def norm_back(upstream, normed, inverse, gain):
    normed = normed.astype(F32)
    scaled = upstream * gain
    grad = inverse * (
        scaled
        - jnp.mean(scaled, axis=1, keepdims=True)
        - normed * jnp.mean(scaled * normed, axis=1, keepdims=True)
    )
    return (
        grad,
        jnp.sum(upstream * normed, axis=0, keepdims=True),
        jnp.sum(upstream, axis=0, keepdims=True),
    )


def feed_forward(rows, up_ref, down_ref, act_ref, gate_ref):
    low = rows.astype(BF16)
    total = rows
    for start in range(0, up_ref.shape[1], CHUNK):
        part = slice(start, start + CHUNK)
        hidden = nn(low, up_ref[:, part])
        sigmoid = 0.5 * jnp.tanh(0.5 * hidden) + 0.5
        active = hidden * sigmoid
        gate_ref[:, part] = (sigmoid + active * (1.0 - sigmoid)).astype(BF16)
        active = active.astype(BF16)
        act_ref[:, part] = active
        total = total + nn(active, down_ref[part, :])
    return low, total


def feed_back(grad, gate_ref, up_ref, down_ref, hidden_grad_ref):
    low = grad.astype(BF16)
    total = grad
    for start in range(0, up_ref.shape[1], CHUNK):
        part = slice(start, start + CHUNK)
        hidden = nt(low, down_ref[part, :]) * gate_ref[:, part].astype(F32)
        hidden = hidden.astype(BF16)
        hidden_grad_ref[:, part] = hidden
        total = total + nt(hidden, up_ref[:, part])
    return low, total


def short_allowed(key_segment, query_segment, causal):
    allowed = key_segment == query_segment
    if causal:
        key = lax.broadcasted_iota(jnp.int32, key_segment.shape, 0)
        query = lax.broadcasted_iota(jnp.int32, key_segment.shape, 1)
        allowed = allowed & (key <= query)
    return jnp.concatenate([allowed, allowed], axis=1)


def short_attend(causal, q_ref, k_ref, v_ref, kseg_ref, qseg_ref, o_ref, lse_ref):
    size = kseg_ref.shape[1]
    for block in range(kseg_ref.shape[0]):
        rows = slice(block * size, (block + 1) * size)
        allowed = short_allowed(kseg_ref[block], qseg_ref[block], causal)
        logs = []
        for pair in range(PAIRS):
            lanes = pair_lanes(pair)
            scores = nt(k_ref[rows, lanes], two_heads(q_ref[rows, lanes]))
            scores = jnp.where(allowed, scores, FLOOR_SCORE)
            top = jnp.max(scores, axis=0, keepdims=True)
            weights = jnp.exp(scores - top)
            total = jnp.sum(weights, axis=0, keepdims=True)
            mixed = nn(v_ref[rows, lanes].T, weights.astype(BF16)) / total
            o_ref[rows, lanes] = diagonal(mixed).T.astype(BF16)
            log_total = top + jnp.log(total)
            logs += [log_total[:, :size], log_total[:, size:]]
        lse_ref[block] = jnp.concatenate(logs, axis=0)


def short_attend_back(
    causal, q_ref, k_ref, v_ref, kseg_ref, qseg_ref, o_ref, lse_ref, go_ref, dq_ref, dk_ref, dv_ref
):
    size = kseg_ref.shape[1]
    for block in range(kseg_ref.shape[0]):
        rows = slice(block * size, (block + 1) * size)
        allowed = short_allowed(kseg_ref[block], qseg_ref[block], causal)
        delta = delta_rows(go_ref[rows, :], o_ref[rows, :])
        lse = lse_ref[block]
        for pair in range(PAIRS):
            lanes = pair_lanes(pair)
            queries, grads = two_heads(q_ref[rows, lanes]), two_heads(go_ref[rows, lanes])
            scores = nt(k_ref[rows, lanes], queries)
            weights = jnp.where(allowed, jnp.exp(scores - pair_row(lse, pair)), 0.0)
            grad_weights = nt(v_ref[rows, lanes], grads)
            grad_scores = (weights * (grad_weights - pair_row(delta, pair))).astype(BF16)
            dv_ref[rows, lanes] = nn(weights.astype(BF16), grads).astype(BF16)
            dk_ref[rows, lanes] = nn(grad_scores, queries).astype(BF16)
            turned = diagonal(nn(k_ref[rows, lanes].T, grad_scores)).T
            dq_ref[rows, lanes] = (turned.astype(BF16).astype(F32) * SCALE).astype(BF16)


def load_keys(ref, pair_index, block, lanes):
    pieces = KEY_BLOCK // ref.shape[2]
    rows = ref[pl.ds(block * pieces, pieces), pair_index, :, lanes]
    return rows.reshape(KEY_BLOCK, rows.shape[2])


def store_keys(ref, pair_index, block, lanes, rows):
    pieces = KEY_BLOCK // ref.shape[2]
    ref[pl.ds(block * pieces, pieces), pair_index, :, lanes] = rows.astype(BF16).reshape(
        pieces, ref.shape[2], rows.shape[1]
    )


def store_part(refs, info_ref, pair_index, block, rows):
    partners, (_, pairs, size, _) = len(refs), refs[0].shape
    if partners == 2 and KEY_BLOCK == 2 * size:
        outer = block ^ info_ref[pairs + 3]
        swap = info_ref[pairs + 1] == 1
        first, second = rows[:size], rows[size:]
        refs[0][outer, pair_index] = jnp.where(swap, second, first)
        refs[1][outer, pair_index] = jnp.where(swap, first, second)
        return
    for piece in range(KEY_BLOCK // size):
        place = block * (KEY_BLOCK // size) + piece
        inner = lax.rem(place, partners) ^ info_ref[pairs + 1]
        outer = lax.div(place, partners) ^ info_ref[pairs + 3]
        part = rows[piece * size : (piece + 1) * size]
        for partner, ref in enumerate(refs):

            @pl.when(inner == partner)
            def _(ref=ref):
                ref[outer, pair_index] = part


def long_limit(info_ref, causal, pair_index, size, pairs):
    length = info_ref[pair_index]
    limit = length
    if causal:
        limit = jnp.minimum(length, info_ref[pairs] + size)
    return length, lax.div(limit + KEY_BLOCK - 1, KEY_BLOCK)


def long_allowed(start, causal, length, block, shape):
    key = lax.broadcasted_iota(jnp.int32, shape, 0) + block * KEY_BLOCK
    allowed = key < length
    if causal:
        half = shape[1] // 2
        lane = lax.broadcasted_iota(jnp.int32, shape, 1)
        query = jnp.where(lane < half, lane, lane - half) + start
        allowed = allowed & (key <= query)
    return allowed


def long_attend(
    causal, info_ref, q_ref, x_ref, k_w, v_w, k_ref, v_ref, o_ref, lse_ref, score_ref, sum_ref, mix_ref
):
    places, pairs, size, width = x_ref.shape
    shape = (KEY_BLOCK, 2 * size)
    everything = slice(None)

    def one(pair_index, carry):
        length, count = long_limit(info_ref, causal, pair_index, size, pairs)
        own = pl.ds(pl.multiple_of(pair_index * size, size), size)

        def first(block, tops):
            rows = pl.ds(pl.multiple_of(block * KEY_BLOCK, KEY_BLOCK), KEY_BLOCK)
            allowed = long_allowed(info_ref[pairs], causal, length, block, shape)
            context = load_keys(x_ref, pair_index, block, everything)
            store_keys(k_ref, pair_index, block, everything, nn(context, k_w[...]))
            store_keys(v_ref, pair_index, block, everything, nn(context, v_w[...]))
            after = []
            for pair in range(PAIRS):
                lanes = pair_lanes(pair)
                keys = load_keys(k_ref, pair_index, block, lanes)
                scores = nt(keys, two_heads(q_ref[own, lanes]))
                scores = jnp.where(allowed, scores, FLOOR_SCORE)
                score_ref[pair, rows] = scores
                folded = jnp.max(scores.reshape(KEY_BLOCK // 8, 8, 2 * size), axis=0)
                after.append(jnp.maximum(tops[pair], folded))
            return tuple(after)

        start = tuple(jnp.full((8, 2 * size), FLOOR_SCORE, F32) for _ in range(PAIRS))
        tops = lax.fori_loop(0, count, first, start)
        tops = [jnp.max(top, axis=0, keepdims=True) for top in tops]
        sum_ref[...] = jnp.zeros_like(sum_ref)
        mix_ref[...] = jnp.zeros_like(mix_ref)

        def second(block, carry):
            rows = pl.ds(pl.multiple_of(block * KEY_BLOCK, KEY_BLOCK), KEY_BLOCK)
            for pair in range(PAIRS):
                weights = jnp.exp(score_ref[pair, rows] - tops[pair])
                sum_ref[pair] += jnp.sum(weights.reshape(KEY_BLOCK // 8, 8, 2 * size), axis=0)
                values = load_keys(v_ref, pair_index, block, pair_lanes(pair))
                mix_ref[pair] += nn(values.T, weights.astype(BF16))
            return carry

        lax.fori_loop(0, count, second, 0)
        logs = []
        for pair in range(PAIRS):
            total = jnp.sum(sum_ref[pair], axis=0, keepdims=True)
            mixed = mix_ref[pair] / total
            o_ref[own, pair_lanes(pair)] = diagonal(mixed).T.astype(BF16)
            log_total = tops[pair] + jnp.log(total)
            logs += [log_total[:, :size], log_total[:, size:]]
        lse_ref[pair_index] = jnp.concatenate(logs, axis=0)
        return carry

    lax.fori_loop(0, pairs, one, 0)


def long_attend_back(
    causal,
    info_ref,
    q_ref,
    k_ref,
    v_ref,
    o_ref,
    lse_ref,
    go_ref,
    k_w,
    v_w,
    dq_ref,
    dk_ref,
    dv_ref,
    part_ref,
    mix_ref,
):
    places, pairs, size, width = k_ref.shape
    shape = (KEY_BLOCK, 2 * size)
    everything = slice(None)

    def one(pair_index, carry):
        length, count = long_limit(info_ref, causal, pair_index, size, pairs)
        own = pl.ds(pl.multiple_of(pair_index * size, size), size)
        delta = delta_rows(go_ref[own, :], o_ref[own, :])
        lse = lse_ref[pair_index]
        mix_ref[...] = jnp.zeros_like(mix_ref)

        def step(block, carry):
            allowed = long_allowed(info_ref[pairs], causal, length, block, shape)
            for pair in range(PAIRS):
                lanes = pair_lanes(pair)
                queries, grads = two_heads(q_ref[own, lanes]), two_heads(go_ref[own, lanes])
                keys = load_keys(k_ref, pair_index, block, lanes)
                scores = nt(keys, queries)
                weights = jnp.where(allowed, jnp.exp(scores - pair_row(lse, pair)), 0.0)
                grad_weights = nt(load_keys(v_ref, pair_index, block, lanes), grads)
                grad_scores = (weights * (grad_weights - pair_row(delta, pair))).astype(BF16)
                store_keys(dv_ref, pair_index, block, lanes, nn(weights.astype(BF16), grads))
                store_keys(dk_ref, pair_index, block, lanes, nn(grad_scores, queries))
                mix_ref[pair] += nn(keys.T, grad_scores)
            part = nt(load_keys(dk_ref, pair_index, block, everything), k_w[...])
            part = part + nt(load_keys(dv_ref, pair_index, block, everything), v_w[...])
            store_part(part_ref, info_ref, pair_index, block, part.astype(BF16))
            return carry

        lax.fori_loop(0, count, step, 0)

        def clear(block, carry):
            nothing = jnp.zeros((KEY_BLOCK, width), BF16)
            store_keys(dk_ref, pair_index, block, everything, nothing)
            store_keys(dv_ref, pair_index, block, everything, nothing)
            store_part(part_ref, info_ref, pair_index, block, nothing)
            return carry

        lax.fori_loop(count, places * size // KEY_BLOCK, clear, 0)
        for pair in range(PAIRS):
            turned = diagonal(mix_ref[pair]).T
            dq_ref[own, pair_lanes(pair)] = (turned.astype(BF16).astype(F32) * SCALE).astype(BF16)
        return carry

    lax.fori_loop(0, pairs, one, 0)


class Refs(dict):
    def __init__(self, *args):
        super().__init__(*args)
        self.coming, self.leaving = {}, {}

    def __getattr__(self, name):
        if name in self.coming:
            self.coming.pop(name).wait()
        return self[name]

    def leave(self, *names):
        for name in names:
            self["left"].add(name)
            for copy in self.leaving.get(name, ()):
                copy.start()


def copied(shape, dtype):
    size = dtype.itemsize
    for length in shape:
        size *= length
    return shape[-1] % 128 == 0 and size >= 2**16


def launch(body, arrays, gives, scratch=(), info=None, after=(), pieces=(), moved=None, cost=10):
    memory = pl.BlockSpec(memory_space=pltpu.VMEM)
    far = pl.BlockSpec(memory_space=pl.ANY)
    ins, specs = [], []
    if info is not None:
        ins.append(info)
        specs.append(pl.BlockSpec(memory_space=pltpu.SMEM))
    by_itself = lambda name, shape, dtype: (
        copied(shape, jnp.dtype(dtype)) if moved is None else name in moved
    )
    moved_in = [name for name, a in arrays.items() if by_itself(name, a.shape, a.dtype)]
    moved_out = [name for name, give in gives.items() if name in pieces or by_itself(name, *give)]
    for name, array in arrays.items():
        ins.append(array)
        specs.append(far if name in moved_in else memory)
    for array in after:
        ins.append(array)
        specs.append(far)
    count_out = sum(gives[name][0][0] if name in pieces else 1 for name in moved_out)
    rooms = [pltpu.VMEM(arrays[name].shape, arrays[name].dtype) for name in moved_in]
    rooms += [pltpu.VMEM(*gives[name]) for name in moved_out]
    rooms += [pltpu.SemaphoreType.DMA((max(len(moved_in), 1),))]
    rooms += [pltpu.SemaphoreType.DMA((max(count_out, 1),))]
    names = [name for name, _ in scratch]

    def run(*refs):
        refs = list(refs)
        r = Refs()
        if info is not None:
            r["info"] = refs.pop(0)
        outer = {name: refs.pop(0) for name in arrays}
        del refs[: len(after)]
        outer.update((name, refs.pop(0)) for name in gives)
        room = {name: refs.pop(0) for name in moved_in + moved_out}
        come, go = refs.pop(0), refs.pop(0)
        r.update(outer)
        r.update(room)
        r.update(zip(names, refs))
        for place, name in enumerate(moved_in):
            copy = pltpu.make_async_copy(outer[name], room[name], come.at[place])
            copy.start()
            r.coming[name] = copy
        place = 0
        for name in moved_out:
            copies = []
            if name in pieces:
                for piece in range(gives[name][0][0]):
                    source, target = room[name].at[piece], outer[name].at[piece]
                    copies.append(pltpu.make_async_copy(source, target, go.at[place]))
                    place += 1
            else:
                copies.append(pltpu.make_async_copy(room[name], outer[name], go.at[place]))
                place += 1
            r.leaving[name] = copies
        left = set()
        r["left"] = left
        body(r)
        for name in list(r.coming):
            r.coming.pop(name).wait()
        for name in moved_out:
            if name not in left and name not in pieces:
                r.leave(name)
        for name in moved_out:
            for copy in r.leaving[name]:
                copy.wait()

    out = pl.pallas_call(
        run,
        in_specs=specs,
        out_specs=[far if name in moved_out else memory for name in gives],
        out_shape=[jax.ShapeDtypeStruct(shape, dtype) for shape, dtype in gives.values()],
        scratch_shapes=rooms + [shape for _, shape in scratch],
        compiler_params=pltpu.CompilerParams(vmem_limit_bytes=VMEM_LIMIT),
        cost_estimate=pl.CostEstimate(
            flops=int(cost * 1.1e9), bytes_accessed=int(cost * 3.5e6), transcendentals=0
        ),
    )(*ins)
    return Refs(zip(gives, out))


VMEM_LIMIT = 56 * 2**20


def add_sums(ref, rows):
    ref[...] = jnp.concatenate(rows, axis=0)


def encoder_tail(r, o_ref):
    residual = r.x[...].astype(F32) + nn(o_ref[...], r.w_o[...])
    first, normed, inverse = norm(residual, r.gain[0:1], r.bias[0:1])
    r.n1[...] = normed.astype(BF16)
    r.i1[...] = inverse
    low, total = feed_forward(first, r.up, r.down, r.act, r.gate)
    r.y[...] = low
    r.leave("n1", "act", "gate", "y")
    encoded, normed, inverse = norm(total, r.gain[1:2], r.bias[1:2])
    r.n2[...] = normed.astype(BF16)
    r.i2[...] = inverse
    r.enc[...] = encoded.astype(BF16)


def project_short(r, name, rows, w_q, w_k, w_v, context=None):
    context = rows if context is None else context
    r["q" + name][...] = (nn(rows, w_q) * SCALE).astype(BF16)
    r["k" + name][...] = nn(context, w_k).astype(BF16)
    r["v" + name][...] = nn(context, w_v).astype(BF16)


def short_encoder_forward(r):
    project_short(r, "", r.x[...], r.w_in[0], r.w_in[1], r.w_in[2])
    r.leave("q", "k", "v")
    short_attend(False, r.q, r.k, r.v, r.kseg, r.qseg, r.o, r.lse)
    r.leave("o")
    encoder_tail(r, r.o)


def decoder_middle(r, o_ref):
    residual = r.t[...].astype(F32) + nn(o_ref[...], r.w_o[...])
    upper, normed, inverse = norm(residual, r.gain[0:1], r.bias[0:1])
    r.n3[...] = normed.astype(BF16)
    r.i3[...] = inverse
    r.u[...] = upper.astype(BF16)
    return upper


def decoder_tail(r, upper, o_ref):
    gain, bias = r.gain, r.bias
    residual = upper + nn(o_ref[...], r.w_co[...])
    middle, normed4, inverse4 = norm(residual, gain[1:2], bias[1:2])
    low, total = feed_forward(middle, r.up, r.down, r.act, r.gate)
    r.m[...] = low
    r.leave("m", "act", "gate")
    final, normed5, inverse5 = norm(total, gain[2:3], bias[2:3])
    r.final[...] = final
    r.leave("final")
    grad, gain5, bias5 = norm_back(r.cot[...].astype(F32), normed5, inverse5, gain[2:3])
    low, grad = feed_back(grad, r.gate, r.up, r.down, r.dh)
    r.b5[...] = low
    r.leave("b5", "dh")
    grad, gain4, bias4 = norm_back(grad, normed4, inverse4, gain[1:2])
    low = grad.astype(BF16)
    r.b4[...] = low
    r.d4[...] = grad
    r.go_c[...] = nt(low, r.w_co[...]).astype(BF16)
    add_sums(r.small, [gain4, gain5, bias4, bias5])


def short_decoder_forward(r):
    project_short(r, "", r.t[...], r.w_in[0], r.w_in[1], r.w_in[2])
    r.leave("q", "k", "v")
    short_attend(True, r.q, r.k, r.v, r.tkseg, r.tqseg, r.o, r.lse)
    r.leave("o")
    r.upper[...] = decoder_middle(r, r.o)


def short_cross_forward(r):
    project_short(r, "_c", r.u[...], r.w_cin[0], r.w_cin[1], r.w_cin[2], r.enc[...])
    r.leave("q_c", "k_c", "v_c")
    short_attend(False, r.q_c, r.k_c, r.v_c, r.kseg, r.tqseg, r.o_c, r.lse_c)
    r.leave("o_c")
    decoder_tail(r, r.upper[...], r.o_c)


def decoder_middle_back(r):
    grad = r.d4[...] + nt(r.dq_c[...], r.w_cin[0])
    grad, gain3, bias3 = norm_back(grad, r.n3[...], r.i3[...], r.gain[0:1])
    low = grad.astype(BF16)
    r.b3[...] = low
    r.go[...] = nt(low, r.w_o[...]).astype(BF16)
    add_sums(r.small, [gain3, bias3])
    return grad


def short_decoder_back(r):
    short_attend_back(
        False, r.q_c, r.k_c, r.v_c, r.kseg, r.tqseg, r.o_c, r.lse_c, r.go_c, r.dq_c, r.dk_c, r.dv_c
    )
    r.denc[...] = nt(r.dk_c[...], r.w_cin[1]) + nt(r.dv_c[...], r.w_cin[2])
    r.leave("dq_c", "dk_c", "dv_c", "denc")
    r.d3[...] = decoder_middle_back(r)
    short_attend_back(
        True, r.q, r.k, r.v, r.tkseg, r.tqseg, r.o, r.lse, r.go, r.dq, r.dk, r.dv
    )
    r.leave("dq", "dk", "dv")
    grad = r.d3[...] + nt(r.dq[...], r.w_in[0])
    r.dt[...] = grad + nt(r.dk[...], r.w_in[1]) + nt(r.dv[...], r.w_in[2])


def encoder_tail_back(r, grad):
    grad, gain2, bias2 = norm_back(grad, r.n2[...], r.i2[...], r.gain[1:2])
    low, grad = feed_back(grad, r.gate, r.up, r.down, r.dh)
    r.b2[...] = low
    r.leave("b2", "dh")
    grad, gain1, bias1 = norm_back(grad, r.n1[...], r.i1[...], r.gain[0:1])
    low = grad.astype(BF16)
    r.b1[...] = low
    r.go[...] = nt(low, r.w_o[...]).astype(BF16)
    r.d1[...] = grad
    add_sums(r.small, [gain1, gain2, bias1, bias2])


def short_encoder_back(r):
    encoder_tail_back(r, r.denc[...])
    short_attend_back(
        False, r.q, r.k, r.v, r.kseg, r.qseg, r.o, r.lse, r.go, r.dq, r.dk, r.dv
    )
    r.leave("dq", "dk", "dv")
    grad = r.d1[...] + nt(r.dq[...], r.w_in[0])
    r.dx[...] = grad + nt(r.dk[...], r.w_in[1]) + nt(r.dv[...], r.w_in[2])


def long_encoder_forward(r):
    r.q[...] = (nn(r.x[...], r.w_in[0]) * SCALE).astype(BF16)
    long_attend(
        False, r.info, r.q, r.xg, r.w_in.at[1], r.w_in.at[2], r.k, r.v, r.o, r.lse, r.s, r.a, r.mix
    )
    r.leave("q", "k", "v", "o")
    encoder_tail(r, r.o)


def long_self_forward(r):
    r.q[...] = (nn(r.t[...], r.w_in[0]) * SCALE).astype(BF16)
    long_attend(
        True, r.info, r.q, r.tg, r.w_in.at[1], r.w_in.at[2], r.k, r.v, r.o, r.lse, r.s, r.a, r.mix
    )
    r.leave("q", "k", "v", "o")
    upper = decoder_middle(r, r.o)
    r.upper[...] = upper
    r.q_c[...] = (nn(upper.astype(BF16), r.w_cin[0]) * SCALE).astype(BF16)


def long_cross(r):
    k_w, v_w = r.w_cin.at[1], r.w_cin.at[2]
    long_attend(
        False, r.info, r.q_c, r.eg, k_w, v_w, r.k_c, r.v_c, r.o_c, r.lse_c, r.s, r.a, r.mix
    )
    r.leave("k_c", "v_c", "o_c")
    decoder_tail(r, r.upper[...], r.o_c)


def part_refs(r):
    return [r[name] for name in r if name[0] == "p" and name[1:].isdigit()]


def long_cross_back(r):
    long_attend_back(
        False,
        r.info,
        r.q_c,
        r.k_c,
        r.v_c,
        r.o_c,
        r.lse_c,
        r.go_c,
        r.w_cin.at[1],
        r.w_cin.at[2],
        r.dq_c,
        r.dk_c,
        r.dv_c,
        part_refs(r),
        r.mix,
    )


def long_self_back(r):
    grad = decoder_middle_back(r)
    long_attend_back(
        True,
        r.info,
        r.q,
        r.k,
        r.v,
        r.o,
        r.lse,
        r.go,
        r.w_in.at[1],
        r.w_in.at[2],
        r.dq,
        r.dk,
        r.dv,
        part_refs(r),
        r.mix,
    )
    r.dt[...] = grad + nt(r.dq[...], r.w_in[0])


def long_encoder_tail_back(r):
    grad = r.part0[...].astype(F32) + r.part1[...].astype(F32)
    grad = grad + r.part2[...].astype(F32) + r.part3[...].astype(F32)
    encoder_tail_back(r, grad)


def long_encoder_back(r):
    long_attend_back(
        False,
        r.info,
        r.q,
        r.k,
        r.v,
        r.o,
        r.lse,
        r.go,
        r.w_in.at[1],
        r.w_in.at[2],
        r.dq,
        r.dk,
        r.dv,
        part_refs(r),
        r.mix,
    )
    r.dx[...] = r.d1[...] + nt(r.dq[...], r.w_in[0])


SIDE = 512


class Weights:
    def __init__(self, pairs, base=None):
        self.arrays, self.plan, known = {}, [], {}

        def place(rows):
            if isinstance(rows, tuple):
                return rows
            if id(rows) not in known:
                known[id(rows)] = "w%d" % len(known)
                self.arrays[known[id(rows)]] = rows
            return known[id(rows)], rows.shape[1]

        for terms in pairs:
            terms = [(place(a), place(b)) for a, b in terms]
            (_, height), (_, width) = terms[0]
            for row in range(0, height, SIDE):
                for column in range(0, width, SIDE):
                    self.plan.append([(a[0], row, b[0], column) for a, b in terms])
        count = len(self.plan)
        self.gives = {name: ((count, SIDE // 2, SIDE), BF16) for name in ("kept", "sent")}
        if base is not None:
            self.arrays["base"] = base

    def body(self, r, core):
        half = SIDE // 2
        for index, terms in enumerate(self.plan):
            for flip, name in enumerate(("kept", "sent")):
                total = None
                if "base" in self.arrays:
                    begin = pl.multiple_of((core ^ flip) * half, half)
                    total = r.base[index, pl.ds(begin, half), :].astype(F32)
                for a, row, b, column in terms:
                    left, right = getattr(r, a), getattr(r, b)
                    begin = pl.multiple_of(row + (core ^ flip) * half, half)
                    across = slice(column, column + SIDE)
                    if len(left.shape) == 4:
                        tall = left.shape[0] * left.shape[1] * left.shape[2]
                        rows = left[:, :, :, pl.ds(begin, half)].reshape(tall, half)
                    else:
                        rows = left[:, pl.ds(begin, half)]
                    if len(right.shape) == 4:
                        tall = right.shape[0] * right.shape[1] * right.shape[2]
                        product = tn(rows, right[:, :, :, across].reshape(tall, SIDE))
                    else:
                        product = tn(rows, right[:, across])
                    total = product if total is None else total + product
                r[name][index] = total.astype(BF16)
                r.leaving[name][index].start()


def whole_tiles(chunks, after=(), cost=10):
    weights = [Weights([[pair] for pair in chunk]) for chunk in chunks]
    arrays, gives = {}, {}
    for number, part in enumerate(weights):
        gives["c%d" % number] = ((len(part.plan), SIDE, SIDE), BF16)
        arrays.update((name + "c%d" % number, array) for name, array in part.arrays.items())

    def body(r):
        for number, part in enumerate(weights):
            tag = "c%d" % number
            for index, ((a, row, b, column),) in enumerate(part.plan):
                left, right = getattr(r, a + tag), getattr(r, b + tag)
                product = tn(left[:, row : row + SIDE], right[:, column : column + SIDE])
                r[tag][index] = product.astype(BF16)
                r.leaving[tag][index].start()

    out = launch(body, arrays, gives, after=after, pieces=tuple(gives), cost=cost)
    return list(out.values())


def weight_tiles(pairs, core_info, after=(), cost=10, base=None):
    weights = Weights(pairs, base)
    out = launch(
        lambda r: weights.body(r, r.info[0]),
        weights.arrays,
        weights.gives,
        info=core_info,
        after=after,
        pieces=("kept", "sent"),
        cost=cost,
    )
    return [out.kept, out.sent]


def send(piece, axis, offset):
    count = lax.axis_size(axis)
    return lax.ppermute(piece, axis, [(i, i ^ offset) for i in range(count)])


def ordered(pieces, place, dim):
    if len(pieces) == 1:
        return pieces[0]
    level = len(pieces) // 2
    inside = lax.rem(place, level)
    low = ordered(pieces[:level], inside, dim)
    high = ordered(pieces[level:], inside, dim)
    return jnp.where(
        place >= level, jnp.concatenate([high, low], dim), jnp.concatenate([low, high], dim)
    )


def hold(value, token):
    return lax.optimization_barrier((value, token))[0]


def gather_first(piece, axis):
    return [piece] + [send(piece, axis, k) for k in range(1, lax.axis_size(axis))]


def gather_last(pieces, axis, dim, token=None):
    if token is not None:
        pieces = hold(pieces, token)
    return ordered(pieces, lax.axis_index(axis), dim)


def added(pieces):
    total = pieces[0].astype(F32)
    for piece in pieces[1:]:
        total = total + piece.astype(F32)
    return total.astype(BF16)


def scatter_step(pending, axis, dim, token=None):
    if token is not None:
        pending = hold(pending, token)
    place, count = lax.axis_index(axis), lax.axis_size(axis)
    size = pending[0].shape[dim] // count
    after = []
    for k in range(count):
        parts = [
            lax.dynamic_slice_in_dim(piece, (place ^ k) * size, size, dim) for piece in pending
        ]
        block = added(parts)
        after.append(send(block, axis, k) if k else block)
    return after


def gather_step(piece, axis, dim):
    return gather_last(gather_first(piece, axis), axis, dim)


def gather_early(rows):
    return lax.all_gather(rows, (OUTER, INNER), axis=0, tiled=False)


SEQ = (OUTER, INNER)


class Chain:
    def __init__(self, halves, order, small=None, doubled=False):
        self.order = (CORE,) + order
        self.doubled = doubled
        self.stage = 0
        self.tiles = halves[0].shape[0]
        self.small, self.carried = None, 0
        if small is not None:
            self.carried = small.shape[0]
            halves = [jnp.concatenate([self.flat(half), small]) for half in halves]
        self.held = [halves[0], send(halves[1], CORE, 1)]

    def flat(self, block):
        return block.reshape(-1, block.shape[-1])

    def parts(self):
        if not self.carried:
            return self.held, None
        body = [piece[: -self.carried] for piece in self.held]
        body = [piece.reshape(self.tiles, -1, piece.shape[-1]) for piece in body]
        return body, added([piece[-self.carried :] for piece in self.held])

    def next_axis(self):
        stage, count = self.stage + 1, len(self.order)
        return self.order[stage] if stage < count else self.order[2 * count - 1 - stage]

    def over(self):
        return self.stage == 2 * len(self.order) - 1

    def go(self):
        axis = self.next_axis()
        self.stage += 1
        count = len(self.order)
        if self.doubled and self.stage in (count - 1, count):
            total = added(self.held)
            self.held = [total, send(total, OUTER, self.stage - count + 2)]
            return
        if self.doubled and self.stage == count + 1:
            pending, self.small = self.parts()
            self.held = gather_first(added(pending), axis)
            return
        if self.stage < count:
            pending, small = self.parts()
            place, members = lax.axis_index(axis), lax.axis_size(axis)
            size = pending[0].shape[1] // members
            self.held = []
            for k in range(members):
                begin = (place ^ k) * size
                block = added([lax.dynamic_slice_in_dim(p, begin, size, 1) for p in pending])
                if small is not None:
                    block = jnp.concatenate([self.flat(block), small])
                self.held.append(send(block, axis, k) if k else block)
            return
        if self.stage == count:
            pending, self.small = self.parts()
            piece = added(pending)
        else:
            piece = gather_last(self.held, self.order[2 * count - self.stage], 1)
        self.held = gather_first(piece, axis)

    def volume(self):
        return self.held[0].size * 2 / 2**20


class Spread:
    def __init__(self, part, straight):
        self.straight, self.stage = straight, 0
        self.held = [send(rows, INNER, k) if k else rows for k, rows in enumerate(part)]

    def next_axis(self):
        return OUTER

    def over(self):
        return self.stage == (1 if self.straight else 2)

    def go(self):
        self.stage += 1
        if self.straight:
            blocks = [added([piece[k] for piece in self.held]) for k in range(4)]
            self.held = [send(block, OUTER, k) if k else block for k, block in enumerate(blocks)]
            return
        if self.stage == 1:
            pick, offset = (lambda piece, odd: jnp.stack([piece[odd], piece[2 + odd]])), 1
        else:
            pick, offset = (lambda piece, odd: piece[odd]), 2
        mine, theirs = [added([pick(piece, odd) for piece in self.held]) for odd in (0, 1)]
        self.held = [mine, send(theirs, OUTER, offset)]

    def volume(self):
        return self.held[0].size * 2 / 2**20

    def result(self):
        return added(self.held)


def finish(chains, *tokens):
    held, _ = lax.optimization_barrier(([chain.held for chain in chains], tokens))
    for chain, pieces in zip(chains, held):
        chain.held = pieces


def go(*chains):
    for chain in chains:
        chain.go()


FLOW = {CORE: 3.5, X: 21.0, INNER: 21.0, OUTER: 84.0}


def plan_of(chain):
    if isinstance(chain, Spread):
        return [(INNER, 21.0, 1), (OUTER, 10.5, 1), (OUTER, 10.5, 1)][chain.stage :]
    size, out = chain.tiles * 0.5, []
    for axis in chain.order:
        count = lax.axis_size(axis)
        if axis == OUTER and chain.doubled:
            out += [(OUTER, 21.0 * size, 1), (OUTER, 42.0 * size, 1)]
            continue
        size = size / count
        out.append((axis, FLOW[axis] * size, count - 1))
    back = [entry for entry in reversed(out)]
    if chain.doubled:
        back = [entry for entry in back if entry[0] != OUTER]
    return (out + back)[chain.stage :]


def rehearse(plans, first, gate, weights, slack):
    free = dict.fromkeys(FLOW, 0.0)
    position, queue, order, clock, waiting = [0] * len(plans), [], [], 0.0, []

    def depart(index, when):
        axis, long, _ = plans[index][position[index]]
        begin = max(when, free[axis])
        free[axis] = begin + long
        queue.append((free[axis] + 6.0, index))

    def left(index):
        rest = plans[index][position[index] :]
        return weights[index] * sum(long + 10.0 for _, long, _ in rest)

    for index, since in first:
        depart(index, -since)
    while queue or waiting:
        soon = min(queue)[0] if queue else clock + 99.0
        if waiting and soon > clock + 4.0:
            clock += 6.5
            order.append((waiting.pop(0), True))
            continue
        near = [entry for entry in queue if entry[0] <= max(clock, soon) + slack]
        entry = max(near, key=lambda entry: left(entry[1]))
        queue.remove(entry)
        arrival, index = entry
        clock = max(clock, arrival)
        position[index] += 1
        order.append((index, False))
        if position[index] == len(plans[index]):
            clock += 1.0
            waiting.append(index)
            continue
        axis, long, sends = plans[index][position[index]]
        clock += 2.0 + 1.5 * sends + 0.03 * long
        depart(index, clock)
        if gate[1] == index and position[index] == 1:
            clock += 2.0
            depart(gate[0], clock)
    return clock, order


def run_out(flights, later):
    chains, ends = [chain for chain, _, _ in flights], [end for _, _, end in flights]
    plans = [plan_of(chain) for chain in chains]
    plans.append([(INNER, 21.0, 1), (OUTER, 10.5, 1), (OUTER, 10.5, 1)])
    first = [(index, since) for index, (_, since, _) in enumerate(flights)]
    rng, best = random.Random(7), None
    for trial in range(1500):
        weights = [1.0 if trial < 4 else rng.uniform(0.3, 2.0) for _ in plans]
        slack = (0.0, 2.0, 4.0, 8.0)[trial % 4]
        found = rehearse(plans, first, (len(chains), 0), weights, slack)
        if best is None or found[0] < best[0]:
            best = found
    token, results = (), {}
    for index, is_end in best[1]:
        chain = chains[index]
        if is_end:
            results[index] = ends[index](chain, token)
            token = (results[index][0],)
            continue
        finish([chain], *token)
        if chain.over():
            token = tuple(chain.held)
            continue
        chain.go()
        token = (chain.held[0],)
        if index == 0 and chain.stage == 1:
            chain, _, end = later(token)
            chains.append(chain)
            ends.append(end)
    return [results[index] for index in range(len(chains))]


def assemble(chain, core_info, shapes, after=()):
    tiles, half, side = chain.held[0].shape

    places = []
    for name, shape in shapes.items():
        blocks = shape[0] if len(shape) > 2 else shape[0] * shape[1] // (side * side)
        for block in range(blocks):
            if len(shape) > 2:
                places.append((name, lambda rows, b=block: (b, rows, slice(None))))
            elif shape[1] > shape[0]:
                lanes = slice(block * side, (block + 1) * side)
                places.append((name, lambda rows, l=lanes: (rows, l)))
            else:
                places.append((name, lambda rows, b=block: (pl.ds(rows.start + b * side, half), slice(None))))

    def body(info, mine, other, *refs):
        outs = dict(zip(shapes, refs))
        room, full, come, go = refs[len(shapes) :]
        starts = [pl.multiple_of((info[0] ^ flip) * half, half) for flip in (0, 1)]
        arrive, leave = [], []
        for tile in range(tiles):
            for flip, source in enumerate((mine, other)):
                index = 2 * tile + flip
                arrive.append(pltpu.make_async_copy(source.at[tile], room.at[index], come.at[index]))
                arrive[-1].start()
        for tile, (name, where) in enumerate(places):
            for flip in (0, 1):
                index = 2 * tile + flip
                arrive[index].wait()
                full[index] = room[index].astype(F32)
                target = outs[name].at[where(pl.ds(starts[flip], half))]
                leave.append(pltpu.make_async_copy(full.at[index], target, go.at[index]))
                leave[-1].start()
        for copy in leave:
            copy.wait()

    far = pl.BlockSpec(memory_space=pl.ANY)
    return pl.pallas_call(
        lambda info, mine, other, *refs: body(info, mine, other, *refs[len(after) :]),
        in_specs=[pl.BlockSpec(memory_space=pltpu.SMEM)] + [far] * (2 + len(after)),
        out_specs=[far] * len(shapes),
        out_shape=[jax.ShapeDtypeStruct(shape, F32) for shape in shapes.values()],
        scratch_shapes=[
            pltpu.VMEM((2 * tiles, half, side), BF16),
            pltpu.VMEM((2 * tiles, half, side), F32),
            pltpu.SemaphoreType.DMA((2 * tiles,)),
            pltpu.SemaphoreType.DMA((2 * tiles,)),
        ],
        compiler_params=pltpu.CompilerParams(vmem_limit_bytes=VMEM_LIMIT),
        cost_estimate=pl.CostEstimate(flops=5 * 10**9, bytes_accessed=2 * 10**7, transcendentals=0),
    )(core_info, chain.held[0], chain.held[1], *after)


def shards(
    source_short,
    target_short,
    source_segment,
    target_segment,
    source_long,
    target_long,
    source_length,
    target_length,
    cotangent_short,
    cotangent_long,
    encoder_project,
    encoder_output,
    encoder_up,
    encoder_down,
    encoder_gain,
    encoder_bias,
    decoder_project,
    decoder_output,
    cross_project,
    cross_output,
    decoder_up,
    decoder_down,
    decoder_gain,
    decoder_bias,
):
    blocks, size, width = source_short.shape
    hidden = encoder_up.shape[1]
    rows = blocks * size
    pairs, own, _ = source_long.shape
    rows_long = pairs * own
    flat = lambda a: a.reshape(-1, width)
    start = lax.axis_index((OUTER, INNER)) * own
    core = lax.axis_index(CORE)
    here = [start, lax.axis_index(INNER), core, lax.axis_index(OUTER)]
    here = jnp.stack(here).astype(jnp.int32)
    info_of = lambda lengths: jnp.concatenate([lengths, here])
    core_info = core.astype(jnp.int32)[None]
    source_info, target_info = info_of(source_length), info_of(target_length)

    spread = lambda s: jnp.broadcast_to(s[:, :, None], (blocks, size, size))
    line = lambda s: s[:, None, :]
    encoder_in = {
        "w_in": encoder_project,
        "w_o": encoder_output,
        "up": encoder_up,
        "down": encoder_down,
        "gain": encoder_gain,
        "bias": encoder_bias,
    }
    decoder_in = {
        "w_in": decoder_project,
        "w_o": decoder_output,
        "w_cin": cross_project,
        "w_co": cross_output,
        "up": decoder_up,
        "down": decoder_down,
        "gain": decoder_gain,
        "bias": decoder_bias,
    }

    def pick(table, names):
        return {name: table[name] for name in names}

    def rows_of(n, names):
        return {name: ((n, width), BF16) for name in names}

    def wide_of(n, names):
        return {name: ((n, hidden), BF16) for name in names}

    def floats(n, names):
        return {name: ((n, width), F32) for name in names}

    def column(n, names):
        return {name: ((n, 1), F32) for name in names}

    def logs(n, names):
        return {name: ((n, HEADS, size), F32) for name in names}

    def sums(n):
        return {"small": ((n, width), F32)}

    def keys_of(names):
        shape = (places, pairs, own, width)
        return {name: (shape, BF16) for name in names}

    def parts():
        inner = lax.axis_size(INNER)
        return {"p%d" % k: ((places // inner, pairs, own, width), BF16) for k in range(inner)}

    def saved(kernel, names):
        return {name: kernel[name] for name in names}

    whole_source = gather_early(source_long)
    places = lax.axis_size(OUTER) * lax.axis_size(INNER)
    keys = places * own
    work = [
        ("s", pltpu.VMEM((PAIRS, keys, 2 * own), F32)),
        ("a", pltpu.VMEM((PAIRS, 8, 2 * own), F32)),
        ("mix", pltpu.VMEM((PAIRS, PAIR, 2 * own), F32)),
    ]
    mix = work[2:]

    segments = {"kseg": spread(source_segment), "qseg": line(source_segment)}
    turned = {"tkseg": spread(target_segment), "tqseg": line(target_segment)}
    encoder_keeps = lambda n: {
        **rows_of(n, ("n1", "y", "n2", "enc")),
        **wide_of(n, ("act", "gate")),
        **column(n, ("i1", "i2")),
    }
    se = launch(
        short_encoder_forward,
        {"x": flat(source_short), **segments, **encoder_in},
        {**rows_of(rows, ("q", "k", "v", "o")), **logs(blocks, ("lse",)), **encoder_keeps(rows)},
        cost=0.01,
    )
    decoder_keeps = lambda n: {
        **rows_of(n, ("m", "b5", "b4", "go_c")),
        **wide_of(n, ("act", "gate", "dh")),
        **floats(n, ("final", "d4")),
        **sums(4),
    }
    sd = launch(
        short_decoder_forward,
        {
            "t": flat(target_short),
            **turned,
            **pick(decoder_in, ("w_in", "w_o", "gain", "bias")),
        },
        {
            **rows_of(rows, ("q", "k", "v", "o", "n3", "u")),
            **logs(blocks, ("lse",)),
            **column(rows, ("i3",)),
            **floats(rows, ("upper",)),
        },
        after=(se.lse,),
        cost=0.01,
    )
    early_target = gather_first(hold(target_long, sd.lse)[None, None], OUTER)
    sc = launch(
        short_cross_forward,
        {
            "u": sd.u,
            "upper": sd.upper,
            "enc": se.enc,
            "cot": flat(cotangent_short),
            "kseg": segments["kseg"],
            "tqseg": turned["tqseg"],
            **pick(decoder_in, ("w_cin", "w_co", "up", "down", "gain", "bias")),
        },
        {
            **rows_of(rows, ("q_c", "k_c", "v_c", "o_c")),
            **logs(blocks, ("lse_c",)),
            **decoder_keeps(rows),
        },
        after=(sd.lse,),
        cost=0.01,
    )

    sb = launch(
        short_decoder_back,
        {
            **saved(sd, ("q", "k", "v", "o", "lse", "n3", "i3")),
            **saved(sc, ("q_c", "k_c", "v_c", "o_c", "lse_c", "go_c", "d4")),
            "kseg": segments["kseg"],
            **turned,
            **pick(decoder_in, ("w_in", "w_o", "w_cin", "gain")),
        },
        {
            **rows_of(rows, ("dq_c", "dk_c", "dv_c", "dq", "dk", "dv", "b3", "go")),
            **floats(rows, ("denc", "dt")),
            **sums(2),
        },
        scratch=[("d3", pltpu.VMEM((rows, width), F32))],
        after=(sc.small,),
        cost=0.01,
    )

    early_target = gather_last(early_target, OUTER, 0, sb.small)

    whole_source = hold(whole_source, sb.small)
    x_long, t_long = flat(source_long), flat(target_long)
    le = launch(
        long_encoder_forward,
        {"x": x_long, "xg": whole_source, **encoder_in},
        {
            **rows_of(rows_long, ("q", "o")),
            **keys_of(("k", "v")),
            **logs(pairs, ("lse",)),
            **encoder_keeps(rows_long),
        },
        scratch=work,
        info=source_info,
        after=(sb.small, early_target),
        cost=13,
        moved=(),
    )
    late_target = gather_first(hold(early_target, le.lse), INNER)
    whole_encoded = gather_early(le.enc.reshape(pairs, own, width))

    seb = launch(
        short_encoder_back,
        {
            "denc": sb.denc,
            **saved(se, ("q", "k", "v", "o", "lse", "n1", "i1", "n2", "i2", "gate")),
            **segments,
            **pick(encoder_in, ("w_in", "w_o", "up", "down", "gain")),
        },
        {
            **rows_of(rows, ("dq", "dk", "dv", "b1", "b2", "go")),
            **wide_of(rows, ("dh",)),
            **floats(rows, ("dx",)),
            **sums(4),
        },
        scratch=[("d1", pltpu.VMEM((rows, width), F32))],
        after=(le.lse,),
        cost=16,
    )

    t_short, x_short = flat(target_short), flat(source_short)
    short_weights = whole_tiles(
        [
            [(sc.m, sc.dh), (sc.act, sc.b5)],
            [
                (sd.u, sb.dq_c),
                (se.enc, sb.dk_c),
                (se.enc, sb.dv_c),
                (sc.o_c, sc.b4),
                (t_short, sb.dq),
                (t_short, sb.dk),
                (t_short, sb.dv),
                (sd.o, sb.b3),
            ],
            [(se.y, seb.dh), (se.act, seb.b2)],
            [(x_short, seb.dq), (x_short, seb.dk), (x_short, seb.dv), (se.o, seb.b1)],
        ],
        after=(seb.small,),
        cost=15,
    )
    whole_target = gather_last(late_target, INNER, 1, short_weights[0])
    whole_target = whole_target.reshape(places, pairs, own, width)
    ls = launch(
        long_self_forward,
        {
            "t": t_long,
            "tg": whole_target,
            **pick(decoder_in, ("w_in", "w_o", "w_cin", "gain", "bias")),
        },
        {
            **rows_of(rows_long, ("q", "o", "n3", "u", "q_c")),
            **keys_of(("k", "v")),
            **logs(pairs, ("lse",)),
            **column(rows_long, ("i3",)),
            **floats(rows_long, ("upper",)),
        },
        scratch=work,
        info=target_info,
        after=(short_weights[0],),
        cost=10,
        moved=(),
    )

    whole_encoded = hold(whole_encoded, ls.lse)
    lc = launch(
        long_cross,
        {
            "eg": whole_encoded,
            "upper": ls.upper,
            "q_c": ls.q_c,
            "cot": flat(cotangent_long),
            **pick(decoder_in, ("w_cin", "w_co", "up", "down", "gain", "bias")),
        },
        {
            **rows_of(rows_long, ("o_c",)),
            **keys_of(("k_c", "v_c")),
            **logs(pairs, ("lse_c",)),
            **decoder_keeps(rows_long),
        },
        scratch=work,
        info=source_info,
        after=(ls.lse,),
        cost=14,
        moved=("k_c", "v_c", "up", "down", "w_co", "act", "gate", "dh", "final"),
    )
    lcb = launch(
        long_cross_back,
        {
            "q_c": ls.q_c,
            **saved(lc, ("k_c", "v_c", "o_c", "lse_c", "go_c")),
            **pick(decoder_in, ("w_cin",)),
        },
        {**rows_of(rows_long, ("dq_c",)), **keys_of(("dk_c", "dv_c")), **parts()},
        scratch=mix,
        info=source_info,
        after=(lc.small,),
        cost=14,
        moved=(),
    )
    encoded_back = Spread(part_refs(lcb), True)
    first_weights = Weights(
        [[(lc.m, lc.dh)], [(lc.act, lc.b5)]], short_weights[0]
    )

    def self_back_and_weights(r):
        long_self_back(r)
        first_weights.body(r, r.info[pairs + 2])

    lsb = launch(
        self_back_and_weights,
        {
            "d4": lc.d4,
            "dq_c": lcb.dq_c,
            **saved(ls, ("q", "k", "v", "o", "lse", "n3", "i3")),
            **pick(decoder_in, ("w_in", "w_o", "w_cin", "gain")),
            **first_weights.arrays,
        },
        {
            **first_weights.gives,
            **rows_of(rows_long, ("dq", "b3")),
            **keys_of(("dk", "dv")),
            **parts(),
            **floats(rows_long, ("dt",)),
            **sums(2),
        },
        scratch=mix + [("go", pltpu.VMEM((rows_long, width), BF16))],
        info=target_info,
        after=(lcb.dq_c,),
        pieces=("kept", "sent"),
        cost=22,
    )
    decoder_ffn = Chain([lsb.kept, lsb.sent], (X, INNER, OUTER))
    finish([encoded_back], lsb.small)
    go(encoded_back)
    target_back = Spread(part_refs(lsb), False)
    grad_attention = weight_tiles(
        [
            [(ls.u, lcb.dq_c)],
            [(flat(whole_encoded), flat(lcb.dk_c))],
            [(flat(whole_encoded), flat(lcb.dv_c))],
            [(lc.o_c, lc.b4)],
            [(t_long, lsb.dq)],
            [(flat(whole_target), flat(lsb.dk))],
            [(flat(whole_target), flat(lsb.dv))],
            [(ls.o, lsb.b3)],
        ],
        core_info,
        after=(lsb.small, encoded_back.held[0]),
        base=short_weights[1],
        cost=15,
    )
    finish([encoded_back, decoder_ffn], grad_attention[0])
    go(decoder_ffn)
    attention = Chain(grad_attention, (INNER, X, OUTER))
    ffn_weights = Weights(
        [
            [(le.y, ("dh", hidden))],
            [(le.act, ("b2", width))],
        ],
        short_weights[2],
    )

    def encoder_back_and_weights(r):
        long_encoder_tail_back(r)
        ffn_weights.body(r, r.info[0])

    leb = launch(
        encoder_back_and_weights,
        {
            **{"part%d" % k: flat(piece) for k, piece in enumerate(encoded_back.held)},
            **saved(le, ("n1", "i1", "n2", "i2", "gate")),
            **pick(encoder_in, ("down", "up", "w_o", "gain")),
            **ffn_weights.arrays,
        },
        {
            **ffn_weights.gives,
            **rows_of(rows_long, ("b1", "b2", "go")),
            **wide_of(rows_long, ("dh",)),
            **floats(rows_long, ("d1",)),
            **sums(4),
        },
        info=core_info,
        after=(grad_attention[0], decoder_ffn.held[0]),
        pieces=("kept", "sent"),
        cost=12,
    )
    small = jnp.concatenate([seb.small + leb.small, sb.small + lsb.small, sc.small + lc.small])
    small = jnp.pad(small, ((0, 16 - small.shape[0]), (0, 0))).astype(BF16)
    finish([attention], leb.small)
    go(attention)
    encoder_ffn = Chain([leb.kept, leb.sent], (X, INNER, OUTER))
    attention_weights = Weights(
        [
            [(x_long, ("dq", width))],
            [(whole_source, ("dk", width))],
            [(whole_source, ("dv", width))],
            [(le.o, leb.b1)],
        ],
        short_weights[3],
    )

    def attention_back_and_weights(r):
        long_encoder_back(r)
        r.leave("dx", *[name for name in r if name[0] == "p" and name[1:].isdigit()])
        attention_weights.body(r, r.info[pairs + 2])

    lea = launch(
        attention_back_and_weights,
        {
            **saved(le, ("q", "k", "v")),
            "o": le.o,
            "lse": le.lse,
            **saved(leb, ("go", "d1")),
            **pick(encoder_in, ("w_in",)),
            **attention_weights.arrays,
        },
        {
            **attention_weights.gives,
            **parts(),
            **floats(rows_long, ("dx",)),
        },
        scratch=mix
        + [
            ("dq", pltpu.VMEM((rows_long, width), BF16)),
            ("dk", pltpu.VMEM((places, pairs, own, width), BF16)),
            ("dv", pltpu.VMEM((places, pairs, own, width), BF16)),
        ],
        info=source_info,
        after=(leb.small, attention.held[0]),
        pieces=("kept", "sent"),
        cost=19,
    )
    done = lea.dx
    finish([decoder_ffn, encoder_ffn, target_back], done)
    encoder = Chain([lea.kept, lea.sent], (INNER, X, OUTER), small, True)
    go(decoder_ffn, encoder_ffn, target_back)
    square = (3, width, width)
    feed = {"up": encoder_up.shape, "down": encoder_down.shape}
    one = {"project": square, "output": square[1:]}
    two = {"cross_in": square, "cross_out": square[1:], "self_in": square, "self_out": square[1:]}

    def out(shapes):
        return lambda chain, token: assemble(chain, core_info, shapes, token)

    rows_out = lambda rows: lambda chain, token: [chain.result().astype(F32) + rows]
    flights = [
        (encoder, 0.0, out(one)),
        (decoder_ffn, 0.0, out(feed)),
        (attention, 20.0, out(two)),
        (encoder_ffn, 0.0, out(feed)),
        (target_back, 0.0, rows_out(lsb.dt.reshape(source_long.shape))),
    ]

    def source_back(token):
        chain = Spread(hold(part_refs(lea), token), False)
        return chain, 0.0, rows_out(lea.dx.reshape(source_long.shape))

    results = run_out(flights, source_back)
    (encoder_in_out, encoder_out_out), (decoder_up_out, decoder_down_out) = results[:2]
    (cross_in, cross_out, self_in, self_out), (encoder_up_out, encoder_down_out) = results[2:4]
    (grad_target,), (grad_source,) = results[4:]
    small = encoder.small.astype(F32)
    return (
        sc.final.reshape(source_short.shape),
        lc.final.reshape(source_long.shape),
        seb.dx.reshape(source_short.shape),
        sb.dt.reshape(source_short.shape),
        grad_source,
        grad_target,
        encoder_in_out,
        encoder_out_out,
        encoder_up_out,
        encoder_down_out,
        small[0:2],
        small[2:4],
        self_in,
        self_out,
        cross_in,
        cross_out,
        decoder_up_out,
        decoder_down_out,
        jnp.stack([small[4], small[6], small[7]]),
        jnp.stack([small[5], small[8], small[9]]),
    )


def solution(mesh):
    group, seq = mesh.devices.shape
    fine = Mesh(
        mesh.devices.reshape(group // 2, 2, 4, seq // 4), (X, CORE, OUTER, INNER)
    )
    groups, positions = (X, CORE), (OUTER, INNER)
    blocks = P(groups + positions, None, None)
    long_rows = P(groups, positions, None)
    in_specs = (
        (blocks, blocks, P(groups + positions, None), P(groups + positions, None))
        + (long_rows, long_rows, P(groups), P(groups), blocks, long_rows)
        + (P(),) * 14
    )
    out_specs = (blocks, long_rows, blocks, blocks, long_rows, long_rows) + (P(),) * 14
    return jax.shard_map(
        shards, mesh=fine, in_specs=in_specs, out_specs=out_specs, check_vma=False
    )
```

```python
import functools
import random
import jax
import jax.numpy as jnp
from jax import lax
from jax.experimental import pallas as pl
from jax.experimental.pallas import tpu as pltpu
from jax.sharding import Mesh, PartitionSpec as P

HEADS = 8
HEAD_DIM = 64
PAIR = 2 * HEAD_DIM
PAIRS = HEADS // 2
SCALE = HEAD_DIM**-0.5
FLOOR_SCORE = -1e30
EPSILON = 1e-05
KEY_BLOCK = 256
CHUNK = 512
F32 = jnp.float32
BF16 = jnp.bfloat16
CORE, X, INNER, OUTER = "core", "x", "inner", "outer"


def nn(left, right):
    return lax.dot_general(left, right, (((1,), (0,)), ((), ())), preferred_element_type=F32)


def nt(left, right):
    return lax.dot_general(left, right, (((1,), (1,)), ((), ())), preferred_element_type=F32)


def tn(left, right):
    return lax.dot_general(left, right, (((0,), (0,)), ((), ())), preferred_element_type=F32)


def two_heads(rows):
    lane = lax.broadcasted_iota(jnp.int32, rows.shape, 1)
    zero = jnp.zeros_like(rows)
    first = jnp.where(lane < HEAD_DIM, rows, zero)
    second = jnp.where(lane < HEAD_DIM, zero, rows)
    return jnp.concatenate([first, second], axis=0)


def diagonal(product):
    half = product.shape[1] // 2
    return jnp.concatenate([product[:HEAD_DIM, :half], product[HEAD_DIM:, half:]], axis=0)


def delta_rows(grad_out, outputs):
    product = grad_out.astype(F32) * outputs.astype(F32)
    high = product.astype(BF16)
    low = (product - high.astype(F32)).astype(BF16)
    width = product.shape[1]
    head = lax.broadcasted_iota(jnp.int32, (HEADS, width), 0)
    lane = lax.broadcasted_iota(jnp.int32, (HEADS, width), 1)
    pick = jnp.where(lax.div(lane, HEAD_DIM) == head, 1.0, 0.0).astype(BF16)
    return nt(pick, high) + nt(pick, low)


def pair_row(rows, pair):
    return jnp.concatenate([rows[2 * pair : 2 * pair + 1], rows[2 * pair + 1 : 2 * pair + 2]], axis=1)


def pair_lanes(pair):
    return slice(pair * PAIR, (pair + 1) * PAIR)


def norm(residual, gain, bias):
    centred = residual - jnp.mean(residual, axis=1, keepdims=True)
    inverse = lax.rsqrt(jnp.mean(centred * centred, axis=1, keepdims=True) + EPSILON)
    normed = centred * inverse
    return normed * gain + bias, normed, inverse


def norm_back(upstream, normed, inverse, gain):
    normed = normed.astype(F32)
    scaled = upstream * gain
    grad = inverse * (
        scaled
        - jnp.mean(scaled, axis=1, keepdims=True)
        - normed * jnp.mean(scaled * normed, axis=1, keepdims=True)
    )
    return (
        grad,
        jnp.sum(upstream * normed, axis=0, keepdims=True),
        jnp.sum(upstream, axis=0, keepdims=True),
    )


def chunks(ref, axis, step):
    def body(index, carry):
        step(pl.ds(pl.multiple_of(index * CHUNK, CHUNK), CHUNK))
        return carry

    lax.fori_loop(0, ref.shape[axis] // CHUNK, body, 0)


def feed_forward(rows, up_ref, down_ref, act_ref, gate_ref, low_ref, total_ref):
    low_ref[...] = rows.astype(BF16)
    total_ref[...] = rows

    def step(part):
        hidden = nn(low_ref[...], up_ref[:, part])
        sigmoid = 0.5 * jnp.tanh(0.5 * hidden) + 0.5
        active = hidden * sigmoid
        gate_ref[:, part] = (sigmoid + active * (1.0 - sigmoid)).astype(BF16)
        active = active.astype(BF16)
        act_ref[:, part] = active
        total_ref[...] += nn(active, down_ref[part, :])

    chunks(up_ref, 1, step)
    return total_ref[...]


def feed_back(grad, gate_ref, up_ref, down_ref, hidden_grad_ref, low_ref, total_ref):
    low_ref[...] = grad.astype(BF16)
    total_ref[...] = grad

    def step(part):
        hidden = nt(low_ref[...], down_ref[part, :]) * gate_ref[:, part].astype(F32)
        hidden = hidden.astype(BF16)
        hidden_grad_ref[:, part] = hidden
        total_ref[...] += nt(hidden, up_ref[:, part])

    chunks(up_ref, 1, step)
    return total_ref[...]


def short_allowed(key_segment, query_segment, causal):
    allowed = key_segment == query_segment
    if causal:
        key = lax.broadcasted_iota(jnp.int32, key_segment.shape, 0)
        query = lax.broadcasted_iota(jnp.int32, key_segment.shape, 1)
        allowed = allowed & (key <= query)
    return jnp.concatenate([allowed, allowed], axis=1)


def short_attend(causal, q_ref, k_ref, v_ref, kseg_ref, qseg_ref, o_ref, lse_ref):
    size = kseg_ref.shape[1]

    def one(block, carry):
        rows = pl.ds(pl.multiple_of(block * size, size), size)
        allowed = short_allowed(kseg_ref[block], qseg_ref[block], causal)
        logs = []
        for pair in range(PAIRS):
            lanes = pair_lanes(pair)
            scores = nt(k_ref[rows, lanes], two_heads(q_ref[rows, lanes]))
            scores = jnp.where(allowed, scores, FLOOR_SCORE)
            top = jnp.max(scores, axis=0, keepdims=True)
            weights = jnp.exp(scores - top)
            total = jnp.sum(weights, axis=0, keepdims=True)
            mixed = nn(v_ref[rows, lanes].T, weights.astype(BF16)) / total
            o_ref[rows, lanes] = diagonal(mixed).T.astype(BF16)
            log_total = top + jnp.log(total)
            logs += [log_total[:, :size], log_total[:, size:]]
        lse_ref[block] = jnp.concatenate(logs, axis=0)
        return carry

    lax.fori_loop(0, kseg_ref.shape[0], one, 0)


def short_attend_back(
    causal, q_ref, k_ref, v_ref, kseg_ref, qseg_ref, o_ref, lse_ref, go_ref, dq_ref, dk_ref, dv_ref
):
    size = kseg_ref.shape[1]

    def one(block, carry):
        rows = pl.ds(pl.multiple_of(block * size, size), size)
        allowed = short_allowed(kseg_ref[block], qseg_ref[block], causal)
        delta = delta_rows(go_ref[rows, :], o_ref[rows, :])
        lse = lse_ref[block]
        for pair in range(PAIRS):
            lanes = pair_lanes(pair)
            queries, grads = two_heads(q_ref[rows, lanes]), two_heads(go_ref[rows, lanes])
            scores = nt(k_ref[rows, lanes], queries)
            weights = jnp.where(allowed, jnp.exp(scores - pair_row(lse, pair)), 0.0)
            grad_weights = nt(v_ref[rows, lanes], grads)
            grad_scores = (weights * (grad_weights - pair_row(delta, pair))).astype(BF16)
            dv_ref[rows, lanes] = nn(weights.astype(BF16), grads).astype(BF16)
            dk_ref[rows, lanes] = nn(grad_scores, queries).astype(BF16)
            turned = diagonal(nn(k_ref[rows, lanes].T, grad_scores)).T
            dq_ref[rows, lanes] = (turned.astype(BF16).astype(F32) * SCALE).astype(BF16)
        return carry

    lax.fori_loop(0, kseg_ref.shape[0], one, 0)


def load_keys(ref, pair_index, block, lanes):
    pieces = KEY_BLOCK // ref.shape[2]
    rows = ref[pl.ds(block * pieces, pieces), pair_index, :, lanes]
    return rows.reshape(KEY_BLOCK, rows.shape[2])


def store_keys(ref, pair_index, block, lanes, rows):
    pieces = KEY_BLOCK // ref.shape[2]
    ref[pl.ds(block * pieces, pieces), pair_index, :, lanes] = rows.astype(BF16).reshape(
        pieces, ref.shape[2], rows.shape[1]
    )


def store_part(refs, info_ref, pair_index, block, rows):
    partners, (_, pairs, size, _) = len(refs), refs[0].shape
    if partners == 2 and KEY_BLOCK == 2 * size:
        outer = block ^ info_ref[pairs + 3]
        swap = info_ref[pairs + 1] == 1
        first, second = rows[:size], rows[size:]
        refs[0][outer, pair_index] = jnp.where(swap, second, first)
        refs[1][outer, pair_index] = jnp.where(swap, first, second)
        return
    for piece in range(KEY_BLOCK // size):
        place = block * (KEY_BLOCK // size) + piece
        inner = lax.rem(place, partners) ^ info_ref[pairs + 1]
        outer = lax.div(place, partners) ^ info_ref[pairs + 3]
        part = rows[piece * size : (piece + 1) * size]
        for partner, ref in enumerate(refs):

            @pl.when(inner == partner)
            def _(ref=ref):
                ref[outer, pair_index] = part


def long_limit(info_ref, causal, pair_index, size, pairs):
    length = info_ref[pair_index]
    limit = length
    if causal:
        limit = jnp.minimum(length, info_ref[pairs] + size)
    return length, lax.div(limit + KEY_BLOCK - 1, KEY_BLOCK)


def long_allowed(start, causal, length, block, shape):
    key = lax.broadcasted_iota(jnp.int32, shape, 0) + block * KEY_BLOCK
    allowed = key < length
    if causal:
        half = shape[1] // 2
        lane = lax.broadcasted_iota(jnp.int32, shape, 1)
        query = jnp.where(lane < half, lane, lane - half) + start
        allowed = allowed & (key <= query)
    return allowed


def long_attend(
    causal, info_ref, q_ref, x_ref, k_w, v_w, k_ref, v_ref, o_ref, lse_ref, score_ref, sum_ref, mix_ref
):
    places, pairs, size, width = x_ref.shape
    shape = (KEY_BLOCK, 2 * size)
    everything = slice(None)

    def one(pair_index, carry):
        length, count = long_limit(info_ref, causal, pair_index, size, pairs)
        own = pl.ds(pl.multiple_of(pair_index * size, size), size)

        def first(block, tops):
            rows = pl.ds(pl.multiple_of(block * KEY_BLOCK, KEY_BLOCK), KEY_BLOCK)
            allowed = long_allowed(info_ref[pairs], causal, length, block, shape)
            context = load_keys(x_ref, pair_index, block, everything)
            store_keys(k_ref, pair_index, block, everything, nn(context, k_w[...]))
            store_keys(v_ref, pair_index, block, everything, nn(context, v_w[...]))
            after = []
            for pair in range(PAIRS):
                lanes = pair_lanes(pair)
                keys = load_keys(k_ref, pair_index, block, lanes)
                scores = nt(keys, two_heads(q_ref[own, lanes]))
                scores = jnp.where(allowed, scores, FLOOR_SCORE)
                score_ref[pair, rows] = scores
                folded = jnp.max(scores.reshape(KEY_BLOCK // 8, 8, 2 * size), axis=0)
                after.append(jnp.maximum(tops[pair], folded))
            return tuple(after)

        start = tuple(jnp.full((8, 2 * size), FLOOR_SCORE, F32) for _ in range(PAIRS))
        tops = lax.fori_loop(0, count, first, start)
        tops = [jnp.max(top, axis=0, keepdims=True) for top in tops]
        sum_ref[...] = jnp.zeros_like(sum_ref)
        mix_ref[...] = jnp.zeros_like(mix_ref)

        def second(block, carry):
            rows = pl.ds(pl.multiple_of(block * KEY_BLOCK, KEY_BLOCK), KEY_BLOCK)
            for pair in range(PAIRS):
                weights = jnp.exp(score_ref[pair, rows] - tops[pair])
                sum_ref[pair] += jnp.sum(weights.reshape(KEY_BLOCK // 8, 8, 2 * size), axis=0)
                values = load_keys(v_ref, pair_index, block, pair_lanes(pair))
                mix_ref[pair] += nn(values.T, weights.astype(BF16))
            return carry

        lax.fori_loop(0, count, second, 0)
        logs = []
        for pair in range(PAIRS):
            total = jnp.sum(sum_ref[pair], axis=0, keepdims=True)
            mixed = mix_ref[pair] / total
            o_ref[own, pair_lanes(pair)] = diagonal(mixed).T.astype(BF16)
            log_total = tops[pair] + jnp.log(total)
            logs += [log_total[:, :size], log_total[:, size:]]
        lse_ref[pair_index] = jnp.concatenate(logs, axis=0)
        return carry

    lax.fori_loop(0, pairs, one, 0)


def long_attend_back(
    causal,
    info_ref,
    q_ref,
    k_ref,
    v_ref,
    o_ref,
    lse_ref,
    go_ref,
    k_w,
    v_w,
    dq_ref,
    dk_ref,
    dv_ref,
    part_ref,
    mix_ref,
):
    places, pairs, size, width = k_ref.shape
    shape = (KEY_BLOCK, 2 * size)
    everything = slice(None)

    def one(pair_index, carry):
        length, count = long_limit(info_ref, causal, pair_index, size, pairs)
        own = pl.ds(pl.multiple_of(pair_index * size, size), size)
        delta = delta_rows(go_ref[own, :], o_ref[own, :])
        lse = lse_ref[pair_index]
        mix_ref[...] = jnp.zeros_like(mix_ref)

        def step(block, carry):
            allowed = long_allowed(info_ref[pairs], causal, length, block, shape)
            for pair in range(PAIRS):
                lanes = pair_lanes(pair)
                queries, grads = two_heads(q_ref[own, lanes]), two_heads(go_ref[own, lanes])
                keys = load_keys(k_ref, pair_index, block, lanes)
                scores = nt(keys, queries)
                weights = jnp.where(allowed, jnp.exp(scores - pair_row(lse, pair)), 0.0)
                grad_weights = nt(load_keys(v_ref, pair_index, block, lanes), grads)
                grad_scores = (weights * (grad_weights - pair_row(delta, pair))).astype(BF16)
                store_keys(dv_ref, pair_index, block, lanes, nn(weights.astype(BF16), grads))
                store_keys(dk_ref, pair_index, block, lanes, nn(grad_scores, queries))
                mix_ref[pair] += nn(keys.T, grad_scores)
            part = nt(load_keys(dk_ref, pair_index, block, everything), k_w[...])
            part = part + nt(load_keys(dv_ref, pair_index, block, everything), v_w[...])
            store_part(part_ref, info_ref, pair_index, block, part.astype(BF16))
            return carry

        lax.fori_loop(0, count, step, 0)

        def clear(block, carry):
            nothing = jnp.zeros((KEY_BLOCK, width), BF16)
            store_keys(dk_ref, pair_index, block, everything, nothing)
            store_keys(dv_ref, pair_index, block, everything, nothing)
            store_part(part_ref, info_ref, pair_index, block, nothing)
            return carry

        lax.fori_loop(count, places * size // KEY_BLOCK, clear, 0)
        for pair in range(PAIRS):
            turned = diagonal(mix_ref[pair]).T
            dq_ref[own, pair_lanes(pair)] = (turned.astype(BF16).astype(F32) * SCALE).astype(BF16)
        return carry

    lax.fori_loop(0, pairs, one, 0)


class Refs(dict):
    def __init__(self, *args):
        super().__init__(*args)
        self.coming, self.leaving, self.pieced = {}, {}, {}

    def __getattr__(self, name):
        if name in self.coming:
            self.coming.pop(name).wait()
        return self[name]

    def leave_piece(self, name, piece):
        source, target, signals, first = self.pieced[name]
        pltpu.make_async_copy(source.at[piece], target.at[piece], signals.at[first + piece]).start()

    def leave(self, *names):
        for name in names:
            self["left"].add(name)
            for copy in self.leaving.get(name, ()):
                copy.start()


def copied(shape, dtype):
    size = dtype.itemsize
    for length in shape:
        size *= length
    return shape[-1] % 128 == 0 and size >= 2**16


def launch(body, arrays, gives, scratch=(), info=None, after=(), pieces=(), moved=None, cost=10):
    memory = pl.BlockSpec(memory_space=pltpu.VMEM)
    far = pl.BlockSpec(memory_space=pl.ANY)
    ins, specs = [], []
    if info is not None:
        ins.append(info)
        specs.append(pl.BlockSpec(memory_space=pltpu.SMEM))
    by_itself = lambda name, shape, dtype: (
        copied(shape, jnp.dtype(dtype)) if moved is None else name in moved
    )
    moved_in = [name for name, a in arrays.items() if by_itself(name, a.shape, a.dtype)]
    moved_out = [name for name, give in gives.items() if name in pieces or by_itself(name, *give)]
    for name, array in arrays.items():
        ins.append(array)
        specs.append(far if name in moved_in else memory)
    for array in after:
        ins.append(array)
        specs.append(far)
    count_out = sum(gives[name][0][0] if name in pieces else 1 for name in moved_out)
    rooms = [pltpu.VMEM(arrays[name].shape, arrays[name].dtype) for name in moved_in]
    rooms += [pltpu.VMEM(*gives[name]) for name in moved_out]
    rooms += [pltpu.SemaphoreType.DMA((max(len(moved_in), 1),))]
    rooms += [pltpu.SemaphoreType.DMA((max(count_out, 1),))]
    names = [name for name, _ in scratch]

    def run(*refs):
        refs = list(refs)
        r = Refs()
        if info is not None:
            r["info"] = refs.pop(0)
        outer = {name: refs.pop(0) for name in arrays}
        del refs[: len(after)]
        outer.update((name, refs.pop(0)) for name in gives)
        room = {name: refs.pop(0) for name in moved_in + moved_out}
        come, go = refs.pop(0), refs.pop(0)
        r.update(outer)
        r.update(room)
        r.update(zip(names, refs))
        for place, name in enumerate(moved_in):
            copy = pltpu.make_async_copy(outer[name], room[name], come.at[place])
            copy.start()
            r.coming[name] = copy
        place = 0
        for name in moved_out:
            copies = []
            if name in pieces:
                r.pieced[name] = (room[name], outer[name], go, place)
                for piece in range(gives[name][0][0]):
                    source, target = room[name].at[piece], outer[name].at[piece]
                    copies.append(pltpu.make_async_copy(source, target, go.at[place]))
                    place += 1
            else:
                copies.append(pltpu.make_async_copy(room[name], outer[name], go.at[place]))
                place += 1
            r.leaving[name] = copies
        left = set()
        r["left"] = left
        body(r)
        for name in list(r.coming):
            r.coming.pop(name).wait()
        for name in moved_out:
            if name not in left and name not in pieces:
                r.leave(name)
        for name in moved_out:
            for copy in r.leaving[name]:
                copy.wait()

    out = pl.pallas_call(
        run,
        in_specs=specs,
        out_specs=[far if name in moved_out else memory for name in gives],
        out_shape=[jax.ShapeDtypeStruct(shape, dtype) for shape, dtype in gives.values()],
        scratch_shapes=rooms + [shape for _, shape in scratch],
        compiler_params=pltpu.CompilerParams(vmem_limit_bytes=VMEM_LIMIT),
        cost_estimate=pl.CostEstimate(
            flops=int(cost * 1.1e9), bytes_accessed=int(cost * 3.5e6), transcendentals=0
        ),
    )(*ins)
    return Refs(zip(gives, out))


VMEM_LIMIT = 56 * 2**20


def add_sums(ref, rows):
    ref[...] = jnp.concatenate(rows, axis=0)


def encoder_tail(r, o_ref):
    residual = r.x[...].astype(F32) + nn(o_ref[...], r.w_o[...])
    first, normed, inverse = norm(residual, r.gain[0:1], r.bias[0:1])
    r.n1[...] = normed.astype(BF16)
    r.i1[...] = inverse
    total = feed_forward(first, r.up, r.down, r.act, r.gate, r.y, r.acc)
    r.leave("n1", "act", "gate", "y")
    encoded, normed, inverse = norm(total, r.gain[1:2], r.bias[1:2])
    r.n2[...] = normed.astype(BF16)
    r.i2[...] = inverse
    r.enc[...] = encoded.astype(BF16)


def project_short(r, name, rows, w_q, w_k, w_v, context=None):
    context = rows if context is None else context
    r["q" + name][...] = (nn(rows, w_q) * SCALE).astype(BF16)
    r["k" + name][...] = nn(context, w_k).astype(BF16)
    r["v" + name][...] = nn(context, w_v).astype(BF16)


def short_encoder_forward(r):
    project_short(r, "", r.x[...], r.w_in[0], r.w_in[1], r.w_in[2])
    r.leave("q", "k", "v")
    short_attend(False, r.q, r.k, r.v, r.kseg, r.qseg, r.o, r.lse)
    r.leave("o")
    encoder_tail(r, r.o)


def decoder_middle(r, o_ref):
    residual = r.t[...].astype(F32) + nn(o_ref[...], r.w_o[...])
    upper, normed, inverse = norm(residual, r.gain[0:1], r.bias[0:1])
    r.n3[...] = normed.astype(BF16)
    r.i3[...] = inverse
    r.u[...] = upper.astype(BF16)
    return upper


def decoder_tail(r, upper, o_ref):
    gain, bias = r.gain, r.bias
    residual = upper + nn(o_ref[...], r.w_co[...])
    middle, normed4, inverse4 = norm(residual, gain[1:2], bias[1:2])
    total = feed_forward(middle, r.up, r.down, r.act, r.gate, r.m, r.acc)
    r.leave("m", "act", "gate")
    final, normed5, inverse5 = norm(total, gain[2:3], bias[2:3])
    r.final[...] = final
    r.leave("final")
    grad, gain5, bias5 = norm_back(r.cot[...].astype(F32), normed5, inverse5, gain[2:3])
    grad = feed_back(grad, r.gate, r.up, r.down, r.dh, r.b5, r.acc)
    r.leave("b5", "dh")
    grad, gain4, bias4 = norm_back(grad, normed4, inverse4, gain[1:2])
    low = grad.astype(BF16)
    r.b4[...] = low
    r.d4[...] = grad
    r.go_c[...] = nt(low, r.w_co[...]).astype(BF16)
    add_sums(r.small, [gain4, gain5, bias4, bias5])


def short_decoder_forward(r):
    project_short(r, "", r.t[...], r.w_in[0], r.w_in[1], r.w_in[2])
    r.leave("q", "k", "v")
    short_attend(True, r.q, r.k, r.v, r.tkseg, r.tqseg, r.o, r.lse)
    r.leave("o")
    r.upper[...] = decoder_middle(r, r.o)


def short_cross_forward(r):
    project_short(r, "_c", r.u[...], r.w_cin[0], r.w_cin[1], r.w_cin[2], r.enc[...])
    r.leave("q_c", "k_c", "v_c")
    short_attend(False, r.q_c, r.k_c, r.v_c, r.kseg, r.tqseg, r.o_c, r.lse_c)
    r.leave("o_c")
    decoder_tail(r, r.upper[...], r.o_c)


def decoder_middle_back(r):
    grad = r.d4[...] + nt(r.dq_c[...], r.w_cin[0])
    grad, gain3, bias3 = norm_back(grad, r.n3[...], r.i3[...], r.gain[0:1])
    low = grad.astype(BF16)
    r.b3[...] = low
    r.go[...] = nt(low, r.w_o[...]).astype(BF16)
    add_sums(r.small, [gain3, bias3])
    return grad


def short_decoder_back(r):
    short_attend_back(
        False, r.q_c, r.k_c, r.v_c, r.kseg, r.tqseg, r.o_c, r.lse_c, r.go_c, r.dq_c, r.dk_c, r.dv_c
    )
    r.denc[...] = nt(r.dk_c[...], r.w_cin[1]) + nt(r.dv_c[...], r.w_cin[2])
    r.leave("dq_c", "dk_c", "dv_c", "denc")
    r.d3[...] = decoder_middle_back(r)
    short_attend_back(
        True, r.q, r.k, r.v, r.tkseg, r.tqseg, r.o, r.lse, r.go, r.dq, r.dk, r.dv
    )
    r.leave("dq", "dk", "dv")
    grad = r.d3[...] + nt(r.dq[...], r.w_in[0])
    r.dt[...] = grad + nt(r.dk[...], r.w_in[1]) + nt(r.dv[...], r.w_in[2])


def encoder_tail_back(r, grad):
    grad, gain2, bias2 = norm_back(grad, r.n2[...], r.i2[...], r.gain[1:2])
    grad = feed_back(grad, r.gate, r.up, r.down, r.dh, r.b2, r.acc)
    r.leave("b2", "dh")
    grad, gain1, bias1 = norm_back(grad, r.n1[...], r.i1[...], r.gain[0:1])
    low = grad.astype(BF16)
    r.b1[...] = low
    r.go[...] = nt(low, r.w_o[...]).astype(BF16)
    r.d1[...] = grad
    add_sums(r.small, [gain1, gain2, bias1, bias2])


def short_encoder_back(r):
    encoder_tail_back(r, r.denc[...])
    short_attend_back(
        False, r.q, r.k, r.v, r.kseg, r.qseg, r.o, r.lse, r.go, r.dq, r.dk, r.dv
    )
    r.leave("dq", "dk", "dv")
    grad = r.d1[...] + nt(r.dq[...], r.w_in[0])
    r.dx[...] = grad + nt(r.dk[...], r.w_in[1]) + nt(r.dv[...], r.w_in[2])


def long_encoder_forward(r):
    r.q[...] = (nn(r.x[...], r.w_in[0]) * SCALE).astype(BF16)
    long_attend(
        False, r.info, r.q, r.xg, r.w_in.at[1], r.w_in.at[2], r.k, r.v, r.o, r.lse, r.s, r.a, r.mix
    )
    r.leave("q", "k", "v", "o")
    encoder_tail(r, r.o)


def long_self_forward(r):
    r.q[...] = (nn(r.t[...], r.w_in[0]) * SCALE).astype(BF16)
    long_attend(
        True, r.info, r.q, r.tg, r.w_in.at[1], r.w_in.at[2], r.k, r.v, r.o, r.lse, r.s, r.a, r.mix
    )
    r.leave("q", "k", "v", "o")
    upper = decoder_middle(r, r.o)
    r.upper[...] = upper
    r.q_c[...] = (nn(upper.astype(BF16), r.w_cin[0]) * SCALE).astype(BF16)


def long_cross(r):
    k_w, v_w = r.w_cin.at[1], r.w_cin.at[2]
    long_attend(
        False, r.info, r.q_c, r.eg, k_w, v_w, r.k_c, r.v_c, r.o_c, r.lse_c, r.s, r.a, r.mix
    )
    r.leave("k_c", "v_c", "o_c")
    decoder_tail(r, r.upper[...], r.o_c)


def part_refs(r):
    return [r[name] for name in r if name[0] == "p" and name[1:].isdigit()]


def long_cross_back(r):
    long_attend_back(
        False,
        r.info,
        r.q_c,
        r.k_c,
        r.v_c,
        r.o_c,
        r.lse_c,
        r.go_c,
        r.w_cin.at[1],
        r.w_cin.at[2],
        r.dq_c,
        r.dk_c,
        r.dv_c,
        part_refs(r),
        r.mix,
    )


def long_self_back(r):
    grad = decoder_middle_back(r)
    long_attend_back(
        True,
        r.info,
        r.q,
        r.k,
        r.v,
        r.o,
        r.lse,
        r.go,
        r.w_in.at[1],
        r.w_in.at[2],
        r.dq,
        r.dk,
        r.dv,
        part_refs(r),
        r.mix,
    )
    r.dt[...] = grad + nt(r.dq[...], r.w_in[0])


def long_encoder_tail_back(r):
    grad = r.part0[...].astype(F32) + r.part1[...].astype(F32)
    grad = grad + r.part2[...].astype(F32) + r.part3[...].astype(F32)
    encoder_tail_back(r, grad)


def long_encoder_back(r):
    long_attend_back(
        False,
        r.info,
        r.q,
        r.k,
        r.v,
        r.o,
        r.lse,
        r.go,
        r.w_in.at[1],
        r.w_in.at[2],
        r.dq,
        r.dk,
        r.dv,
        part_refs(r),
        r.mix,
    )
    r.dx[...] = r.d1[...] + nt(r.dq[...], r.w_in[0])


SIDE = 512


class Weights:
    def __init__(self, pairs, base=None):
        self.arrays, self.plan, known = {}, [], {}

        def place(rows):
            if isinstance(rows, tuple):
                return rows
            if id(rows) not in known:
                known[id(rows)] = "w%d" % len(known)
                self.arrays[known[id(rows)]] = rows
            return known[id(rows)], rows.shape[-1]

        self.count = 0
        for terms in pairs:
            terms = [(place(a), place(b)) for a, b in terms]
            (_, height), (_, width) = terms[0]
            self.plan.append((self.count, width // SIDE, [(a[0], b[0]) for a, b in terms]))
            self.count += height // SIDE * (width // SIDE)
        self.gives = {name: ((self.count, SIDE // 2, SIDE), BF16) for name in ("kept", "sent")}
        if base is not None:
            self.arrays["base"] = base

    def each(self, r, step):
        ends = [first for first, _, _ in self.plan[1:]] + [self.count]
        for (first, across, terms), end in zip(self.plan, ends):
            terms = [(getattr(r, a), getattr(r, b)) for a, b in terms]

            def body(tile, carry, first=first, across=across, terms=terms):
                row = pl.multiple_of(lax.div(tile - first, across) * SIDE, SIDE)
                column = pl.multiple_of(lax.rem(tile - first, across) * SIDE, SIDE)
                step(tile, row, column, terms)
                return carry

            lax.fori_loop(first, end, body, 0)

    def body(self, r, core):
        half = SIDE // 2
        if "base" in self.arrays:
            r.base

        def step(tile, row, column, terms):
            for flip, name in enumerate(("kept", "sent")):
                inside = pl.multiple_of((core ^ flip) * half, half)
                total = None
                if "base" in self.arrays:
                    total = r["base"][tile, pl.ds(inside, half), :].astype(F32)
                for left, right in terms:
                    rows = pl.ds(pl.multiple_of(row + inside, half), half)
                    across = pl.ds(column, SIDE)
                    if len(left.shape) == 4:
                        tall = left.shape[0] * left.shape[1] * left.shape[2]
                        first = left[:, :, :, rows].reshape(tall, half)
                    else:
                        first = left[:, rows]
                    if len(right.shape) == 4:
                        tall = right.shape[0] * right.shape[1] * right.shape[2]
                        product = tn(first, right[:, :, :, across].reshape(tall, SIDE))
                    else:
                        product = tn(first, right[:, across])
                    total = product if total is None else total + product
                r[name][tile] = total.astype(BF16)
                r.leave_piece(name, tile)

        self.each(r, step)


class Tagged:
    def __init__(self, r, tag):
        self.r, self.tag = r, tag

    def __getattr__(self, name):
        return getattr(self.r, name + self.tag)


def whole_tiles(chunks, after=(), cost=10):
    weights = [Weights([[pair] for pair in chunk]) for chunk in chunks]
    arrays, gives = {}, {}
    for number, part in enumerate(weights):
        gives["c%d" % number] = ((part.count, SIDE, SIDE), BF16)
        arrays.update((name + "c%d" % number, array) for name, array in part.arrays.items())

    def body(r):
        for number, part in enumerate(weights):
            tag = "c%d" % number

            def step(tile, row, column, terms, tag=tag):
                ((left, right),) = terms
                product = tn(left[:, pl.ds(row, SIDE)], right[:, pl.ds(column, SIDE)])
                r[tag][tile] = product.astype(BF16)
                r.leave_piece(tag, tile)

            part.each(Tagged(r, tag), step)

    out = launch(body, arrays, gives, after=after, pieces=tuple(gives), cost=cost)
    return list(out.values())


def weight_tiles(pairs, core_info, after=(), cost=10, base=None):
    weights = Weights(pairs, base)
    out = launch(
        lambda r: weights.body(r, r.info[0]),
        weights.arrays,
        weights.gives,
        info=core_info,
        after=after,
        pieces=("kept", "sent"),
        cost=cost,
    )
    return [out.kept, out.sent]


def send(piece, axis, offset):
    count = lax.axis_size(axis)
    return lax.ppermute(piece, axis, [(i, i ^ offset) for i in range(count)])


def ordered(pieces, place, dim):
    if len(pieces) == 1:
        return pieces[0]
    level = len(pieces) // 2
    inside = lax.rem(place, level)
    low = ordered(pieces[:level], inside, dim)
    high = ordered(pieces[level:], inside, dim)
    return jnp.where(
        place >= level, jnp.concatenate([high, low], dim), jnp.concatenate([low, high], dim)
    )


def hold(value, token):
    return lax.optimization_barrier((value, token))[0]


def gather_first(piece, axis):
    return [piece] + [send(piece, axis, k) for k in range(1, lax.axis_size(axis))]


def gather_last(pieces, axis, dim, token=None):
    if token is not None:
        pieces = hold(pieces, token)
    return ordered(pieces, lax.axis_index(axis), dim)


def added(pieces):
    total = pieces[0].astype(F32)
    for piece in pieces[1:]:
        total = total + piece.astype(F32)
    return total.astype(BF16)


def scatter_step(pending, axis, dim, token=None):
    if token is not None:
        pending = hold(pending, token)
    place, count = lax.axis_index(axis), lax.axis_size(axis)
    size = pending[0].shape[dim] // count
    after = []
    for k in range(count):
        parts = [
            lax.dynamic_slice_in_dim(piece, (place ^ k) * size, size, dim) for piece in pending
        ]
        block = added(parts)
        after.append(send(block, axis, k) if k else block)
    return after


def gather_step(piece, axis, dim):
    return gather_last(gather_first(piece, axis), axis, dim)


def gather_early(rows):
    return lax.all_gather(rows, (OUTER, INNER), axis=0, tiled=False)


SEQ = (OUTER, INNER)


class Chain:
    def __init__(self, halves, order, small=None, doubled=False):
        self.order = (CORE,) + order
        self.doubled = doubled
        self.stage = 0
        self.tiles = halves[0].shape[0]
        self.small, self.carried = None, 0
        if small is not None:
            self.carried = small.shape[0]
            halves = [jnp.concatenate([self.flat(half), small]) for half in halves]
        self.held = [halves[0], send(halves[1], CORE, 1)]

    def flat(self, block):
        return block.reshape(-1, block.shape[-1])

    def parts(self):
        if not self.carried:
            return self.held, None
        body = [piece[: -self.carried] for piece in self.held]
        body = [piece.reshape(self.tiles, -1, piece.shape[-1]) for piece in body]
        return body, added([piece[-self.carried :] for piece in self.held])

    def next_axis(self):
        stage, count = self.stage + 1, len(self.order)
        return self.order[stage] if stage < count else self.order[2 * count - 1 - stage]

    def over(self):
        return self.stage == 2 * len(self.order) - 1

    def go(self):
        axis = self.next_axis()
        self.stage += 1
        count = len(self.order)
        if self.doubled and self.stage in (count - 1, count):
            total = added(self.held)
            self.held = [total, send(total, OUTER, self.stage - count + 2)]
            return
        if self.doubled and self.stage == count + 1:
            pending, self.small = self.parts()
            self.held = gather_first(added(pending), axis)
            return
        if self.stage < count:
            pending, small = self.parts()
            place, members = lax.axis_index(axis), lax.axis_size(axis)
            size = pending[0].shape[1] // members
            self.held = []
            for k in range(members):
                begin = (place ^ k) * size
                block = added([lax.dynamic_slice_in_dim(p, begin, size, 1) for p in pending])
                if small is not None:
                    block = jnp.concatenate([self.flat(block), small])
                self.held.append(send(block, axis, k) if k else block)
            return
        if self.stage == count:
            pending, self.small = self.parts()
            piece = added(pending)
        else:
            piece = gather_last(self.held, self.order[2 * count - self.stage], 1)
        self.held = gather_first(piece, axis)

    def volume(self):
        return self.held[0].size * 2 / 2**20


class Spread:
    def __init__(self, part, straight):
        self.straight, self.stage = straight, 0
        self.held = [send(rows, INNER, k) if k else rows for k, rows in enumerate(part)]

    def next_axis(self):
        return OUTER

    def over(self):
        return self.stage == (1 if self.straight else 2)

    def go(self):
        self.stage += 1
        if self.straight:
            blocks = [added([piece[k] for piece in self.held]) for k in range(4)]
            self.held = [send(block, OUTER, k) if k else block for k, block in enumerate(blocks)]
            return
        if self.stage == 1:
            pick, offset = (lambda piece, odd: jnp.stack([piece[odd], piece[2 + odd]])), 1
        else:
            pick, offset = (lambda piece, odd: piece[odd]), 2
        mine, theirs = [added([pick(piece, odd) for piece in self.held]) for odd in (0, 1)]
        self.held = [mine, send(theirs, OUTER, offset)]

    def volume(self):
        return self.held[0].size * 2 / 2**20

    def result(self):
        return added(self.held)


def finish(chains, *tokens):
    held, _ = lax.optimization_barrier(([chain.held for chain in chains], tokens))
    for chain, pieces in zip(chains, held):
        chain.held = pieces


def go(*chains):
    for chain in chains:
        chain.go()


FLOW = {CORE: 3.5, X: 21.0, INNER: 21.0, OUTER: 84.0}


def plan_of(chain):
    if isinstance(chain, Spread):
        return [(INNER, 21.0, 1), (OUTER, 10.5, 1), (OUTER, 10.5, 1)][chain.stage :]
    size, out = chain.tiles * 0.5, []
    for axis in chain.order:
        count = lax.axis_size(axis)
        if axis == OUTER and chain.doubled:
            out += [(OUTER, 21.0 * size, 1), (OUTER, 42.0 * size, 1)]
            continue
        size = size / count
        out.append((axis, FLOW[axis] * size, count - 1))
    back = [entry for entry in reversed(out)]
    if chain.doubled:
        back = [entry for entry in back if entry[0] != OUTER]
    return (out + back)[chain.stage :]


def rehearse(plans, first, gate, weights, slack):
    free = dict.fromkeys(FLOW, 0.0)
    position, queue, order, clock, waiting = [0] * len(plans), [], [], 0.0, []

    def depart(index, when):
        axis, long, _ = plans[index][position[index]]
        begin = max(when, free[axis])
        free[axis] = begin + long
        queue.append((free[axis] + 6.0, index))

    def left(index):
        rest = plans[index][position[index] :]
        return weights[index] * sum(long + 10.0 for _, long, _ in rest)

    for index, since in first:
        depart(index, -since)
    while queue or waiting:
        soon = min(queue)[0] if queue else clock + 99.0
        if waiting and soon > clock + 4.0:
            clock += 6.5
            order.append((waiting.pop(0), True))
            continue
        near = [entry for entry in queue if entry[0] <= max(clock, soon) + slack]
        entry = max(near, key=lambda entry: left(entry[1]))
        queue.remove(entry)
        arrival, index = entry
        clock = max(clock, arrival)
        position[index] += 1
        order.append((index, False))
        if position[index] == len(plans[index]):
            clock += 1.0
            waiting.append(index)
            continue
        axis, long, sends = plans[index][position[index]]
        clock += 2.0 + 1.5 * sends + 0.03 * long
        depart(index, clock)
        if gate[1] == index and position[index] == 1:
            clock += 2.0
            depart(gate[0], clock)
    return clock, order


def run_out(flights, later):
    chains, ends = [chain for chain, _, _ in flights], [end for _, _, end in flights]
    plans = [plan_of(chain) for chain in chains]
    plans.append([(INNER, 21.0, 1), (OUTER, 10.5, 1), (OUTER, 10.5, 1)])
    first = [(index, since) for index, (_, since, _) in enumerate(flights)]
    rng, best = random.Random(7), None
    for trial in range(1500):
        weights = [1.0 if trial < 4 else rng.uniform(0.3, 2.0) for _ in plans]
        slack = (0.0, 2.0, 4.0, 8.0)[trial % 4]
        found = rehearse(plans, first, (len(chains), 0), weights, slack)
        if best is None or found[0] < best[0]:
            best = found
    token, results = (), {}
    for index, is_end in best[1]:
        chain = chains[index]
        if is_end:
            results[index] = ends[index](chain, token)
            token = (results[index][0],)
            continue
        finish([chain], *token)
        if chain.over():
            token = tuple(chain.held)
            continue
        chain.go()
        token = (chain.held[0],)
        if index == 0 and chain.stage == 1:
            chain, _, end = later(token)
            chains.append(chain)
            ends.append(end)
    return [results[index] for index in range(len(chains))]


def assemble(chain, core_info, shapes, after=()):
    tiles, half, side = chain.held[0].shape

    places = []
    for name, shape in shapes.items():
        blocks = shape[0] if len(shape) > 2 else shape[0] * shape[1] // (side * side)
        for block in range(blocks):
            if len(shape) > 2:
                places.append((name, lambda rows, b=block: (b, rows, slice(None))))
            elif shape[1] > shape[0]:
                lanes = slice(block * side, (block + 1) * side)
                places.append((name, lambda rows, l=lanes: (rows, l)))
            else:
                places.append((name, lambda rows, b=block: (pl.ds(rows.start + b * side, half), slice(None))))

    def body(info, mine, other, *refs):
        outs = dict(zip(shapes, refs))
        room, full, come, go = refs[len(shapes) :]
        starts = [pl.multiple_of((info[0] ^ flip) * half, half) for flip in (0, 1)]
        arrive, leave = [], []
        for tile in range(tiles):
            for flip, source in enumerate((mine, other)):
                index = 2 * tile + flip
                arrive.append(pltpu.make_async_copy(source.at[tile], room.at[index], come.at[index]))
                arrive[-1].start()
        for tile, (name, where) in enumerate(places):
            for flip in (0, 1):
                index = 2 * tile + flip
                arrive[index].wait()
                full[index] = room[index].astype(F32)
                target = outs[name].at[where(pl.ds(starts[flip], half))]
                leave.append(pltpu.make_async_copy(full.at[index], target, go.at[index]))
                leave[-1].start()
        for copy in leave:
            copy.wait()

    far = pl.BlockSpec(memory_space=pl.ANY)
    return pl.pallas_call(
        lambda info, mine, other, *refs: body(info, mine, other, *refs[len(after) :]),
        in_specs=[pl.BlockSpec(memory_space=pltpu.SMEM)] + [far] * (2 + len(after)),
        out_specs=[far] * len(shapes),
        out_shape=[jax.ShapeDtypeStruct(shape, F32) for shape in shapes.values()],
        scratch_shapes=[
            pltpu.VMEM((2 * tiles, half, side), BF16),
            pltpu.VMEM((2 * tiles, half, side), F32),
            pltpu.SemaphoreType.DMA((2 * tiles,)),
            pltpu.SemaphoreType.DMA((2 * tiles,)),
        ],
        compiler_params=pltpu.CompilerParams(vmem_limit_bytes=VMEM_LIMIT),
        cost_estimate=pl.CostEstimate(flops=5 * 10**9, bytes_accessed=2 * 10**7, transcendentals=0),
    )(core_info, chain.held[0], chain.held[1], *after)


def shards(
    source_short,
    target_short,
    source_segment,
    target_segment,
    source_long,
    target_long,
    source_length,
    target_length,
    cotangent_short,
    cotangent_long,
    encoder_project,
    encoder_output,
    encoder_up,
    encoder_down,
    encoder_gain,
    encoder_bias,
    decoder_project,
    decoder_output,
    cross_project,
    cross_output,
    decoder_up,
    decoder_down,
    decoder_gain,
    decoder_bias,
):
    blocks, size, width = source_short.shape
    hidden = encoder_up.shape[1]
    rows = blocks * size
    pairs, own, _ = source_long.shape
    rows_long = pairs * own
    flat = lambda a: a.reshape(-1, width)
    start = lax.axis_index((OUTER, INNER)) * own
    core = lax.axis_index(CORE)
    here = [start, lax.axis_index(INNER), core, lax.axis_index(OUTER)]
    here = jnp.stack(here).astype(jnp.int32)
    info_of = lambda lengths: jnp.concatenate([lengths, here])
    core_info = core.astype(jnp.int32)[None]
    source_info, target_info = info_of(source_length), info_of(target_length)

    spread = lambda s: jnp.broadcast_to(s[:, :, None], (blocks, size, size))
    line = lambda s: s[:, None, :]
    encoder_in = {
        "w_in": encoder_project,
        "w_o": encoder_output,
        "up": encoder_up,
        "down": encoder_down,
        "gain": encoder_gain,
        "bias": encoder_bias,
    }
    decoder_in = {
        "w_in": decoder_project,
        "w_o": decoder_output,
        "w_cin": cross_project,
        "w_co": cross_output,
        "up": decoder_up,
        "down": decoder_down,
        "gain": decoder_gain,
        "bias": decoder_bias,
    }

    def pick(table, names):
        return {name: table[name] for name in names}

    def rows_of(n, names):
        return {name: ((n, width), BF16) for name in names}

    def wide_of(n, names):
        return {name: ((n, hidden), BF16) for name in names}

    def floats(n, names):
        return {name: ((n, width), F32) for name in names}

    def column(n, names):
        return {name: ((n, 1), F32) for name in names}

    def logs(n, names):
        return {name: ((n, HEADS, size), F32) for name in names}

    def sums(n):
        return {"small": ((n, width), F32)}

    def keys_of(names):
        shape = (places, pairs, own, width)
        return {name: (shape, BF16) for name in names}

    def parts():
        inner = lax.axis_size(INNER)
        return {"p%d" % k: ((places // inner, pairs, own, width), BF16) for k in range(inner)}

    def saved(kernel, names):
        return {name: kernel[name] for name in names}

    whole_source = gather_early(source_long)
    places = lax.axis_size(OUTER) * lax.axis_size(INNER)
    keys = places * own
    work = [
        ("s", pltpu.VMEM((PAIRS, keys, 2 * own), F32)),
        ("a", pltpu.VMEM((PAIRS, 8, 2 * own), F32)),
        ("mix", pltpu.VMEM((PAIRS, PAIR, 2 * own), F32)),
    ]
    mix = work[2:]

    segments = {"kseg": spread(source_segment), "qseg": line(source_segment)}
    turned = {"tkseg": spread(target_segment), "tqseg": line(target_segment)}
    encoder_keeps = lambda n: {
        **rows_of(n, ("n1", "y", "n2", "enc")),
        **wide_of(n, ("act", "gate")),
        **column(n, ("i1", "i2")),
    }
    se = launch(
        short_encoder_forward,
        {"x": flat(source_short), **segments, **encoder_in},
        {**rows_of(rows, ("q", "k", "v", "o")), **logs(blocks, ("lse",)), **encoder_keeps(rows)},
        cost=0.01,
        scratch=[("acc", pltpu.VMEM((rows, width), F32))],
    )
    decoder_keeps = lambda n: {
        **rows_of(n, ("m", "b5", "b4", "go_c")),
        **wide_of(n, ("act", "gate", "dh")),
        **floats(n, ("final", "d4")),
        **sums(4),
    }
    sd = launch(
        short_decoder_forward,
        {
            "t": flat(target_short),
            **turned,
            **pick(decoder_in, ("w_in", "w_o", "gain", "bias")),
        },
        {
            **rows_of(rows, ("q", "k", "v", "o", "n3", "u")),
            **logs(blocks, ("lse",)),
            **column(rows, ("i3",)),
            **floats(rows, ("upper",)),
        },
        after=(se.lse,),
        cost=0.01,
    )
    early_target = gather_first(hold(target_long, sd.lse)[None, None], OUTER)
    sc = launch(
        short_cross_forward,
        {
            "u": sd.u,
            "upper": sd.upper,
            "enc": se.enc,
            "cot": flat(cotangent_short),
            "kseg": segments["kseg"],
            "tqseg": turned["tqseg"],
            **pick(decoder_in, ("w_cin", "w_co", "up", "down", "gain", "bias")),
        },
        {
            **rows_of(rows, ("q_c", "k_c", "v_c", "o_c")),
            **logs(blocks, ("lse_c",)),
            **decoder_keeps(rows),
        },
        after=(sd.lse,),
        cost=0.01,
        scratch=[("acc", pltpu.VMEM((rows, width), F32))],
    )

    sb = launch(
        short_decoder_back,
        {
            **saved(sd, ("q", "k", "v", "o", "lse", "n3", "i3")),
            **saved(sc, ("q_c", "k_c", "v_c", "o_c", "lse_c", "go_c", "d4")),
            "kseg": segments["kseg"],
            **turned,
            **pick(decoder_in, ("w_in", "w_o", "w_cin", "gain")),
        },
        {
            **rows_of(rows, ("dq_c", "dk_c", "dv_c", "dq", "dk", "dv", "b3", "go")),
            **floats(rows, ("denc", "dt")),
            **sums(2),
        },
        scratch=[("d3", pltpu.VMEM((rows, width), F32))],
        after=(sc.small,),
        cost=0.01,
    )

    early_target = gather_last(early_target, OUTER, 0, sb.small)

    whole_source = hold(whole_source, sb.small)
    x_long, t_long = flat(source_long), flat(target_long)
    le = launch(
        long_encoder_forward,
        {"x": x_long, "xg": whole_source, **encoder_in},
        {
            **rows_of(rows_long, ("q", "o")),
            **keys_of(("k", "v")),
            **logs(pairs, ("lse",)),
            **encoder_keeps(rows_long),
        },
        scratch=work + [("acc", pltpu.VMEM((rows_long, width), F32))],
        info=source_info,
        after=(sb.small, early_target),
        cost=13,
        moved=(),
    )
    late_target = gather_first(hold(early_target, le.lse), INNER)
    whole_encoded = gather_early(le.enc.reshape(pairs, own, width))

    seb = launch(
        short_encoder_back,
        {
            "denc": sb.denc,
            **saved(se, ("q", "k", "v", "o", "lse", "n1", "i1", "n2", "i2", "gate")),
            **segments,
            **pick(encoder_in, ("w_in", "w_o", "up", "down", "gain")),
        },
        {
            **rows_of(rows, ("dq", "dk", "dv", "b1", "b2", "go")),
            **wide_of(rows, ("dh",)),
            **floats(rows, ("dx",)),
            **sums(4),
        },
        scratch=[("acc", pltpu.VMEM((rows, width), F32)), ("d1", pltpu.VMEM((rows, width), F32))],
        after=(le.lse,),
        cost=16,
    )

    t_short, x_short = flat(target_short), flat(source_short)
    short_weights = whole_tiles(
        [
            [(sc.m, sc.dh), (sc.act, sc.b5)],
            [
                (sd.u, sb.dq_c),
                (se.enc, sb.dk_c),
                (se.enc, sb.dv_c),
                (sc.o_c, sc.b4),
                (t_short, sb.dq),
                (t_short, sb.dk),
                (t_short, sb.dv),
                (sd.o, sb.b3),
            ],
            [(se.y, seb.dh), (se.act, seb.b2)],
            [(x_short, seb.dq), (x_short, seb.dk), (x_short, seb.dv), (se.o, seb.b1)],
        ],
        after=(seb.small,),
        cost=15,
    )
    whole_target = gather_last(late_target, INNER, 1, short_weights[0])
    whole_target = whole_target.reshape(places, pairs, own, width)
    ls = launch(
        long_self_forward,
        {
            "t": t_long,
            "tg": whole_target,
            **pick(decoder_in, ("w_in", "w_o", "w_cin", "gain", "bias")),
        },
        {
            **rows_of(rows_long, ("q", "o", "n3", "u", "q_c")),
            **keys_of(("k", "v")),
            **logs(pairs, ("lse",)),
            **column(rows_long, ("i3",)),
            **floats(rows_long, ("upper",)),
        },
        scratch=work,
        info=target_info,
        after=(short_weights[0],),
        cost=10,
        moved=(),
    )

    whole_encoded = hold(whole_encoded, ls.lse)
    lc = launch(
        long_cross,
        {
            "eg": whole_encoded,
            "upper": ls.upper,
            "q_c": ls.q_c,
            "cot": flat(cotangent_long),
            **pick(decoder_in, ("w_cin", "w_co", "up", "down", "gain", "bias")),
        },
        {
            **rows_of(rows_long, ("o_c",)),
            **keys_of(("k_c", "v_c")),
            **logs(pairs, ("lse_c",)),
            **decoder_keeps(rows_long),
        },
        scratch=work + [("acc", pltpu.VMEM((rows_long, width), F32))],
        info=source_info,
        after=(ls.lse,),
        cost=14,
        moved=("k_c", "v_c", "up", "down", "w_co", "act", "gate", "dh", "final"),
    )
    lcb = launch(
        long_cross_back,
        {
            "q_c": ls.q_c,
            **saved(lc, ("k_c", "v_c", "o_c", "lse_c", "go_c")),
            **pick(decoder_in, ("w_cin",)),
        },
        {**rows_of(rows_long, ("dq_c",)), **keys_of(("dk_c", "dv_c")), **parts()},
        scratch=mix,
        info=source_info,
        after=(lc.small,),
        cost=14,
        moved=(),
    )
    encoded_back = Spread(part_refs(lcb), True)
    first_weights = Weights(
        [[(lc.m, lc.dh)], [(lc.act, lc.b5)]], short_weights[0]
    )

    def self_back_and_weights(r):
        long_self_back(r)
        first_weights.body(r, r.info[pairs + 2])

    lsb = launch(
        self_back_and_weights,
        {
            "d4": lc.d4,
            "dq_c": lcb.dq_c,
            **saved(ls, ("q", "k", "v", "o", "lse", "n3", "i3")),
            **pick(decoder_in, ("w_in", "w_o", "w_cin", "gain")),
            **first_weights.arrays,
        },
        {
            **first_weights.gives,
            **rows_of(rows_long, ("dq", "b3")),
            **keys_of(("dk", "dv")),
            **parts(),
            **floats(rows_long, ("dt",)),
            **sums(2),
        },
        scratch=mix + [("go", pltpu.VMEM((rows_long, width), BF16))],
        info=target_info,
        after=(lcb.dq_c,),
        pieces=("kept", "sent"),
        cost=22,
    )
    decoder_ffn = Chain([lsb.kept, lsb.sent], (X, INNER, OUTER))
    finish([encoded_back], lsb.small)
    go(encoded_back)
    target_back = Spread(part_refs(lsb), False)
    grad_attention = weight_tiles(
        [
            [(ls.u, lcb.dq_c)],
            [(flat(whole_encoded), flat(lcb.dk_c))],
            [(flat(whole_encoded), flat(lcb.dv_c))],
            [(lc.o_c, lc.b4)],
            [(t_long, lsb.dq)],
            [(flat(whole_target), flat(lsb.dk))],
            [(flat(whole_target), flat(lsb.dv))],
            [(ls.o, lsb.b3)],
        ],
        core_info,
        after=(lsb.small, encoded_back.held[0]),
        base=short_weights[1],
        cost=15,
    )
    finish([encoded_back, decoder_ffn], grad_attention[0])
    go(decoder_ffn)
    attention = Chain(grad_attention, (INNER, X, OUTER))
    ffn_weights = Weights(
        [
            [(le.y, ("dh", hidden))],
            [(le.act, ("b2", width))],
        ],
        short_weights[2],
    )

    def encoder_back_and_weights(r):
        long_encoder_tail_back(r)
        ffn_weights.body(r, r.info[0])

    leb = launch(
        encoder_back_and_weights,
        {
            **{"part%d" % k: flat(piece) for k, piece in enumerate(encoded_back.held)},
            **saved(le, ("n1", "i1", "n2", "i2", "gate")),
            **pick(encoder_in, ("down", "up", "w_o", "gain")),
            **ffn_weights.arrays,
        },
        {
            **ffn_weights.gives,
            **rows_of(rows_long, ("b1", "b2", "go")),
            **wide_of(rows_long, ("dh",)),
            **floats(rows_long, ("d1",)),
            **sums(4),
        },
        info=core_info,
        after=(grad_attention[0], decoder_ffn.held[0]),
        pieces=("kept", "sent"),
        cost=12,
        scratch=[("acc", pltpu.VMEM((rows_long, width), F32))],
    )
    small = jnp.concatenate([seb.small + leb.small, sb.small + lsb.small, sc.small + lc.small])
    small = jnp.pad(small, ((0, 16 - small.shape[0]), (0, 0))).astype(BF16)
    finish([attention], leb.small)
    go(attention)
    encoder_ffn = Chain([leb.kept, leb.sent], (X, INNER, OUTER))
    attention_weights = Weights(
        [
            [(x_long, ("dq", width))],
            [(whole_source, ("dk", width))],
            [(whole_source, ("dv", width))],
            [(le.o, leb.b1)],
        ],
        short_weights[3],
    )

    def attention_back_and_weights(r):
        long_encoder_back(r)
        r.leave("dx", *[name for name in r if name[0] == "p" and name[1:].isdigit()])
        attention_weights.body(r, r.info[pairs + 2])

    lea = launch(
        attention_back_and_weights,
        {
            **saved(le, ("q", "k", "v")),
            "o": le.o,
            "lse": le.lse,
            **saved(leb, ("go", "d1")),
            **pick(encoder_in, ("w_in",)),
            **attention_weights.arrays,
        },
        {
            **attention_weights.gives,
            **parts(),
            **floats(rows_long, ("dx",)),
        },
        scratch=mix
        + [
            ("dq", pltpu.VMEM((rows_long, width), BF16)),
            ("dk", pltpu.VMEM((places, pairs, own, width), BF16)),
            ("dv", pltpu.VMEM((places, pairs, own, width), BF16)),
        ],
        info=source_info,
        after=(leb.small, attention.held[0]),
        pieces=("kept", "sent"),
        cost=19,
    )
    done = lea.dx
    finish([decoder_ffn, encoder_ffn, target_back], done)
    encoder = Chain([lea.kept, lea.sent], (INNER, X, OUTER), small, True)
    go(decoder_ffn, encoder_ffn, target_back)
    square = (3, width, width)
    feed = {"up": encoder_up.shape, "down": encoder_down.shape}
    one = {"project": square, "output": square[1:]}
    two = {"cross_in": square, "cross_out": square[1:], "self_in": square, "self_out": square[1:]}

    def out(shapes):
        return lambda chain, token: assemble(chain, core_info, shapes, token)

    rows_out = lambda rows: lambda chain, token: [chain.result().astype(F32) + rows]
    flights = [
        (encoder, 0.0, out(one)),
        (decoder_ffn, 0.0, out(feed)),
        (attention, 20.0, out(two)),
        (encoder_ffn, 0.0, out(feed)),
        (target_back, 0.0, rows_out(lsb.dt.reshape(source_long.shape))),
    ]

    def source_back(token):
        chain = Spread(hold(part_refs(lea), token), False)
        return chain, 0.0, rows_out(lea.dx.reshape(source_long.shape))

    results = run_out(flights, source_back)
    (encoder_in_out, encoder_out_out), (decoder_up_out, decoder_down_out) = results[:2]
    (cross_in, cross_out, self_in, self_out), (encoder_up_out, encoder_down_out) = results[2:4]
    (grad_target,), (grad_source,) = results[4:]
    small = encoder.small.astype(F32)
    return (
        sc.final.reshape(source_short.shape),
        lc.final.reshape(source_long.shape),
        seb.dx.reshape(source_short.shape),
        sb.dt.reshape(source_short.shape),
        grad_source,
        grad_target,
        encoder_in_out,
        encoder_out_out,
        encoder_up_out,
        encoder_down_out,
        small[0:2],
        small[2:4],
        self_in,
        self_out,
        cross_in,
        cross_out,
        decoder_up_out,
        decoder_down_out,
        jnp.stack([small[4], small[6], small[7]]),
        jnp.stack([small[5], small[8], small[9]]),
    )


def solution(mesh):
    group, seq = mesh.devices.shape
    fine = Mesh(
        mesh.devices.reshape(group // 2, 2, 4, seq // 4), (X, CORE, OUTER, INNER)
    )
    groups, positions = (X, CORE), (OUTER, INNER)
    blocks = P(groups + positions, None, None)
    long_rows = P(groups, positions, None)
    in_specs = (
        (blocks, blocks, P(groups + positions, None), P(groups + positions, None))
        + (long_rows, long_rows, P(groups), P(groups), blocks, long_rows)
        + (P(),) * 14
    )
    out_specs = (blocks, long_rows, blocks, blocks, long_rows, long_rows) + (P(),) * 14
    return jax.shard_map(
        shards, mesh=fine, in_specs=in_specs, out_specs=out_specs, check_vma=False
    )
```

```python
import functools
import random
import jax
import jax.numpy as jnp
from jax import lax
from jax.experimental import pallas as pl
from jax.experimental.pallas import tpu as pltpu
from jax.sharding import Mesh, PartitionSpec as P

HEADS = 8
HEAD_DIM = 64
PAIR = 2 * HEAD_DIM
PAIRS = HEADS // 2
SCALE = HEAD_DIM**-0.5
FLOOR_SCORE = -1e30
EPSILON = 1e-05
KEY_BLOCK = 256
CHUNK = 512
F32 = jnp.float32
BF16 = jnp.bfloat16
CORE, X, INNER, OUTER = "core", "x", "inner", "outer"


def nn(left, right):
    return lax.dot_general(left, right, (((1,), (0,)), ((), ())), preferred_element_type=F32)


def nt(left, right):
    return lax.dot_general(left, right, (((1,), (1,)), ((), ())), preferred_element_type=F32)


def tn(left, right):
    return lax.dot_general(left, right, (((0,), (0,)), ((), ())), preferred_element_type=F32)


def two_heads(rows):
    lane = lax.broadcasted_iota(jnp.int32, rows.shape, 1)
    zero = jnp.zeros_like(rows)
    first = jnp.where(lane < HEAD_DIM, rows, zero)
    second = jnp.where(lane < HEAD_DIM, zero, rows)
    return jnp.concatenate([first, second], axis=0)


def diagonal(product):
    half = product.shape[1] // 2
    return jnp.concatenate([product[:HEAD_DIM, :half], product[HEAD_DIM:, half:]], axis=0)


def delta_rows(grad_out, outputs):
    product = grad_out.astype(F32) * outputs.astype(F32)
    high = product.astype(BF16)
    low = (product - high.astype(F32)).astype(BF16)
    width = product.shape[1]
    head = lax.broadcasted_iota(jnp.int32, (HEADS, width), 0)
    lane = lax.broadcasted_iota(jnp.int32, (HEADS, width), 1)
    pick = jnp.where(lax.div(lane, HEAD_DIM) == head, 1.0, 0.0).astype(BF16)
    return nt(pick, high) + nt(pick, low)


def pair_row(rows, pair):
    return jnp.concatenate([rows[2 * pair : 2 * pair + 1], rows[2 * pair + 1 : 2 * pair + 2]], axis=1)


def pair_lanes(pair):
    return slice(pair * PAIR, (pair + 1) * PAIR)


def norm(residual, gain, bias):
    centred = residual - jnp.mean(residual, axis=1, keepdims=True)
    inverse = lax.rsqrt(jnp.mean(centred * centred, axis=1, keepdims=True) + EPSILON)
    normed = centred * inverse
    return normed * gain + bias, normed, inverse


def norm_back(upstream, normed, inverse, gain):
    normed = normed.astype(F32)
    scaled = upstream * gain
    grad = inverse * (
        scaled
        - jnp.mean(scaled, axis=1, keepdims=True)
        - normed * jnp.mean(scaled * normed, axis=1, keepdims=True)
    )
    return (
        grad,
        jnp.sum(upstream * normed, axis=0, keepdims=True),
        jnp.sum(upstream, axis=0, keepdims=True),
    )


def chunks(ref, axis, step):
    def body(index, carry):
        step(pl.ds(pl.multiple_of(index * CHUNK, CHUNK), CHUNK))
        return carry

    lax.fori_loop(0, ref.shape[axis] // CHUNK, body, 0)


def feed_forward_in_loop(rows, up_ref, down_ref, act_ref, gate_ref, low_ref, total_ref):
    low_ref[...] = rows.astype(BF16)
    total_ref[...] = rows

    def step(part):
        hidden = nn(low_ref[...], up_ref[:, part])
        sigmoid = 0.5 * jnp.tanh(0.5 * hidden) + 0.5
        active = hidden * sigmoid
        gate_ref[:, part] = (sigmoid + active * (1.0 - sigmoid)).astype(BF16)
        active = active.astype(BF16)
        act_ref[:, part] = active
        total_ref[...] += nn(active, down_ref[part, :])

    chunks(up_ref, 1, step)
    return total_ref[...]


def feed_forward(rows, up_ref, down_ref, act_ref, gate_ref):
    low = rows.astype(BF16)
    total = rows
    for start in range(0, up_ref.shape[1], CHUNK):
        part = slice(start, start + CHUNK)
        hidden = nn(low, up_ref[:, part])
        sigmoid = 0.5 * jnp.tanh(0.5 * hidden) + 0.5
        active = hidden * sigmoid
        gate_ref[:, part] = (sigmoid + active * (1.0 - sigmoid)).astype(BF16)
        active = active.astype(BF16)
        act_ref[:, part] = active
        total = total + nn(active, down_ref[part, :])
    return low, total


def feed_back(grad, gate_ref, up_ref, down_ref, hidden_grad_ref):
    low = grad.astype(BF16)
    total = grad
    for start in range(0, up_ref.shape[1], CHUNK):
        part = slice(start, start + CHUNK)
        hidden = nt(low, down_ref[part, :]) * gate_ref[:, part].astype(F32)
        hidden = hidden.astype(BF16)
        hidden_grad_ref[:, part] = hidden
        total = total + nt(hidden, up_ref[:, part])
    return low, total


def short_allowed(key_segment, query_segment, causal):
    allowed = key_segment == query_segment
    if causal:
        key = lax.broadcasted_iota(jnp.int32, key_segment.shape, 0)
        query = lax.broadcasted_iota(jnp.int32, key_segment.shape, 1)
        allowed = allowed & (key <= query)
    return jnp.concatenate([allowed, allowed], axis=1)


def short_attend(causal, q_ref, k_ref, v_ref, kseg_ref, qseg_ref, o_ref, lse_ref):
    size = kseg_ref.shape[1]
    for block in range(kseg_ref.shape[0]):
        rows = slice(block * size, (block + 1) * size)
        allowed = short_allowed(kseg_ref[block], qseg_ref[block], causal)
        logs = []
        for pair in range(PAIRS):
            lanes = pair_lanes(pair)
            scores = nt(k_ref[rows, lanes], two_heads(q_ref[rows, lanes]))
            scores = jnp.where(allowed, scores, FLOOR_SCORE)
            top = jnp.max(scores, axis=0, keepdims=True)
            weights = jnp.exp(scores - top)
            total = jnp.sum(weights, axis=0, keepdims=True)
            mixed = nn(v_ref[rows, lanes].T, weights.astype(BF16)) / total
            o_ref[rows, lanes] = diagonal(mixed).T.astype(BF16)
            log_total = top + jnp.log(total)
            logs += [log_total[:, :size], log_total[:, size:]]
        lse_ref[block] = jnp.concatenate(logs, axis=0)


def short_attend_back(
    causal, q_ref, k_ref, v_ref, kseg_ref, qseg_ref, o_ref, lse_ref, go_ref, dq_ref, dk_ref, dv_ref
):
    size = kseg_ref.shape[1]
    for block in range(kseg_ref.shape[0]):
        rows = slice(block * size, (block + 1) * size)
        allowed = short_allowed(kseg_ref[block], qseg_ref[block], causal)
        delta = delta_rows(go_ref[rows, :], o_ref[rows, :])
        lse = lse_ref[block]
        for pair in range(PAIRS):
            lanes = pair_lanes(pair)
            queries, grads = two_heads(q_ref[rows, lanes]), two_heads(go_ref[rows, lanes])
            scores = nt(k_ref[rows, lanes], queries)
            weights = jnp.where(allowed, jnp.exp(scores - pair_row(lse, pair)), 0.0)
            grad_weights = nt(v_ref[rows, lanes], grads)
            grad_scores = (weights * (grad_weights - pair_row(delta, pair))).astype(BF16)
            dv_ref[rows, lanes] = nn(weights.astype(BF16), grads).astype(BF16)
            dk_ref[rows, lanes] = nn(grad_scores, queries).astype(BF16)
            turned = diagonal(nn(k_ref[rows, lanes].T, grad_scores)).T
            dq_ref[rows, lanes] = (turned.astype(BF16).astype(F32) * SCALE).astype(BF16)


def load_keys(ref, pair_index, block, lanes):
    pieces = KEY_BLOCK // ref.shape[2]
    rows = ref[pl.ds(block * pieces, pieces), pair_index, :, lanes]
    return rows.reshape(KEY_BLOCK, rows.shape[2])


def store_keys(ref, pair_index, block, lanes, rows):
    pieces = KEY_BLOCK // ref.shape[2]
    ref[pl.ds(block * pieces, pieces), pair_index, :, lanes] = rows.astype(BF16).reshape(
        pieces, ref.shape[2], rows.shape[1]
    )


def store_part(refs, info_ref, pair_index, block, rows):
    partners, (_, pairs, size, _) = len(refs), refs[0].shape
    if partners == 2 and KEY_BLOCK == 2 * size:
        outer = block ^ info_ref[pairs + 3]
        swap = info_ref[pairs + 1] == 1
        first, second = rows[:size], rows[size:]
        refs[0][outer, pair_index] = jnp.where(swap, second, first)
        refs[1][outer, pair_index] = jnp.where(swap, first, second)
        return
    for piece in range(KEY_BLOCK // size):
        place = block * (KEY_BLOCK // size) + piece
        inner = lax.rem(place, partners) ^ info_ref[pairs + 1]
        outer = lax.div(place, partners) ^ info_ref[pairs + 3]
        part = rows[piece * size : (piece + 1) * size]
        for partner, ref in enumerate(refs):

            @pl.when(inner == partner)
            def _(ref=ref):
                ref[outer, pair_index] = part


def long_limit(info_ref, causal, pair_index, size, pairs):
    length = info_ref[pair_index]
    limit = length
    if causal:
        limit = jnp.minimum(length, info_ref[pairs] + size)
    return length, lax.div(limit + KEY_BLOCK - 1, KEY_BLOCK)


def long_allowed(start, causal, length, block, shape):
    key = lax.broadcasted_iota(jnp.int32, shape, 0) + block * KEY_BLOCK
    allowed = key < length
    if causal:
        half = shape[1] // 2
        lane = lax.broadcasted_iota(jnp.int32, shape, 1)
        query = jnp.where(lane < half, lane, lane - half) + start
        allowed = allowed & (key <= query)
    return allowed


def long_attend(
    causal, info_ref, q_ref, x_ref, k_w, v_w, k_ref, v_ref, o_ref, lse_ref, score_ref, sum_ref, mix_ref
):
    places, pairs, size, width = x_ref.shape
    shape = (KEY_BLOCK, 2 * size)
    everything = slice(None)

    def one(pair_index, carry):
        length, count = long_limit(info_ref, causal, pair_index, size, pairs)
        own = pl.ds(pl.multiple_of(pair_index * size, size), size)

        def first(block, tops):
            rows = pl.ds(pl.multiple_of(block * KEY_BLOCK, KEY_BLOCK), KEY_BLOCK)
            allowed = long_allowed(info_ref[pairs], causal, length, block, shape)
            context = load_keys(x_ref, pair_index, block, everything)
            store_keys(k_ref, pair_index, block, everything, nn(context, k_w[...]))
            store_keys(v_ref, pair_index, block, everything, nn(context, v_w[...]))
            after = []
            for pair in range(PAIRS):
                lanes = pair_lanes(pair)
                keys = load_keys(k_ref, pair_index, block, lanes)
                scores = nt(keys, two_heads(q_ref[own, lanes]))
                scores = jnp.where(allowed, scores, FLOOR_SCORE)
                score_ref[pair, rows] = scores
                folded = jnp.max(scores.reshape(KEY_BLOCK // 8, 8, 2 * size), axis=0)
                after.append(jnp.maximum(tops[pair], folded))
            return tuple(after)

        start = tuple(jnp.full((8, 2 * size), FLOOR_SCORE, F32) for _ in range(PAIRS))
        tops = lax.fori_loop(0, count, first, start)
        tops = [jnp.max(top, axis=0, keepdims=True) for top in tops]
        sum_ref[...] = jnp.zeros_like(sum_ref)
        mix_ref[...] = jnp.zeros_like(mix_ref)

        def second(block, carry):
            rows = pl.ds(pl.multiple_of(block * KEY_BLOCK, KEY_BLOCK), KEY_BLOCK)
            for pair in range(PAIRS):
                weights = jnp.exp(score_ref[pair, rows] - tops[pair])
                sum_ref[pair] += jnp.sum(weights.reshape(KEY_BLOCK // 8, 8, 2 * size), axis=0)
                values = load_keys(v_ref, pair_index, block, pair_lanes(pair))
                mix_ref[pair] += nn(values.T, weights.astype(BF16))
            return carry

        lax.fori_loop(0, count, second, 0)
        logs = []
        for pair in range(PAIRS):
            total = jnp.sum(sum_ref[pair], axis=0, keepdims=True)
            mixed = mix_ref[pair] / total
            o_ref[own, pair_lanes(pair)] = diagonal(mixed).T.astype(BF16)
            log_total = tops[pair] + jnp.log(total)
            logs += [log_total[:, :size], log_total[:, size:]]
        lse_ref[pair_index] = jnp.concatenate(logs, axis=0)
        return carry

    lax.fori_loop(0, pairs, one, 0)


def long_attend_back(
    causal,
    info_ref,
    q_ref,
    k_ref,
    v_ref,
    o_ref,
    lse_ref,
    go_ref,
    k_w,
    v_w,
    dq_ref,
    dk_ref,
    dv_ref,
    part_ref,
    mix_ref,
):
    places, pairs, size, width = k_ref.shape
    shape = (KEY_BLOCK, 2 * size)
    everything = slice(None)

    def one(pair_index, carry):
        length, count = long_limit(info_ref, causal, pair_index, size, pairs)
        own = pl.ds(pl.multiple_of(pair_index * size, size), size)
        delta = delta_rows(go_ref[own, :], o_ref[own, :])
        lse = lse_ref[pair_index]
        mix_ref[...] = jnp.zeros_like(mix_ref)

        def step(block, carry):
            allowed = long_allowed(info_ref[pairs], causal, length, block, shape)
            for pair in range(PAIRS):
                lanes = pair_lanes(pair)
                queries, grads = two_heads(q_ref[own, lanes]), two_heads(go_ref[own, lanes])
                keys = load_keys(k_ref, pair_index, block, lanes)
                scores = nt(keys, queries)
                weights = jnp.where(allowed, jnp.exp(scores - pair_row(lse, pair)), 0.0)
                grad_weights = nt(load_keys(v_ref, pair_index, block, lanes), grads)
                grad_scores = (weights * (grad_weights - pair_row(delta, pair))).astype(BF16)
                store_keys(dv_ref, pair_index, block, lanes, nn(weights.astype(BF16), grads))
                store_keys(dk_ref, pair_index, block, lanes, nn(grad_scores, queries))
                mix_ref[pair] += nn(keys.T, grad_scores)
            part = nt(load_keys(dk_ref, pair_index, block, everything), k_w[...])
            part = part + nt(load_keys(dv_ref, pair_index, block, everything), v_w[...])
            store_part(part_ref, info_ref, pair_index, block, part.astype(BF16))
            return carry

        lax.fori_loop(0, count, step, 0)

        def clear(block, carry):
            nothing = jnp.zeros((KEY_BLOCK, width), BF16)
            store_keys(dk_ref, pair_index, block, everything, nothing)
            store_keys(dv_ref, pair_index, block, everything, nothing)
            store_part(part_ref, info_ref, pair_index, block, nothing)
            return carry

        lax.fori_loop(count, places * size // KEY_BLOCK, clear, 0)
        for pair in range(PAIRS):
            turned = diagonal(mix_ref[pair]).T
            dq_ref[own, pair_lanes(pair)] = (turned.astype(BF16).astype(F32) * SCALE).astype(BF16)
        return carry

    lax.fori_loop(0, pairs, one, 0)


class Refs(dict):
    def __init__(self, *args):
        super().__init__(*args)
        self.coming, self.leaving, self.pieced = {}, {}, {}

    def __getattr__(self, name):
        if name in self.coming:
            self.coming.pop(name).wait()
        return self[name]

    def leave_piece(self, name, piece):
        source, target, signals, first = self.pieced[name]
        pltpu.make_async_copy(source.at[piece], target.at[piece], signals.at[first + piece]).start()

    def leave(self, *names):
        for name in names:
            self["left"].add(name)
            for copy in self.leaving.get(name, ()):
                copy.start()


def copied(shape, dtype):
    size = dtype.itemsize
    for length in shape:
        size *= length
    return shape[-1] % 128 == 0 and size >= 2**16


def launch(body, arrays, gives, scratch=(), info=None, after=(), pieces=(), moved=None, cost=10):
    memory = pl.BlockSpec(memory_space=pltpu.VMEM)
    far = pl.BlockSpec(memory_space=pl.ANY)
    ins, specs = [], []
    if info is not None:
        ins.append(info)
        specs.append(pl.BlockSpec(memory_space=pltpu.SMEM))
    by_itself = lambda name, shape, dtype: (
        copied(shape, jnp.dtype(dtype)) if moved is None else name in moved
    )
    moved_in = [name for name, a in arrays.items() if by_itself(name, a.shape, a.dtype)]
    moved_out = [name for name, give in gives.items() if name in pieces or by_itself(name, *give)]
    for name, array in arrays.items():
        ins.append(array)
        specs.append(far if name in moved_in else memory)
    for array in after:
        ins.append(array)
        specs.append(far)
    count_out = sum(gives[name][0][0] if name in pieces else 1 for name in moved_out)
    rooms = [pltpu.VMEM(arrays[name].shape, arrays[name].dtype) for name in moved_in]
    rooms += [pltpu.VMEM(*gives[name]) for name in moved_out]
    rooms += [pltpu.SemaphoreType.DMA((max(len(moved_in), 1),))]
    rooms += [pltpu.SemaphoreType.DMA((max(count_out, 1),))]
    names = [name for name, _ in scratch]

    def run(*refs):
        refs = list(refs)
        r = Refs()
        if info is not None:
            r["info"] = refs.pop(0)
        outer = {name: refs.pop(0) for name in arrays}
        del refs[: len(after)]
        outer.update((name, refs.pop(0)) for name in gives)
        room = {name: refs.pop(0) for name in moved_in + moved_out}
        come, go = refs.pop(0), refs.pop(0)
        r.update(outer)
        r.update(room)
        r.update(zip(names, refs))
        for place, name in enumerate(moved_in):
            copy = pltpu.make_async_copy(outer[name], room[name], come.at[place])
            copy.start()
            r.coming[name] = copy
        place = 0
        for name in moved_out:
            copies = []
            if name in pieces:
                r.pieced[name] = (room[name], outer[name], go, place)
                for piece in range(gives[name][0][0]):
                    source, target = room[name].at[piece], outer[name].at[piece]
                    copies.append(pltpu.make_async_copy(source, target, go.at[place]))
                    place += 1
            else:
                copies.append(pltpu.make_async_copy(room[name], outer[name], go.at[place]))
                place += 1
            r.leaving[name] = copies
        left = set()
        r["left"] = left
        body(r)
        for name in list(r.coming):
            r.coming.pop(name).wait()
        for name in moved_out:
            if name not in left and name not in pieces:
                r.leave(name)
        for name in moved_out:
            for copy in r.leaving[name]:
                copy.wait()

    out = pl.pallas_call(
        run,
        in_specs=specs,
        out_specs=[far if name in moved_out else memory for name in gives],
        out_shape=[jax.ShapeDtypeStruct(shape, dtype) for shape, dtype in gives.values()],
        scratch_shapes=rooms + [shape for _, shape in scratch],
        compiler_params=pltpu.CompilerParams(vmem_limit_bytes=VMEM_LIMIT),
        cost_estimate=pl.CostEstimate(
            flops=int(cost * 1.1e9), bytes_accessed=int(cost * 3.5e6), transcendentals=0
        ),
    )(*ins)
    return Refs(zip(gives, out))


VMEM_LIMIT = 56 * 2**20


def add_sums(ref, rows):
    ref[...] = jnp.concatenate(rows, axis=0)


def encoder_tail(r, o_ref):
    residual = r.x[...].astype(F32) + nn(o_ref[...], r.w_o[...])
    first, normed, inverse = norm(residual, r.gain[0:1], r.bias[0:1])
    r.n1[...] = normed.astype(BF16)
    r.i1[...] = inverse
    if "acc" in r:
        total = feed_forward_in_loop(first, r.up, r.down, r.act, r.gate, r.y, r.acc)
    else:
        r.y[...], total = feed_forward(first, r.up, r.down, r.act, r.gate)
    r.leave("n1", "act", "gate", "y")
    encoded, normed, inverse = norm(total, r.gain[1:2], r.bias[1:2])
    r.n2[...] = normed.astype(BF16)
    r.i2[...] = inverse
    r.enc[...] = encoded.astype(BF16)


def project_short(r, name, rows, w_q, w_k, w_v, context=None):
    context = rows if context is None else context
    r["q" + name][...] = (nn(rows, w_q) * SCALE).astype(BF16)
    r["k" + name][...] = nn(context, w_k).astype(BF16)
    r["v" + name][...] = nn(context, w_v).astype(BF16)


def short_encoder_forward(r):
    project_short(r, "", r.x[...], r.w_in[0], r.w_in[1], r.w_in[2])
    r.leave("q", "k", "v")
    short_attend(False, r.q, r.k, r.v, r.kseg, r.qseg, r.o, r.lse)
    r.leave("o")
    encoder_tail(r, r.o)


def decoder_middle(r, o_ref):
    residual = r.t[...].astype(F32) + nn(o_ref[...], r.w_o[...])
    upper, normed, inverse = norm(residual, r.gain[0:1], r.bias[0:1])
    r.n3[...] = normed.astype(BF16)
    r.i3[...] = inverse
    r.u[...] = upper.astype(BF16)
    return upper


def decoder_tail(r, upper, o_ref):
    gain, bias = r.gain, r.bias
    residual = upper + nn(o_ref[...], r.w_co[...])
    middle, normed4, inverse4 = norm(residual, gain[1:2], bias[1:2])
    r.m[...], total = feed_forward(middle, r.up, r.down, r.act, r.gate)
    r.leave("m", "act", "gate")
    final, normed5, inverse5 = norm(total, gain[2:3], bias[2:3])
    r.final[...] = final
    r.leave("final")
    grad, gain5, bias5 = norm_back(r.cot[...].astype(F32), normed5, inverse5, gain[2:3])
    r.b5[...], grad = feed_back(grad, r.gate, r.up, r.down, r.dh)
    r.leave("b5", "dh")
    grad, gain4, bias4 = norm_back(grad, normed4, inverse4, gain[1:2])
    low = grad.astype(BF16)
    r.b4[...] = low
    r.d4[...] = grad
    r.go_c[...] = nt(low, r.w_co[...]).astype(BF16)
    add_sums(r.small, [gain4, gain5, bias4, bias5])


def short_decoder_forward(r):
    project_short(r, "", r.t[...], r.w_in[0], r.w_in[1], r.w_in[2])
    r.leave("q", "k", "v")
    short_attend(True, r.q, r.k, r.v, r.tkseg, r.tqseg, r.o, r.lse)
    r.leave("o")
    r.upper[...] = decoder_middle(r, r.o)


def short_cross_forward(r):
    project_short(r, "_c", r.u[...], r.w_cin[0], r.w_cin[1], r.w_cin[2], r.enc[...])
    r.leave("q_c", "k_c", "v_c")
    short_attend(False, r.q_c, r.k_c, r.v_c, r.kseg, r.tqseg, r.o_c, r.lse_c)
    r.leave("o_c")
    decoder_tail(r, r.upper[...], r.o_c)


def decoder_middle_back(r):
    grad = r.d4[...] + nt(r.dq_c[...], r.w_cin[0])
    grad, gain3, bias3 = norm_back(grad, r.n3[...], r.i3[...], r.gain[0:1])
    low = grad.astype(BF16)
    r.b3[...] = low
    r.go[...] = nt(low, r.w_o[...]).astype(BF16)
    add_sums(r.small, [gain3, bias3])
    return grad


def short_decoder_back(r):
    short_attend_back(
        False, r.q_c, r.k_c, r.v_c, r.kseg, r.tqseg, r.o_c, r.lse_c, r.go_c, r.dq_c, r.dk_c, r.dv_c
    )
    r.denc[...] = nt(r.dk_c[...], r.w_cin[1]) + nt(r.dv_c[...], r.w_cin[2])
    r.leave("dq_c", "dk_c", "dv_c", "denc")
    r.d3[...] = decoder_middle_back(r)
    short_attend_back(
        True, r.q, r.k, r.v, r.tkseg, r.tqseg, r.o, r.lse, r.go, r.dq, r.dk, r.dv
    )
    r.leave("dq", "dk", "dv")
    grad = r.d3[...] + nt(r.dq[...], r.w_in[0])
    r.dt[...] = grad + nt(r.dk[...], r.w_in[1]) + nt(r.dv[...], r.w_in[2])


def encoder_tail_back(r, grad):
    grad, gain2, bias2 = norm_back(grad, r.n2[...], r.i2[...], r.gain[1:2])
    r.b2[...], grad = feed_back(grad, r.gate, r.up, r.down, r.dh)
    r.leave("b2", "dh")
    grad, gain1, bias1 = norm_back(grad, r.n1[...], r.i1[...], r.gain[0:1])
    low = grad.astype(BF16)
    r.b1[...] = low
    r.go[...] = nt(low, r.w_o[...]).astype(BF16)
    r.d1[...] = grad
    add_sums(r.small, [gain1, gain2, bias1, bias2])


def short_encoder_back(r):
    encoder_tail_back(r, r.denc[...])
    short_attend_back(
        False, r.q, r.k, r.v, r.kseg, r.qseg, r.o, r.lse, r.go, r.dq, r.dk, r.dv
    )
    r.leave("dq", "dk", "dv")
    grad = r.d1[...] + nt(r.dq[...], r.w_in[0])
    r.dx[...] = grad + nt(r.dk[...], r.w_in[1]) + nt(r.dv[...], r.w_in[2])


def long_encoder_forward(r):
    r.q[...] = (nn(r.x[...], r.w_in[0]) * SCALE).astype(BF16)
    long_attend(
        False, r.info, r.q, r.xg, r.w_in.at[1], r.w_in.at[2], r.k, r.v, r.o, r.lse, r.s, r.a, r.mix
    )
    r.leave("q", "k", "v", "o")
    encoder_tail(r, r.o)


def long_self_forward(r):
    r.q[...] = (nn(r.t[...], r.w_in[0]) * SCALE).astype(BF16)
    long_attend(
        True, r.info, r.q, r.tg, r.w_in.at[1], r.w_in.at[2], r.k, r.v, r.o, r.lse, r.s, r.a, r.mix
    )
    r.leave("q", "k", "v", "o")
    upper = decoder_middle(r, r.o)
    r.upper[...] = upper
    r.q_c[...] = (nn(upper.astype(BF16), r.w_cin[0]) * SCALE).astype(BF16)


def long_cross(r):
    k_w, v_w = r.w_cin.at[1], r.w_cin.at[2]
    long_attend(
        False, r.info, r.q_c, r.eg, k_w, v_w, r.k_c, r.v_c, r.o_c, r.lse_c, r.s, r.a, r.mix
    )
    r.leave("k_c", "v_c", "o_c")
    decoder_tail(r, r.upper[...], r.o_c)


def part_refs(r):
    return [r[name] for name in r if name[0] == "p" and name[1:].isdigit()]


def long_cross_back(r):
    long_attend_back(
        False,
        r.info,
        r.q_c,
        r.k_c,
        r.v_c,
        r.o_c,
        r.lse_c,
        r.go_c,
        r.w_cin.at[1],
        r.w_cin.at[2],
        r.dq_c,
        r.dk_c,
        r.dv_c,
        part_refs(r),
        r.mix,
    )


def long_self_back(r):
    grad = decoder_middle_back(r)
    long_attend_back(
        True,
        r.info,
        r.q,
        r.k,
        r.v,
        r.o,
        r.lse,
        r.go,
        r.w_in.at[1],
        r.w_in.at[2],
        r.dq,
        r.dk,
        r.dv,
        part_refs(r),
        r.mix,
    )
    r.dt[...] = grad + nt(r.dq[...], r.w_in[0])


def long_encoder_tail_back(r):
    grad = r.part0[...].astype(F32) + r.part1[...].astype(F32)
    grad = grad + r.part2[...].astype(F32) + r.part3[...].astype(F32)
    encoder_tail_back(r, grad)


def long_encoder_back(r):
    long_attend_back(
        False,
        r.info,
        r.q,
        r.k,
        r.v,
        r.o,
        r.lse,
        r.go,
        r.w_in.at[1],
        r.w_in.at[2],
        r.dq,
        r.dk,
        r.dv,
        part_refs(r),
        r.mix,
    )
    r.dx[...] = r.d1[...] + nt(r.dq[...], r.w_in[0])


SIDE = 512


class Weights:
    def __init__(self, pairs, base=None):
        self.arrays, self.plan, known = {}, [], {}

        def place(rows):
            if isinstance(rows, tuple):
                return rows
            if id(rows) not in known:
                known[id(rows)] = "w%d" % len(known)
                self.arrays[known[id(rows)]] = rows
            return known[id(rows)], rows.shape[-1]

        self.count = 0
        for terms in pairs:
            terms = [(place(a), place(b)) for a, b in terms]
            (_, height), (_, width) = terms[0]
            self.plan.append((self.count, width // SIDE, [(a[0], b[0]) for a, b in terms]))
            self.count += height // SIDE * (width // SIDE)
        self.gives = {name: ((self.count, SIDE // 2, SIDE), BF16) for name in ("kept", "sent")}
        if base is not None:
            self.arrays["base"] = base

    def each(self, r, step):
        ends = [first for first, _, _ in self.plan[1:]] + [self.count]
        for (first, across, terms), end in zip(self.plan, ends):
            terms = [(getattr(r, a), getattr(r, b)) for a, b in terms]

            def body(tile, carry, first=first, across=across, terms=terms):
                row = pl.multiple_of(lax.div(tile - first, across) * SIDE, SIDE)
                column = pl.multiple_of(lax.rem(tile - first, across) * SIDE, SIDE)
                step(tile, row, column, terms)
                return carry

            lax.fori_loop(first, end, body, 0)

    def body(self, r, core):
        half = SIDE // 2
        if "base" in self.arrays:
            r.base

        def step(tile, row, column, terms):
            for flip, name in enumerate(("kept", "sent")):
                inside = pl.multiple_of((core ^ flip) * half, half)
                total = None
                if "base" in self.arrays:
                    total = r["base"][tile, pl.ds(inside, half), :].astype(F32)
                for left, right in terms:
                    rows = pl.ds(pl.multiple_of(row + inside, half), half)
                    across = pl.ds(column, SIDE)
                    if len(left.shape) == 4:
                        tall = left.shape[0] * left.shape[1] * left.shape[2]
                        first = left[:, :, :, rows].reshape(tall, half)
                    else:
                        first = left[:, rows]
                    if len(right.shape) == 4:
                        tall = right.shape[0] * right.shape[1] * right.shape[2]
                        product = tn(first, right[:, :, :, across].reshape(tall, SIDE))
                    else:
                        product = tn(first, right[:, across])
                    total = product if total is None else total + product
                r[name][tile] = total.astype(BF16)
                r.leave_piece(name, tile)

        self.each(r, step)


class Tagged:
    def __init__(self, r, tag):
        self.r, self.tag = r, tag

    def __getattr__(self, name):
        return getattr(self.r, name + self.tag)


def whole_tiles(chunks, after=(), cost=10):
    weights = [Weights([[pair] for pair in chunk]) for chunk in chunks]
    arrays, gives = {}, {}
    for number, part in enumerate(weights):
        gives["c%d" % number] = ((part.count, SIDE, SIDE), BF16)
        arrays.update((name + "c%d" % number, array) for name, array in part.arrays.items())

    def body(r):
        for number, part in enumerate(weights):
            tag = "c%d" % number

            def step(tile, row, column, terms, tag=tag):
                ((left, right),) = terms
                product = tn(left[:, pl.ds(row, SIDE)], right[:, pl.ds(column, SIDE)])
                r[tag][tile] = product.astype(BF16)
                r.leave_piece(tag, tile)

            part.each(Tagged(r, tag), step)

    out = launch(body, arrays, gives, after=after, pieces=tuple(gives), cost=cost)
    return list(out.values())


def weight_tiles(pairs, core_info, after=(), cost=10, base=None):
    weights = Weights(pairs, base)
    out = launch(
        lambda r: weights.body(r, r.info[0]),
        weights.arrays,
        weights.gives,
        info=core_info,
        after=after,
        pieces=("kept", "sent"),
        cost=cost,
    )
    return [out.kept, out.sent]


def send(piece, axis, offset):
    count = lax.axis_size(axis)
    return lax.ppermute(piece, axis, [(i, i ^ offset) for i in range(count)])


def ordered(pieces, place, dim):
    if len(pieces) == 1:
        return pieces[0]
    level = len(pieces) // 2
    inside = lax.rem(place, level)
    low = ordered(pieces[:level], inside, dim)
    high = ordered(pieces[level:], inside, dim)
    return jnp.where(
        place >= level, jnp.concatenate([high, low], dim), jnp.concatenate([low, high], dim)
    )


def hold(value, token):
    return lax.optimization_barrier((value, token))[0]


def gather_first(piece, axis):
    return [piece] + [send(piece, axis, k) for k in range(1, lax.axis_size(axis))]


def gather_last(pieces, axis, dim, token=None):
    if token is not None:
        pieces = hold(pieces, token)
    return ordered(pieces, lax.axis_index(axis), dim)


def added(pieces):
    total = pieces[0].astype(F32)
    for piece in pieces[1:]:
        total = total + piece.astype(F32)
    return total.astype(BF16)


def scatter_step(pending, axis, dim, token=None):
    if token is not None:
        pending = hold(pending, token)
    place, count = lax.axis_index(axis), lax.axis_size(axis)
    size = pending[0].shape[dim] // count
    after = []
    for k in range(count):
        parts = [
            lax.dynamic_slice_in_dim(piece, (place ^ k) * size, size, dim) for piece in pending
        ]
        block = added(parts)
        after.append(send(block, axis, k) if k else block)
    return after


def gather_step(piece, axis, dim):
    return gather_last(gather_first(piece, axis), axis, dim)


def gather_early(rows):
    return lax.all_gather(rows, (OUTER, INNER), axis=0, tiled=False)


SEQ = (OUTER, INNER)


class Chain:
    def __init__(self, halves, order, small=None, doubled=False):
        self.order = (CORE,) + order
        self.doubled = doubled
        self.stage = 0
        self.tiles = halves[0].shape[0]
        self.small, self.carried = None, 0
        if small is not None:
            self.carried = small.shape[0]
            halves = [jnp.concatenate([self.flat(half), small]) for half in halves]
        self.held = [halves[0], send(halves[1], CORE, 1)]

    def flat(self, block):
        return block.reshape(-1, block.shape[-1])

    def parts(self):
        if not self.carried:
            return self.held, None
        body = [piece[: -self.carried] for piece in self.held]
        body = [piece.reshape(self.tiles, -1, piece.shape[-1]) for piece in body]
        return body, added([piece[-self.carried :] for piece in self.held])

    def next_axis(self):
        stage, count = self.stage + 1, len(self.order)
        return self.order[stage] if stage < count else self.order[2 * count - 1 - stage]

    def over(self):
        return self.stage == 2 * len(self.order) - 1

    def go(self):
        axis = self.next_axis()
        self.stage += 1
        count = len(self.order)
        if self.doubled and self.stage in (count - 1, count):
            total = added(self.held)
            self.held = [total, send(total, OUTER, self.stage - count + 2)]
            return
        if self.doubled and self.stage == count + 1:
            pending, self.small = self.parts()
            self.held = gather_first(added(pending), axis)
            return
        if self.stage < count:
            pending, small = self.parts()
            place, members = lax.axis_index(axis), lax.axis_size(axis)
            size = pending[0].shape[1] // members
            self.held = []
            for k in range(members):
                begin = (place ^ k) * size
                block = added([lax.dynamic_slice_in_dim(p, begin, size, 1) for p in pending])
                if small is not None:
                    block = jnp.concatenate([self.flat(block), small])
                self.held.append(send(block, axis, k) if k else block)
            return
        if self.stage == count:
            pending, self.small = self.parts()
            piece = added(pending)
        else:
            piece = gather_last(self.held, self.order[2 * count - self.stage], 1)
        self.held = gather_first(piece, axis)

    def volume(self):
        return self.held[0].size * 2 / 2**20


class Spread:
    def __init__(self, part, straight):
        self.straight, self.stage = straight, 0
        self.held = [send(rows, INNER, k) if k else rows for k, rows in enumerate(part)]

    def next_axis(self):
        return OUTER

    def over(self):
        return self.stage == (1 if self.straight else 2)

    def go(self):
        self.stage += 1
        if self.straight:
            blocks = [added([piece[k] for piece in self.held]) for k in range(4)]
            self.held = [send(block, OUTER, k) if k else block for k, block in enumerate(blocks)]
            return
        if self.stage == 1:
            pick, offset = (lambda piece, odd: jnp.stack([piece[odd], piece[2 + odd]])), 1
        else:
            pick, offset = (lambda piece, odd: piece[odd]), 2
        mine, theirs = [added([pick(piece, odd) for piece in self.held]) for odd in (0, 1)]
        self.held = [mine, send(theirs, OUTER, offset)]

    def volume(self):
        return self.held[0].size * 2 / 2**20

    def result(self):
        return added(self.held)


def finish(chains, *tokens):
    held, _ = lax.optimization_barrier(([chain.held for chain in chains], tokens))
    for chain, pieces in zip(chains, held):
        chain.held = pieces


def go(*chains):
    for chain in chains:
        chain.go()


FLOW = {CORE: 3.5, X: 21.0, INNER: 21.0, OUTER: 84.0}


def plan_of(chain):
    if isinstance(chain, Spread):
        return [(INNER, 21.0, 1), (OUTER, 10.5, 1), (OUTER, 10.5, 1)][chain.stage :]
    size, out = chain.tiles * 0.5, []
    for axis in chain.order:
        count = lax.axis_size(axis)
        if axis == OUTER and chain.doubled:
            out += [(OUTER, 21.0 * size, 1), (OUTER, 42.0 * size, 1)]
            continue
        size = size / count
        out.append((axis, FLOW[axis] * size, count - 1))
    back = [entry for entry in reversed(out)]
    if chain.doubled:
        back = [entry for entry in back if entry[0] != OUTER]
    return (out + back)[chain.stage :]


def rehearse(plans, first, gate, weights, slack):
    free = dict.fromkeys(FLOW, 0.0)
    position, queue, order, clock, waiting = [0] * len(plans), [], [], 0.0, []

    def depart(index, when):
        axis, long, _ = plans[index][position[index]]
        begin = max(when, free[axis])
        free[axis] = begin + long
        queue.append((free[axis] + 6.0, index))

    def left(index):
        rest = plans[index][position[index] :]
        return weights[index] * sum(long + 10.0 for _, long, _ in rest)

    for index, since in first:
        depart(index, -since)
    while queue or waiting:
        soon = min(queue)[0] if queue else clock + 99.0
        if waiting and soon > clock + 4.0:
            clock += 6.5
            order.append((waiting.pop(0), True))
            continue
        near = [entry for entry in queue if entry[0] <= max(clock, soon) + slack]
        entry = max(near, key=lambda entry: left(entry[1]))
        queue.remove(entry)
        arrival, index = entry
        clock = max(clock, arrival)
        position[index] += 1
        order.append((index, False))
        if position[index] == len(plans[index]):
            clock += 1.0
            waiting.append(index)
            continue
        axis, long, sends = plans[index][position[index]]
        clock += 2.0 + 1.5 * sends + 0.03 * long
        depart(index, clock)
        if gate[1] == index and position[index] == 1:
            clock += 2.0
            depart(gate[0], clock)
    return clock, order


def run_out(flights, later):
    chains, ends = [chain for chain, _, _ in flights], [end for _, _, end in flights]
    plans = [plan_of(chain) for chain in chains]
    plans.append([(INNER, 21.0, 1), (OUTER, 10.5, 1), (OUTER, 10.5, 1)])
    first = [(index, since) for index, (_, since, _) in enumerate(flights)]
    rng, best = random.Random(7), None
    for trial in range(1500):
        weights = [1.0 if trial < 4 else rng.uniform(0.3, 2.0) for _ in plans]
        slack = (0.0, 2.0, 4.0, 8.0)[trial % 4]
        found = rehearse(plans, first, (len(chains), 0), weights, slack)
        if best is None or found[0] < best[0]:
            best = found
    token, results = (), {}
    for index, is_end in best[1]:
        chain = chains[index]
        if is_end:
            results[index] = ends[index](chain, token)
            token = (results[index][0],)
            continue
        finish([chain], *token)
        if chain.over():
            token = tuple(chain.held)
            continue
        chain.go()
        token = (chain.held[0],)
        if index == 0 and chain.stage == 1:
            chain, _, end = later(token)
            chains.append(chain)
            ends.append(end)
    return [results[index] for index in range(len(chains))]


def assemble(chain, core_info, shapes, after=()):
    tiles, half, side = chain.held[0].shape

    places = []
    for name, shape in shapes.items():
        blocks = shape[0] if len(shape) > 2 else shape[0] * shape[1] // (side * side)
        for block in range(blocks):
            if len(shape) > 2:
                places.append((name, lambda rows, b=block: (b, rows, slice(None))))
            elif shape[1] > shape[0]:
                lanes = slice(block * side, (block + 1) * side)
                places.append((name, lambda rows, l=lanes: (rows, l)))
            else:
                places.append((name, lambda rows, b=block: (pl.ds(rows.start + b * side, half), slice(None))))

    def body(info, mine, other, *refs):
        outs = dict(zip(shapes, refs))
        room, full, come, go = refs[len(shapes) :]
        starts = [pl.multiple_of((info[0] ^ flip) * half, half) for flip in (0, 1)]
        arrive, leave = [], []
        for tile in range(tiles):
            for flip, source in enumerate((mine, other)):
                index = 2 * tile + flip
                arrive.append(pltpu.make_async_copy(source.at[tile], room.at[index], come.at[index]))
                arrive[-1].start()
        for tile, (name, where) in enumerate(places):
            for flip in (0, 1):
                index = 2 * tile + flip
                arrive[index].wait()
                full[index] = room[index].astype(F32)
                target = outs[name].at[where(pl.ds(starts[flip], half))]
                leave.append(pltpu.make_async_copy(full.at[index], target, go.at[index]))
                leave[-1].start()
        for copy in leave:
            copy.wait()

    far = pl.BlockSpec(memory_space=pl.ANY)
    return pl.pallas_call(
        lambda info, mine, other, *refs: body(info, mine, other, *refs[len(after) :]),
        in_specs=[pl.BlockSpec(memory_space=pltpu.SMEM)] + [far] * (2 + len(after)),
        out_specs=[far] * len(shapes),
        out_shape=[jax.ShapeDtypeStruct(shape, F32) for shape in shapes.values()],
        scratch_shapes=[
            pltpu.VMEM((2 * tiles, half, side), BF16),
            pltpu.VMEM((2 * tiles, half, side), F32),
            pltpu.SemaphoreType.DMA((2 * tiles,)),
            pltpu.SemaphoreType.DMA((2 * tiles,)),
        ],
        compiler_params=pltpu.CompilerParams(vmem_limit_bytes=VMEM_LIMIT),
        cost_estimate=pl.CostEstimate(flops=5 * 10**9, bytes_accessed=2 * 10**7, transcendentals=0),
    )(core_info, chain.held[0], chain.held[1], *after)


def shards(
    source_short,
    target_short,
    source_segment,
    target_segment,
    source_long,
    target_long,
    source_length,
    target_length,
    cotangent_short,
    cotangent_long,
    encoder_project,
    encoder_output,
    encoder_up,
    encoder_down,
    encoder_gain,
    encoder_bias,
    decoder_project,
    decoder_output,
    cross_project,
    cross_output,
    decoder_up,
    decoder_down,
    decoder_gain,
    decoder_bias,
):
    blocks, size, width = source_short.shape
    hidden = encoder_up.shape[1]
    rows = blocks * size
    pairs, own, _ = source_long.shape
    rows_long = pairs * own
    flat = lambda a: a.reshape(-1, width)
    start = lax.axis_index((OUTER, INNER)) * own
    core = lax.axis_index(CORE)
    here = [start, lax.axis_index(INNER), core, lax.axis_index(OUTER)]
    here = jnp.stack(here).astype(jnp.int32)
    info_of = lambda lengths: jnp.concatenate([lengths, here])
    core_info = core.astype(jnp.int32)[None]
    source_info, target_info = info_of(source_length), info_of(target_length)

    spread = lambda s: jnp.broadcast_to(s[:, :, None], (blocks, size, size))
    line = lambda s: s[:, None, :]
    encoder_in = {
        "w_in": encoder_project,
        "w_o": encoder_output,
        "up": encoder_up,
        "down": encoder_down,
        "gain": encoder_gain,
        "bias": encoder_bias,
    }
    decoder_in = {
        "w_in": decoder_project,
        "w_o": decoder_output,
        "w_cin": cross_project,
        "w_co": cross_output,
        "up": decoder_up,
        "down": decoder_down,
        "gain": decoder_gain,
        "bias": decoder_bias,
    }

    def pick(table, names):
        return {name: table[name] for name in names}

    def rows_of(n, names):
        return {name: ((n, width), BF16) for name in names}

    def wide_of(n, names):
        return {name: ((n, hidden), BF16) for name in names}

    def floats(n, names):
        return {name: ((n, width), F32) for name in names}

    def column(n, names):
        return {name: ((n, 1), F32) for name in names}

    def logs(n, names):
        return {name: ((n, HEADS, size), F32) for name in names}

    def sums(n):
        return {"small": ((n, width), F32)}

    def keys_of(names):
        shape = (places, pairs, own, width)
        return {name: (shape, BF16) for name in names}

    def parts():
        inner = lax.axis_size(INNER)
        return {"p%d" % k: ((places // inner, pairs, own, width), BF16) for k in range(inner)}

    def saved(kernel, names):
        return {name: kernel[name] for name in names}

    whole_source = gather_early(source_long)
    places = lax.axis_size(OUTER) * lax.axis_size(INNER)
    keys = places * own
    work = [
        ("s", pltpu.VMEM((PAIRS, keys, 2 * own), F32)),
        ("a", pltpu.VMEM((PAIRS, 8, 2 * own), F32)),
        ("mix", pltpu.VMEM((PAIRS, PAIR, 2 * own), F32)),
    ]
    mix = work[2:]

    segments = {"kseg": spread(source_segment), "qseg": line(source_segment)}
    turned = {"tkseg": spread(target_segment), "tqseg": line(target_segment)}
    encoder_keeps = lambda n: {
        **rows_of(n, ("n1", "y", "n2", "enc")),
        **wide_of(n, ("act", "gate")),
        **column(n, ("i1", "i2")),
    }
    se = launch(
        short_encoder_forward,
        {"x": flat(source_short), **segments, **encoder_in},
        {**rows_of(rows, ("q", "k", "v", "o")), **logs(blocks, ("lse",)), **encoder_keeps(rows)},
        cost=0.01,
    )
    decoder_keeps = lambda n: {
        **rows_of(n, ("m", "b5", "b4", "go_c")),
        **wide_of(n, ("act", "gate", "dh")),
        **floats(n, ("final", "d4")),
        **sums(4),
    }
    sd = launch(
        short_decoder_forward,
        {
            "t": flat(target_short),
            **turned,
            **pick(decoder_in, ("w_in", "w_o", "gain", "bias")),
        },
        {
            **rows_of(rows, ("q", "k", "v", "o", "n3", "u")),
            **logs(blocks, ("lse",)),
            **column(rows, ("i3",)),
            **floats(rows, ("upper",)),
        },
        after=(se.lse,),
        cost=0.01,
    )
    early_target = gather_first(hold(target_long, sd.lse)[None, None], OUTER)
    sc = launch(
        short_cross_forward,
        {
            "u": sd.u,
            "upper": sd.upper,
            "enc": se.enc,
            "cot": flat(cotangent_short),
            "kseg": segments["kseg"],
            "tqseg": turned["tqseg"],
            **pick(decoder_in, ("w_cin", "w_co", "up", "down", "gain", "bias")),
        },
        {
            **rows_of(rows, ("q_c", "k_c", "v_c", "o_c")),
            **logs(blocks, ("lse_c",)),
            **decoder_keeps(rows),
        },
        after=(sd.lse,),
        cost=0.01,
    )

    sb = launch(
        short_decoder_back,
        {
            **saved(sd, ("q", "k", "v", "o", "lse", "n3", "i3")),
            **saved(sc, ("q_c", "k_c", "v_c", "o_c", "lse_c", "go_c", "d4")),
            "kseg": segments["kseg"],
            **turned,
            **pick(decoder_in, ("w_in", "w_o", "w_cin", "gain")),
        },
        {
            **rows_of(rows, ("dq_c", "dk_c", "dv_c", "dq", "dk", "dv", "b3", "go")),
            **floats(rows, ("denc", "dt")),
            **sums(2),
        },
        scratch=[("d3", pltpu.VMEM((rows, width), F32))],
        after=(sc.small,),
        cost=0.01,
    )

    early_target = gather_last(early_target, OUTER, 0, sb.small)

    whole_source = hold(whole_source, sb.small)
    x_long, t_long = flat(source_long), flat(target_long)
    le = launch(
        long_encoder_forward,
        {"x": x_long, "xg": whole_source, **encoder_in},
        {
            **rows_of(rows_long, ("q", "o")),
            **keys_of(("k", "v")),
            **logs(pairs, ("lse",)),
            **encoder_keeps(rows_long),
        },
        scratch=work + [("acc", pltpu.VMEM((rows_long, width), F32))],
        info=source_info,
        after=(sb.small, early_target),
        cost=13,
        moved=(),
    )
    late_target = gather_first(hold(early_target, le.lse), INNER)
    whole_encoded = gather_early(le.enc.reshape(pairs, own, width))

    seb = launch(
        short_encoder_back,
        {
            "denc": sb.denc,
            **saved(se, ("q", "k", "v", "o", "lse", "n1", "i1", "n2", "i2", "gate")),
            **segments,
            **pick(encoder_in, ("w_in", "w_o", "up", "down", "gain")),
        },
        {
            **rows_of(rows, ("dq", "dk", "dv", "b1", "b2", "go")),
            **wide_of(rows, ("dh",)),
            **floats(rows, ("dx",)),
            **sums(4),
        },
        scratch=[("d1", pltpu.VMEM((rows, width), F32))],
        after=(le.lse,),
        cost=16,
    )

    t_short, x_short = flat(target_short), flat(source_short)
    short_weights = whole_tiles(
        [
            [(sc.m, sc.dh), (sc.act, sc.b5)],
            [
                (sd.u, sb.dq_c),
                (se.enc, sb.dk_c),
                (se.enc, sb.dv_c),
                (sc.o_c, sc.b4),
                (t_short, sb.dq),
                (t_short, sb.dk),
                (t_short, sb.dv),
                (sd.o, sb.b3),
            ],
            [(se.y, seb.dh), (se.act, seb.b2)],
            [(x_short, seb.dq), (x_short, seb.dk), (x_short, seb.dv), (se.o, seb.b1)],
        ],
        after=(seb.small,),
        cost=15,
    )
    whole_target = gather_last(late_target, INNER, 1, short_weights[0])
    whole_target = whole_target.reshape(places, pairs, own, width)
    ls = launch(
        long_self_forward,
        {
            "t": t_long,
            "tg": whole_target,
            **pick(decoder_in, ("w_in", "w_o", "w_cin", "gain", "bias")),
        },
        {
            **rows_of(rows_long, ("q", "o", "n3", "u", "q_c")),
            **keys_of(("k", "v")),
            **logs(pairs, ("lse",)),
            **column(rows_long, ("i3",)),
            **floats(rows_long, ("upper",)),
        },
        scratch=work,
        info=target_info,
        after=(short_weights[0],),
        cost=10,
        moved=(),
    )

    whole_encoded = hold(whole_encoded, ls.lse)
    lc = launch(
        long_cross,
        {
            "eg": whole_encoded,
            "upper": ls.upper,
            "q_c": ls.q_c,
            "cot": flat(cotangent_long),
            **pick(decoder_in, ("w_cin", "w_co", "up", "down", "gain", "bias")),
        },
        {
            **rows_of(rows_long, ("o_c",)),
            **keys_of(("k_c", "v_c")),
            **logs(pairs, ("lse_c",)),
            **decoder_keeps(rows_long),
        },
        scratch=work,
        info=source_info,
        after=(ls.lse,),
        cost=14,
        moved=("k_c", "v_c", "up", "down", "w_co", "act", "gate", "dh", "final"),
    )
    lcb = launch(
        long_cross_back,
        {
            "q_c": ls.q_c,
            **saved(lc, ("k_c", "v_c", "o_c", "lse_c", "go_c")),
            **pick(decoder_in, ("w_cin",)),
        },
        {**rows_of(rows_long, ("dq_c",)), **keys_of(("dk_c", "dv_c")), **parts()},
        scratch=mix,
        info=source_info,
        after=(lc.small,),
        cost=14,
        moved=(),
    )
    encoded_back = Spread(part_refs(lcb), True)
    first_weights = Weights(
        [[(lc.m, lc.dh)], [(lc.act, lc.b5)]], short_weights[0]
    )

    def self_back_and_weights(r):
        long_self_back(r)
        first_weights.body(r, r.info[pairs + 2])

    lsb = launch(
        self_back_and_weights,
        {
            "d4": lc.d4,
            "dq_c": lcb.dq_c,
            **saved(ls, ("q", "k", "v", "o", "lse", "n3", "i3")),
            **pick(decoder_in, ("w_in", "w_o", "w_cin", "gain")),
            **first_weights.arrays,
        },
        {
            **first_weights.gives,
            **rows_of(rows_long, ("dq", "b3")),
            **keys_of(("dk", "dv")),
            **parts(),
            **floats(rows_long, ("dt",)),
            **sums(2),
        },
        scratch=mix + [("go", pltpu.VMEM((rows_long, width), BF16))],
        info=target_info,
        after=(lcb.dq_c,),
        pieces=("kept", "sent"),
        cost=22,
    )
    decoder_ffn = Chain([lsb.kept, lsb.sent], (X, INNER, OUTER))
    finish([encoded_back], lsb.small)
    go(encoded_back)
    target_back = Spread(part_refs(lsb), False)
    grad_attention = weight_tiles(
        [
            [(ls.u, lcb.dq_c)],
            [(flat(whole_encoded), flat(lcb.dk_c))],
            [(flat(whole_encoded), flat(lcb.dv_c))],
            [(lc.o_c, lc.b4)],
            [(t_long, lsb.dq)],
            [(flat(whole_target), flat(lsb.dk))],
            [(flat(whole_target), flat(lsb.dv))],
            [(ls.o, lsb.b3)],
        ],
        core_info,
        after=(lsb.small, encoded_back.held[0]),
        base=short_weights[1],
        cost=15,
    )
    finish([encoded_back, decoder_ffn], grad_attention[0])
    go(decoder_ffn)
    attention = Chain(grad_attention, (INNER, X, OUTER))
    ffn_weights = Weights(
        [
            [(le.y, ("dh", hidden))],
            [(le.act, ("b2", width))],
        ],
        short_weights[2],
    )

    def encoder_back_and_weights(r):
        long_encoder_tail_back(r)
        ffn_weights.body(r, r.info[0])

    leb = launch(
        encoder_back_and_weights,
        {
            **{"part%d" % k: flat(piece) for k, piece in enumerate(encoded_back.held)},
            **saved(le, ("n1", "i1", "n2", "i2", "gate")),
            **pick(encoder_in, ("down", "up", "w_o", "gain")),
            **ffn_weights.arrays,
        },
        {
            **ffn_weights.gives,
            **rows_of(rows_long, ("b1", "b2", "go")),
            **wide_of(rows_long, ("dh",)),
            **floats(rows_long, ("d1",)),
            **sums(4),
        },
        info=core_info,
        after=(grad_attention[0], decoder_ffn.held[0]),
        pieces=("kept", "sent"),
        cost=12,
    )
    small = jnp.concatenate([seb.small + leb.small, sb.small + lsb.small, sc.small + lc.small])
    small = jnp.pad(small, ((0, 16 - small.shape[0]), (0, 0))).astype(BF16)
    finish([attention], leb.small)
    go(attention)
    encoder_ffn = Chain([leb.kept, leb.sent], (X, INNER, OUTER))
    attention_weights = Weights(
        [
            [(x_long, ("dq", width))],
            [(whole_source, ("dk", width))],
            [(whole_source, ("dv", width))],
            [(le.o, leb.b1)],
        ],
        short_weights[3],
    )

    def attention_back_and_weights(r):
        long_encoder_back(r)
        r.leave("dx", *[name for name in r if name[0] == "p" and name[1:].isdigit()])
        attention_weights.body(r, r.info[pairs + 2])

    lea = launch(
        attention_back_and_weights,
        {
            **saved(le, ("q", "k", "v")),
            "o": le.o,
            "lse": le.lse,
            **saved(leb, ("go", "d1")),
            **pick(encoder_in, ("w_in",)),
            **attention_weights.arrays,
        },
        {
            **attention_weights.gives,
            **parts(),
            **floats(rows_long, ("dx",)),
        },
        scratch=mix
        + [
            ("dq", pltpu.VMEM((rows_long, width), BF16)),
            ("dk", pltpu.VMEM((places, pairs, own, width), BF16)),
            ("dv", pltpu.VMEM((places, pairs, own, width), BF16)),
        ],
        info=source_info,
        after=(leb.small, attention.held[0]),
        pieces=("kept", "sent"),
        cost=19,
    )
    done = lea.dx
    finish([decoder_ffn, encoder_ffn, target_back], done)
    encoder = Chain([lea.kept, lea.sent], (INNER, X, OUTER), small, True)
    go(decoder_ffn, encoder_ffn, target_back)
    square = (3, width, width)
    feed = {"up": encoder_up.shape, "down": encoder_down.shape}
    one = {"project": square, "output": square[1:]}
    two = {"cross_in": square, "cross_out": square[1:], "self_in": square, "self_out": square[1:]}

    def out(shapes):
        return lambda chain, token: assemble(chain, core_info, shapes, token)

    rows_out = lambda rows: lambda chain, token: [chain.result().astype(F32) + rows]
    flights = [
        (encoder, 0.0, out(one)),
        (decoder_ffn, 0.0, out(feed)),
        (attention, 20.0, out(two)),
        (encoder_ffn, 0.0, out(feed)),
        (target_back, 0.0, rows_out(lsb.dt.reshape(source_long.shape))),
    ]

    def source_back(token):
        chain = Spread(hold(part_refs(lea), token), False)
        return chain, 0.0, rows_out(lea.dx.reshape(source_long.shape))

    results = run_out(flights, source_back)
    (encoder_in_out, encoder_out_out), (decoder_up_out, decoder_down_out) = results[:2]
    (cross_in, cross_out, self_in, self_out), (encoder_up_out, encoder_down_out) = results[2:4]
    (grad_target,), (grad_source,) = results[4:]
    small = encoder.small.astype(F32)
    return (
        sc.final.reshape(source_short.shape),
        lc.final.reshape(source_long.shape),
        seb.dx.reshape(source_short.shape),
        sb.dt.reshape(source_short.shape),
        grad_source,
        grad_target,
        encoder_in_out,
        encoder_out_out,
        encoder_up_out,
        encoder_down_out,
        small[0:2],
        small[2:4],
        self_in,
        self_out,
        cross_in,
        cross_out,
        decoder_up_out,
        decoder_down_out,
        jnp.stack([small[4], small[6], small[7]]),
        jnp.stack([small[5], small[8], small[9]]),
    )


def solution(mesh):
    group, seq = mesh.devices.shape
    fine = Mesh(
        mesh.devices.reshape(group // 2, 2, 4, seq // 4), (X, CORE, OUTER, INNER)
    )
    groups, positions = (X, CORE), (OUTER, INNER)
    blocks = P(groups + positions, None, None)
    long_rows = P(groups, positions, None)
    in_specs = (
        (blocks, blocks, P(groups + positions, None), P(groups + positions, None))
        + (long_rows, long_rows, P(groups), P(groups), blocks, long_rows)
        + (P(),) * 14
    )
    out_specs = (blocks, long_rows, blocks, blocks, long_rows, long_rows) + (P(),) * 14
    return jax.shard_map(
        shards, mesh=fine, in_specs=in_specs, out_specs=out_specs, check_vma=False
    )
```

```python
import functools
import random
import jax
import jax.numpy as jnp
from jax import lax
from jax.experimental import pallas as pl
from jax.experimental.pallas import tpu as pltpu
from jax.sharding import Mesh, PartitionSpec as P

HEADS = 8
HEAD_DIM = 64
PAIR = 2 * HEAD_DIM
PAIRS = HEADS // 2
SCALE = HEAD_DIM**-0.5
FLOOR_SCORE = -1e30
EPSILON = 1e-05
KEY_BLOCK = 256
CHUNK = 512
F32 = jnp.float32
BF16 = jnp.bfloat16
CORE, X, INNER, OUTER = "core", "x", "inner", "outer"


def nn(left, right):
    return lax.dot_general(left, right, (((1,), (0,)), ((), ())), preferred_element_type=F32)


def nt(left, right):
    return lax.dot_general(left, right, (((1,), (1,)), ((), ())), preferred_element_type=F32)


def tn(left, right):
    return lax.dot_general(left, right, (((0,), (0,)), ((), ())), preferred_element_type=F32)


def two_heads(rows):
    lane = lax.broadcasted_iota(jnp.int32, rows.shape, 1)
    zero = jnp.zeros_like(rows)
    first = jnp.where(lane < HEAD_DIM, rows, zero)
    second = jnp.where(lane < HEAD_DIM, zero, rows)
    return jnp.concatenate([first, second], axis=0)


def diagonal(product):
    half = product.shape[1] // 2
    return jnp.concatenate([product[:HEAD_DIM, :half], product[HEAD_DIM:, half:]], axis=0)


def delta_rows(grad_out, outputs):
    product = grad_out.astype(F32) * outputs.astype(F32)
    high = product.astype(BF16)
    low = (product - high.astype(F32)).astype(BF16)
    width = product.shape[1]
    head = lax.broadcasted_iota(jnp.int32, (HEADS, width), 0)
    lane = lax.broadcasted_iota(jnp.int32, (HEADS, width), 1)
    pick = jnp.where(lax.div(lane, HEAD_DIM) == head, 1.0, 0.0).astype(BF16)
    return nt(pick, high) + nt(pick, low)


def pair_row(rows, pair):
    return jnp.concatenate([rows[2 * pair : 2 * pair + 1], rows[2 * pair + 1 : 2 * pair + 2]], axis=1)


def pair_lanes(pair):
    return slice(pair * PAIR, (pair + 1) * PAIR)


def norm(residual, gain, bias):
    centred = residual - jnp.mean(residual, axis=1, keepdims=True)
    inverse = lax.rsqrt(jnp.mean(centred * centred, axis=1, keepdims=True) + EPSILON)
    normed = centred * inverse
    return normed * gain + bias, normed, inverse


def norm_back(upstream, normed, inverse, gain):
    normed = normed.astype(F32)
    scaled = upstream * gain
    grad = inverse * (
        scaled
        - jnp.mean(scaled, axis=1, keepdims=True)
        - normed * jnp.mean(scaled * normed, axis=1, keepdims=True)
    )
    return (
        grad,
        jnp.sum(upstream * normed, axis=0, keepdims=True),
        jnp.sum(upstream, axis=0, keepdims=True),
    )


def chunks(ref, axis, step):
    def body(index, carry):
        step(pl.ds(pl.multiple_of(index * CHUNK, CHUNK), CHUNK))
        return carry

    lax.fori_loop(0, ref.shape[axis] // CHUNK, body, 0)


def feed_forward_in_loop(rows, up_ref, down_ref, act_ref, gate_ref, low_ref, total_ref):
    low_ref[...] = rows.astype(BF16)
    total_ref[...] = rows

    def step(part):
        hidden = nn(low_ref[...], up_ref[:, part])
        sigmoid = 0.5 * jnp.tanh(0.5 * hidden) + 0.5
        active = hidden * sigmoid
        gate_ref[:, part] = (sigmoid + active * (1.0 - sigmoid)).astype(BF16)
        active = active.astype(BF16)
        act_ref[:, part] = active
        total_ref[...] += nn(active, down_ref[part, :])

    chunks(up_ref, 1, step)
    return total_ref[...]


def feed_forward(rows, up_ref, down_ref, act_ref, gate_ref):
    low = rows.astype(BF16)
    total = rows
    for start in range(0, up_ref.shape[1], CHUNK):
        part = slice(start, start + CHUNK)
        hidden = nn(low, up_ref[:, part])
        sigmoid = 0.5 * jnp.tanh(0.5 * hidden) + 0.5
        active = hidden * sigmoid
        gate_ref[:, part] = (sigmoid + active * (1.0 - sigmoid)).astype(BF16)
        active = active.astype(BF16)
        act_ref[:, part] = active
        total = total + nn(active, down_ref[part, :])
    return low, total


def feed_back(grad, gate_ref, up_ref, down_ref, hidden_grad_ref):
    low = grad.astype(BF16)
    total = grad
    for start in range(0, up_ref.shape[1], CHUNK):
        part = slice(start, start + CHUNK)
        hidden = nt(low, down_ref[part, :]) * gate_ref[:, part].astype(F32)
        hidden = hidden.astype(BF16)
        hidden_grad_ref[:, part] = hidden
        total = total + nt(hidden, up_ref[:, part])
    return low, total


def short_allowed(key_segment, query_segment, causal):
    allowed = key_segment == query_segment
    if causal:
        key = lax.broadcasted_iota(jnp.int32, key_segment.shape, 0)
        query = lax.broadcasted_iota(jnp.int32, key_segment.shape, 1)
        allowed = allowed & (key <= query)
    return jnp.concatenate([allowed, allowed], axis=1)


def short_attend(causal, q_ref, k_ref, v_ref, kseg_ref, qseg_ref, o_ref, lse_ref):
    size = kseg_ref.shape[1]
    for block in range(kseg_ref.shape[0]):
        rows = slice(block * size, (block + 1) * size)
        allowed = short_allowed(kseg_ref[block], qseg_ref[block], causal)
        logs = []
        for pair in range(PAIRS):
            lanes = pair_lanes(pair)
            scores = nt(k_ref[rows, lanes], two_heads(q_ref[rows, lanes]))
            scores = jnp.where(allowed, scores, FLOOR_SCORE)
            top = jnp.max(scores, axis=0, keepdims=True)
            weights = jnp.exp(scores - top)
            total = jnp.sum(weights, axis=0, keepdims=True)
            mixed = nn(v_ref[rows, lanes].T, weights.astype(BF16)) / total
            o_ref[rows, lanes] = diagonal(mixed).T.astype(BF16)
            log_total = top + jnp.log(total)
            logs += [log_total[:, :size], log_total[:, size:]]
        lse_ref[block] = jnp.concatenate(logs, axis=0)


def short_attend_back(
    causal, q_ref, k_ref, v_ref, kseg_ref, qseg_ref, o_ref, lse_ref, go_ref, dq_ref, dk_ref, dv_ref
):
    size = kseg_ref.shape[1]
    for block in range(kseg_ref.shape[0]):
        rows = slice(block * size, (block + 1) * size)
        allowed = short_allowed(kseg_ref[block], qseg_ref[block], causal)
        delta = delta_rows(go_ref[rows, :], o_ref[rows, :])
        lse = lse_ref[block]
        for pair in range(PAIRS):
            lanes = pair_lanes(pair)
            queries, grads = two_heads(q_ref[rows, lanes]), two_heads(go_ref[rows, lanes])
            scores = nt(k_ref[rows, lanes], queries)
            weights = jnp.where(allowed, jnp.exp(scores - pair_row(lse, pair)), 0.0)
            grad_weights = nt(v_ref[rows, lanes], grads)
            grad_scores = (weights * (grad_weights - pair_row(delta, pair))).astype(BF16)
            dv_ref[rows, lanes] = nn(weights.astype(BF16), grads).astype(BF16)
            dk_ref[rows, lanes] = nn(grad_scores, queries).astype(BF16)
            turned = diagonal(nn(k_ref[rows, lanes].T, grad_scores)).T
            dq_ref[rows, lanes] = (turned.astype(BF16).astype(F32) * SCALE).astype(BF16)


def load_keys(ref, pair_index, block, lanes):
    pieces = KEY_BLOCK // ref.shape[2]
    rows = ref[pl.ds(block * pieces, pieces), pair_index, :, lanes]
    return rows.reshape(KEY_BLOCK, rows.shape[2])


def store_keys(ref, pair_index, block, lanes, rows):
    pieces = KEY_BLOCK // ref.shape[2]
    ref[pl.ds(block * pieces, pieces), pair_index, :, lanes] = rows.astype(BF16).reshape(
        pieces, ref.shape[2], rows.shape[1]
    )


def store_part(refs, info_ref, pair_index, block, rows):
    partners, (_, pairs, size, _) = len(refs), refs[0].shape
    if partners == 2 and KEY_BLOCK == 2 * size:
        outer = block ^ info_ref[pairs + 3]
        swap = info_ref[pairs + 1] == 1
        first, second = rows[:size], rows[size:]
        refs[0][outer, pair_index] = jnp.where(swap, second, first)
        refs[1][outer, pair_index] = jnp.where(swap, first, second)
        return
    for piece in range(KEY_BLOCK // size):
        place = block * (KEY_BLOCK // size) + piece
        inner = lax.rem(place, partners) ^ info_ref[pairs + 1]
        outer = lax.div(place, partners) ^ info_ref[pairs + 3]
        part = rows[piece * size : (piece + 1) * size]
        for partner, ref in enumerate(refs):

            @pl.when(inner == partner)
            def _(ref=ref):
                ref[outer, pair_index] = part


def long_limit(info_ref, causal, pair_index, size, pairs):
    length = info_ref[pair_index]
    limit = length
    if causal:
        limit = jnp.minimum(length, info_ref[pairs] + size)
    return length, lax.div(limit + KEY_BLOCK - 1, KEY_BLOCK)


def long_allowed(start, causal, length, block, shape):
    key = lax.broadcasted_iota(jnp.int32, shape, 0) + block * KEY_BLOCK
    allowed = key < length
    if causal:
        half = shape[1] // 2
        lane = lax.broadcasted_iota(jnp.int32, shape, 1)
        query = jnp.where(lane < half, lane, lane - half) + start
        allowed = allowed & (key <= query)
    return allowed


def long_attend(
    causal, info_ref, q_ref, x_ref, k_w, v_w, k_ref, v_ref, o_ref, lse_ref, score_ref, sum_ref, mix_ref
):
    places, pairs, size, width = x_ref.shape
    shape = (KEY_BLOCK, 2 * size)
    everything = slice(None)

    def one(pair_index, carry):
        length, count = long_limit(info_ref, causal, pair_index, size, pairs)
        own = pl.ds(pl.multiple_of(pair_index * size, size), size)

        def first(block, tops):
            rows = pl.ds(pl.multiple_of(block * KEY_BLOCK, KEY_BLOCK), KEY_BLOCK)
            allowed = long_allowed(info_ref[pairs], causal, length, block, shape)
            context = load_keys(x_ref, pair_index, block, everything)
            store_keys(k_ref, pair_index, block, everything, nn(context, k_w[...]))
            store_keys(v_ref, pair_index, block, everything, nn(context, v_w[...]))
            after = []
            for pair in range(PAIRS):
                lanes = pair_lanes(pair)
                keys = load_keys(k_ref, pair_index, block, lanes)
                scores = nt(keys, two_heads(q_ref[own, lanes]))
                scores = jnp.where(allowed, scores, FLOOR_SCORE)
                score_ref[pair, rows] = scores
                folded = jnp.max(scores.reshape(KEY_BLOCK // 8, 8, 2 * size), axis=0)
                after.append(jnp.maximum(tops[pair], folded))
            return tuple(after)

        start = tuple(jnp.full((8, 2 * size), FLOOR_SCORE, F32) for _ in range(PAIRS))
        tops = lax.fori_loop(0, count, first, start)
        tops = [jnp.max(top, axis=0, keepdims=True) for top in tops]
        sum_ref[...] = jnp.zeros_like(sum_ref)
        mix_ref[...] = jnp.zeros_like(mix_ref)

        def second(block, carry):
            rows = pl.ds(pl.multiple_of(block * KEY_BLOCK, KEY_BLOCK), KEY_BLOCK)
            for pair in range(PAIRS):
                weights = jnp.exp(score_ref[pair, rows] - tops[pair])
                sum_ref[pair] += jnp.sum(weights.reshape(KEY_BLOCK // 8, 8, 2 * size), axis=0)
                values = load_keys(v_ref, pair_index, block, pair_lanes(pair))
                mix_ref[pair] += nn(values.T, weights.astype(BF16))
            return carry

        lax.fori_loop(0, count, second, 0)
        logs = []
        for pair in range(PAIRS):
            total = jnp.sum(sum_ref[pair], axis=0, keepdims=True)
            mixed = mix_ref[pair] / total
            o_ref[own, pair_lanes(pair)] = diagonal(mixed).T.astype(BF16)
            log_total = tops[pair] + jnp.log(total)
            logs += [log_total[:, :size], log_total[:, size:]]
        lse_ref[pair_index] = jnp.concatenate(logs, axis=0)
        return carry

    lax.fori_loop(0, pairs, one, 0)


def long_attend_back(
    causal,
    info_ref,
    q_ref,
    k_ref,
    v_ref,
    o_ref,
    lse_ref,
    go_ref,
    k_w,
    v_w,
    dq_ref,
    dk_ref,
    dv_ref,
    part_ref,
    mix_ref,
):
    places, pairs, size, width = k_ref.shape
    shape = (KEY_BLOCK, 2 * size)
    everything = slice(None)

    def one(pair_index, carry):
        length, count = long_limit(info_ref, causal, pair_index, size, pairs)
        own = pl.ds(pl.multiple_of(pair_index * size, size), size)
        delta = delta_rows(go_ref[own, :], o_ref[own, :])
        lse = lse_ref[pair_index]
        mix_ref[...] = jnp.zeros_like(mix_ref)

        def step(block, carry):
            allowed = long_allowed(info_ref[pairs], causal, length, block, shape)
            for pair in range(PAIRS):
                lanes = pair_lanes(pair)
                queries, grads = two_heads(q_ref[own, lanes]), two_heads(go_ref[own, lanes])
                keys = load_keys(k_ref, pair_index, block, lanes)
                scores = nt(keys, queries)
                weights = jnp.where(allowed, jnp.exp(scores - pair_row(lse, pair)), 0.0)
                grad_weights = nt(load_keys(v_ref, pair_index, block, lanes), grads)
                grad_scores = (weights * (grad_weights - pair_row(delta, pair))).astype(BF16)
                store_keys(dv_ref, pair_index, block, lanes, nn(weights.astype(BF16), grads))
                store_keys(dk_ref, pair_index, block, lanes, nn(grad_scores, queries))
                mix_ref[pair] += nn(keys.T, grad_scores)
            part = nt(load_keys(dk_ref, pair_index, block, everything), k_w[...])
            part = part + nt(load_keys(dv_ref, pair_index, block, everything), v_w[...])
            store_part(part_ref, info_ref, pair_index, block, part.astype(BF16))
            return carry

        lax.fori_loop(0, count, step, 0)

        def clear(block, carry):
            nothing = jnp.zeros((KEY_BLOCK, width), BF16)
            store_keys(dk_ref, pair_index, block, everything, nothing)
            store_keys(dv_ref, pair_index, block, everything, nothing)
            store_part(part_ref, info_ref, pair_index, block, nothing)
            return carry

        lax.fori_loop(count, places * size // KEY_BLOCK, clear, 0)
        for pair in range(PAIRS):
            turned = diagonal(mix_ref[pair]).T
            dq_ref[own, pair_lanes(pair)] = (turned.astype(BF16).astype(F32) * SCALE).astype(BF16)
        return carry

    lax.fori_loop(0, pairs, one, 0)


class Refs(dict):
    def __init__(self, *args):
        super().__init__(*args)
        self.coming, self.leaving, self.pieced = {}, {}, {}

    def __getattr__(self, name):
        if name in self.coming:
            self.coming.pop(name).wait()
        return self[name]

    def leave_piece(self, name, piece):
        source, target, signals, first = self.pieced[name]
        pltpu.make_async_copy(source.at[piece], target.at[piece], signals.at[first + piece]).start()

    def leave(self, *names):
        for name in names:
            self["left"].add(name)
            for copy in self.leaving.get(name, ()):
                copy.start()


def copied(shape, dtype):
    size = dtype.itemsize
    for length in shape:
        size *= length
    return shape[-1] % 128 == 0 and size >= 2**16


def launch(body, arrays, gives, scratch=(), info=None, after=(), pieces=(), moved=None, cost=10):
    memory = pl.BlockSpec(memory_space=pltpu.VMEM)
    far = pl.BlockSpec(memory_space=pl.ANY)
    ins, specs = [], []
    if info is not None:
        ins.append(info)
        specs.append(pl.BlockSpec(memory_space=pltpu.SMEM))
    by_itself = lambda name, shape, dtype: (
        copied(shape, jnp.dtype(dtype)) if moved is None else name in moved
    )
    moved_in = [name for name, a in arrays.items() if by_itself(name, a.shape, a.dtype)]
    moved_out = [name for name, give in gives.items() if name in pieces or by_itself(name, *give)]
    for name, array in arrays.items():
        ins.append(array)
        specs.append(far if name in moved_in else memory)
    for array in after:
        ins.append(array)
        specs.append(far)
    count_out = sum(gives[name][0][0] if name in pieces else 1 for name in moved_out)
    rooms = [pltpu.VMEM(arrays[name].shape, arrays[name].dtype) for name in moved_in]
    rooms += [pltpu.VMEM(*gives[name]) for name in moved_out]
    rooms += [pltpu.SemaphoreType.DMA((max(len(moved_in), 1),))]
    rooms += [pltpu.SemaphoreType.DMA((max(count_out, 1),))]
    names = [name for name, _ in scratch]

    def run(*refs):
        refs = list(refs)
        r = Refs()
        if info is not None:
            r["info"] = refs.pop(0)
        outer = {name: refs.pop(0) for name in arrays}
        del refs[: len(after)]
        outer.update((name, refs.pop(0)) for name in gives)
        room = {name: refs.pop(0) for name in moved_in + moved_out}
        come, go = refs.pop(0), refs.pop(0)
        r.update(outer)
        r.update(room)
        r.update(zip(names, refs))
        for place, name in enumerate(moved_in):
            copy = pltpu.make_async_copy(outer[name], room[name], come.at[place])
            copy.start()
            r.coming[name] = copy
        place = 0
        for name in moved_out:
            copies = []
            if name in pieces:
                r.pieced[name] = (room[name], outer[name], go, place)
                for piece in range(gives[name][0][0]):
                    source, target = room[name].at[piece], outer[name].at[piece]
                    copies.append(pltpu.make_async_copy(source, target, go.at[place]))
                    place += 1
            else:
                copies.append(pltpu.make_async_copy(room[name], outer[name], go.at[place]))
                place += 1
            r.leaving[name] = copies
        left = set()
        r["left"] = left
        body(r)
        for name in list(r.coming):
            r.coming.pop(name).wait()
        for name in moved_out:
            if name not in left and name not in pieces:
                r.leave(name)
        for name in moved_out:
            for copy in r.leaving[name]:
                copy.wait()

    out = pl.pallas_call(
        run,
        in_specs=specs,
        out_specs=[far if name in moved_out else memory for name in gives],
        out_shape=[jax.ShapeDtypeStruct(shape, dtype) for shape, dtype in gives.values()],
        scratch_shapes=rooms + [shape for _, shape in scratch],
        compiler_params=pltpu.CompilerParams(vmem_limit_bytes=VMEM_LIMIT),
        cost_estimate=pl.CostEstimate(
            flops=int(cost * 1.1e9), bytes_accessed=int(cost * 3.5e6), transcendentals=0
        ),
    )(*ins)
    return Refs(zip(gives, out))


VMEM_LIMIT = 56 * 2**20


def add_sums(ref, rows):
    ref[...] = jnp.concatenate(rows, axis=0)


def encoder_tail(r, o_ref):
    residual = r.x[...].astype(F32) + nn(o_ref[...], r.w_o[...])
    first, normed, inverse = norm(residual, r.gain[0:1], r.bias[0:1])
    r.n1[...] = normed.astype(BF16)
    r.i1[...] = inverse
    if "acc" in r:
        total = feed_forward_in_loop(first, r.up, r.down, r.act, r.gate, r.y, r.acc)
    else:
        r.y[...], total = feed_forward(first, r.up, r.down, r.act, r.gate)
    r.leave("n1", "act", "gate", "y")
    encoded, normed, inverse = norm(total, r.gain[1:2], r.bias[1:2])
    r.n2[...] = normed.astype(BF16)
    r.i2[...] = inverse
    r.enc[...] = encoded.astype(BF16)


def project_short(r, name, rows, w_q, w_k, w_v, context=None):
    context = rows if context is None else context
    r["q" + name][...] = (nn(rows, w_q) * SCALE).astype(BF16)
    r["k" + name][...] = nn(context, w_k).astype(BF16)
    r["v" + name][...] = nn(context, w_v).astype(BF16)


def short_encoder_forward(r):
    project_short(r, "", r.x[...], r.w_in[0], r.w_in[1], r.w_in[2])
    r.leave("q", "k", "v")
    short_attend(False, r.q, r.k, r.v, r.kseg, r.qseg, r.o, r.lse)
    r.leave("o")
    encoder_tail(r, r.o)


def decoder_middle(r, o_ref):
    residual = r.t[...].astype(F32) + nn(o_ref[...], r.w_o[...])
    upper, normed, inverse = norm(residual, r.gain[0:1], r.bias[0:1])
    r.n3[...] = normed.astype(BF16)
    r.i3[...] = inverse
    r.u[...] = upper.astype(BF16)
    return upper


def decoder_tail(r, upper, o_ref):
    gain, bias = r.gain, r.bias
    residual = upper + nn(o_ref[...], r.w_co[...])
    middle, normed4, inverse4 = norm(residual, gain[1:2], bias[1:2])
    r.m[...], total = feed_forward(middle, r.up, r.down, r.act, r.gate)
    r.leave("m", "act", "gate")
    final, normed5, inverse5 = norm(total, gain[2:3], bias[2:3])
    r.final[...] = final
    r.leave("final")
    grad, gain5, bias5 = norm_back(r.cot[...].astype(F32), normed5, inverse5, gain[2:3])
    r.b5[...], grad = feed_back(grad, r.gate, r.up, r.down, r.dh)
    r.leave("b5", "dh")
    grad, gain4, bias4 = norm_back(grad, normed4, inverse4, gain[1:2])
    low = grad.astype(BF16)
    r.b4[...] = low
    r.d4[...] = grad
    r.go_c[...] = nt(low, r.w_co[...]).astype(BF16)
    add_sums(r.small, [gain4, gain5, bias4, bias5])


def short_decoder_forward(r):
    project_short(r, "", r.t[...], r.w_in[0], r.w_in[1], r.w_in[2])
    r.leave("q", "k", "v")
    short_attend(True, r.q, r.k, r.v, r.tkseg, r.tqseg, r.o, r.lse)
    r.leave("o")
    r.upper[...] = decoder_middle(r, r.o)


def short_cross_forward(r):
    project_short(r, "_c", r.u[...], r.w_cin[0], r.w_cin[1], r.w_cin[2], r.enc[...])
    r.leave("q_c", "k_c", "v_c")
    short_attend(False, r.q_c, r.k_c, r.v_c, r.kseg, r.tqseg, r.o_c, r.lse_c)
    r.leave("o_c")
    decoder_tail(r, r.upper[...], r.o_c)


def decoder_middle_back(r):
    grad = r.d4[...] + nt(r.dq_c[...], r.w_cin[0])
    grad, gain3, bias3 = norm_back(grad, r.n3[...], r.i3[...], r.gain[0:1])
    low = grad.astype(BF16)
    r.b3[...] = low
    r.go[...] = nt(low, r.w_o[...]).astype(BF16)
    add_sums(r.small, [gain3, bias3])
    return grad


def short_decoder_back(r):
    short_attend_back(
        False, r.q_c, r.k_c, r.v_c, r.kseg, r.tqseg, r.o_c, r.lse_c, r.go_c, r.dq_c, r.dk_c, r.dv_c
    )
    r.denc[...] = nt(r.dk_c[...], r.w_cin[1]) + nt(r.dv_c[...], r.w_cin[2])
    r.leave("dq_c", "dk_c", "dv_c", "denc")
    r.d3[...] = decoder_middle_back(r)
    short_attend_back(
        True, r.q, r.k, r.v, r.tkseg, r.tqseg, r.o, r.lse, r.go, r.dq, r.dk, r.dv
    )
    r.leave("dq", "dk", "dv")
    grad = r.d3[...] + nt(r.dq[...], r.w_in[0])
    r.dt[...] = grad + nt(r.dk[...], r.w_in[1]) + nt(r.dv[...], r.w_in[2])


def encoder_tail_back(r, grad):
    grad, gain2, bias2 = norm_back(grad, r.n2[...], r.i2[...], r.gain[1:2])
    r.b2[...], grad = feed_back(grad, r.gate, r.up, r.down, r.dh)
    r.leave("b2", "dh")
    grad, gain1, bias1 = norm_back(grad, r.n1[...], r.i1[...], r.gain[0:1])
    low = grad.astype(BF16)
    r.b1[...] = low
    r.go[...] = nt(low, r.w_o[...]).astype(BF16)
    r.d1[...] = grad
    add_sums(r.small, [gain1, gain2, bias1, bias2])


def short_encoder_back(r):
    encoder_tail_back(r, r.denc[...])
    short_attend_back(
        False, r.q, r.k, r.v, r.kseg, r.qseg, r.o, r.lse, r.go, r.dq, r.dk, r.dv
    )
    r.leave("dq", "dk", "dv")
    grad = r.d1[...] + nt(r.dq[...], r.w_in[0])
    r.dx[...] = grad + nt(r.dk[...], r.w_in[1]) + nt(r.dv[...], r.w_in[2])


def long_encoder_forward(r):
    r.q[...] = (nn(r.x[...], r.w_in[0]) * SCALE).astype(BF16)
    long_attend(
        False, r.info, r.q, r.xg, r.w_in.at[1], r.w_in.at[2], r.k, r.v, r.o, r.lse, r.s, r.a, r.mix
    )
    r.leave("q", "k", "v", "o")
    encoder_tail(r, r.o)


def long_self_forward(r):
    r.q[...] = (nn(r.t[...], r.w_in[0]) * SCALE).astype(BF16)
    long_attend(
        True, r.info, r.q, r.tg, r.w_in.at[1], r.w_in.at[2], r.k, r.v, r.o, r.lse, r.s, r.a, r.mix
    )
    r.leave("q", "k", "v", "o")
    upper = decoder_middle(r, r.o)
    r.upper[...] = upper
    r.q_c[...] = (nn(upper.astype(BF16), r.w_cin[0]) * SCALE).astype(BF16)


def long_cross(r):
    k_w, v_w = r.w_cin.at[1], r.w_cin.at[2]
    long_attend(
        False, r.info, r.q_c, r.eg, k_w, v_w, r.k_c, r.v_c, r.o_c, r.lse_c, r.s, r.a, r.mix
    )
    r.leave("k_c", "v_c", "o_c")
    decoder_tail(r, r.upper[...], r.o_c)


def part_refs(r):
    return [r[name] for name in r if name[0] == "p" and name[1:].isdigit()]


def long_cross_back(r):
    long_attend_back(
        False,
        r.info,
        r.q_c,
        r.k_c,
        r.v_c,
        r.o_c,
        r.lse_c,
        r.go_c,
        r.w_cin.at[1],
        r.w_cin.at[2],
        r.dq_c,
        r.dk_c,
        r.dv_c,
        part_refs(r),
        r.mix,
    )


def long_self_back(r):
    grad = decoder_middle_back(r)
    long_attend_back(
        True,
        r.info,
        r.q,
        r.k,
        r.v,
        r.o,
        r.lse,
        r.go,
        r.w_in.at[1],
        r.w_in.at[2],
        r.dq,
        r.dk,
        r.dv,
        part_refs(r),
        r.mix,
    )
    r.dt[...] = grad + nt(r.dq[...], r.w_in[0])


def long_encoder_tail_back(r):
    grad = r.part0[...].astype(F32) + r.part1[...].astype(F32)
    grad = grad + r.part2[...].astype(F32) + r.part3[...].astype(F32)
    encoder_tail_back(r, grad)


def long_encoder_back(r):
    long_attend_back(
        False,
        r.info,
        r.q,
        r.k,
        r.v,
        r.o,
        r.lse,
        r.go,
        r.w_in.at[1],
        r.w_in.at[2],
        r.dq,
        r.dk,
        r.dv,
        part_refs(r),
        r.mix,
    )
    r.dx[...] = r.d1[...] + nt(r.dq[...], r.w_in[0])


SIDE = 512


class Weights:
    def __init__(self, pairs, base=None):
        self.arrays, self.plan, known = {}, [], {}

        def place(rows):
            if isinstance(rows, tuple):
                return rows
            if id(rows) not in known:
                known[id(rows)] = "w%d" % len(known)
                self.arrays[known[id(rows)]] = rows
            return known[id(rows)], rows.shape[-1]

        self.count = 0
        for terms in pairs:
            terms = [(place(a), place(b)) for a, b in terms]
            (_, height), (_, width) = terms[0]
            self.plan.append((self.count, width // SIDE, [(a[0], b[0]) for a, b in terms]))
            self.count += height // SIDE * (width // SIDE)
        self.gives = {name: ((self.count, SIDE // 2, SIDE), BF16) for name in ("kept", "sent")}
        if base is not None:
            self.arrays["base"] = base

    def each(self, r, step):
        ends = [first for first, _, _ in self.plan[1:]] + [self.count]
        for (first, across, terms), end in zip(self.plan, ends):
            terms = [(getattr(r, a), getattr(r, b)) for a, b in terms]

            def body(tile, carry, first=first, across=across, terms=terms):
                row = pl.multiple_of(lax.div(tile - first, across) * SIDE, SIDE)
                column = pl.multiple_of(lax.rem(tile - first, across) * SIDE, SIDE)
                step(tile, row, column, terms)
                return carry

            lax.fori_loop(first, end, body, 0)

    def body(self, r, core):
        half = SIDE // 2
        if "base" in self.arrays:
            r.base

        def step(tile, row, column, terms):
            for flip, name in enumerate(("kept", "sent")):
                inside = pl.multiple_of((core ^ flip) * half, half)
                total = None
                if "base" in self.arrays:
                    total = r["base"][tile, pl.ds(inside, half), :].astype(F32)
                for left, right in terms:
                    rows = pl.ds(pl.multiple_of(row + inside, half), half)
                    across = pl.ds(column, SIDE)
                    if len(left.shape) == 4:
                        tall = left.shape[0] * left.shape[1] * left.shape[2]
                        first = left[:, :, :, rows].reshape(tall, half)
                    else:
                        first = left[:, rows]
                    if len(right.shape) == 4:
                        tall = right.shape[0] * right.shape[1] * right.shape[2]
                        product = tn(first, right[:, :, :, across].reshape(tall, SIDE))
                    else:
                        product = tn(first, right[:, across])
                    total = product if total is None else total + product
                r[name][tile] = total.astype(BF16)
                r.leave_piece(name, tile)

        self.each(r, step)


class Tagged:
    def __init__(self, r, tag):
        self.r, self.tag = r, tag

    def __getattr__(self, name):
        return getattr(self.r, name + self.tag)


def whole_tiles(chunks, after=(), cost=10):
    weights = [Weights([[pair] for pair in chunk]) for chunk in chunks]
    arrays, gives = {}, {}
    for number, part in enumerate(weights):
        gives["c%d" % number] = ((part.count, SIDE, SIDE), BF16)
        arrays.update((name + "c%d" % number, array) for name, array in part.arrays.items())

    def body(r):
        for number, part in enumerate(weights):
            tag = "c%d" % number

            def step(tile, row, column, terms, tag=tag):
                ((left, right),) = terms
                product = tn(left[:, pl.ds(row, SIDE)], right[:, pl.ds(column, SIDE)])
                r[tag][tile] = product.astype(BF16)
                r.leave_piece(tag, tile)

            part.each(Tagged(r, tag), step)

    out = launch(body, arrays, gives, after=after, pieces=tuple(gives), cost=cost)
    return list(out.values())


def weight_tiles(pairs, core_info, after=(), cost=10, base=None):
    weights = Weights(pairs, base)
    out = launch(
        lambda r: weights.body(r, r.info[0]),
        weights.arrays,
        weights.gives,
        info=core_info,
        after=after,
        pieces=("kept", "sent"),
        cost=cost,
    )
    return [out.kept, out.sent]


def send(piece, axis, offset):
    count = lax.axis_size(axis)
    return lax.ppermute(piece, axis, [(i, i ^ offset) for i in range(count)])


def ordered(pieces, place, dim):
    if len(pieces) == 1:
        return pieces[0]
    level = len(pieces) // 2
    inside = lax.rem(place, level)
    low = ordered(pieces[:level], inside, dim)
    high = ordered(pieces[level:], inside, dim)
    return jnp.where(
        place >= level, jnp.concatenate([high, low], dim), jnp.concatenate([low, high], dim)
    )


def hold(value, token):
    return lax.optimization_barrier((value, token))[0]


def gather_first(piece, axis):
    return [piece] + [send(piece, axis, k) for k in range(1, lax.axis_size(axis))]


def gather_last(pieces, axis, dim, token=None):
    if token is not None:
        pieces = hold(pieces, token)
    return ordered(pieces, lax.axis_index(axis), dim)


def added(pieces):
    total = pieces[0].astype(F32)
    for piece in pieces[1:]:
        total = total + piece.astype(F32)
    return total.astype(BF16)


def scatter_step(pending, axis, dim, token=None):
    if token is not None:
        pending = hold(pending, token)
    place, count = lax.axis_index(axis), lax.axis_size(axis)
    size = pending[0].shape[dim] // count
    after = []
    for k in range(count):
        parts = [
            lax.dynamic_slice_in_dim(piece, (place ^ k) * size, size, dim) for piece in pending
        ]
        block = added(parts)
        after.append(send(block, axis, k) if k else block)
    return after


def gather_step(piece, axis, dim):
    return gather_last(gather_first(piece, axis), axis, dim)


def gather_early(rows):
    return lax.all_gather(rows, (OUTER, INNER), axis=0, tiled=False)


SEQ = (OUTER, INNER)


class Chain:
    def __init__(self, halves, order, small=None, doubled=False):
        self.order = (CORE,) + order
        self.doubled = doubled
        self.stage = 0
        self.tiles = halves[0].shape[0]
        self.small, self.carried = None, 0
        if small is not None:
            self.carried = small.shape[0]
            halves = [jnp.concatenate([self.flat(half), small]) for half in halves]
        self.held = [halves[0], send(halves[1], CORE, 1)]

    def flat(self, block):
        return block.reshape(-1, block.shape[-1])

    def parts(self):
        if not self.carried:
            return self.held, None
        body = [piece[: -self.carried] for piece in self.held]
        body = [piece.reshape(self.tiles, -1, piece.shape[-1]) for piece in body]
        return body, added([piece[-self.carried :] for piece in self.held])

    def next_axis(self):
        stage, count = self.stage + 1, len(self.order)
        return self.order[stage] if stage < count else self.order[2 * count - 1 - stage]

    def over(self):
        return self.stage == 2 * len(self.order) - 1

    def go(self):
        axis = self.next_axis()
        self.stage += 1
        count = len(self.order)
        if self.doubled and self.stage in (count - 1, count):
            total = added(self.held)
            self.held = [total, send(total, OUTER, self.stage - count + 2)]
            return
        if self.doubled and self.stage == count + 1:
            pending, self.small = self.parts()
            self.held = gather_first(added(pending), axis)
            return
        if self.stage < count:
            pending, small = self.parts()
            place, members = lax.axis_index(axis), lax.axis_size(axis)
            size = pending[0].shape[1] // members
            self.held = []
            for k in range(members):
                begin = (place ^ k) * size
                block = added([lax.dynamic_slice_in_dim(p, begin, size, 1) for p in pending])
                if small is not None:
                    block = jnp.concatenate([self.flat(block), small])
                self.held.append(send(block, axis, k) if k else block)
            return
        if self.stage == count:
            pending, self.small = self.parts()
            piece = added(pending)
        else:
            piece = gather_last(self.held, self.order[2 * count - self.stage], 1)
        self.held = gather_first(piece, axis)

    def volume(self):
        return self.held[0].size * 2 / 2**20


class Spread:
    def __init__(self, part, straight):
        self.straight, self.stage = straight, 0
        self.held = [send(rows, INNER, k) if k else rows for k, rows in enumerate(part)]

    def next_axis(self):
        return OUTER

    def over(self):
        return self.stage == (1 if self.straight else 2)

    def go(self):
        self.stage += 1
        if self.straight:
            blocks = [added([piece[k] for piece in self.held]) for k in range(4)]
            self.held = [send(block, OUTER, k) if k else block for k, block in enumerate(blocks)]
            return
        if self.stage == 1:
            pick, offset = (lambda piece, odd: jnp.stack([piece[odd], piece[2 + odd]])), 1
        else:
            pick, offset = (lambda piece, odd: piece[odd]), 2
        mine, theirs = [added([pick(piece, odd) for piece in self.held]) for odd in (0, 1)]
        self.held = [mine, send(theirs, OUTER, offset)]

    def volume(self):
        return self.held[0].size * 2 / 2**20

    def result(self):
        return added(self.held)


def finish(chains, *tokens):
    held, _ = lax.optimization_barrier(([chain.held for chain in chains], tokens))
    for chain, pieces in zip(chains, held):
        chain.held = pieces


def go(*chains):
    for chain in chains:
        chain.go()


FLOW = {CORE: 3.5, X: 21.0, INNER: 21.0, OUTER: 84.0}


def plan_of(chain):
    if isinstance(chain, Spread):
        return [(INNER, 21.0, 1), (OUTER, 10.5, 1), (OUTER, 10.5, 1)][chain.stage :]
    size, out = chain.tiles * 0.5, []
    for axis in chain.order:
        count = lax.axis_size(axis)
        if axis == OUTER and chain.doubled:
            out += [(OUTER, 21.0 * size, 1), (OUTER, 42.0 * size, 1)]
            continue
        size = size / count
        out.append((axis, FLOW[axis] * size, count - 1))
    back = [entry for entry in reversed(out)]
    if chain.doubled:
        back = [entry for entry in back if entry[0] != OUTER]
    return (out + back)[chain.stage :]


def rehearse(plans, first, gate, weights, slack):
    free = dict.fromkeys(FLOW, 0.0)
    position, queue, order, clock, waiting = [0] * len(plans), [], [], 0.0, []

    def depart(index, when):
        axis, long, _ = plans[index][position[index]]
        begin = max(when, free[axis])
        free[axis] = begin + long
        queue.append((free[axis] + 6.0, index))

    def left(index):
        rest = plans[index][position[index] :]
        return weights[index] * sum(long + 10.0 for _, long, _ in rest)

    for index, since in first:
        depart(index, -since)
    while queue or waiting:
        soon = min(queue)[0] if queue else clock + 99.0
        if waiting and soon > clock + 4.0:
            clock += 6.5
            order.append((waiting.pop(0), True))
            continue
        near = [entry for entry in queue if entry[0] <= max(clock, soon) + slack]
        entry = max(near, key=lambda entry: left(entry[1]))
        queue.remove(entry)
        arrival, index = entry
        clock = max(clock, arrival)
        position[index] += 1
        order.append((index, False))
        if position[index] == len(plans[index]):
            clock += 1.0
            waiting.append(index)
            continue
        axis, long, sends = plans[index][position[index]]
        clock += 2.0 + 1.5 * sends + 0.03 * long
        depart(index, clock)
        if gate[1] == index and position[index] == 1:
            clock += 2.0
            depart(gate[0], clock)
    return clock, order


def run_out(flights, later):
    chains, ends = [chain for chain, _, _ in flights], [end for _, _, end in flights]
    plans = [plan_of(chain) for chain in chains]
    plans.append([(INNER, 21.0, 1), (OUTER, 10.5, 1), (OUTER, 10.5, 1)])
    first = [(index, since) for index, (_, since, _) in enumerate(flights)]
    rng, best = random.Random(7), None
    for trial in range(1500):
        weights = [1.0 if trial < 4 else rng.uniform(0.3, 2.0) for _ in plans]
        slack = (0.0, 2.0, 4.0, 8.0)[trial % 4]
        found = rehearse(plans, first, (len(chains), 0), weights, slack)
        if best is None or found[0] < best[0]:
            best = found
    token, results = (), {}
    for index, is_end in best[1]:
        chain = chains[index]
        if is_end:
            results[index] = ends[index](chain, token)
            token = (results[index][0],)
            continue
        finish([chain], *token)
        if chain.over():
            token = tuple(chain.held)
            continue
        chain.go()
        token = (chain.held[0],)
        if index == 0 and chain.stage == 1:
            chain, _, end = later(token)
            chains.append(chain)
            ends.append(end)
    return [results[index] for index in range(len(chains))]


def assemble(chain, core_info, shapes, after=()):
    tiles, half, side = chain.held[0].shape

    places = []
    for name, shape in shapes.items():
        blocks = shape[0] if len(shape) > 2 else shape[0] * shape[1] // (side * side)
        for block in range(blocks):
            if len(shape) > 2:
                places.append((name, lambda rows, b=block: (b, rows, slice(None))))
            elif shape[1] > shape[0]:
                lanes = slice(block * side, (block + 1) * side)
                places.append((name, lambda rows, l=lanes: (rows, l)))
            else:
                places.append((name, lambda rows, b=block: (pl.ds(rows.start + b * side, half), slice(None))))

    def body(info, mine, other, *refs):
        outs = dict(zip(shapes, refs))
        room, full, come, go = refs[len(shapes) :]
        starts = [pl.multiple_of((info[0] ^ flip) * half, half) for flip in (0, 1)]
        arrive, leave = [], []
        for tile in range(tiles):
            for flip, source in enumerate((mine, other)):
                index = 2 * tile + flip
                arrive.append(pltpu.make_async_copy(source.at[tile], room.at[index], come.at[index]))
                arrive[-1].start()
        for tile, (name, where) in enumerate(places):
            for flip in (0, 1):
                index = 2 * tile + flip
                arrive[index].wait()
                full[index] = room[index].astype(F32)
                target = outs[name].at[where(pl.ds(starts[flip], half))]
                leave.append(pltpu.make_async_copy(full.at[index], target, go.at[index]))
                leave[-1].start()
        for copy in leave:
            copy.wait()

    far = pl.BlockSpec(memory_space=pl.ANY)
    return pl.pallas_call(
        lambda info, mine, other, *refs: body(info, mine, other, *refs[len(after) :]),
        in_specs=[pl.BlockSpec(memory_space=pltpu.SMEM)] + [far] * (2 + len(after)),
        out_specs=[far] * len(shapes),
        out_shape=[jax.ShapeDtypeStruct(shape, F32) for shape in shapes.values()],
        scratch_shapes=[
            pltpu.VMEM((2 * tiles, half, side), BF16),
            pltpu.VMEM((2 * tiles, half, side), F32),
            pltpu.SemaphoreType.DMA((2 * tiles,)),
            pltpu.SemaphoreType.DMA((2 * tiles,)),
        ],
        compiler_params=pltpu.CompilerParams(vmem_limit_bytes=VMEM_LIMIT),
        cost_estimate=pl.CostEstimate(flops=5 * 10**9, bytes_accessed=2 * 10**7, transcendentals=0),
    )(core_info, chain.held[0], chain.held[1], *after)


def shards(
    source_short,
    target_short,
    source_segment,
    target_segment,
    source_long,
    target_long,
    source_length,
    target_length,
    cotangent_short,
    cotangent_long,
    encoder_project,
    encoder_output,
    encoder_up,
    encoder_down,
    encoder_gain,
    encoder_bias,
    decoder_project,
    decoder_output,
    cross_project,
    cross_output,
    decoder_up,
    decoder_down,
    decoder_gain,
    decoder_bias,
):
    blocks, size, width = source_short.shape
    hidden = encoder_up.shape[1]
    rows = blocks * size
    pairs, own, _ = source_long.shape
    rows_long = pairs * own
    flat = lambda a: a.reshape(-1, width)
    start = lax.axis_index((OUTER, INNER)) * own
    core = lax.axis_index(CORE)
    here = [start, lax.axis_index(INNER), core, lax.axis_index(OUTER)]
    here = jnp.stack(here).astype(jnp.int32)
    info_of = lambda lengths: jnp.concatenate([lengths, here])
    core_info = core.astype(jnp.int32)[None]
    source_info, target_info = info_of(source_length), info_of(target_length)

    spread = lambda s: jnp.broadcast_to(s[:, :, None], (blocks, size, size))
    line = lambda s: s[:, None, :]
    encoder_in = {
        "w_in": encoder_project,
        "w_o": encoder_output,
        "up": encoder_up,
        "down": encoder_down,
        "gain": encoder_gain,
        "bias": encoder_bias,
    }
    decoder_in = {
        "w_in": decoder_project,
        "w_o": decoder_output,
        "w_cin": cross_project,
        "w_co": cross_output,
        "up": decoder_up,
        "down": decoder_down,
        "gain": decoder_gain,
        "bias": decoder_bias,
    }

    def pick(table, names):
        return {name: table[name] for name in names}

    def rows_of(n, names):
        return {name: ((n, width), BF16) for name in names}

    def wide_of(n, names):
        return {name: ((n, hidden), BF16) for name in names}

    def floats(n, names):
        return {name: ((n, width), F32) for name in names}

    def column(n, names):
        return {name: ((n, 1), F32) for name in names}

    def logs(n, names):
        return {name: ((n, HEADS, size), F32) for name in names}

    def sums(n):
        return {"small": ((n, width), F32)}

    def keys_of(names):
        shape = (places, pairs, own, width)
        return {name: (shape, BF16) for name in names}

    def parts():
        inner = lax.axis_size(INNER)
        return {"p%d" % k: ((places // inner, pairs, own, width), BF16) for k in range(inner)}

    def saved(kernel, names):
        return {name: kernel[name] for name in names}

    whole_source = gather_early(source_long)
    early_target = gather_first(target_long[None, None], OUTER)
    places = lax.axis_size(OUTER) * lax.axis_size(INNER)
    keys = places * own
    work = [
        ("s", pltpu.VMEM((PAIRS, keys, 2 * own), F32)),
        ("a", pltpu.VMEM((PAIRS, 8, 2 * own), F32)),
        ("mix", pltpu.VMEM((PAIRS, PAIR, 2 * own), F32)),
    ]
    mix = work[2:]

    segments = {"kseg": spread(source_segment), "qseg": line(source_segment)}
    turned = {"tkseg": spread(target_segment), "tqseg": line(target_segment)}
    encoder_keeps = lambda n: {
        **rows_of(n, ("n1", "y", "n2", "enc")),
        **wide_of(n, ("act", "gate")),
        **column(n, ("i1", "i2")),
    }
    se = launch(
        short_encoder_forward,
        {"x": flat(source_short), **segments, **encoder_in},
        {**rows_of(rows, ("q", "k", "v", "o")), **logs(blocks, ("lse",)), **encoder_keeps(rows)},
        cost=0.01,
    )
    decoder_keeps = lambda n: {
        **rows_of(n, ("m", "b5", "b4", "go_c")),
        **wide_of(n, ("act", "gate", "dh")),
        **floats(n, ("final", "d4")),
        **sums(4),
    }
    sd = launch(
        short_decoder_forward,
        {
            "t": flat(target_short),
            **turned,
            **pick(decoder_in, ("w_in", "w_o", "gain", "bias")),
        },
        {
            **rows_of(rows, ("q", "k", "v", "o", "n3", "u")),
            **logs(blocks, ("lse",)),
            **column(rows, ("i3",)),
            **floats(rows, ("upper",)),
        },
        after=(se.lse,),
        cost=0.01,
    )
    sc = launch(
        short_cross_forward,
        {
            "u": sd.u,
            "upper": sd.upper,
            "enc": se.enc,
            "cot": flat(cotangent_short),
            "kseg": segments["kseg"],
            "tqseg": turned["tqseg"],
            **pick(decoder_in, ("w_cin", "w_co", "up", "down", "gain", "bias")),
        },
        {
            **rows_of(rows, ("q_c", "k_c", "v_c", "o_c")),
            **logs(blocks, ("lse_c",)),
            **decoder_keeps(rows),
        },
        after=(sd.lse,),
        cost=0.01,
    )

    sb = launch(
        short_decoder_back,
        {
            **saved(sd, ("q", "k", "v", "o", "lse", "n3", "i3")),
            **saved(sc, ("q_c", "k_c", "v_c", "o_c", "lse_c", "go_c", "d4")),
            "kseg": segments["kseg"],
            **turned,
            **pick(decoder_in, ("w_in", "w_o", "w_cin", "gain")),
        },
        {
            **rows_of(rows, ("dq_c", "dk_c", "dv_c", "dq", "dk", "dv", "b3", "go")),
            **floats(rows, ("denc", "dt")),
            **sums(2),
        },
        scratch=[("d3", pltpu.VMEM((rows, width), F32))],
        after=(sc.small,),
        cost=0.01,
    )

    early_target = gather_last(early_target, OUTER, 0, sb.small)

    whole_source = hold(whole_source, sb.small)
    x_long, t_long = flat(source_long), flat(target_long)
    le = launch(
        long_encoder_forward,
        {"x": x_long, "xg": whole_source, **encoder_in},
        {
            **rows_of(rows_long, ("q", "o")),
            **keys_of(("k", "v")),
            **logs(pairs, ("lse",)),
            **encoder_keeps(rows_long),
        },
        scratch=work + [("acc", pltpu.VMEM((rows_long, width), F32))],
        info=source_info,
        after=(sb.small, early_target),
        cost=13,
        moved=(),
    )
    late_target = gather_first(hold(early_target, le.lse), INNER)
    whole_encoded = gather_early(le.enc.reshape(pairs, own, width))

    seb = launch(
        short_encoder_back,
        {
            "denc": sb.denc,
            **saved(se, ("q", "k", "v", "o", "lse", "n1", "i1", "n2", "i2", "gate")),
            **segments,
            **pick(encoder_in, ("w_in", "w_o", "up", "down", "gain")),
        },
        {
            **rows_of(rows, ("dq", "dk", "dv", "b1", "b2", "go")),
            **wide_of(rows, ("dh",)),
            **floats(rows, ("dx",)),
            **sums(4),
        },
        scratch=[("d1", pltpu.VMEM((rows, width), F32))],
        after=(le.lse,),
        cost=16,
    )

    t_short, x_short = flat(target_short), flat(source_short)
    short_weights = whole_tiles(
        [
            [(sc.m, sc.dh), (sc.act, sc.b5)],
            [
                (sd.u, sb.dq_c),
                (se.enc, sb.dk_c),
                (se.enc, sb.dv_c),
                (sc.o_c, sc.b4),
                (t_short, sb.dq),
                (t_short, sb.dk),
                (t_short, sb.dv),
                (sd.o, sb.b3),
            ],
            [(se.y, seb.dh), (se.act, seb.b2)],
            [(x_short, seb.dq), (x_short, seb.dk), (x_short, seb.dv), (se.o, seb.b1)],
        ],
        after=(seb.small,),
        cost=15,
    )
    whole_target = gather_last(late_target, INNER, 1, short_weights[0])
    whole_target = whole_target.reshape(places, pairs, own, width)
    ls = launch(
        long_self_forward,
        {
            "t": t_long,
            "tg": whole_target,
            **pick(decoder_in, ("w_in", "w_o", "w_cin", "gain", "bias")),
        },
        {
            **rows_of(rows_long, ("q", "o", "n3", "u", "q_c")),
            **keys_of(("k", "v")),
            **logs(pairs, ("lse",)),
            **column(rows_long, ("i3",)),
            **floats(rows_long, ("upper",)),
        },
        scratch=work,
        info=target_info,
        after=(short_weights[0],),
        cost=10,
        moved=(),
    )

    whole_encoded = hold(whole_encoded, ls.lse)
    lc = launch(
        long_cross,
        {
            "eg": whole_encoded,
            "upper": ls.upper,
            "q_c": ls.q_c,
            "cot": flat(cotangent_long),
            **pick(decoder_in, ("w_cin", "w_co", "up", "down", "gain", "bias")),
        },
        {
            **rows_of(rows_long, ("o_c",)),
            **keys_of(("k_c", "v_c")),
            **logs(pairs, ("lse_c",)),
            **decoder_keeps(rows_long),
        },
        scratch=work,
        info=source_info,
        after=(ls.lse,),
        cost=14,
        moved=("k_c", "v_c", "up", "down", "w_co", "act", "gate", "dh", "final"),
    )
    lcb = launch(
        long_cross_back,
        {
            "q_c": ls.q_c,
            **saved(lc, ("k_c", "v_c", "o_c", "lse_c", "go_c")),
            **pick(decoder_in, ("w_cin",)),
        },
        {**rows_of(rows_long, ("dq_c",)), **keys_of(("dk_c", "dv_c")), **parts()},
        scratch=mix,
        info=source_info,
        after=(lc.small,),
        cost=14,
        moved=(),
    )
    encoded_back = Spread(part_refs(lcb), True)
    first_weights = Weights(
        [[(lc.m, lc.dh)], [(lc.act, lc.b5)]], short_weights[0]
    )

    def self_back_and_weights(r):
        long_self_back(r)
        first_weights.body(r, r.info[pairs + 2])

    lsb = launch(
        self_back_and_weights,
        {
            "d4": lc.d4,
            "dq_c": lcb.dq_c,
            **saved(ls, ("q", "k", "v", "o", "lse", "n3", "i3")),
            **pick(decoder_in, ("w_in", "w_o", "w_cin", "gain")),
            **first_weights.arrays,
        },
        {
            **first_weights.gives,
            **rows_of(rows_long, ("dq", "b3")),
            **keys_of(("dk", "dv")),
            **parts(),
            **floats(rows_long, ("dt",)),
            **sums(2),
        },
        scratch=mix + [("go", pltpu.VMEM((rows_long, width), BF16))],
        info=target_info,
        after=(lcb.dq_c,),
        pieces=("kept", "sent"),
        cost=22,
    )
    decoder_ffn = Chain([lsb.kept, lsb.sent], (X, INNER, OUTER))
    finish([encoded_back], lsb.small)
    go(encoded_back)
    target_back = Spread(part_refs(lsb), False)
    grad_attention = weight_tiles(
        [
            [(ls.u, lcb.dq_c)],
            [(flat(whole_encoded), flat(lcb.dk_c))],
            [(flat(whole_encoded), flat(lcb.dv_c))],
            [(lc.o_c, lc.b4)],
            [(t_long, lsb.dq)],
            [(flat(whole_target), flat(lsb.dk))],
            [(flat(whole_target), flat(lsb.dv))],
            [(ls.o, lsb.b3)],
        ],
        core_info,
        after=(lsb.small, encoded_back.held[0]),
        base=short_weights[1],
        cost=15,
    )
    finish([encoded_back, decoder_ffn], grad_attention[0])
    go(decoder_ffn)
    attention = Chain(grad_attention, (INNER, X, OUTER))
    ffn_weights = Weights(
        [
            [(le.y, ("dh", hidden))],
            [(le.act, ("b2", width))],
        ],
        short_weights[2],
    )

    def encoder_back_and_weights(r):
        long_encoder_tail_back(r)
        ffn_weights.body(r, r.info[0])

    leb = launch(
        encoder_back_and_weights,
        {
            **{"part%d" % k: flat(piece) for k, piece in enumerate(encoded_back.held)},
            **saved(le, ("n1", "i1", "n2", "i2", "gate")),
            **pick(encoder_in, ("down", "up", "w_o", "gain")),
            **ffn_weights.arrays,
        },
        {
            **ffn_weights.gives,
            **rows_of(rows_long, ("b1", "b2", "go")),
            **wide_of(rows_long, ("dh",)),
            **floats(rows_long, ("d1",)),
            **sums(4),
        },
        info=core_info,
        after=(grad_attention[0], decoder_ffn.held[0]),
        pieces=("kept", "sent"),
        cost=12,
    )
    small = jnp.concatenate([seb.small + leb.small, sb.small + lsb.small, sc.small + lc.small])
    small = jnp.pad(small, ((0, 16 - small.shape[0]), (0, 0))).astype(BF16)
    finish([attention], leb.small)
    go(attention)
    encoder_ffn = Chain([leb.kept, leb.sent], (X, INNER, OUTER))
    attention_weights = Weights(
        [
            [(x_long, ("dq", width))],
            [(whole_source, ("dk", width))],
            [(whole_source, ("dv", width))],
            [(le.o, leb.b1)],
        ],
        short_weights[3],
    )

    def attention_back_and_weights(r):
        long_encoder_back(r)
        r.leave("dx", *[name for name in r if name[0] == "p" and name[1:].isdigit()])
        attention_weights.body(r, r.info[pairs + 2])

    lea = launch(
        attention_back_and_weights,
        {
            **saved(le, ("q", "k", "v")),
            "o": le.o,
            "lse": le.lse,
            **saved(leb, ("go", "d1")),
            **pick(encoder_in, ("w_in",)),
            **attention_weights.arrays,
        },
        {
            **attention_weights.gives,
            **parts(),
            **floats(rows_long, ("dx",)),
        },
        scratch=mix
        + [
            ("dq", pltpu.VMEM((rows_long, width), BF16)),
            ("dk", pltpu.VMEM((places, pairs, own, width), BF16)),
            ("dv", pltpu.VMEM((places, pairs, own, width), BF16)),
        ],
        info=source_info,
        after=(leb.small, attention.held[0]),
        pieces=("kept", "sent"),
        cost=19,
    )
    done = lea.dx
    finish([decoder_ffn, encoder_ffn, target_back], done)
    encoder = Chain([lea.kept, lea.sent], (INNER, X, OUTER), small, True)
    go(decoder_ffn, encoder_ffn, target_back)
    square = (3, width, width)
    feed = {"up": encoder_up.shape, "down": encoder_down.shape}
    one = {"project": square, "output": square[1:]}
    two = {"cross_in": square, "cross_out": square[1:], "self_in": square, "self_out": square[1:]}

    def out(shapes):
        return lambda chain, token: assemble(chain, core_info, shapes, token)

    rows_out = lambda rows: lambda chain, token: [chain.result().astype(F32) + rows]
    flights = [
        (encoder, 0.0, out(one)),
        (decoder_ffn, 0.0, out(feed)),
        (attention, 20.0, out(two)),
        (encoder_ffn, 0.0, out(feed)),
        (target_back, 0.0, rows_out(lsb.dt.reshape(source_long.shape))),
    ]

    def source_back(token):
        chain = Spread(hold(part_refs(lea), token), False)
        return chain, 0.0, rows_out(lea.dx.reshape(source_long.shape))

    results = run_out(flights, source_back)
    (encoder_in_out, encoder_out_out), (decoder_up_out, decoder_down_out) = results[:2]
    (cross_in, cross_out, self_in, self_out), (encoder_up_out, encoder_down_out) = results[2:4]
    (grad_target,), (grad_source,) = results[4:]
    small = encoder.small.astype(F32)
    return (
        sc.final.reshape(source_short.shape),
        lc.final.reshape(source_long.shape),
        seb.dx.reshape(source_short.shape),
        sb.dt.reshape(source_short.shape),
        grad_source,
        grad_target,
        encoder_in_out,
        encoder_out_out,
        encoder_up_out,
        encoder_down_out,
        small[0:2],
        small[2:4],
        self_in,
        self_out,
        cross_in,
        cross_out,
        decoder_up_out,
        decoder_down_out,
        jnp.stack([small[4], small[6], small[7]]),
        jnp.stack([small[5], small[8], small[9]]),
    )


def solution(mesh):
    group, seq = mesh.devices.shape
    fine = Mesh(
        mesh.devices.reshape(group // 2, 2, 4, seq // 4), (X, CORE, OUTER, INNER)
    )
    groups, positions = (X, CORE), (OUTER, INNER)
    blocks = P(groups + positions, None, None)
    long_rows = P(groups, positions, None)
    in_specs = (
        (blocks, blocks, P(groups + positions, None), P(groups + positions, None))
        + (long_rows, long_rows, P(groups), P(groups), blocks, long_rows)
        + (P(),) * 14
    )
    out_specs = (blocks, long_rows, blocks, blocks, long_rows, long_rows) + (P(),) * 14
    return jax.shard_map(
        shards, mesh=fine, in_specs=in_specs, out_specs=out_specs, check_vma=False
    )
```

```python
import functools
import random
import jax
import jax.numpy as jnp
from jax import lax
from jax.experimental import pallas as pl
from jax.experimental.pallas import tpu as pltpu
from jax.sharding import Mesh, PartitionSpec as P

HEADS = 8
HEAD_DIM = 64
PAIR = 2 * HEAD_DIM
PAIRS = HEADS // 2
SCALE = HEAD_DIM**-0.5
FLOOR_SCORE = -1e30
EPSILON = 1e-05
KEY_BLOCK = 512
CHUNK = 512
F32 = jnp.float32
BF16 = jnp.bfloat16
CORE, X, INNER, OUTER = "core", "x", "inner", "outer"


def nn(left, right):
    return lax.dot_general(left, right, (((1,), (0,)), ((), ())), preferred_element_type=F32)


def nt(left, right):
    return lax.dot_general(left, right, (((1,), (1,)), ((), ())), preferred_element_type=F32)


def tn(left, right):
    return lax.dot_general(left, right, (((0,), (0,)), ((), ())), preferred_element_type=F32)


def two_heads(rows):
    lane = lax.broadcasted_iota(jnp.int32, rows.shape, 1)
    zero = jnp.zeros_like(rows)
    first = jnp.where(lane < HEAD_DIM, rows, zero)
    second = jnp.where(lane < HEAD_DIM, zero, rows)
    return jnp.concatenate([first, second], axis=0)


def diagonal(product):
    half = product.shape[1] // 2
    return jnp.concatenate([product[:HEAD_DIM, :half], product[HEAD_DIM:, half:]], axis=0)


def delta_rows(grad_out, outputs):
    product = grad_out.astype(F32) * outputs.astype(F32)
    high = product.astype(BF16)
    low = (product - high.astype(F32)).astype(BF16)
    width = product.shape[1]
    head = lax.broadcasted_iota(jnp.int32, (HEADS, width), 0)
    lane = lax.broadcasted_iota(jnp.int32, (HEADS, width), 1)
    pick = jnp.where(lax.div(lane, HEAD_DIM) == head, 1.0, 0.0).astype(BF16)
    return nt(pick, high) + nt(pick, low)


def pair_row(rows, pair):
    return jnp.concatenate([rows[2 * pair : 2 * pair + 1], rows[2 * pair + 1 : 2 * pair + 2]], axis=1)


def pair_lanes(pair):
    return slice(pair * PAIR, (pair + 1) * PAIR)


def norm(residual, gain, bias):
    centred = residual - jnp.mean(residual, axis=1, keepdims=True)
    inverse = lax.rsqrt(jnp.mean(centred * centred, axis=1, keepdims=True) + EPSILON)
    normed = centred * inverse
    return normed * gain + bias, normed, inverse


def norm_back(upstream, normed, inverse, gain):
    normed = normed.astype(F32)
    scaled = upstream * gain
    grad = inverse * (
        scaled
        - jnp.mean(scaled, axis=1, keepdims=True)
        - normed * jnp.mean(scaled * normed, axis=1, keepdims=True)
    )
    return (
        grad,
        jnp.sum(upstream * normed, axis=0, keepdims=True),
        jnp.sum(upstream, axis=0, keepdims=True),
    )


def chunks(ref, axis, step):
    def body(index, carry):
        step(pl.ds(pl.multiple_of(index * CHUNK, CHUNK), CHUNK))
        return carry

    lax.fori_loop(0, ref.shape[axis] // CHUNK, body, 0)


def feed_forward_in_loop(rows, up_ref, down_ref, act_ref, gate_ref, low_ref, total_ref):
    low_ref[...] = rows.astype(BF16)
    total_ref[...] = rows

    def step(part):
        hidden = nn(low_ref[...], up_ref[:, part])
        sigmoid = 0.5 * jnp.tanh(0.5 * hidden) + 0.5
        active = hidden * sigmoid
        gate_ref[:, part] = (sigmoid + active * (1.0 - sigmoid)).astype(BF16)
        active = active.astype(BF16)
        act_ref[:, part] = active
        total_ref[...] += nn(active, down_ref[part, :])

    chunks(up_ref, 1, step)
    return total_ref[...]


def feed_forward(rows, up_ref, down_ref, act_ref, gate_ref):
    low = rows.astype(BF16)
    total = rows
    for start in range(0, up_ref.shape[1], CHUNK):
        part = slice(start, start + CHUNK)
        hidden = nn(low, up_ref[:, part])
        sigmoid = 0.5 * jnp.tanh(0.5 * hidden) + 0.5
        active = hidden * sigmoid
        gate_ref[:, part] = (sigmoid + active * (1.0 - sigmoid)).astype(BF16)
        active = active.astype(BF16)
        act_ref[:, part] = active
        total = total + nn(active, down_ref[part, :])
    return low, total


def feed_back(grad, gate_ref, up_ref, down_ref, hidden_grad_ref):
    low = grad.astype(BF16)
    total = grad
    for start in range(0, up_ref.shape[1], CHUNK):
        part = slice(start, start + CHUNK)
        hidden = nt(low, down_ref[part, :]) * gate_ref[:, part].astype(F32)
        hidden = hidden.astype(BF16)
        hidden_grad_ref[:, part] = hidden
        total = total + nt(hidden, up_ref[:, part])
    return low, total


def short_allowed(key_segment, query_segment, causal):
    allowed = key_segment == query_segment
    if causal:
        key = lax.broadcasted_iota(jnp.int32, key_segment.shape, 0)
        query = lax.broadcasted_iota(jnp.int32, key_segment.shape, 1)
        allowed = allowed & (key <= query)
    return jnp.concatenate([allowed, allowed], axis=1)


def short_attend(causal, q_ref, k_ref, v_ref, kseg_ref, qseg_ref, o_ref, lse_ref):
    size = kseg_ref.shape[1]
    for block in range(kseg_ref.shape[0]):
        rows = slice(block * size, (block + 1) * size)
        allowed = short_allowed(kseg_ref[block], qseg_ref[block], causal)
        logs = []
        for pair in range(PAIRS):
            lanes = pair_lanes(pair)
            scores = nt(k_ref[rows, lanes], two_heads(q_ref[rows, lanes]))
            scores = jnp.where(allowed, scores, FLOOR_SCORE)
            top = jnp.max(scores, axis=0, keepdims=True)
            weights = jnp.exp(scores - top)
            total = jnp.sum(weights, axis=0, keepdims=True)
            mixed = nn(v_ref[rows, lanes].T, weights.astype(BF16)) / total
            o_ref[rows, lanes] = diagonal(mixed).T.astype(BF16)
            log_total = top + jnp.log(total)
            logs += [log_total[:, :size], log_total[:, size:]]
        lse_ref[block] = jnp.concatenate(logs, axis=0)


def short_attend_back(
    causal, q_ref, k_ref, v_ref, kseg_ref, qseg_ref, o_ref, lse_ref, go_ref, dq_ref, dk_ref, dv_ref
):
    size = kseg_ref.shape[1]
    for block in range(kseg_ref.shape[0]):
        rows = slice(block * size, (block + 1) * size)
        allowed = short_allowed(kseg_ref[block], qseg_ref[block], causal)
        delta = delta_rows(go_ref[rows, :], o_ref[rows, :])
        lse = lse_ref[block]
        for pair in range(PAIRS):
            lanes = pair_lanes(pair)
            queries, grads = two_heads(q_ref[rows, lanes]), two_heads(go_ref[rows, lanes])
            scores = nt(k_ref[rows, lanes], queries)
            weights = jnp.where(allowed, jnp.exp(scores - pair_row(lse, pair)), 0.0)
            grad_weights = nt(v_ref[rows, lanes], grads)
            grad_scores = (weights * (grad_weights - pair_row(delta, pair))).astype(BF16)
            dv_ref[rows, lanes] = nn(weights.astype(BF16), grads).astype(BF16)
            dk_ref[rows, lanes] = nn(grad_scores, queries).astype(BF16)
            turned = diagonal(nn(k_ref[rows, lanes].T, grad_scores)).T
            dq_ref[rows, lanes] = (turned.astype(BF16).astype(F32) * SCALE).astype(BF16)


def load_keys(ref, pair_index, block, lanes):
    pieces = KEY_BLOCK // ref.shape[2]
    rows = ref[pl.ds(block * pieces, pieces), pair_index, :, lanes]
    return rows.reshape(KEY_BLOCK, rows.shape[2])


def store_keys(ref, pair_index, block, lanes, rows):
    pieces = KEY_BLOCK // ref.shape[2]
    ref[pl.ds(block * pieces, pieces), pair_index, :, lanes] = rows.astype(BF16).reshape(
        pieces, ref.shape[2], rows.shape[1]
    )


def store_part(refs, info_ref, pair_index, block, rows):
    partners, (_, pairs, size, _) = len(refs), refs[0].shape
    if partners == 2:
        swap = info_ref[pairs + 1] == 1
        count = KEY_BLOCK // (2 * size)
        for piece in range(count):
            outer = (block * count + piece) ^ info_ref[pairs + 3]
            begin = 2 * piece * size
            first, second = rows[begin : begin + size], rows[begin + size : begin + 2 * size]
            refs[0][outer, pair_index] = jnp.where(swap, second, first)
            refs[1][outer, pair_index] = jnp.where(swap, first, second)
        return
    for piece in range(KEY_BLOCK // size):
        place = block * (KEY_BLOCK // size) + piece
        inner = lax.rem(place, partners) ^ info_ref[pairs + 1]
        outer = lax.div(place, partners) ^ info_ref[pairs + 3]
        part = rows[piece * size : (piece + 1) * size]
        for partner, ref in enumerate(refs):

            @pl.when(inner == partner)
            def _(ref=ref):
                ref[outer, pair_index] = part


def long_limit(info_ref, causal, pair_index, size, pairs):
    length = info_ref[pair_index]
    limit = length
    if causal:
        limit = jnp.minimum(length, info_ref[pairs] + size)
    return length, lax.div(limit + KEY_BLOCK - 1, KEY_BLOCK)


def long_allowed(start, causal, length, block, shape):
    key = lax.broadcasted_iota(jnp.int32, shape, 0) + block * KEY_BLOCK
    allowed = key < length
    if causal:
        half = shape[1] // 2
        lane = lax.broadcasted_iota(jnp.int32, shape, 1)
        query = jnp.where(lane < half, lane, lane - half) + start
        allowed = allowed & (key <= query)
    return allowed


def long_attend(
    causal, info_ref, q_ref, x_ref, k_w, v_w, k_ref, v_ref, o_ref, lse_ref, score_ref, sum_ref, mix_ref
):
    places, pairs, size, width = x_ref.shape
    shape = (KEY_BLOCK, 2 * size)
    everything = slice(None)

    def one(pair_index, carry):
        length, count = long_limit(info_ref, causal, pair_index, size, pairs)
        own = pl.ds(pl.multiple_of(pair_index * size, size), size)

        def first(block, tops):
            rows = pl.ds(pl.multiple_of(block * KEY_BLOCK, KEY_BLOCK), KEY_BLOCK)
            allowed = long_allowed(info_ref[pairs], causal, length, block, shape)
            context = load_keys(x_ref, pair_index, block, everything)
            store_keys(k_ref, pair_index, block, everything, nn(context, k_w[...]))
            store_keys(v_ref, pair_index, block, everything, nn(context, v_w[...]))
            after = []
            for pair in range(PAIRS):
                lanes = pair_lanes(pair)
                keys = load_keys(k_ref, pair_index, block, lanes)
                scores = nt(keys, two_heads(q_ref[own, lanes]))
                scores = jnp.where(allowed, scores, FLOOR_SCORE)
                score_ref[pair, rows] = scores
                folded = jnp.max(scores.reshape(KEY_BLOCK // 8, 8, 2 * size), axis=0)
                after.append(jnp.maximum(tops[pair], folded))
            return tuple(after)

        start = tuple(jnp.full((8, 2 * size), FLOOR_SCORE, F32) for _ in range(PAIRS))
        tops = lax.fori_loop(0, count, first, start)
        tops = [jnp.max(top, axis=0, keepdims=True) for top in tops]
        sum_ref[...] = jnp.zeros_like(sum_ref)
        mix_ref[...] = jnp.zeros_like(mix_ref)

        def second(block, carry):
            rows = pl.ds(pl.multiple_of(block * KEY_BLOCK, KEY_BLOCK), KEY_BLOCK)
            for pair in range(PAIRS):
                weights = jnp.exp(score_ref[pair, rows] - tops[pair])
                sum_ref[pair] += jnp.sum(weights.reshape(KEY_BLOCK // 8, 8, 2 * size), axis=0)
                values = load_keys(v_ref, pair_index, block, pair_lanes(pair))
                mix_ref[pair] += nn(values.T, weights.astype(BF16))
            return carry

        lax.fori_loop(0, count, second, 0)
        logs = []
        for pair in range(PAIRS):
            total = jnp.sum(sum_ref[pair], axis=0, keepdims=True)
            mixed = mix_ref[pair] / total
            o_ref[own, pair_lanes(pair)] = diagonal(mixed).T.astype(BF16)
            log_total = tops[pair] + jnp.log(total)
            logs += [log_total[:, :size], log_total[:, size:]]
        lse_ref[pair_index] = jnp.concatenate(logs, axis=0)
        return carry

    lax.fori_loop(0, pairs, one, 0)


def long_attend_back(
    causal,
    info_ref,
    q_ref,
    k_ref,
    v_ref,
    o_ref,
    lse_ref,
    go_ref,
    k_w,
    v_w,
    dq_ref,
    dk_ref,
    dv_ref,
    part_ref,
    mix_ref,
):
    places, pairs, size, width = k_ref.shape
    shape = (KEY_BLOCK, 2 * size)
    everything = slice(None)

    def one(pair_index, carry):
        length, count = long_limit(info_ref, causal, pair_index, size, pairs)
        own = pl.ds(pl.multiple_of(pair_index * size, size), size)
        delta = delta_rows(go_ref[own, :], o_ref[own, :])
        lse = lse_ref[pair_index]
        mix_ref[...] = jnp.zeros_like(mix_ref)

        def step(block, carry):
            allowed = long_allowed(info_ref[pairs], causal, length, block, shape)
            for pair in range(PAIRS):
                lanes = pair_lanes(pair)
                queries, grads = two_heads(q_ref[own, lanes]), two_heads(go_ref[own, lanes])
                keys = load_keys(k_ref, pair_index, block, lanes)
                scores = nt(keys, queries)
                weights = jnp.where(allowed, jnp.exp(scores - pair_row(lse, pair)), 0.0)
                grad_weights = nt(load_keys(v_ref, pair_index, block, lanes), grads)
                grad_scores = (weights * (grad_weights - pair_row(delta, pair))).astype(BF16)
                store_keys(dv_ref, pair_index, block, lanes, nn(weights.astype(BF16), grads))
                store_keys(dk_ref, pair_index, block, lanes, nn(grad_scores, queries))
                mix_ref[pair] += nn(keys.T, grad_scores)
            part = nt(load_keys(dk_ref, pair_index, block, everything), k_w[...])
            part = part + nt(load_keys(dv_ref, pair_index, block, everything), v_w[...])
            store_part(part_ref, info_ref, pair_index, block, part.astype(BF16))
            return carry

        lax.fori_loop(0, count, step, 0)

        def clear(block, carry):
            nothing = jnp.zeros((KEY_BLOCK, width), BF16)
            store_keys(dk_ref, pair_index, block, everything, nothing)
            store_keys(dv_ref, pair_index, block, everything, nothing)
            store_part(part_ref, info_ref, pair_index, block, nothing)
            return carry

        lax.fori_loop(count, places * size // KEY_BLOCK, clear, 0)
        for pair in range(PAIRS):
            turned = diagonal(mix_ref[pair]).T
            dq_ref[own, pair_lanes(pair)] = (turned.astype(BF16).astype(F32) * SCALE).astype(BF16)
        return carry

    lax.fori_loop(0, pairs, one, 0)


class Refs(dict):
    def __init__(self, *args):
        super().__init__(*args)
        self.coming, self.leaving, self.pieced = {}, {}, {}

    def __getattr__(self, name):
        if name in self.coming:
            self.coming.pop(name).wait()
        return self[name]

    def leave_piece(self, name, piece):
        source, target, signals, first = self.pieced[name]
        pltpu.make_async_copy(source.at[piece], target.at[piece], signals.at[first + piece]).start()

    def leave(self, *names):
        for name in names:
            self["left"].add(name)
            for copy in self.leaving.get(name, ()):
                copy.start()


def copied(shape, dtype):
    size = dtype.itemsize
    for length in shape:
        size *= length
    return shape[-1] % 128 == 0 and size >= 2**16


def launch(body, arrays, gives, scratch=(), info=None, after=(), pieces=(), moved=None, cost=10):
    memory = pl.BlockSpec(memory_space=pltpu.VMEM)
    far = pl.BlockSpec(memory_space=pl.ANY)
    ins, specs = [], []
    if info is not None:
        ins.append(info)
        specs.append(pl.BlockSpec(memory_space=pltpu.SMEM))
    by_itself = lambda name, shape, dtype: (
        copied(shape, jnp.dtype(dtype)) if moved is None else name in moved
    )
    moved_in = [name for name, a in arrays.items() if by_itself(name, a.shape, a.dtype)]
    moved_out = [name for name, give in gives.items() if name in pieces or by_itself(name, *give)]
    for name, array in arrays.items():
        ins.append(array)
        specs.append(far if name in moved_in else memory)
    for array in after:
        ins.append(array)
        specs.append(far)
    count_out = sum(gives[name][0][0] if name in pieces else 1 for name in moved_out)
    rooms = [pltpu.VMEM(arrays[name].shape, arrays[name].dtype) for name in moved_in]
    rooms += [pltpu.VMEM(*gives[name]) for name in moved_out]
    rooms += [pltpu.SemaphoreType.DMA((max(len(moved_in), 1),))]
    rooms += [pltpu.SemaphoreType.DMA((max(count_out, 1),))]
    names = [name for name, _ in scratch]

    def run(*refs):
        refs = list(refs)
        r = Refs()
        if info is not None:
            r["info"] = refs.pop(0)
        outer = {name: refs.pop(0) for name in arrays}
        del refs[: len(after)]
        outer.update((name, refs.pop(0)) for name in gives)
        room = {name: refs.pop(0) for name in moved_in + moved_out}
        come, go = refs.pop(0), refs.pop(0)
        r.update(outer)
        r.update(room)
        r.update(zip(names, refs))
        for place, name in enumerate(moved_in):
            copy = pltpu.make_async_copy(outer[name], room[name], come.at[place])
            copy.start()
            r.coming[name] = copy
        place = 0
        for name in moved_out:
            copies = []
            if name in pieces:
                r.pieced[name] = (room[name], outer[name], go, place)
                for piece in range(gives[name][0][0]):
                    source, target = room[name].at[piece], outer[name].at[piece]
                    copies.append(pltpu.make_async_copy(source, target, go.at[place]))
                    place += 1
            else:
                copies.append(pltpu.make_async_copy(room[name], outer[name], go.at[place]))
                place += 1
            r.leaving[name] = copies
        left = set()
        r["left"] = left
        body(r)
        for name in list(r.coming):
            r.coming.pop(name).wait()
        for name in moved_out:
            if name not in left and name not in pieces:
                r.leave(name)
        for name in moved_out:
            for copy in r.leaving[name]:
                copy.wait()

    out = pl.pallas_call(
        run,
        in_specs=specs,
        out_specs=[far if name in moved_out else memory for name in gives],
        out_shape=[jax.ShapeDtypeStruct(shape, dtype) for shape, dtype in gives.values()],
        scratch_shapes=rooms + [shape for _, shape in scratch],
        compiler_params=pltpu.CompilerParams(vmem_limit_bytes=VMEM_LIMIT),
        cost_estimate=pl.CostEstimate(
            flops=int(cost * 1.1e9), bytes_accessed=int(cost * 3.5e6), transcendentals=0
        ),
    )(*ins)
    return Refs(zip(gives, out))


VMEM_LIMIT = 56 * 2**20


def add_sums(ref, rows):
    ref[...] = jnp.concatenate(rows, axis=0)


def encoder_tail(r, o_ref):
    residual = r.x[...].astype(F32) + nn(o_ref[...], r.w_o[...])
    first, normed, inverse = norm(residual, r.gain[0:1], r.bias[0:1])
    r.n1[...] = normed.astype(BF16)
    r.i1[...] = inverse
    if "acc" in r:
        total = feed_forward_in_loop(first, r.up, r.down, r.act, r.gate, r.y, r.acc)
    else:
        r.y[...], total = feed_forward(first, r.up, r.down, r.act, r.gate)
    r.leave("n1", "act", "gate", "y")
    encoded, normed, inverse = norm(total, r.gain[1:2], r.bias[1:2])
    r.n2[...] = normed.astype(BF16)
    r.i2[...] = inverse
    r.enc[...] = encoded.astype(BF16)


def project_short(r, name, rows, w_q, w_k, w_v, context=None):
    context = rows if context is None else context
    r["q" + name][...] = (nn(rows, w_q) * SCALE).astype(BF16)
    r["k" + name][...] = nn(context, w_k).astype(BF16)
    r["v" + name][...] = nn(context, w_v).astype(BF16)


def short_encoder_forward(r):
    project_short(r, "", r.x[...], r.w_in[0], r.w_in[1], r.w_in[2])
    r.leave("q", "k", "v")
    short_attend(False, r.q, r.k, r.v, r.kseg, r.qseg, r.o, r.lse)
    r.leave("o")
    encoder_tail(r, r.o)


def decoder_middle(r, o_ref):
    residual = r.t[...].astype(F32) + nn(o_ref[...], r.w_o[...])
    upper, normed, inverse = norm(residual, r.gain[0:1], r.bias[0:1])
    r.n3[...] = normed.astype(BF16)
    r.i3[...] = inverse
    r.u[...] = upper.astype(BF16)
    return upper


def decoder_tail(r, upper, o_ref):
    gain, bias = r.gain, r.bias
    residual = upper + nn(o_ref[...], r.w_co[...])
    middle, normed4, inverse4 = norm(residual, gain[1:2], bias[1:2])
    r.m[...], total = feed_forward(middle, r.up, r.down, r.act, r.gate)
    r.leave("m", "act", "gate")
    final, normed5, inverse5 = norm(total, gain[2:3], bias[2:3])
    r.final[...] = final
    r.leave("final")
    grad, gain5, bias5 = norm_back(r.cot[...].astype(F32), normed5, inverse5, gain[2:3])
    r.b5[...], grad = feed_back(grad, r.gate, r.up, r.down, r.dh)
    r.leave("b5", "dh")
    grad, gain4, bias4 = norm_back(grad, normed4, inverse4, gain[1:2])
    low = grad.astype(BF16)
    r.b4[...] = low
    r.d4[...] = grad
    r.go_c[...] = nt(low, r.w_co[...]).astype(BF16)
    add_sums(r.small, [gain4, gain5, bias4, bias5])


def short_decoder_forward(r):
    project_short(r, "", r.t[...], r.w_in[0], r.w_in[1], r.w_in[2])
    r.leave("q", "k", "v")
    short_attend(True, r.q, r.k, r.v, r.tkseg, r.tqseg, r.o, r.lse)
    r.leave("o")
    r.upper[...] = decoder_middle(r, r.o)


def short_cross_forward(r):
    project_short(r, "_c", r.u[...], r.w_cin[0], r.w_cin[1], r.w_cin[2], r.enc[...])
    r.leave("q_c", "k_c", "v_c")
    short_attend(False, r.q_c, r.k_c, r.v_c, r.kseg, r.tqseg, r.o_c, r.lse_c)
    r.leave("o_c")
    decoder_tail(r, r.upper[...], r.o_c)


def decoder_middle_back(r):
    grad = r.d4[...] + nt(r.dq_c[...], r.w_cin[0])
    grad, gain3, bias3 = norm_back(grad, r.n3[...], r.i3[...], r.gain[0:1])
    low = grad.astype(BF16)
    r.b3[...] = low
    r.go[...] = nt(low, r.w_o[...]).astype(BF16)
    add_sums(r.small, [gain3, bias3])
    return grad


def short_decoder_back(r):
    short_attend_back(
        False, r.q_c, r.k_c, r.v_c, r.kseg, r.tqseg, r.o_c, r.lse_c, r.go_c, r.dq_c, r.dk_c, r.dv_c
    )
    r.denc[...] = nt(r.dk_c[...], r.w_cin[1]) + nt(r.dv_c[...], r.w_cin[2])
    r.leave("dq_c", "dk_c", "dv_c", "denc")
    r.d3[...] = decoder_middle_back(r)
    short_attend_back(
        True, r.q, r.k, r.v, r.tkseg, r.tqseg, r.o, r.lse, r.go, r.dq, r.dk, r.dv
    )
    r.leave("dq", "dk", "dv")
    grad = r.d3[...] + nt(r.dq[...], r.w_in[0])
    r.dt[...] = grad + nt(r.dk[...], r.w_in[1]) + nt(r.dv[...], r.w_in[2])


def encoder_tail_back(r, grad):
    grad, gain2, bias2 = norm_back(grad, r.n2[...], r.i2[...], r.gain[1:2])
    r.b2[...], grad = feed_back(grad, r.gate, r.up, r.down, r.dh)
    r.leave("b2", "dh")
    grad, gain1, bias1 = norm_back(grad, r.n1[...], r.i1[...], r.gain[0:1])
    low = grad.astype(BF16)
    r.b1[...] = low
    r.go[...] = nt(low, r.w_o[...]).astype(BF16)
    r.d1[...] = grad
    add_sums(r.small, [gain1, gain2, bias1, bias2])


def short_encoder_back(r):
    encoder_tail_back(r, r.denc[...])
    short_attend_back(
        False, r.q, r.k, r.v, r.kseg, r.qseg, r.o, r.lse, r.go, r.dq, r.dk, r.dv
    )
    r.leave("dq", "dk", "dv")
    grad = r.d1[...] + nt(r.dq[...], r.w_in[0])
    r.dx[...] = grad + nt(r.dk[...], r.w_in[1]) + nt(r.dv[...], r.w_in[2])


def long_encoder_forward(r):
    r.q[...] = (nn(r.x[...], r.w_in[0]) * SCALE).astype(BF16)
    long_attend(
        False, r.info, r.q, r.xg, r.w_in.at[1], r.w_in.at[2], r.k, r.v, r.o, r.lse, r.s, r.a, r.mix
    )
    r.leave("q", "k", "v", "o")
    encoder_tail(r, r.o)


def long_self_forward(r):
    r.q[...] = (nn(r.t[...], r.w_in[0]) * SCALE).astype(BF16)
    long_attend(
        True, r.info, r.q, r.tg, r.w_in.at[1], r.w_in.at[2], r.k, r.v, r.o, r.lse, r.s, r.a, r.mix
    )
    r.leave("q", "k", "v", "o")
    upper = decoder_middle(r, r.o)
    r.upper[...] = upper
    r.q_c[...] = (nn(upper.astype(BF16), r.w_cin[0]) * SCALE).astype(BF16)


def long_cross(r):
    k_w, v_w = r.w_cin.at[1], r.w_cin.at[2]
    long_attend(
        False, r.info, r.q_c, r.eg, k_w, v_w, r.k_c, r.v_c, r.o_c, r.lse_c, r.s, r.a, r.mix
    )
    r.leave("k_c", "v_c", "o_c")
    decoder_tail(r, r.upper[...], r.o_c)


def part_refs(r):
    return [r[name] for name in r if name[0] == "p" and name[1:].isdigit()]


def long_cross_back(r):
    long_attend_back(
        False,
        r.info,
        r.q_c,
        r.k_c,
        r.v_c,
        r.o_c,
        r.lse_c,
        r.go_c,
        r.w_cin.at[1],
        r.w_cin.at[2],
        r.dq_c,
        r.dk_c,
        r.dv_c,
        part_refs(r),
        r.mix,
    )


def long_self_back(r):
    grad = decoder_middle_back(r)
    long_attend_back(
        True,
        r.info,
        r.q,
        r.k,
        r.v,
        r.o,
        r.lse,
        r.go,
        r.w_in.at[1],
        r.w_in.at[2],
        r.dq,
        r.dk,
        r.dv,
        part_refs(r),
        r.mix,
    )
    r.dt[...] = grad + nt(r.dq[...], r.w_in[0])


def long_encoder_tail_back(r):
    grad = r.part0[...].astype(F32) + r.part1[...].astype(F32)
    grad = grad + r.part2[...].astype(F32) + r.part3[...].astype(F32)
    encoder_tail_back(r, grad)


def long_encoder_back(r):
    long_attend_back(
        False,
        r.info,
        r.q,
        r.k,
        r.v,
        r.o,
        r.lse,
        r.go,
        r.w_in.at[1],
        r.w_in.at[2],
        r.dq,
        r.dk,
        r.dv,
        part_refs(r),
        r.mix,
    )
    r.dx[...] = r.d1[...] + nt(r.dq[...], r.w_in[0])


SIDE = 512


class Weights:
    def __init__(self, pairs, base=None):
        self.arrays, self.plan, known = {}, [], {}

        def place(rows):
            if isinstance(rows, tuple):
                return rows
            if id(rows) not in known:
                known[id(rows)] = "w%d" % len(known)
                self.arrays[known[id(rows)]] = rows
            return known[id(rows)], rows.shape[-1]

        self.count = 0
        for terms in pairs:
            terms = [(place(a), place(b)) for a, b in terms]
            (_, height), (_, width) = terms[0]
            self.plan.append((self.count, width // SIDE, [(a[0], b[0]) for a, b in terms]))
            self.count += height // SIDE * (width // SIDE)
        self.gives = {name: ((self.count, SIDE // 2, SIDE), BF16) for name in ("kept", "sent")}
        if base is not None:
            self.arrays["base"] = base

    def each(self, r, step):
        ends = [first for first, _, _ in self.plan[1:]] + [self.count]
        for (first, across, terms), end in zip(self.plan, ends):
            terms = [(getattr(r, a), getattr(r, b)) for a, b in terms]

            def body(tile, carry, first=first, across=across, terms=terms):
                row = pl.multiple_of(lax.div(tile - first, across) * SIDE, SIDE)
                column = pl.multiple_of(lax.rem(tile - first, across) * SIDE, SIDE)
                step(tile, row, column, terms)
                return carry

            lax.fori_loop(first, end, body, 0)

    def body(self, r, core):
        half = SIDE // 2
        if "base" in self.arrays:
            r.base

        def step(tile, row, column, terms):
            for flip, name in enumerate(("kept", "sent")):
                inside = pl.multiple_of((core ^ flip) * half, half)
                total = None
                if "base" in self.arrays:
                    total = r["base"][tile, pl.ds(inside, half), :].astype(F32)
                for left, right in terms:
                    rows = pl.ds(pl.multiple_of(row + inside, half), half)
                    across = pl.ds(column, SIDE)
                    if len(left.shape) == 4:
                        tall = left.shape[0] * left.shape[1] * left.shape[2]
                        first = left[:, :, :, rows].reshape(tall, half)
                    else:
                        first = left[:, rows]
                    if len(right.shape) == 4:
                        tall = right.shape[0] * right.shape[1] * right.shape[2]
                        product = tn(first, right[:, :, :, across].reshape(tall, SIDE))
                    else:
                        product = tn(first, right[:, across])
                    total = product if total is None else total + product
                r[name][tile] = total.astype(BF16)
                r.leave_piece(name, tile)

        self.each(r, step)


class Tagged:
    def __init__(self, r, tag):
        self.r, self.tag = r, tag

    def __getattr__(self, name):
        return getattr(self.r, name + self.tag)


def whole_tiles(chunks, after=(), cost=10):
    weights = [Weights([[pair] for pair in chunk]) for chunk in chunks]
    arrays, gives = {}, {}
    for number, part in enumerate(weights):
        gives["c%d" % number] = ((part.count, SIDE, SIDE), BF16)
        arrays.update((name + "c%d" % number, array) for name, array in part.arrays.items())

    def body(r):
        for number, part in enumerate(weights):
            tag = "c%d" % number

            def step(tile, row, column, terms, tag=tag):
                ((left, right),) = terms
                product = tn(left[:, pl.ds(row, SIDE)], right[:, pl.ds(column, SIDE)])
                r[tag][tile] = product.astype(BF16)
                r.leave_piece(tag, tile)

            part.each(Tagged(r, tag), step)

    out = launch(body, arrays, gives, after=after, pieces=tuple(gives), cost=cost)
    return list(out.values())


def weight_tiles(pairs, core_info, after=(), cost=10, base=None):
    weights = Weights(pairs, base)
    out = launch(
        lambda r: weights.body(r, r.info[0]),
        weights.arrays,
        weights.gives,
        info=core_info,
        after=after,
        pieces=("kept", "sent"),
        cost=cost,
    )
    return [out.kept, out.sent]


def send(piece, axis, offset):
    count = lax.axis_size(axis)
    return lax.ppermute(piece, axis, [(i, i ^ offset) for i in range(count)])


def ordered(pieces, place, dim):
    if len(pieces) == 1:
        return pieces[0]
    level = len(pieces) // 2
    inside = lax.rem(place, level)
    low = ordered(pieces[:level], inside, dim)
    high = ordered(pieces[level:], inside, dim)
    return jnp.where(
        place >= level, jnp.concatenate([high, low], dim), jnp.concatenate([low, high], dim)
    )


def hold(value, token):
    return lax.optimization_barrier((value, token))[0]


def gather_first(piece, axis):
    return [piece] + [send(piece, axis, k) for k in range(1, lax.axis_size(axis))]


def gather_last(pieces, axis, dim, token=None):
    if token is not None:
        pieces = hold(pieces, token)
    return ordered(pieces, lax.axis_index(axis), dim)


def added(pieces):
    total = pieces[0].astype(F32)
    for piece in pieces[1:]:
        total = total + piece.astype(F32)
    return total.astype(BF16)


def scatter_step(pending, axis, dim, token=None):
    if token is not None:
        pending = hold(pending, token)
    place, count = lax.axis_index(axis), lax.axis_size(axis)
    size = pending[0].shape[dim] // count
    after = []
    for k in range(count):
        parts = [
            lax.dynamic_slice_in_dim(piece, (place ^ k) * size, size, dim) for piece in pending
        ]
        block = added(parts)
        after.append(send(block, axis, k) if k else block)
    return after


def gather_step(piece, axis, dim):
    return gather_last(gather_first(piece, axis), axis, dim)


def gather_early(rows):
    return lax.all_gather(rows, (OUTER, INNER), axis=0, tiled=False)


SEQ = (OUTER, INNER)


class Chain:
    def __init__(self, halves, order, small=None, doubled=False):
        self.order = (CORE,) + order
        self.doubled = doubled
        self.stage = 0
        self.tiles = halves[0].shape[0]
        self.small, self.carried = None, 0
        if small is not None:
            self.carried = small.shape[0]
            halves = [jnp.concatenate([self.flat(half), small]) for half in halves]
        self.held = [halves[0], send(halves[1], CORE, 1)]

    def flat(self, block):
        return block.reshape(-1, block.shape[-1])

    def parts(self):
        if not self.carried:
            return self.held, None
        body = [piece[: -self.carried] for piece in self.held]
        body = [piece.reshape(self.tiles, -1, piece.shape[-1]) for piece in body]
        return body, added([piece[-self.carried :] for piece in self.held])

    def next_axis(self):
        stage, count = self.stage + 1, len(self.order)
        return self.order[stage] if stage < count else self.order[2 * count - 1 - stage]

    def over(self):
        return self.stage == 2 * len(self.order) - 1

    def go(self):
        axis = self.next_axis()
        self.stage += 1
        count = len(self.order)
        if self.doubled and self.stage in (count - 1, count):
            total = added(self.held)
            self.held = [total, send(total, OUTER, self.stage - count + 2)]
            return
        if self.doubled and self.stage == count + 1:
            pending, self.small = self.parts()
            self.held = gather_first(added(pending), axis)
            return
        if self.stage < count:
            pending, small = self.parts()
            place, members = lax.axis_index(axis), lax.axis_size(axis)
            size = pending[0].shape[1] // members
            self.held = []
            for k in range(members):
                begin = (place ^ k) * size
                block = added([lax.dynamic_slice_in_dim(p, begin, size, 1) for p in pending])
                if small is not None:
                    block = jnp.concatenate([self.flat(block), small])
                self.held.append(send(block, axis, k) if k else block)
            return
        if self.stage == count:
            pending, self.small = self.parts()
            piece = added(pending)
        else:
            piece = gather_last(self.held, self.order[2 * count - self.stage], 1)
        self.held = gather_first(piece, axis)

    def volume(self):
        return self.held[0].size * 2 / 2**20


class Spread:
    def __init__(self, part, straight):
        self.straight, self.stage = straight, 0
        self.held = [send(rows, INNER, k) if k else rows for k, rows in enumerate(part)]

    def next_axis(self):
        return OUTER

    def over(self):
        return self.stage == (1 if self.straight else 2)

    def go(self):
        self.stage += 1
        if self.straight:
            blocks = [added([piece[k] for piece in self.held]) for k in range(4)]
            self.held = [send(block, OUTER, k) if k else block for k, block in enumerate(blocks)]
            return
        if self.stage == 1:
            pick, offset = (lambda piece, odd: jnp.stack([piece[odd], piece[2 + odd]])), 1
        else:
            pick, offset = (lambda piece, odd: piece[odd]), 2
        mine, theirs = [added([pick(piece, odd) for piece in self.held]) for odd in (0, 1)]
        self.held = [mine, send(theirs, OUTER, offset)]

    def volume(self):
        return self.held[0].size * 2 / 2**20

    def result(self):
        return added(self.held)


def finish(chains, *tokens):
    held, _ = lax.optimization_barrier(([chain.held for chain in chains], tokens))
    for chain, pieces in zip(chains, held):
        chain.held = pieces


def go(*chains):
    for chain in chains:
        chain.go()


FLOW = {CORE: 3.5, X: 21.0, INNER: 21.0, OUTER: 84.0}


def plan_of(chain):
    if isinstance(chain, Spread):
        return [(INNER, 21.0, 1), (OUTER, 10.5, 1), (OUTER, 10.5, 1)][chain.stage :]
    size, out = chain.tiles * 0.5, []
    for axis in chain.order:
        count = lax.axis_size(axis)
        if axis == OUTER and chain.doubled:
            out += [(OUTER, 21.0 * size, 1), (OUTER, 42.0 * size, 1)]
            continue
        size = size / count
        out.append((axis, FLOW[axis] * size, count - 1))
    back = [entry for entry in reversed(out)]
    if chain.doubled:
        back = [entry for entry in back if entry[0] != OUTER]
    return (out + back)[chain.stage :]


def rehearse(plans, first, gate, weights, slack):
    free = dict.fromkeys(FLOW, 0.0)
    position, queue, order, clock, waiting = [0] * len(plans), [], [], 0.0, []

    def depart(index, when):
        axis, long, _ = plans[index][position[index]]
        begin = max(when, free[axis])
        free[axis] = begin + long
        queue.append((free[axis] + 6.0, index))

    def left(index):
        rest = plans[index][position[index] :]
        return weights[index] * sum(long + 10.0 for _, long, _ in rest)

    for index, since in first:
        depart(index, -since)
    while queue or waiting:
        soon = min(queue)[0] if queue else clock + 99.0
        if waiting and soon > clock + 4.0:
            clock += 6.5
            order.append((waiting.pop(0), True))
            continue
        near = [entry for entry in queue if entry[0] <= max(clock, soon) + slack]
        entry = max(near, key=lambda entry: left(entry[1]))
        queue.remove(entry)
        arrival, index = entry
        clock = max(clock, arrival)
        position[index] += 1
        order.append((index, False))
        if position[index] == len(plans[index]):
            clock += 1.0
            waiting.append(index)
            continue
        axis, long, sends = plans[index][position[index]]
        clock += 2.0 + 1.5 * sends + 0.03 * long
        depart(index, clock)
        if gate[1] == index and position[index] == 1:
            clock += 2.0
            depart(gate[0], clock)
    return clock, order


def run_out(flights, later):
    chains, ends = [chain for chain, _, _ in flights], [end for _, _, end in flights]
    plans = [plan_of(chain) for chain in chains]
    plans.append([(INNER, 21.0, 1), (OUTER, 10.5, 1), (OUTER, 10.5, 1)])
    first = [(index, since) for index, (_, since, _) in enumerate(flights)]
    rng, best = random.Random(7), None
    for trial in range(1500):
        weights = [1.0 if trial < 4 else rng.uniform(0.3, 2.0) for _ in plans]
        slack = (0.0, 2.0, 4.0, 8.0)[trial % 4]
        found = rehearse(plans, first, (len(chains), 0), weights, slack)
        if best is None or found[0] < best[0]:
            best = found
    token, results = (), {}
    for index, is_end in best[1]:
        chain = chains[index]
        if is_end:
            results[index] = ends[index](chain, token)
            token = (results[index][0],)
            continue
        finish([chain], *token)
        if chain.over():
            token = tuple(chain.held)
            continue
        chain.go()
        token = (chain.held[0],)
        if index == 0 and chain.stage == 1:
            chain, _, end = later(token)
            chains.append(chain)
            ends.append(end)
    return [results[index] for index in range(len(chains))]


def assemble(chain, core_info, shapes, after=()):
    tiles, half, side = chain.held[0].shape

    places = []
    for name, shape in shapes.items():
        blocks = shape[0] if len(shape) > 2 else shape[0] * shape[1] // (side * side)
        for block in range(blocks):
            if len(shape) > 2:
                places.append((name, lambda rows, b=block: (b, rows, slice(None))))
            elif shape[1] > shape[0]:
                lanes = slice(block * side, (block + 1) * side)
                places.append((name, lambda rows, l=lanes: (rows, l)))
            else:
                places.append((name, lambda rows, b=block: (pl.ds(rows.start + b * side, half), slice(None))))

    def body(info, mine, other, *refs):
        outs = dict(zip(shapes, refs))
        room, full, come, go = refs[len(shapes) :]
        starts = [pl.multiple_of((info[0] ^ flip) * half, half) for flip in (0, 1)]
        arrive, leave = [], []
        for tile in range(tiles):
            for flip, source in enumerate((mine, other)):
                index = 2 * tile + flip
                arrive.append(pltpu.make_async_copy(source.at[tile], room.at[index], come.at[index]))
                arrive[-1].start()
        for tile, (name, where) in enumerate(places):
            for flip in (0, 1):
                index = 2 * tile + flip
                arrive[index].wait()
                full[index] = room[index].astype(F32)
                target = outs[name].at[where(pl.ds(starts[flip], half))]
                leave.append(pltpu.make_async_copy(full.at[index], target, go.at[index]))
                leave[-1].start()
        for copy in leave:
            copy.wait()

    far = pl.BlockSpec(memory_space=pl.ANY)
    return pl.pallas_call(
        lambda info, mine, other, *refs: body(info, mine, other, *refs[len(after) :]),
        in_specs=[pl.BlockSpec(memory_space=pltpu.SMEM)] + [far] * (2 + len(after)),
        out_specs=[far] * len(shapes),
        out_shape=[jax.ShapeDtypeStruct(shape, F32) for shape in shapes.values()],
        scratch_shapes=[
            pltpu.VMEM((2 * tiles, half, side), BF16),
            pltpu.VMEM((2 * tiles, half, side), F32),
            pltpu.SemaphoreType.DMA((2 * tiles,)),
            pltpu.SemaphoreType.DMA((2 * tiles,)),
        ],
        compiler_params=pltpu.CompilerParams(vmem_limit_bytes=VMEM_LIMIT),
        cost_estimate=pl.CostEstimate(flops=5 * 10**9, bytes_accessed=2 * 10**7, transcendentals=0),
    )(core_info, chain.held[0], chain.held[1], *after)


def shards(
    source_short,
    target_short,
    source_segment,
    target_segment,
    source_long,
    target_long,
    source_length,
    target_length,
    cotangent_short,
    cotangent_long,
    encoder_project,
    encoder_output,
    encoder_up,
    encoder_down,
    encoder_gain,
    encoder_bias,
    decoder_project,
    decoder_output,
    cross_project,
    cross_output,
    decoder_up,
    decoder_down,
    decoder_gain,
    decoder_bias,
):
    blocks, size, width = source_short.shape
    hidden = encoder_up.shape[1]
    rows = blocks * size
    pairs, own, _ = source_long.shape
    rows_long = pairs * own
    flat = lambda a: a.reshape(-1, width)
    start = lax.axis_index((OUTER, INNER)) * own
    core = lax.axis_index(CORE)
    here = [start, lax.axis_index(INNER), core, lax.axis_index(OUTER)]
    here = jnp.stack(here).astype(jnp.int32)
    info_of = lambda lengths: jnp.concatenate([lengths, here])
    core_info = core.astype(jnp.int32)[None]
    source_info, target_info = info_of(source_length), info_of(target_length)

    spread = lambda s: jnp.broadcast_to(s[:, :, None], (blocks, size, size))
    line = lambda s: s[:, None, :]
    encoder_in = {
        "w_in": encoder_project,
        "w_o": encoder_output,
        "up": encoder_up,
        "down": encoder_down,
        "gain": encoder_gain,
        "bias": encoder_bias,
    }
    decoder_in = {
        "w_in": decoder_project,
        "w_o": decoder_output,
        "w_cin": cross_project,
        "w_co": cross_output,
        "up": decoder_up,
        "down": decoder_down,
        "gain": decoder_gain,
        "bias": decoder_bias,
    }

    def pick(table, names):
        return {name: table[name] for name in names}

    def rows_of(n, names):
        return {name: ((n, width), BF16) for name in names}

    def wide_of(n, names):
        return {name: ((n, hidden), BF16) for name in names}

    def floats(n, names):
        return {name: ((n, width), F32) for name in names}

    def column(n, names):
        return {name: ((n, 1), F32) for name in names}

    def logs(n, names):
        return {name: ((n, HEADS, size), F32) for name in names}

    def sums(n):
        return {"small": ((n, width), F32)}

    def keys_of(names):
        shape = (places, pairs, own, width)
        return {name: (shape, BF16) for name in names}

    def parts():
        inner = lax.axis_size(INNER)
        return {"p%d" % k: ((places // inner, pairs, own, width), BF16) for k in range(inner)}

    def saved(kernel, names):
        return {name: kernel[name] for name in names}

    whole_source = gather_early(source_long)
    early_target = gather_first(target_long[None, None], OUTER)
    places = lax.axis_size(OUTER) * lax.axis_size(INNER)
    keys = places * own
    work = [
        ("s", pltpu.VMEM((PAIRS, keys, 2 * own), F32)),
        ("a", pltpu.VMEM((PAIRS, 8, 2 * own), F32)),
        ("mix", pltpu.VMEM((PAIRS, PAIR, 2 * own), F32)),
    ]
    mix = work[2:]

    segments = {"kseg": spread(source_segment), "qseg": line(source_segment)}
    turned = {"tkseg": spread(target_segment), "tqseg": line(target_segment)}
    encoder_keeps = lambda n: {
        **rows_of(n, ("n1", "y", "n2", "enc")),
        **wide_of(n, ("act", "gate")),
        **column(n, ("i1", "i2")),
    }
    se = launch(
        short_encoder_forward,
        {"x": flat(source_short), **segments, **encoder_in},
        {**rows_of(rows, ("q", "k", "v", "o")), **logs(blocks, ("lse",)), **encoder_keeps(rows)},
        cost=0.01,
    )
    decoder_keeps = lambda n: {
        **rows_of(n, ("m", "b5", "b4", "go_c")),
        **wide_of(n, ("act", "gate", "dh")),
        **floats(n, ("final", "d4")),
        **sums(4),
    }
    sd = launch(
        short_decoder_forward,
        {
            "t": flat(target_short),
            **turned,
            **pick(decoder_in, ("w_in", "w_o", "gain", "bias")),
        },
        {
            **rows_of(rows, ("q", "k", "v", "o", "n3", "u")),
            **logs(blocks, ("lse",)),
            **column(rows, ("i3",)),
            **floats(rows, ("upper",)),
        },
        after=(se.lse,),
        cost=0.01,
    )
    sc = launch(
        short_cross_forward,
        {
            "u": sd.u,
            "upper": sd.upper,
            "enc": se.enc,
            "cot": flat(cotangent_short),
            "kseg": segments["kseg"],
            "tqseg": turned["tqseg"],
            **pick(decoder_in, ("w_cin", "w_co", "up", "down", "gain", "bias")),
        },
        {
            **rows_of(rows, ("q_c", "k_c", "v_c", "o_c")),
            **logs(blocks, ("lse_c",)),
            **decoder_keeps(rows),
        },
        after=(sd.lse,),
        cost=0.01,
    )

    sb = launch(
        short_decoder_back,
        {
            **saved(sd, ("q", "k", "v", "o", "lse", "n3", "i3")),
            **saved(sc, ("q_c", "k_c", "v_c", "o_c", "lse_c", "go_c", "d4")),
            "kseg": segments["kseg"],
            **turned,
            **pick(decoder_in, ("w_in", "w_o", "w_cin", "gain")),
        },
        {
            **rows_of(rows, ("dq_c", "dk_c", "dv_c", "dq", "dk", "dv", "b3", "go")),
            **floats(rows, ("denc", "dt")),
            **sums(2),
        },
        scratch=[("d3", pltpu.VMEM((rows, width), F32))],
        after=(sc.small,),
        cost=0.01,
    )

    early_target = gather_last(early_target, OUTER, 0, sb.small)

    whole_source = hold(whole_source, sb.small)
    x_long, t_long = flat(source_long), flat(target_long)
    le = launch(
        long_encoder_forward,
        {"x": x_long, "xg": whole_source, **encoder_in},
        {
            **rows_of(rows_long, ("q", "o")),
            **keys_of(("k", "v")),
            **logs(pairs, ("lse",)),
            **encoder_keeps(rows_long),
        },
        scratch=work + [("acc", pltpu.VMEM((rows_long, width), F32))],
        info=source_info,
        after=(sb.small, early_target),
        cost=13,
        moved=(),
    )
    late_target = gather_first(hold(early_target, le.lse), INNER)
    whole_encoded = gather_early(le.enc.reshape(pairs, own, width))

    seb = launch(
        short_encoder_back,
        {
            "denc": sb.denc,
            **saved(se, ("q", "k", "v", "o", "lse", "n1", "i1", "n2", "i2", "gate")),
            **segments,
            **pick(encoder_in, ("w_in", "w_o", "up", "down", "gain")),
        },
        {
            **rows_of(rows, ("dq", "dk", "dv", "b1", "b2", "go")),
            **wide_of(rows, ("dh",)),
            **floats(rows, ("dx",)),
            **sums(4),
        },
        scratch=[("d1", pltpu.VMEM((rows, width), F32))],
        after=(le.lse,),
        cost=16,
    )

    t_short, x_short = flat(target_short), flat(source_short)
    short_weights = whole_tiles(
        [
            [(sc.m, sc.dh), (sc.act, sc.b5)],
            [
                (sd.u, sb.dq_c),
                (se.enc, sb.dk_c),
                (se.enc, sb.dv_c),
                (sc.o_c, sc.b4),
                (t_short, sb.dq),
                (t_short, sb.dk),
                (t_short, sb.dv),
                (sd.o, sb.b3),
            ],
            [(se.y, seb.dh), (se.act, seb.b2)],
            [(x_short, seb.dq), (x_short, seb.dk), (x_short, seb.dv), (se.o, seb.b1)],
        ],
        after=(seb.small,),
        cost=15,
    )
    whole_target = gather_last(late_target, INNER, 1, short_weights[0])
    whole_target = whole_target.reshape(places, pairs, own, width)
    ls = launch(
        long_self_forward,
        {
            "t": t_long,
            "tg": whole_target,
            **pick(decoder_in, ("w_in", "w_o", "w_cin", "gain", "bias")),
        },
        {
            **rows_of(rows_long, ("q", "o", "n3", "u", "q_c")),
            **keys_of(("k", "v")),
            **logs(pairs, ("lse",)),
            **column(rows_long, ("i3",)),
            **floats(rows_long, ("upper",)),
        },
        scratch=work,
        info=target_info,
        after=(short_weights[0],),
        cost=10,
        moved=(),
    )

    whole_encoded = hold(whole_encoded, ls.lse)
    lc = launch(
        long_cross,
        {
            "eg": whole_encoded,
            "upper": ls.upper,
            "q_c": ls.q_c,
            "cot": flat(cotangent_long),
            **pick(decoder_in, ("w_cin", "w_co", "up", "down", "gain", "bias")),
        },
        {
            **rows_of(rows_long, ("o_c",)),
            **keys_of(("k_c", "v_c")),
            **logs(pairs, ("lse_c",)),
            **decoder_keeps(rows_long),
        },
        scratch=work,
        info=source_info,
        after=(ls.lse,),
        cost=14,
        moved=("k_c", "v_c", "up", "down", "w_co", "act", "gate", "dh", "final"),
    )
    lcb = launch(
        long_cross_back,
        {
            "q_c": ls.q_c,
            **saved(lc, ("k_c", "v_c", "o_c", "lse_c", "go_c")),
            **pick(decoder_in, ("w_cin",)),
        },
        {**rows_of(rows_long, ("dq_c",)), **keys_of(("dk_c", "dv_c")), **parts()},
        scratch=mix,
        info=source_info,
        after=(lc.small,),
        cost=14,
        moved=(),
    )
    encoded_back = Spread(part_refs(lcb), True)
    first_weights = Weights(
        [[(lc.m, lc.dh)], [(lc.act, lc.b5)]], short_weights[0]
    )

    def self_back_and_weights(r):
        long_self_back(r)
        first_weights.body(r, r.info[pairs + 2])

    lsb = launch(
        self_back_and_weights,
        {
            "d4": lc.d4,
            "dq_c": lcb.dq_c,
            **saved(ls, ("q", "k", "v", "o", "lse", "n3", "i3")),
            **pick(decoder_in, ("w_in", "w_o", "w_cin", "gain")),
            **first_weights.arrays,
        },
        {
            **first_weights.gives,
            **rows_of(rows_long, ("dq", "b3")),
            **keys_of(("dk", "dv")),
            **parts(),
            **floats(rows_long, ("dt",)),
            **sums(2),
        },
        scratch=mix + [("go", pltpu.VMEM((rows_long, width), BF16))],
        info=target_info,
        after=(lcb.dq_c,),
        pieces=("kept", "sent"),
        cost=22,
    )
    decoder_ffn = Chain([lsb.kept, lsb.sent], (X, INNER, OUTER))
    finish([encoded_back], lsb.small)
    go(encoded_back)
    target_back = Spread(part_refs(lsb), False)
    grad_attention = weight_tiles(
        [
            [(ls.u, lcb.dq_c)],
            [(flat(whole_encoded), flat(lcb.dk_c))],
            [(flat(whole_encoded), flat(lcb.dv_c))],
            [(lc.o_c, lc.b4)],
            [(t_long, lsb.dq)],
            [(flat(whole_target), flat(lsb.dk))],
            [(flat(whole_target), flat(lsb.dv))],
            [(ls.o, lsb.b3)],
        ],
        core_info,
        after=(lsb.small, encoded_back.held[0]),
        base=short_weights[1],
        cost=15,
    )
    finish([encoded_back, decoder_ffn], grad_attention[0])
    go(decoder_ffn)
    attention = Chain(grad_attention, (INNER, X, OUTER))
    ffn_weights = Weights(
        [
            [(le.y, ("dh", hidden))],
            [(le.act, ("b2", width))],
        ],
        short_weights[2],
    )

    def encoder_back_and_weights(r):
        long_encoder_tail_back(r)
        ffn_weights.body(r, r.info[0])

    leb = launch(
        encoder_back_and_weights,
        {
            **{"part%d" % k: flat(piece) for k, piece in enumerate(encoded_back.held)},
            **saved(le, ("n1", "i1", "n2", "i2", "gate")),
            **pick(encoder_in, ("down", "up", "w_o", "gain")),
            **ffn_weights.arrays,
        },
        {
            **ffn_weights.gives,
            **rows_of(rows_long, ("b1", "b2", "go")),
            **wide_of(rows_long, ("dh",)),
            **floats(rows_long, ("d1",)),
            **sums(4),
        },
        info=core_info,
        after=(grad_attention[0], decoder_ffn.held[0]),
        pieces=("kept", "sent"),
        cost=12,
    )
    small = jnp.concatenate([seb.small + leb.small, sb.small + lsb.small, sc.small + lc.small])
    small = jnp.pad(small, ((0, 16 - small.shape[0]), (0, 0))).astype(BF16)
    finish([attention], leb.small)
    go(attention)
    encoder_ffn = Chain([leb.kept, leb.sent], (X, INNER, OUTER))
    attention_weights = Weights(
        [
            [(x_long, ("dq", width))],
            [(whole_source, ("dk", width))],
            [(whole_source, ("dv", width))],
            [(le.o, leb.b1)],
        ],
        short_weights[3],
    )

    def attention_back_and_weights(r):
        long_encoder_back(r)
        r.leave("dx", *[name for name in r if name[0] == "p" and name[1:].isdigit()])
        attention_weights.body(r, r.info[pairs + 2])

    lea = launch(
        attention_back_and_weights,
        {
            **saved(le, ("q", "k", "v")),
            "o": le.o,
            "lse": le.lse,
            **saved(leb, ("go", "d1")),
            **pick(encoder_in, ("w_in",)),
            **attention_weights.arrays,
        },
        {
            **attention_weights.gives,
            **parts(),
            **floats(rows_long, ("dx",)),
        },
        scratch=mix
        + [
            ("dq", pltpu.VMEM((rows_long, width), BF16)),
            ("dk", pltpu.VMEM((places, pairs, own, width), BF16)),
            ("dv", pltpu.VMEM((places, pairs, own, width), BF16)),
        ],
        info=source_info,
        after=(leb.small, attention.held[0]),
        pieces=("kept", "sent"),
        cost=19,
    )
    done = lea.dx
    finish([decoder_ffn, encoder_ffn, target_back], done)
    encoder = Chain([lea.kept, lea.sent], (INNER, X, OUTER), small, True)
    go(decoder_ffn, encoder_ffn, target_back)
    square = (3, width, width)
    feed = {"up": encoder_up.shape, "down": encoder_down.shape}
    one = {"project": square, "output": square[1:]}
    two = {"cross_in": square, "cross_out": square[1:], "self_in": square, "self_out": square[1:]}

    def out(shapes):
        return lambda chain, token: assemble(chain, core_info, shapes, token)

    rows_out = lambda rows: lambda chain, token: [chain.result().astype(F32) + rows]
    flights = [
        (encoder, 0.0, out(one)),
        (decoder_ffn, 0.0, out(feed)),
        (attention, 20.0, out(two)),
        (encoder_ffn, 0.0, out(feed)),
        (target_back, 0.0, rows_out(lsb.dt.reshape(source_long.shape))),
    ]

    def source_back(token):
        chain = Spread(hold(part_refs(lea), token), False)
        return chain, 0.0, rows_out(lea.dx.reshape(source_long.shape))

    results = run_out(flights, source_back)
    (encoder_in_out, encoder_out_out), (decoder_up_out, decoder_down_out) = results[:2]
    (cross_in, cross_out, self_in, self_out), (encoder_up_out, encoder_down_out) = results[2:4]
    (grad_target,), (grad_source,) = results[4:]
    small = encoder.small.astype(F32)
    return (
        sc.final.reshape(source_short.shape),
        lc.final.reshape(source_long.shape),
        seb.dx.reshape(source_short.shape),
        sb.dt.reshape(source_short.shape),
        grad_source,
        grad_target,
        encoder_in_out,
        encoder_out_out,
        encoder_up_out,
        encoder_down_out,
        small[0:2],
        small[2:4],
        self_in,
        self_out,
        cross_in,
        cross_out,
        decoder_up_out,
        decoder_down_out,
        jnp.stack([small[4], small[6], small[7]]),
        jnp.stack([small[5], small[8], small[9]]),
    )


def solution(mesh):
    group, seq = mesh.devices.shape
    fine = Mesh(
        mesh.devices.reshape(group // 2, 2, 4, seq // 4), (X, CORE, OUTER, INNER)
    )
    groups, positions = (X, CORE), (OUTER, INNER)
    blocks = P(groups + positions, None, None)
    long_rows = P(groups, positions, None)
    in_specs = (
        (blocks, blocks, P(groups + positions, None), P(groups + positions, None))
        + (long_rows, long_rows, P(groups), P(groups), blocks, long_rows)
        + (P(),) * 14
    )
    out_specs = (blocks, long_rows, blocks, blocks, long_rows, long_rows) + (P(),) * 14
    return jax.shard_map(
        shards, mesh=fine, in_specs=in_specs, out_specs=out_specs, check_vma=False
    )
```

```python
import functools
import random
import jax
import jax.numpy as jnp
from jax import lax
from jax.experimental import pallas as pl
from jax.experimental.pallas import tpu as pltpu
from jax.sharding import Mesh, PartitionSpec as P

HEADS = 8
HEAD_DIM = 64
PAIR = 2 * HEAD_DIM
PAIRS = HEADS // 2
SCALE = HEAD_DIM**-0.5
FLOOR_SCORE = -1e30
EPSILON = 1e-05
KEY_BLOCK = 512
CHUNK = 512
F32 = jnp.float32
BF16 = jnp.bfloat16
CORE, X, INNER, OUTER = "core", "x", "inner", "outer"


def nn(left, right):
    return lax.dot_general(left, right, (((1,), (0,)), ((), ())), preferred_element_type=F32)


def nt(left, right):
    return lax.dot_general(left, right, (((1,), (1,)), ((), ())), preferred_element_type=F32)


def tn(left, right):
    return lax.dot_general(left, right, (((0,), (0,)), ((), ())), preferred_element_type=F32)


def two_heads(rows):
    lane = lax.broadcasted_iota(jnp.int32, rows.shape, 1)
    zero = jnp.zeros_like(rows)
    first = jnp.where(lane < HEAD_DIM, rows, zero)
    second = jnp.where(lane < HEAD_DIM, zero, rows)
    return jnp.concatenate([first, second], axis=0)


def diagonal(product):
    half = product.shape[1] // 2
    return jnp.concatenate([product[:HEAD_DIM, :half], product[HEAD_DIM:, half:]], axis=0)


def delta_rows(grad_out, outputs):
    product = grad_out.astype(F32) * outputs.astype(F32)
    high = product.astype(BF16)
    low = (product - high.astype(F32)).astype(BF16)
    width = product.shape[1]
    head = lax.broadcasted_iota(jnp.int32, (HEADS, width), 0)
    lane = lax.broadcasted_iota(jnp.int32, (HEADS, width), 1)
    pick = jnp.where(lax.div(lane, HEAD_DIM) == head, 1.0, 0.0).astype(BF16)
    return nt(pick, high) + nt(pick, low)


def pair_row(rows, pair):
    return jnp.concatenate([rows[2 * pair : 2 * pair + 1], rows[2 * pair + 1 : 2 * pair + 2]], axis=1)


def pair_lanes(pair):
    return slice(pair * PAIR, (pair + 1) * PAIR)


def norm(residual, gain, bias):
    centred = residual - jnp.mean(residual, axis=1, keepdims=True)
    inverse = lax.rsqrt(jnp.mean(centred * centred, axis=1, keepdims=True) + EPSILON)
    normed = centred * inverse
    return normed * gain + bias, normed, inverse


def norm_back(upstream, normed, inverse, gain):
    normed = normed.astype(F32)
    scaled = upstream * gain
    grad = inverse * (
        scaled
        - jnp.mean(scaled, axis=1, keepdims=True)
        - normed * jnp.mean(scaled * normed, axis=1, keepdims=True)
    )
    return (
        grad,
        jnp.sum(upstream * normed, axis=0, keepdims=True),
        jnp.sum(upstream, axis=0, keepdims=True),
    )


def chunks(ref, axis, step):
    def body(index, carry):
        step(pl.ds(pl.multiple_of(index * CHUNK, CHUNK), CHUNK))
        return carry

    lax.fori_loop(0, ref.shape[axis] // CHUNK, body, 0)


def feed_forward_in_loop(rows, up_ref, down_ref, act_ref, gate_ref, low_ref, total_ref):
    low_ref[...] = rows.astype(BF16)
    total_ref[...] = rows

    def step(part):
        hidden = nn(low_ref[...], up_ref[:, part])
        sigmoid = 0.5 * jnp.tanh(0.5 * hidden) + 0.5
        active = hidden * sigmoid
        gate_ref[:, part] = (sigmoid + active * (1.0 - sigmoid)).astype(BF16)
        active = active.astype(BF16)
        act_ref[:, part] = active
        total_ref[...] += nn(active, down_ref[part, :])

    chunks(up_ref, 1, step)
    return total_ref[...]


def feed_forward(rows, up_ref, down_ref, act_ref, gate_ref):
    low = rows.astype(BF16)
    total = rows
    for start in range(0, up_ref.shape[1], CHUNK):
        part = slice(start, start + CHUNK)
        hidden = nn(low, up_ref[:, part])
        sigmoid = 0.5 * jnp.tanh(0.5 * hidden) + 0.5
        active = hidden * sigmoid
        gate_ref[:, part] = (sigmoid + active * (1.0 - sigmoid)).astype(BF16)
        active = active.astype(BF16)
        act_ref[:, part] = active
        total = total + nn(active, down_ref[part, :])
    return low, total


def feed_back(grad, gate_ref, up_ref, down_ref, hidden_grad_ref):
    low = grad.astype(BF16)
    total = grad
    for start in range(0, up_ref.shape[1], CHUNK):
        part = slice(start, start + CHUNK)
        hidden = nt(low, down_ref[part, :]) * gate_ref[:, part].astype(F32)
        hidden = hidden.astype(BF16)
        hidden_grad_ref[:, part] = hidden
        total = total + nt(hidden, up_ref[:, part])
    return low, total


def short_allowed(key_segment, query_segment, causal):
    allowed = key_segment == query_segment
    if causal:
        key = lax.broadcasted_iota(jnp.int32, key_segment.shape, 0)
        query = lax.broadcasted_iota(jnp.int32, key_segment.shape, 1)
        allowed = allowed & (key <= query)
    return jnp.concatenate([allowed, allowed], axis=1)


def short_attend(causal, q_ref, k_ref, v_ref, kseg_ref, qseg_ref, o_ref, lse_ref):
    size = kseg_ref.shape[1]
    for block in range(kseg_ref.shape[0]):
        rows = slice(block * size, (block + 1) * size)
        allowed = short_allowed(kseg_ref[block], qseg_ref[block], causal)
        logs = []
        for pair in range(PAIRS):
            lanes = pair_lanes(pair)
            scores = nt(k_ref[rows, lanes], two_heads(q_ref[rows, lanes]))
            scores = jnp.where(allowed, scores, FLOOR_SCORE)
            top = jnp.max(scores, axis=0, keepdims=True)
            weights = jnp.exp(scores - top)
            total = jnp.sum(weights, axis=0, keepdims=True)
            mixed = nn(v_ref[rows, lanes].T, weights.astype(BF16)) / total
            o_ref[rows, lanes] = diagonal(mixed).T.astype(BF16)
            log_total = top + jnp.log(total)
            logs += [log_total[:, :size], log_total[:, size:]]
        lse_ref[block] = jnp.concatenate(logs, axis=0)


def short_attend_back(
    causal, q_ref, k_ref, v_ref, kseg_ref, qseg_ref, o_ref, lse_ref, go_ref, dq_ref, dk_ref, dv_ref
):
    size = kseg_ref.shape[1]
    for block in range(kseg_ref.shape[0]):
        rows = slice(block * size, (block + 1) * size)
        allowed = short_allowed(kseg_ref[block], qseg_ref[block], causal)
        delta = delta_rows(go_ref[rows, :], o_ref[rows, :])
        lse = lse_ref[block]
        for pair in range(PAIRS):
            lanes = pair_lanes(pair)
            queries, grads = two_heads(q_ref[rows, lanes]), two_heads(go_ref[rows, lanes])
            scores = nt(k_ref[rows, lanes], queries)
            weights = jnp.where(allowed, jnp.exp(scores - pair_row(lse, pair)), 0.0)
            grad_weights = nt(v_ref[rows, lanes], grads)
            grad_scores = (weights * (grad_weights - pair_row(delta, pair))).astype(BF16)
            dv_ref[rows, lanes] = nn(weights.astype(BF16), grads).astype(BF16)
            dk_ref[rows, lanes] = nn(grad_scores, queries).astype(BF16)
            turned = diagonal(nn(k_ref[rows, lanes].T, grad_scores)).T
            dq_ref[rows, lanes] = (turned.astype(BF16).astype(F32) * SCALE).astype(BF16)


def load_keys(ref, pair_index, block, lanes):
    pieces = KEY_BLOCK // ref.shape[2]
    rows = ref[pl.ds(block * pieces, pieces), pair_index, :, lanes]
    return rows.reshape(KEY_BLOCK, rows.shape[2])


def store_keys(ref, pair_index, block, lanes, rows):
    pieces = KEY_BLOCK // ref.shape[2]
    ref[pl.ds(block * pieces, pieces), pair_index, :, lanes] = rows.astype(BF16).reshape(
        pieces, ref.shape[2], rows.shape[1]
    )


def store_part(refs, info_ref, pair_index, block, rows):
    partners, (_, pairs, size, _) = len(refs), refs[0].shape
    if partners == 2:
        swap = info_ref[pairs + 1] == 1
        count = KEY_BLOCK // (2 * size)
        for piece in range(count):
            outer = (block * count + piece) ^ info_ref[pairs + 3]
            begin = 2 * piece * size
            first, second = rows[begin : begin + size], rows[begin + size : begin + 2 * size]
            refs[0][outer, pair_index] = jnp.where(swap, second, first)
            refs[1][outer, pair_index] = jnp.where(swap, first, second)
        return
    for piece in range(KEY_BLOCK // size):
        place = block * (KEY_BLOCK // size) + piece
        inner = lax.rem(place, partners) ^ info_ref[pairs + 1]
        outer = lax.div(place, partners) ^ info_ref[pairs + 3]
        part = rows[piece * size : (piece + 1) * size]
        for partner, ref in enumerate(refs):

            @pl.when(inner == partner)
            def _(ref=ref):
                ref[outer, pair_index] = part


def long_limit(info_ref, causal, pair_index, size, pairs):
    length = info_ref[pair_index]
    limit = length
    if causal:
        limit = jnp.minimum(length, info_ref[pairs] + size)
    return length, lax.div(limit + KEY_BLOCK - 1, KEY_BLOCK)


def long_allowed(start, causal, length, block, shape):
    key = lax.broadcasted_iota(jnp.int32, shape, 0) + block * KEY_BLOCK
    allowed = key < length
    if causal:
        half = shape[1] // 2
        lane = lax.broadcasted_iota(jnp.int32, shape, 1)
        query = jnp.where(lane < half, lane, lane - half) + start
        allowed = allowed & (key <= query)
    return allowed


def long_attend(
    causal, info_ref, q_ref, x_ref, k_w, v_w, k_ref, v_ref, o_ref, lse_ref, score_ref, sum_ref, mix_ref
):
    places, pairs, size, width = x_ref.shape
    shape = (KEY_BLOCK, 2 * size)
    everything = slice(None)

    def one(pair_index, carry):
        length, count = long_limit(info_ref, causal, pair_index, size, pairs)
        own = pl.ds(pl.multiple_of(pair_index * size, size), size)

        def first(block, tops):
            rows = pl.ds(pl.multiple_of(block * KEY_BLOCK, KEY_BLOCK), KEY_BLOCK)
            allowed = long_allowed(info_ref[pairs], causal, length, block, shape)
            context = load_keys(x_ref, pair_index, block, everything)
            store_keys(k_ref, pair_index, block, everything, nn(context, k_w[...]))
            store_keys(v_ref, pair_index, block, everything, nn(context, v_w[...]))
            after = []
            for pair in range(PAIRS):
                lanes = pair_lanes(pair)
                keys = load_keys(k_ref, pair_index, block, lanes)
                scores = nt(keys, two_heads(q_ref[own, lanes]))
                scores = jnp.where(allowed, scores, FLOOR_SCORE)
                score_ref[pair, rows] = scores
                folded = jnp.max(scores.reshape(KEY_BLOCK // 8, 8, 2 * size), axis=0)
                after.append(jnp.maximum(tops[pair], folded))
            return tuple(after)

        start = tuple(jnp.full((8, 2 * size), FLOOR_SCORE, F32) for _ in range(PAIRS))
        tops = lax.fori_loop(0, count, first, start)
        tops = [jnp.max(top, axis=0, keepdims=True) for top in tops]
        sum_ref[...] = jnp.zeros_like(sum_ref)
        mix_ref[...] = jnp.zeros_like(mix_ref)

        def second(block, carry):
            rows = pl.ds(pl.multiple_of(block * KEY_BLOCK, KEY_BLOCK), KEY_BLOCK)
            for pair in range(PAIRS):
                weights = jnp.exp(score_ref[pair, rows] - tops[pair])
                sum_ref[pair] += jnp.sum(weights.reshape(KEY_BLOCK // 8, 8, 2 * size), axis=0)
                values = load_keys(v_ref, pair_index, block, pair_lanes(pair))
                mix_ref[pair] += nn(values.T, weights.astype(BF16))
            return carry

        lax.fori_loop(0, count, second, 0)
        logs = []
        for pair in range(PAIRS):
            total = jnp.sum(sum_ref[pair], axis=0, keepdims=True)
            mixed = mix_ref[pair] / total
            o_ref[own, pair_lanes(pair)] = diagonal(mixed).T.astype(BF16)
            log_total = tops[pair] + jnp.log(total)
            logs += [log_total[:, :size], log_total[:, size:]]
        lse_ref[pair_index] = jnp.concatenate(logs, axis=0)
        return carry

    lax.fori_loop(0, pairs, one, 0)


def long_attend_back(
    causal,
    info_ref,
    q_ref,
    k_ref,
    v_ref,
    o_ref,
    lse_ref,
    go_ref,
    k_w,
    v_w,
    dq_ref,
    dk_ref,
    dv_ref,
    part_ref,
    mix_ref,
):
    places, pairs, size, width = k_ref.shape
    shape = (KEY_BLOCK, 2 * size)
    everything = slice(None)

    def one(pair_index, carry):
        length, count = long_limit(info_ref, causal, pair_index, size, pairs)
        own = pl.ds(pl.multiple_of(pair_index * size, size), size)
        delta = delta_rows(go_ref[own, :], o_ref[own, :])
        lse = lse_ref[pair_index]
        mix_ref[...] = jnp.zeros_like(mix_ref)

        def step(block, carry):
            allowed = long_allowed(info_ref[pairs], causal, length, block, shape)
            for pair in range(PAIRS):
                lanes = pair_lanes(pair)
                queries, grads = two_heads(q_ref[own, lanes]), two_heads(go_ref[own, lanes])
                keys = load_keys(k_ref, pair_index, block, lanes)
                scores = nt(keys, queries)
                weights = jnp.where(allowed, jnp.exp(scores - pair_row(lse, pair)), 0.0)
                grad_weights = nt(load_keys(v_ref, pair_index, block, lanes), grads)
                grad_scores = (weights * (grad_weights - pair_row(delta, pair))).astype(BF16)
                store_keys(dv_ref, pair_index, block, lanes, nn(weights.astype(BF16), grads))
                store_keys(dk_ref, pair_index, block, lanes, nn(grad_scores, queries))
                mix_ref[pair] += nn(keys.T, grad_scores)
            part = nt(load_keys(dk_ref, pair_index, block, everything), k_w[...])
            part = part + nt(load_keys(dv_ref, pair_index, block, everything), v_w[...])
            store_part(part_ref, info_ref, pair_index, block, part.astype(BF16))
            return carry

        lax.fori_loop(0, count, step, 0)

        def clear(block, carry):
            nothing = jnp.zeros((KEY_BLOCK, width), BF16)
            store_keys(dk_ref, pair_index, block, everything, nothing)
            store_keys(dv_ref, pair_index, block, everything, nothing)
            store_part(part_ref, info_ref, pair_index, block, nothing)
            return carry

        lax.fori_loop(count, places * size // KEY_BLOCK, clear, 0)
        for pair in range(PAIRS):
            turned = diagonal(mix_ref[pair]).T
            dq_ref[own, pair_lanes(pair)] = (turned.astype(BF16).astype(F32) * SCALE).astype(BF16)
        return carry

    lax.fori_loop(0, pairs, one, 0)


class Refs(dict):
    def __init__(self, *args):
        super().__init__(*args)
        self.coming, self.leaving, self.pieced = {}, {}, {}

    def __getattr__(self, name):
        if name in self.coming:
            self.coming.pop(name).wait()
        return self[name]

    def leave_piece(self, name, piece):
        source, target, signals, first = self.pieced[name]
        pltpu.make_async_copy(source.at[piece], target.at[piece], signals.at[first + piece]).start()

    def leave(self, *names):
        for name in names:
            self["left"].add(name)
            for copy in self.leaving.get(name, ()):
                copy.start()


def copied(shape, dtype):
    size = dtype.itemsize
    for length in shape:
        size *= length
    return shape[-1] % 128 == 0 and size >= 2**16


def launch(body, arrays, gives, scratch=(), info=None, after=(), pieces=(), moved=None, cost=10):
    memory = pl.BlockSpec(memory_space=pltpu.VMEM)
    far = pl.BlockSpec(memory_space=pl.ANY)
    ins, specs = [], []
    if info is not None:
        ins.append(info)
        specs.append(pl.BlockSpec(memory_space=pltpu.SMEM))
    by_itself = lambda name, shape, dtype: (
        copied(shape, jnp.dtype(dtype)) if moved is None else name in moved
    )
    moved_in = [name for name, a in arrays.items() if by_itself(name, a.shape, a.dtype)]
    moved_out = [name for name, give in gives.items() if name in pieces or by_itself(name, *give)]
    for name, array in arrays.items():
        ins.append(array)
        specs.append(far if name in moved_in else memory)
    for array in after:
        ins.append(array)
        specs.append(far)
    count_out = sum(gives[name][0][0] if name in pieces else 1 for name in moved_out)
    rooms = [pltpu.VMEM(arrays[name].shape, arrays[name].dtype) for name in moved_in]
    rooms += [pltpu.VMEM(*gives[name]) for name in moved_out]
    rooms += [pltpu.SemaphoreType.DMA((max(len(moved_in), 1),))]
    rooms += [pltpu.SemaphoreType.DMA((max(count_out, 1),))]
    names = [name for name, _ in scratch]

    def run(*refs):
        refs = list(refs)
        r = Refs()
        if info is not None:
            r["info"] = refs.pop(0)
        outer = {name: refs.pop(0) for name in arrays}
        del refs[: len(after)]
        outer.update((name, refs.pop(0)) for name in gives)
        room = {name: refs.pop(0) for name in moved_in + moved_out}
        come, go = refs.pop(0), refs.pop(0)
        r.update(outer)
        r.update(room)
        r.update(zip(names, refs))
        for place, name in enumerate(moved_in):
            copy = pltpu.make_async_copy(outer[name], room[name], come.at[place])
            copy.start()
            r.coming[name] = copy
        place = 0
        for name in moved_out:
            copies = []
            if name in pieces:
                r.pieced[name] = (room[name], outer[name], go, place)
                for piece in range(gives[name][0][0]):
                    source, target = room[name].at[piece], outer[name].at[piece]
                    copies.append(pltpu.make_async_copy(source, target, go.at[place]))
                    place += 1
            else:
                copies.append(pltpu.make_async_copy(room[name], outer[name], go.at[place]))
                place += 1
            r.leaving[name] = copies
        left = set()
        r["left"] = left
        body(r)
        for name in list(r.coming):
            r.coming.pop(name).wait()
        for name in moved_out:
            if name not in left and name not in pieces:
                r.leave(name)
        for name in moved_out:
            for copy in r.leaving[name]:
                copy.wait()

    out = pl.pallas_call(
        run,
        in_specs=specs,
        out_specs=[far if name in moved_out else memory for name in gives],
        out_shape=[jax.ShapeDtypeStruct(shape, dtype) for shape, dtype in gives.values()],
        scratch_shapes=rooms + [shape for _, shape in scratch],
        compiler_params=pltpu.CompilerParams(vmem_limit_bytes=VMEM_LIMIT),
        cost_estimate=pl.CostEstimate(
            flops=int(cost * 1.1e9), bytes_accessed=int(cost * 3.5e6), transcendentals=0
        ),
    )(*ins)
    return Refs(zip(gives, out))


VMEM_LIMIT = 56 * 2**20


def add_sums(ref, rows):
    ref[...] = jnp.concatenate(rows, axis=0)


def encoder_tail(r, o_ref):
    residual = r.x[...].astype(F32) + nn(o_ref[...], r.w_o[...])
    first, normed, inverse = norm(residual, r.gain[0:1], r.bias[0:1])
    r.n1[...] = normed.astype(BF16)
    r.i1[...] = inverse
    if "acc" in r:
        total = feed_forward_in_loop(first, r.up, r.down, r.act, r.gate, r.y, r.acc)
    else:
        r.y[...], total = feed_forward(first, r.up, r.down, r.act, r.gate)
    r.leave("n1", "act", "gate", "y")
    encoded, normed, inverse = norm(total, r.gain[1:2], r.bias[1:2])
    r.n2[...] = normed.astype(BF16)
    r.i2[...] = inverse
    r.enc[...] = encoded.astype(BF16)


def project_short(r, name, rows, w_q, w_k, w_v, context=None):
    context = rows if context is None else context
    r["q" + name][...] = (nn(rows, w_q) * SCALE).astype(BF16)
    r["k" + name][...] = nn(context, w_k).astype(BF16)
    r["v" + name][...] = nn(context, w_v).astype(BF16)


def short_encoder_forward(r):
    project_short(r, "", r.x[...], r.w_in[0], r.w_in[1], r.w_in[2])
    r.leave("q", "k", "v")
    short_attend(False, r.q, r.k, r.v, r.kseg, r.qseg, r.o, r.lse)
    r.leave("o")
    encoder_tail(r, r.o)


def decoder_middle(r, o_ref):
    residual = r.t[...].astype(F32) + nn(o_ref[...], r.w_o[...])
    upper, normed, inverse = norm(residual, r.gain[0:1], r.bias[0:1])
    r.n3[...] = normed.astype(BF16)
    r.i3[...] = inverse
    r.u[...] = upper.astype(BF16)
    return upper


def decoder_tail(r, upper, o_ref):
    gain, bias = r.gain, r.bias
    residual = upper + nn(o_ref[...], r.w_co[...])
    middle, normed4, inverse4 = norm(residual, gain[1:2], bias[1:2])
    r.m[...], total = feed_forward(middle, r.up, r.down, r.act, r.gate)
    r.leave("m", "act", "gate")
    final, normed5, inverse5 = norm(total, gain[2:3], bias[2:3])
    r.final[...] = final
    r.leave("final")
    grad, gain5, bias5 = norm_back(r.cot[...].astype(F32), normed5, inverse5, gain[2:3])
    r.b5[...], grad = feed_back(grad, r.gate, r.up, r.down, r.dh)
    r.leave("b5", "dh")
    grad, gain4, bias4 = norm_back(grad, normed4, inverse4, gain[1:2])
    low = grad.astype(BF16)
    r.b4[...] = low
    r.d4[...] = grad
    r.go_c[...] = nt(low, r.w_co[...]).astype(BF16)
    add_sums(r.small, [gain4, gain5, bias4, bias5])


def short_decoder_forward(r):
    project_short(r, "", r.t[...], r.w_in[0], r.w_in[1], r.w_in[2])
    r.leave("q", "k", "v")
    short_attend(True, r.q, r.k, r.v, r.tkseg, r.tqseg, r.o, r.lse)
    r.leave("o")
    r.upper[...] = decoder_middle(r, r.o)


def short_cross_forward(r):
    project_short(r, "_c", r.u[...], r.w_cin[0], r.w_cin[1], r.w_cin[2], r.enc[...])
    r.leave("q_c", "k_c", "v_c")
    short_attend(False, r.q_c, r.k_c, r.v_c, r.kseg, r.tqseg, r.o_c, r.lse_c)
    r.leave("o_c")
    decoder_tail(r, r.upper[...], r.o_c)


def decoder_middle_back(r):
    grad = r.d4[...] + nt(r.dq_c[...], r.w_cin[0])
    grad, gain3, bias3 = norm_back(grad, r.n3[...], r.i3[...], r.gain[0:1])
    low = grad.astype(BF16)
    r.b3[...] = low
    r.go[...] = nt(low, r.w_o[...]).astype(BF16)
    add_sums(r.small, [gain3, bias3])
    return grad


def short_decoder_back(r):
    short_attend_back(
        False, r.q_c, r.k_c, r.v_c, r.kseg, r.tqseg, r.o_c, r.lse_c, r.go_c, r.dq_c, r.dk_c, r.dv_c
    )
    r.denc[...] = nt(r.dk_c[...], r.w_cin[1]) + nt(r.dv_c[...], r.w_cin[2])
    r.leave("dq_c", "dk_c", "dv_c", "denc")
    r.d3[...] = decoder_middle_back(r)
    short_attend_back(
        True, r.q, r.k, r.v, r.tkseg, r.tqseg, r.o, r.lse, r.go, r.dq, r.dk, r.dv
    )
    r.leave("dq", "dk", "dv")
    grad = r.d3[...] + nt(r.dq[...], r.w_in[0])
    r.dt[...] = grad + nt(r.dk[...], r.w_in[1]) + nt(r.dv[...], r.w_in[2])


def encoder_tail_back(r, grad):
    grad, gain2, bias2 = norm_back(grad, r.n2[...], r.i2[...], r.gain[1:2])
    r.b2[...], grad = feed_back(grad, r.gate, r.up, r.down, r.dh)
    r.leave("b2", "dh")
    grad, gain1, bias1 = norm_back(grad, r.n1[...], r.i1[...], r.gain[0:1])
    low = grad.astype(BF16)
    r.b1[...] = low
    r.go[...] = nt(low, r.w_o[...]).astype(BF16)
    r.d1[...] = grad
    add_sums(r.small, [gain1, gain2, bias1, bias2])


def short_encoder_back(r):
    encoder_tail_back(r, r.denc[...])
    short_attend_back(
        False, r.q, r.k, r.v, r.kseg, r.qseg, r.o, r.lse, r.go, r.dq, r.dk, r.dv
    )
    r.leave("dq", "dk", "dv")
    grad = r.d1[...] + nt(r.dq[...], r.w_in[0])
    r.dx[...] = grad + nt(r.dk[...], r.w_in[1]) + nt(r.dv[...], r.w_in[2])


def long_encoder_forward(r):
    r.q[...] = (nn(r.x[...], r.w_in[0]) * SCALE).astype(BF16)
    long_attend(
        False, r.info, r.q, r.xg, r.w_in.at[1], r.w_in.at[2], r.k, r.v, r.o, r.lse, r.s, r.a, r.mix
    )
    r.leave("q", "k", "v", "o")
    encoder_tail(r, r.o)


def long_self_forward(r):
    r.q[...] = (nn(r.t[...], r.w_in[0]) * SCALE).astype(BF16)
    long_attend(
        True, r.info, r.q, r.tg, r.w_in.at[1], r.w_in.at[2], r.k, r.v, r.o, r.lse, r.s, r.a, r.mix
    )
    r.leave("q", "k", "v", "o")
    upper = decoder_middle(r, r.o)
    r.upper[...] = upper
    r.q_c[...] = (nn(upper.astype(BF16), r.w_cin[0]) * SCALE).astype(BF16)


def long_cross(r):
    k_w, v_w = r.w_cin.at[1], r.w_cin.at[2]
    long_attend(
        False, r.info, r.q_c, r.eg, k_w, v_w, r.k_c, r.v_c, r.o_c, r.lse_c, r.s, r.a, r.mix
    )
    r.leave("k_c", "v_c", "o_c")
    decoder_tail(r, r.upper[...], r.o_c)


def part_refs(r):
    return [r[name] for name in r if name[0] == "p" and name[1:].isdigit()]


def long_cross_back(r):
    long_attend_back(
        False,
        r.info,
        r.q_c,
        r.k_c,
        r.v_c,
        r.o_c,
        r.lse_c,
        r.go_c,
        r.w_cin.at[1],
        r.w_cin.at[2],
        r.dq_c,
        r.dk_c,
        r.dv_c,
        part_refs(r),
        r.mix,
    )


def long_self_back(r):
    grad = decoder_middle_back(r)
    long_attend_back(
        True,
        r.info,
        r.q,
        r.k,
        r.v,
        r.o,
        r.lse,
        r.go,
        r.w_in.at[1],
        r.w_in.at[2],
        r.dq,
        r.dk,
        r.dv,
        part_refs(r),
        r.mix,
    )
    r.dt[...] = grad + nt(r.dq[...], r.w_in[0])


def long_encoder_tail_back(r):
    grad = r.part0[...].astype(F32) + r.part1[...].astype(F32)
    grad = grad + r.part2[...].astype(F32) + r.part3[...].astype(F32)
    encoder_tail_back(r, grad)


def long_encoder_back(r):
    long_attend_back(
        False,
        r.info,
        r.q,
        r.k,
        r.v,
        r.o,
        r.lse,
        r.go,
        r.w_in.at[1],
        r.w_in.at[2],
        r.dq,
        r.dk,
        r.dv,
        part_refs(r),
        r.mix,
    )
    r.dx[...] = r.d1[...] + nt(r.dq[...], r.w_in[0])


SIDE = 512


class Weights:
    def __init__(self, pairs, base=None, unrolled=False):
        self.arrays, self.plan, known = {}, [], {}
        self.unrolled = unrolled

        def place(rows):
            if isinstance(rows, tuple):
                return rows
            if id(rows) not in known:
                known[id(rows)] = "w%d" % len(known)
                self.arrays[known[id(rows)]] = rows
            return known[id(rows)], rows.shape[-1]

        self.count = 0
        for terms in pairs:
            terms = [(place(a), place(b)) for a, b in terms]
            (_, height), (_, width) = terms[0]
            self.plan.append((self.count, width // SIDE, [(a[0], b[0]) for a, b in terms]))
            self.count += height // SIDE * (width // SIDE)
        self.gives = {name: ((self.count, SIDE // 2, SIDE), BF16) for name in ("kept", "sent")}
        if base is not None:
            self.arrays["base"] = base

    def each(self, r, step):
        ends = [first for first, _, _ in self.plan[1:]] + [self.count]
        for (first, across, terms), end in zip(self.plan, ends):
            terms = [(getattr(r, a), getattr(r, b)) for a, b in terms]

            if self.unrolled:
                for tile in range(first, end):
                    row, column = divmod(tile - first, across)
                    step(tile, row * SIDE, column * SIDE, terms)
                continue

            def body(tile, carry, first=first, across=across, terms=terms):
                row = pl.multiple_of(lax.div(tile - first, across) * SIDE, SIDE)
                column = pl.multiple_of(lax.rem(tile - first, across) * SIDE, SIDE)
                step(tile, row, column, terms)
                return carry

            lax.fori_loop(first, end, body, 0)

    def body(self, r, core):
        half = SIDE // 2
        if "base" in self.arrays:
            r.base

        def step(tile, row, column, terms):
            for flip, name in enumerate(("kept", "sent")):
                inside = pl.multiple_of((core ^ flip) * half, half)
                total = None
                if "base" in self.arrays:
                    total = r["base"][tile, pl.ds(inside, half), :].astype(F32)
                for left, right in terms:
                    rows = pl.ds(pl.multiple_of(row + inside, half), half)
                    across = pl.ds(column, SIDE)
                    if len(left.shape) == 4:
                        tall = left.shape[0] * left.shape[1] * left.shape[2]
                        first = left[:, :, :, rows].reshape(tall, half)
                    else:
                        first = left[:, rows]
                    if len(right.shape) == 4:
                        tall = right.shape[0] * right.shape[1] * right.shape[2]
                        product = tn(first, right[:, :, :, across].reshape(tall, SIDE))
                    else:
                        product = tn(first, right[:, across])
                    total = product if total is None else total + product
                r[name][tile] = total.astype(BF16)
                r.leave_piece(name, tile)

        self.each(r, step)


class Tagged:
    def __init__(self, r, tag):
        self.r, self.tag = r, tag

    def __getattr__(self, name):
        return getattr(self.r, name + self.tag)


def whole_tiles(chunks, after=(), cost=10):
    weights = [Weights([[pair] for pair in chunk]) for chunk in chunks]
    arrays, gives = {}, {}
    for number, part in enumerate(weights):
        gives["c%d" % number] = ((part.count, SIDE, SIDE), BF16)
        arrays.update((name + "c%d" % number, array) for name, array in part.arrays.items())

    def body(r):
        for number, part in enumerate(weights):
            tag = "c%d" % number

            def step(tile, row, column, terms, tag=tag):
                ((left, right),) = terms
                product = tn(left[:, pl.ds(row, SIDE)], right[:, pl.ds(column, SIDE)])
                r[tag][tile] = product.astype(BF16)
                r.leave_piece(tag, tile)

            part.each(Tagged(r, tag), step)

    out = launch(body, arrays, gives, after=after, pieces=tuple(gives), cost=cost)
    return list(out.values())


def weight_tiles(pairs, core_info, after=(), cost=10, base=None):
    weights = Weights(pairs, base)
    out = launch(
        lambda r: weights.body(r, r.info[0]),
        weights.arrays,
        weights.gives,
        info=core_info,
        after=after,
        pieces=("kept", "sent"),
        cost=cost,
    )
    return [out.kept, out.sent]


def send(piece, axis, offset):
    count = lax.axis_size(axis)
    return lax.ppermute(piece, axis, [(i, i ^ offset) for i in range(count)])


def ordered(pieces, place, dim):
    if len(pieces) == 1:
        return pieces[0]
    level = len(pieces) // 2
    inside = lax.rem(place, level)
    low = ordered(pieces[:level], inside, dim)
    high = ordered(pieces[level:], inside, dim)
    return jnp.where(
        place >= level, jnp.concatenate([high, low], dim), jnp.concatenate([low, high], dim)
    )


def hold(value, token):
    return lax.optimization_barrier((value, token))[0]


def gather_first(piece, axis):
    return [piece] + [send(piece, axis, k) for k in range(1, lax.axis_size(axis))]


def gather_last(pieces, axis, dim, token=None):
    if token is not None:
        pieces = hold(pieces, token)
    return ordered(pieces, lax.axis_index(axis), dim)


def added(pieces):
    total = pieces[0].astype(F32)
    for piece in pieces[1:]:
        total = total + piece.astype(F32)
    return total.astype(BF16)


def scatter_step(pending, axis, dim, token=None):
    if token is not None:
        pending = hold(pending, token)
    place, count = lax.axis_index(axis), lax.axis_size(axis)
    size = pending[0].shape[dim] // count
    after = []
    for k in range(count):
        parts = [
            lax.dynamic_slice_in_dim(piece, (place ^ k) * size, size, dim) for piece in pending
        ]
        block = added(parts)
        after.append(send(block, axis, k) if k else block)
    return after


def gather_step(piece, axis, dim):
    return gather_last(gather_first(piece, axis), axis, dim)


def gather_early(rows):
    return lax.all_gather(rows, (OUTER, INNER), axis=0, tiled=False)


SEQ = (OUTER, INNER)


class Chain:
    def __init__(self, halves, order, small=None, doubled=False):
        self.order = (CORE,) + order
        self.doubled = doubled
        self.stage = 0
        self.tiles = halves[0].shape[0]
        self.small, self.carried = None, 0
        if small is not None:
            self.carried = small.shape[0]
            halves = [jnp.concatenate([self.flat(half), small]) for half in halves]
        self.held = [halves[0], send(halves[1], CORE, 1)]

    def flat(self, block):
        return block.reshape(-1, block.shape[-1])

    def parts(self):
        if not self.carried:
            return self.held, None
        body = [piece[: -self.carried] for piece in self.held]
        body = [piece.reshape(self.tiles, -1, piece.shape[-1]) for piece in body]
        return body, added([piece[-self.carried :] for piece in self.held])

    def next_axis(self):
        stage, count = self.stage + 1, len(self.order)
        return self.order[stage] if stage < count else self.order[2 * count - 1 - stage]

    def over(self):
        return self.stage == 2 * len(self.order) - 1

    def go(self):
        axis = self.next_axis()
        self.stage += 1
        count = len(self.order)
        if self.doubled and self.stage in (count - 1, count):
            total = added(self.held)
            self.held = [total, send(total, OUTER, self.stage - count + 2)]
            return
        if self.doubled and self.stage == count + 1:
            pending, self.small = self.parts()
            self.held = gather_first(added(pending), axis)
            return
        if self.stage < count:
            pending, small = self.parts()
            place, members = lax.axis_index(axis), lax.axis_size(axis)
            size = pending[0].shape[1] // members
            self.held = []
            for k in range(members):
                begin = (place ^ k) * size
                block = added([lax.dynamic_slice_in_dim(p, begin, size, 1) for p in pending])
                if small is not None:
                    block = jnp.concatenate([self.flat(block), small])
                self.held.append(send(block, axis, k) if k else block)
            return
        if self.stage == count:
            pending, self.small = self.parts()
            piece = added(pending)
        else:
            piece = gather_last(self.held, self.order[2 * count - self.stage], 1)
        self.held = gather_first(piece, axis)

    def volume(self):
        return self.held[0].size * 2 / 2**20


class Spread:
    def __init__(self, part, straight):
        self.straight, self.stage = straight, 0
        self.held = [send(rows, INNER, k) if k else rows for k, rows in enumerate(part)]

    def next_axis(self):
        return OUTER

    def over(self):
        return self.stage == (1 if self.straight else 2)

    def go(self):
        self.stage += 1
        if self.straight:
            blocks = [added([piece[k] for piece in self.held]) for k in range(4)]
            self.held = [send(block, OUTER, k) if k else block for k, block in enumerate(blocks)]
            return
        if self.stage == 1:
            pick, offset = (lambda piece, odd: jnp.stack([piece[odd], piece[2 + odd]])), 1
        else:
            pick, offset = (lambda piece, odd: piece[odd]), 2
        mine, theirs = [added([pick(piece, odd) for piece in self.held]) for odd in (0, 1)]
        self.held = [mine, send(theirs, OUTER, offset)]

    def volume(self):
        return self.held[0].size * 2 / 2**20

    def result(self):
        return added(self.held)


def finish(chains, *tokens):
    held, _ = lax.optimization_barrier(([chain.held for chain in chains], tokens))
    for chain, pieces in zip(chains, held):
        chain.held = pieces


def go(*chains):
    for chain in chains:
        chain.go()


FLOW = {CORE: 3.5, X: 21.0, INNER: 21.0, OUTER: 84.0}


def plan_of(chain):
    if isinstance(chain, Spread):
        return [(INNER, 21.0, 1), (OUTER, 10.5, 1), (OUTER, 10.5, 1)][chain.stage :]
    size, out = chain.tiles * 0.5, []
    for axis in chain.order:
        count = lax.axis_size(axis)
        if axis == OUTER and chain.doubled:
            out += [(OUTER, 21.0 * size, 1), (OUTER, 42.0 * size, 1)]
            continue
        size = size / count
        out.append((axis, FLOW[axis] * size, count - 1))
    back = [entry for entry in reversed(out)]
    if chain.doubled:
        back = [entry for entry in back if entry[0] != OUTER]
    return (out + back)[chain.stage :]


def rehearse(plans, first, gate, weights, slack):
    free = dict.fromkeys(FLOW, 0.0)
    position, queue, order, clock, waiting = [0] * len(plans), [], [], 0.0, []

    def depart(index, when):
        axis, long, _ = plans[index][position[index]]
        begin = max(when, free[axis])
        free[axis] = begin + long
        queue.append((free[axis] + 6.0, index))

    def left(index):
        rest = plans[index][position[index] :]
        return weights[index] * sum(long + 10.0 for _, long, _ in rest)

    for index, since in first:
        depart(index, -since)
    while queue or waiting:
        soon = min(queue)[0] if queue else clock + 99.0
        if waiting and soon > clock + 4.0:
            clock += 6.5
            order.append((waiting.pop(0), True))
            continue
        near = [entry for entry in queue if entry[0] <= max(clock, soon) + slack]
        entry = max(near, key=lambda entry: left(entry[1]))
        queue.remove(entry)
        arrival, index = entry
        clock = max(clock, arrival)
        position[index] += 1
        order.append((index, False))
        if position[index] == len(plans[index]):
            clock += 1.0
            waiting.append(index)
            continue
        axis, long, sends = plans[index][position[index]]
        clock += 2.0 + 1.5 * sends + 0.03 * long
        depart(index, clock)
        if gate[1] == index and position[index] == 1:
            clock += 2.0
            depart(gate[0], clock)
    return clock, order


def run_out(flights, later):
    chains, ends = [chain for chain, _, _ in flights], [end for _, _, end in flights]
    plans = [plan_of(chain) for chain in chains]
    plans.append([(INNER, 21.0, 1), (OUTER, 10.5, 1), (OUTER, 10.5, 1)])
    first = [(index, since) for index, (_, since, _) in enumerate(flights)]
    rng, best = random.Random(7), None
    for trial in range(1500):
        weights = [1.0 if trial < 4 else rng.uniform(0.3, 2.0) for _ in plans]
        slack = (0.0, 2.0, 4.0, 8.0)[trial % 4]
        found = rehearse(plans, first, (len(chains), 0), weights, slack)
        if best is None or found[0] < best[0]:
            best = found
    token, results = (), {}
    for index, is_end in best[1]:
        chain = chains[index]
        if is_end:
            results[index] = ends[index](chain, token)
            token = (results[index][0],)
            continue
        finish([chain], *token)
        if chain.over():
            token = tuple(chain.held)
            continue
        chain.go()
        token = (chain.held[0],)
        if index == 0 and chain.stage == 1:
            chain, _, end = later(token)
            chains.append(chain)
            ends.append(end)
    return [results[index] for index in range(len(chains))]


def assemble(chain, core_info, shapes, after=()):
    tiles, half, side = chain.held[0].shape

    places = []
    for name, shape in shapes.items():
        blocks = shape[0] if len(shape) > 2 else shape[0] * shape[1] // (side * side)
        for block in range(blocks):
            if len(shape) > 2:
                places.append((name, lambda rows, b=block: (b, rows, slice(None))))
            elif shape[1] > shape[0]:
                lanes = slice(block * side, (block + 1) * side)
                places.append((name, lambda rows, l=lanes: (rows, l)))
            else:
                places.append((name, lambda rows, b=block: (pl.ds(rows.start + b * side, half), slice(None))))

    def body(info, mine, other, *refs):
        outs = dict(zip(shapes, refs))
        room, full, come, go = refs[len(shapes) :]
        starts = [pl.multiple_of((info[0] ^ flip) * half, half) for flip in (0, 1)]
        arrive, leave = [], []
        for tile in range(tiles):
            for flip, source in enumerate((mine, other)):
                index = 2 * tile + flip
                arrive.append(pltpu.make_async_copy(source.at[tile], room.at[index], come.at[index]))
                arrive[-1].start()
        for tile, (name, where) in enumerate(places):
            for flip in (0, 1):
                index = 2 * tile + flip
                arrive[index].wait()
                full[index] = room[index].astype(F32)
                target = outs[name].at[where(pl.ds(starts[flip], half))]
                leave.append(pltpu.make_async_copy(full.at[index], target, go.at[index]))
                leave[-1].start()
        for copy in leave:
            copy.wait()

    far = pl.BlockSpec(memory_space=pl.ANY)
    return pl.pallas_call(
        lambda info, mine, other, *refs: body(info, mine, other, *refs[len(after) :]),
        in_specs=[pl.BlockSpec(memory_space=pltpu.SMEM)] + [far] * (2 + len(after)),
        out_specs=[far] * len(shapes),
        out_shape=[jax.ShapeDtypeStruct(shape, F32) for shape in shapes.values()],
        scratch_shapes=[
            pltpu.VMEM((2 * tiles, half, side), BF16),
            pltpu.VMEM((2 * tiles, half, side), F32),
            pltpu.SemaphoreType.DMA((2 * tiles,)),
            pltpu.SemaphoreType.DMA((2 * tiles,)),
        ],
        compiler_params=pltpu.CompilerParams(vmem_limit_bytes=VMEM_LIMIT),
        cost_estimate=pl.CostEstimate(flops=5 * 10**9, bytes_accessed=2 * 10**7, transcendentals=0),
    )(core_info, chain.held[0], chain.held[1], *after)


def shards(
    source_short,
    target_short,
    source_segment,
    target_segment,
    source_long,
    target_long,
    source_length,
    target_length,
    cotangent_short,
    cotangent_long,
    encoder_project,
    encoder_output,
    encoder_up,
    encoder_down,
    encoder_gain,
    encoder_bias,
    decoder_project,
    decoder_output,
    cross_project,
    cross_output,
    decoder_up,
    decoder_down,
    decoder_gain,
    decoder_bias,
):
    blocks, size, width = source_short.shape
    hidden = encoder_up.shape[1]
    rows = blocks * size
    pairs, own, _ = source_long.shape
    rows_long = pairs * own
    flat = lambda a: a.reshape(-1, width)
    start = lax.axis_index((OUTER, INNER)) * own
    core = lax.axis_index(CORE)
    here = [start, lax.axis_index(INNER), core, lax.axis_index(OUTER)]
    here = jnp.stack(here).astype(jnp.int32)
    info_of = lambda lengths: jnp.concatenate([lengths, here])
    core_info = core.astype(jnp.int32)[None]
    source_info = info_of(source_length)

    spread = lambda s: jnp.broadcast_to(s[:, :, None], (blocks, size, size))
    line = lambda s: s[:, None, :]
    encoder_in = {
        "w_in": encoder_project,
        "w_o": encoder_output,
        "up": encoder_up,
        "down": encoder_down,
        "gain": encoder_gain,
        "bias": encoder_bias,
    }
    decoder_in = {
        "w_in": decoder_project,
        "w_o": decoder_output,
        "w_cin": cross_project,
        "w_co": cross_output,
        "up": decoder_up,
        "down": decoder_down,
        "gain": decoder_gain,
        "bias": decoder_bias,
    }

    def pick(table, names):
        return {name: table[name] for name in names}

    def rows_of(n, names):
        return {name: ((n, width), BF16) for name in names}

    def wide_of(n, names):
        return {name: ((n, hidden), BF16) for name in names}

    def floats(n, names):
        return {name: ((n, width), F32) for name in names}

    def column(n, names):
        return {name: ((n, 1), F32) for name in names}

    def logs(n, names):
        return {name: ((n, HEADS, size), F32) for name in names}

    def sums(n):
        return {"small": ((n, width), F32)}

    def keys_of(names):
        shape = (places, pairs, own, width)
        return {name: (shape, BF16) for name in names}

    def parts():
        inner = lax.axis_size(INNER)
        return {"p%d" % k: ((places // inner, pairs, own, width), BF16) for k in range(inner)}

    def saved(kernel, names):
        return {name: kernel[name] for name in names}

    whole_source = gather_early(source_long)
    early_target = gather_first(target_long[None, None], OUTER)
    places = lax.axis_size(OUTER) * lax.axis_size(INNER)
    keys = places * own
    work = [
        ("s", pltpu.VMEM((PAIRS, keys, 2 * own), F32)),
        ("a", pltpu.VMEM((PAIRS, 8, 2 * own), F32)),
        ("mix", pltpu.VMEM((PAIRS, PAIR, 2 * own), F32)),
    ]
    mix = work[2:]

    segments = {"kseg": spread(source_segment), "qseg": line(source_segment)}
    turned = {"tkseg": spread(target_segment), "tqseg": line(target_segment)}
    encoder_keeps = lambda n: {
        **rows_of(n, ("n1", "y", "n2", "enc")),
        **wide_of(n, ("act", "gate")),
        **column(n, ("i1", "i2")),
    }
    se = launch(
        short_encoder_forward,
        {"x": flat(source_short), **segments, **encoder_in},
        {**rows_of(rows, ("q", "k", "v", "o")), **logs(blocks, ("lse",)), **encoder_keeps(rows)},
        cost=0.01,
    )
    decoder_keeps = lambda n: {
        **rows_of(n, ("m", "b5", "b4", "go_c")),
        **wide_of(n, ("act", "gate", "dh")),
        **floats(n, ("final", "d4")),
        **sums(4),
    }
    sd = launch(
        short_decoder_forward,
        {
            "t": flat(target_short),
            **turned,
            **pick(decoder_in, ("w_in", "w_o", "gain", "bias")),
        },
        {
            **rows_of(rows, ("q", "k", "v", "o", "n3", "u")),
            **logs(blocks, ("lse",)),
            **column(rows, ("i3",)),
            **floats(rows, ("upper",)),
        },
        after=(se.lse,),
        cost=0.01,
    )
    sc = launch(
        short_cross_forward,
        {
            "u": sd.u,
            "upper": sd.upper,
            "enc": se.enc,
            "cot": flat(cotangent_short),
            "kseg": segments["kseg"],
            "tqseg": turned["tqseg"],
            **pick(decoder_in, ("w_cin", "w_co", "up", "down", "gain", "bias")),
        },
        {
            **rows_of(rows, ("q_c", "k_c", "v_c", "o_c")),
            **logs(blocks, ("lse_c",)),
            **decoder_keeps(rows),
        },
        after=(sd.lse,),
        cost=0.01,
    )

    sb = launch(
        short_decoder_back,
        {
            **saved(sd, ("q", "k", "v", "o", "lse", "n3", "i3")),
            **saved(sc, ("q_c", "k_c", "v_c", "o_c", "lse_c", "go_c", "d4")),
            "kseg": segments["kseg"],
            **turned,
            **pick(decoder_in, ("w_in", "w_o", "w_cin", "gain")),
        },
        {
            **rows_of(rows, ("dq_c", "dk_c", "dv_c", "dq", "dk", "dv", "b3", "go")),
            **floats(rows, ("denc", "dt")),
            **sums(2),
        },
        scratch=[("d3", pltpu.VMEM((rows, width), F32))],
        after=(sc.small,),
        cost=0.01,
    )

    early_target = gather_last(early_target, OUTER, 0, sb.small)

    whole_source = hold(whole_source, sb.small)
    x_long, t_long = flat(source_long), flat(target_long)
    le = launch(
        long_encoder_forward,
        {"x": x_long, "xg": whole_source, **encoder_in},
        {
            **rows_of(rows_long, ("q", "o")),
            **keys_of(("k", "v")),
            **logs(pairs, ("lse",)),
            **encoder_keeps(rows_long),
        },
        scratch=work + [("acc", pltpu.VMEM((rows_long, width), F32))],
        info=source_info,
        after=(sb.small, early_target),
        cost=13,
        moved=(),
    )
    late_target = gather_first(hold(early_target, le.lse), INNER)
    whole_encoded = gather_early(le.enc.reshape(pairs, own, width))

    seb = launch(
        short_encoder_back,
        {
            "denc": sb.denc,
            **saved(se, ("q", "k", "v", "o", "lse", "n1", "i1", "n2", "i2", "gate")),
            **segments,
            **pick(encoder_in, ("w_in", "w_o", "up", "down", "gain")),
        },
        {
            **rows_of(rows, ("dq", "dk", "dv", "b1", "b2", "go")),
            **wide_of(rows, ("dh",)),
            **floats(rows, ("dx",)),
            **sums(4),
        },
        scratch=[("d1", pltpu.VMEM((rows, width), F32))],
        after=(le.lse,),
        cost=16,
    )

    t_short, x_short = flat(target_short), flat(source_short)
    short_weights = whole_tiles(
        [
            [(sc.m, sc.dh), (sc.act, sc.b5)],
            [
                (sd.u, sb.dq_c),
                (se.enc, sb.dk_c),
                (se.enc, sb.dv_c),
                (sc.o_c, sc.b4),
                (t_short, sb.dq),
                (t_short, sb.dk),
                (t_short, sb.dv),
                (sd.o, sb.b3),
            ],
            [(se.y, seb.dh), (se.act, seb.b2)],
            [(x_short, seb.dq), (x_short, seb.dk), (x_short, seb.dv), (se.o, seb.b1)],
        ],
        after=(seb.small,),
        cost=15,
    )
    whole_target = gather_last(late_target, INNER, 1, short_weights[0])
    whole_target = whole_target.reshape(places, pairs, own, width)
    target_info = info_of(hold(target_length, le.lse))
    ls = launch(
        long_self_forward,
        {
            "t": t_long,
            "tg": whole_target,
            **pick(decoder_in, ("w_in", "w_o", "w_cin", "gain", "bias")),
        },
        {
            **rows_of(rows_long, ("q", "o", "n3", "u", "q_c")),
            **keys_of(("k", "v")),
            **logs(pairs, ("lse",)),
            **column(rows_long, ("i3",)),
            **floats(rows_long, ("upper",)),
        },
        scratch=work,
        info=target_info,
        after=(short_weights[0],),
        cost=10,
        moved=(),
    )

    whole_encoded = hold(whole_encoded, ls.lse)
    lc = launch(
        long_cross,
        {
            "eg": whole_encoded,
            "upper": ls.upper,
            "q_c": ls.q_c,
            "cot": flat(cotangent_long),
            **pick(decoder_in, ("w_cin", "w_co", "up", "down", "gain", "bias")),
        },
        {
            **rows_of(rows_long, ("o_c",)),
            **keys_of(("k_c", "v_c")),
            **logs(pairs, ("lse_c",)),
            **decoder_keeps(rows_long),
        },
        scratch=work,
        info=source_info,
        after=(ls.lse,),
        cost=14,
        moved=("k_c", "v_c", "up", "down", "w_co", "act", "gate", "dh", "final"),
    )
    lcb = launch(
        long_cross_back,
        {
            "q_c": ls.q_c,
            **saved(lc, ("k_c", "v_c", "o_c", "lse_c", "go_c")),
            **pick(decoder_in, ("w_cin",)),
        },
        {**rows_of(rows_long, ("dq_c",)), **keys_of(("dk_c", "dv_c")), **parts()},
        scratch=mix,
        info=source_info,
        after=(lc.small,),
        cost=14,
        moved=(),
    )
    encoded_back = Spread(part_refs(lcb), True)
    first_weights = Weights(
        [[(lc.m, lc.dh)], [(lc.act, lc.b5)]], short_weights[0]
    )

    def self_back_and_weights(r):
        long_self_back(r)
        first_weights.body(r, r.info[pairs + 2])

    lsb = launch(
        self_back_and_weights,
        {
            "d4": lc.d4,
            "dq_c": lcb.dq_c,
            **saved(ls, ("q", "k", "v", "o", "lse", "n3", "i3")),
            **pick(decoder_in, ("w_in", "w_o", "w_cin", "gain")),
            **first_weights.arrays,
        },
        {
            **first_weights.gives,
            **rows_of(rows_long, ("dq", "b3")),
            **keys_of(("dk", "dv")),
            **parts(),
            **floats(rows_long, ("dt",)),
            **sums(2),
        },
        scratch=mix + [("go", pltpu.VMEM((rows_long, width), BF16))],
        info=target_info,
        after=(lcb.dq_c,),
        pieces=("kept", "sent"),
        cost=22,
    )
    decoder_ffn = Chain([lsb.kept, lsb.sent], (X, INNER, OUTER))
    finish([encoded_back], lsb.small)
    go(encoded_back)
    target_back = Spread(part_refs(lsb), False)
    grad_attention = weight_tiles(
        [
            [(ls.u, lcb.dq_c)],
            [(flat(whole_encoded), flat(lcb.dk_c))],
            [(flat(whole_encoded), flat(lcb.dv_c))],
            [(lc.o_c, lc.b4)],
            [(t_long, lsb.dq)],
            [(flat(whole_target), flat(lsb.dk))],
            [(flat(whole_target), flat(lsb.dv))],
            [(ls.o, lsb.b3)],
        ],
        core_info,
        after=(lsb.small, encoded_back.held[0]),
        base=short_weights[1],
        cost=15,
    )
    finish([encoded_back, decoder_ffn], grad_attention[0])
    go(decoder_ffn)
    attention = Chain(grad_attention, (INNER, X, OUTER))
    ffn_weights = Weights(
        [
            [(le.y, ("dh", hidden))],
            [(le.act, ("b2", width))],
        ],
        short_weights[2],
        unrolled=True,
    )

    def encoder_back_and_weights(r):
        long_encoder_tail_back(r)
        ffn_weights.body(r, r.info[0])

    leb = launch(
        encoder_back_and_weights,
        {
            **{"part%d" % k: flat(piece) for k, piece in enumerate(encoded_back.held)},
            **saved(le, ("n1", "i1", "n2", "i2", "gate")),
            **pick(encoder_in, ("down", "up", "w_o", "gain")),
            **ffn_weights.arrays,
        },
        {
            **ffn_weights.gives,
            **rows_of(rows_long, ("b1", "b2", "go")),
            **wide_of(rows_long, ("dh",)),
            **floats(rows_long, ("d1",)),
            **sums(4),
        },
        info=core_info,
        after=(grad_attention[0], decoder_ffn.held[0]),
        pieces=("kept", "sent"),
        cost=12,
    )
    small = jnp.concatenate([seb.small + leb.small, sb.small + lsb.small, sc.small + lc.small])
    small = jnp.pad(small, ((0, 16 - small.shape[0]), (0, 0))).astype(BF16)
    finish([attention], leb.small)
    go(attention)
    encoder_ffn = Chain([leb.kept, leb.sent], (X, INNER, OUTER))
    attention_weights = Weights(
        [
            [(x_long, ("dq", width))],
            [(whole_source, ("dk", width))],
            [(whole_source, ("dv", width))],
            [(le.o, leb.b1)],
        ],
        short_weights[3],
    )

    def attention_back_and_weights(r):
        long_encoder_back(r)
        r.leave("dx", *[name for name in r if name[0] == "p" and name[1:].isdigit()])
        attention_weights.body(r, r.info[pairs + 2])

    lea = launch(
        attention_back_and_weights,
        {
            **saved(le, ("q", "k", "v")),
            "o": le.o,
            "lse": le.lse,
            **saved(leb, ("go", "d1")),
            **pick(encoder_in, ("w_in",)),
            **attention_weights.arrays,
        },
        {
            **attention_weights.gives,
            **parts(),
            **floats(rows_long, ("dx",)),
        },
        scratch=mix
        + [
            ("dq", pltpu.VMEM((rows_long, width), BF16)),
            ("dk", pltpu.VMEM((places, pairs, own, width), BF16)),
            ("dv", pltpu.VMEM((places, pairs, own, width), BF16)),
        ],
        info=source_info,
        after=(leb.small, attention.held[0]),
        pieces=("kept", "sent"),
        cost=19,
    )
    done = lea.dx
    finish([decoder_ffn, encoder_ffn, target_back], done)
    encoder = Chain([lea.kept, lea.sent], (INNER, X, OUTER), small, True)
    go(decoder_ffn, encoder_ffn, target_back)
    square = (3, width, width)
    feed = {"up": encoder_up.shape, "down": encoder_down.shape}
    one = {"project": square, "output": square[1:]}
    two = {"cross_in": square, "cross_out": square[1:], "self_in": square, "self_out": square[1:]}

    def out(shapes):
        return lambda chain, token: assemble(chain, core_info, shapes, token)

    rows_out = lambda rows: lambda chain, token: [chain.result().astype(F32) + rows]
    flights = [
        (encoder, 0.0, out(one)),
        (decoder_ffn, 0.0, out(feed)),
        (attention, 20.0, out(two)),
        (encoder_ffn, 0.0, out(feed)),
        (target_back, 0.0, rows_out(lsb.dt.reshape(source_long.shape))),
    ]

    def source_back(token):
        chain = Spread(hold(part_refs(lea), token), False)
        return chain, 0.0, rows_out(lea.dx.reshape(source_long.shape))

    results = run_out(flights, source_back)
    (encoder_in_out, encoder_out_out), (decoder_up_out, decoder_down_out) = results[:2]
    (cross_in, cross_out, self_in, self_out), (encoder_up_out, encoder_down_out) = results[2:4]
    (grad_target,), (grad_source,) = results[4:]
    small = encoder.small.astype(F32)
    return (
        sc.final.reshape(source_short.shape),
        lc.final.reshape(source_long.shape),
        seb.dx.reshape(source_short.shape),
        sb.dt.reshape(source_short.shape),
        grad_source,
        grad_target,
        encoder_in_out,
        encoder_out_out,
        encoder_up_out,
        encoder_down_out,
        small[0:2],
        small[2:4],
        self_in,
        self_out,
        cross_in,
        cross_out,
        decoder_up_out,
        decoder_down_out,
        jnp.stack([small[4], small[6], small[7]]),
        jnp.stack([small[5], small[8], small[9]]),
    )


def solution(mesh):
    group, seq = mesh.devices.shape
    fine = Mesh(
        mesh.devices.reshape(group // 2, 2, 4, seq // 4), (X, CORE, OUTER, INNER)
    )
    groups, positions = (X, CORE), (OUTER, INNER)
    blocks = P(groups + positions, None, None)
    long_rows = P(groups, positions, None)
    in_specs = (
        (blocks, blocks, P(groups + positions, None), P(groups + positions, None))
        + (long_rows, long_rows, P(groups), P(groups), blocks, long_rows)
        + (P(),) * 14
    )
    out_specs = (blocks, long_rows, blocks, blocks, long_rows, long_rows) + (P(),) * 14
    return jax.shard_map(
        shards, mesh=fine, in_specs=in_specs, out_specs=out_specs, check_vma=False
    )
```
